32 devices in a mesh: fsdp: 8 (over z, y), dp: 4 (over x, core).
Axes of the slice: x: 2, y: 2, z: 4, core: 2. Of those that a mesh axis runs over, the one named last changes fastest.
Arguments:
- images: bfloat16 [128, 14, 14, 1024], P(('fsdp', 'dp')), may hold values from -6 to 6
- image_sides: int32 [128], P(('fsdp', 'dp')), may hold values from 0 to 14, as said below
- widths: int32 [2], replicated, may hold values from 128 to 512, as said below
- keep_gate: int32 [128], P(('fsdp', 'dp')), may hold values 0 or 1
- w_in_a: bfloat16 [1024, 512], P('fsdp'), may hold values from -0.1875 to 0.1875
- w_mid_a: bfloat16 [4608, 512], P('fsdp'), may hold values from -0.09375 to 0.09375
- w_out_a: bfloat16 [512, 2048], P('fsdp'), may hold values from -0.25 to 0.25
- w_proj_a: bfloat16 [1024, 2048], P('fsdp'), may hold values from -0.1875 to 0.1875
- norm_in_a: bfloat16 [2, 512], P(None, 'fsdp'), may hold values from -0.5 to 1.5, as said below
- norm_mid_a: bfloat16 [2, 512], P(None, 'fsdp'), may hold values from -0.5 to 1.5, as said below
- norm_out_a: bfloat16 [2, 2048], P(None, 'fsdp'), may hold values from -0.5 to 1.5, as said below
- norm_proj_a: bfloat16 [2, 2048], P(None, 'fsdp'), may hold values from -0.5 to 1.5, as said below
- w_in_b: bfloat16 [2048, 512], P('fsdp'), may hold values from -0.125 to 0.125
- w_mid_b: bfloat16 [4608, 512], P('fsdp'), may hold values from -0.09375 to 0.09375
- w_out_b: bfloat16 [512, 2048], P('fsdp'), may hold values from -0.25 to 0.25
- norm_in_b: bfloat16 [2, 512], P(None, 'fsdp'), may hold values from -0.5 to 1.5, as said below
- norm_mid_b: bfloat16 [2, 512], P(None, 'fsdp'), may hold values from -0.5 to 1.5, as said below
- norm_out_b: bfloat16 [2, 2048], P(None, 'fsdp'), may hold values from -0.5 to 1.5, as said below
- cotangent: bfloat16 [128, 7, 7, 2048], P(('fsdp', 'dp')), may hold values from -6 to 6
Outputs:
- result: bfloat16 [128, 7, 7, 2048], P(('fsdp', 'dp'))
- grad_images: bfloat16 [128, 14, 14, 1024], P(('fsdp', 'dp'))
- grad_w_in_a: float32 [1024, 512], P('fsdp')
- grad_w_mid_a: float32 [4608, 512], P('fsdp')
- grad_w_out_a: float32 [512, 2048], P('fsdp')
- grad_w_proj_a: float32 [1024, 2048], P('fsdp')
- grad_norm_in_a: float32 [2, 512], P(None, 'fsdp')
- grad_norm_mid_a: float32 [2, 512], P(None, 'fsdp')
- grad_norm_out_a: float32 [2, 2048], P(None, 'fsdp')
- grad_norm_proj_a: float32 [2, 2048], P(None, 'fsdp')
- grad_w_in_b: float32 [2048, 512], P('fsdp')
- grad_w_mid_b: float32 [4608, 512], P('fsdp')
- grad_w_out_b: float32 [512, 2048], P('fsdp')
- grad_norm_in_b: float32 [2, 512], P(None, 'fsdp')
- grad_norm_mid_b: float32 [2, 512], P(None, 'fsdp')
- grad_norm_out_b: float32 [2, 2048], P(None, 'fsdp')
The draws below stay inside these ranges and needn't reach their ends.
Inputs may be any that keep to these rules, and one draw needn't show every extreme that they name: `image_sides`: each slot's side is 0 (empty), 10, 12 or 14; on each device the live slots come first and at least 2 of its 4 slots are live; some device has all 4 slots live, one of them of side 14. `widths`: both are multiples of 128, and one of them is 512. `norm_in_a`: row 0 (gains) lies in 0.6 to 1.5, row 1 (shifts) in -0.5 to 0.5. `norm_mid_a`: row 0 (gains) lies in 0.6 to 1.5, row 1 (shifts) in -0.5 to 0.5. `norm_out_a`: row 0 (gains) lies in 0.6 to 1.5, row 1 (shifts) in -0.5 to 0.5. `norm_proj_a`: row 0 (gains) lies in 0.6 to 1.5, row 1 (shifts) in -0.5 to 0.5. `norm_in_b`: row 0 (gains) lies in 0.6 to 1.5, row 1 (shifts) in -0.5 to 0.5. `norm_mid_b`: row 0 (gains) lies in 0.6 to 1.5, row 1 (shifts) in -0.5 to 0.5. `norm_out_b`: row 0 (gains) lies in 0.6 to 1.5, row 1 (shifts) in -0.5 to 0.5.
All inputs are finite; a program needn't handle non-finite values. No bound on the sum of `keep_gate` on one device may be relied on, other than what follows from the above.
Results may differ from the reference program's by a relative error of at most 0.019.
Values may be sent and summed in bfloat16 or wider, within the bound.
A program may use at most 192 MiB of HBM per device.

```python
import jax
import jax.numpy as jnp
from jax import lax

CIN = 1024
MID = 512
COUT = 2048
HIN = 14
HOUT = 7
IMG_DEV = 4
IMAGES = 128


def gain_shift(key, lane_count):
    gain_key, shift_key = jax.random.split(key)
    gains = jax.random.uniform(gain_key, (lane_count,), jnp.float32, 0.6, 1.5)
    shifts = jax.random.uniform(shift_key, (lane_count,), jnp.float32, -0.5, 0.5)
    return jnp.stack([gains, shifts]).astype(jnp.bfloat16)


def draw_image_sides(key, part):
    key = jax.random.fold_in(key, 3)
    device_count = IMAGES // IMG_DEV
    live_key, full_key, side_key = jax.random.split(key, 3)
    live_slots = jax.random.randint(live_key, (device_count,), IMG_DEV // 2, IMG_DEV + 1)
    busiest = jax.random.randint(full_key, (), 0, device_count)
    device_ids = jnp.arange(device_count)
    live_slots = jnp.where(device_ids == busiest, IMG_DEV, live_slots)
    side_picks = jax.random.randint(side_key, (device_count, IMG_DEV), 0, 3)
    side_values = HIN - 4 + 2 * side_picks
    slot_ids = jnp.arange(IMG_DEV)
    side_values = jnp.where((device_ids[:, None] == busiest) & (slot_ids[None, :] == 0), HIN, side_values)
    side_values = jnp.where(slot_ids[None, :] < live_slots[:, None], side_values, 0)
    return side_values.reshape(-1).astype(jnp.int32)


def draw_widths(key, part):
    key = jax.random.fold_in(key, 5)
    pick_key, order_key = jax.random.split(key)
    narrow = jax.random.randint(pick_key, (), 1, 4) * (MID // 4)
    widest = jnp.full((), MID, jnp.int32)
    flipped = jax.random.randint(order_key, (), 0, 2)
    return jnp.where(flipped == 0, jnp.stack([widest, narrow]), jnp.stack([narrow, widest])).astype(jnp.int32)


def draw_norm_in_a(key, part):
    key = jax.random.fold_in(key, 11)
    return gain_shift(key, MID)


def draw_norm_mid_a(key, part):
    key = jax.random.fold_in(key, 12)
    return gain_shift(key, MID)


def draw_norm_out_a(key, part):
    key = jax.random.fold_in(key, 13)
    return gain_shift(key, COUT)


def draw_norm_proj_a(key, part):
    key = jax.random.fold_in(key, 14)
    return gain_shift(key, COUT)


def draw_norm_in_b(key, part):
    key = jax.random.fold_in(key, 15)
    return gain_shift(key, MID)


def draw_norm_mid_b(key, part):
    key = jax.random.fold_in(key, 16)
    return gain_shift(key, MID)


def draw_norm_out_b(key, part):
    key = jax.random.fold_in(key, 17)
    return gain_shift(key, COUT)


def plant(drawn, key, low, top_value):
    dims = drawn.shape
    place = [jax.random.randint(jax.random.fold_in(key, axis), (), 0, dims[axis]) for axis in range(len(dims))]
    drawn = drawn.at[tuple(place)].set(low)
    longest = dims.index(max(dims))
    place[longest] = (place[longest] + 1) % dims[longest]
    return drawn.at[tuple(place)].set(top_value)


def levels(stream_key, extent, cuts, low, high):
    def one(position, blocks):
        heights = jax.random.uniform(jax.random.fold_in(jax.random.fold_in(stream_key, 6), position), (blocks,), jnp.float32, low / len(cuts), high / len(cuts))
        return jnp.repeat(jnp.exp(heights), extent[position] // blocks).reshape((-1,) + (1,) * (len(extent) - position - 1))

    factor_of = one(*cuts[0])
    for cut in cuts[1:]:
        factor_of = factor_of * one(*cut)
    return factor_of


def normal_values(key, dims, spread, reach, shards=(), held_as=jnp.bfloat16):
    factor_of = levels(key, dims, shards, -0.22, 0.18) if shards else 1.0
    values = jax.random.normal(key, dims, jnp.float32) * spread * factor_of
    return jnp.minimum(jnp.maximum(values, -reach), reach).astype(held_as)


def setup_inputs(seed: int = 0) -> dict:
    key_list = jax.random.split(jax.random.key(seed), 20)
    images = normal_values(key_list[0], (IMAGES, HIN, HIN, CIN), 1.0, 6.0, ((0, 32),))
    image_sides = draw_image_sides(jax.random.fold_in(key_list[19], 71), 0)
    widths = draw_widths(jax.random.fold_in(key_list[19], 71), 0)
    keep_gate = plant((jax.random.randint(key_list[3], (IMAGES,), 0, 4) < 3).astype(jnp.int32), jax.random.fold_in(key_list[3], 1), 0, 1)
    w_in_a = normal_values(key_list[4], (CIN, MID), CIN ** -0.5, 0.1875, ((0, 8),))
    w_mid_a = normal_values(key_list[5], (9 * MID, MID), (9 * MID) ** -0.5, 0.09375, ((0, 8),))
    w_out_a = normal_values(key_list[6], (MID, COUT), MID ** -0.5, 0.25, ((0, 8),))
    w_proj_a = normal_values(key_list[7], (CIN, COUT), CIN ** -0.5, 0.1875, ((0, 8),))
    norm_in_a = draw_norm_in_a(jax.random.fold_in(key_list[19], 71), 0)
    norm_mid_a = draw_norm_mid_a(jax.random.fold_in(key_list[19], 71), 0)
    norm_out_a = draw_norm_out_a(jax.random.fold_in(key_list[19], 71), 0)
    norm_proj_a = draw_norm_proj_a(jax.random.fold_in(key_list[19], 71), 0)
    w_in_b = normal_values(key_list[12], (COUT, MID), COUT ** -0.5, 0.125, ((0, 8),))
    w_mid_b = normal_values(key_list[13], (9 * MID, MID), (9 * MID) ** -0.5, 0.09375, ((0, 8),))
    w_out_b = normal_values(key_list[14], (MID, COUT), MID ** -0.5, 0.25, ((0, 8),))
    norm_in_b = draw_norm_in_b(jax.random.fold_in(key_list[19], 71), 0)
    norm_mid_b = draw_norm_mid_b(jax.random.fold_in(key_list[19], 71), 0)
    norm_out_b = draw_norm_out_b(jax.random.fold_in(key_list[19], 71), 0)
    cotangent = normal_values(key_list[18], (IMAGES, HOUT, HOUT, COUT), 1.0, 6.0, ((0, 32),))
    return {"images": images, "image_sides": image_sides, "widths": widths, "keep_gate": keep_gate, "w_in_a": w_in_a, "w_mid_a": w_mid_a, "w_out_a": w_out_a, "w_proj_a": w_proj_a, "norm_in_a": norm_in_a, "norm_mid_a": norm_mid_a, "norm_out_a": norm_out_a, "norm_proj_a": norm_proj_a, "w_in_b": w_in_b, "w_mid_b": w_mid_b, "w_out_b": w_out_b, "norm_in_b": norm_in_b, "norm_mid_b": norm_mid_b, "norm_out_b": norm_out_b, "cotangent": cotangent}


EPSILON = 1e-05

@jax.custom_vjp
def low(v):
    return lax.optimization_barrier(v.astype(jnp.bfloat16)).astype(jnp.float32)

@jax.custom_vjp
def low_back(v):
    return v

def low_keep(v):
    return (low(v), None)

def low_pass(kept, grad):
    return (grad,)

def back_keep(v):
    return (v, None)

def back_low(kept, grad):
    return (low(grad),)
low.defvjp(low_keep, low_pass)
low_back.defvjp(back_keep, back_low)

def pixel_masks(image_sides):
    half_sides = image_sides // 2
    rows_in = jnp.arange(HIN, dtype=jnp.int32)
    rows_out = jnp.arange(HOUT, dtype=jnp.int32)
    inside_in = (rows_in[None, :, None] < image_sides[:, None, None]) & (rows_in[None, None, :] < image_sides[:, None, None])
    inside_out = (rows_out[None, :, None] < half_sides[:, None, None]) & (rows_out[None, None, :] < half_sides[:, None, None])
    count_in = jnp.sum(image_sides * image_sides).astype(jnp.float32)
    count_out = jnp.sum(half_sides * half_sides).astype(jnp.float32)
    return (inside_in.astype(jnp.float32)[..., None], inside_out.astype(jnp.float32)[..., None], count_in, count_out)

def batch_norm(hidden, pixel_mask, pixel_total, params, channel):
    sum_values = lax.optimization_barrier(jnp.sum(hidden * pixel_mask, axis=(0, 1, 2)))
    sum_squares = lax.optimization_barrier(jnp.sum(hidden * hidden * pixel_mask, axis=(0, 1, 2)))
    average = sum_values / pixel_total
    inv_std = lax.rsqrt(sum_squares / pixel_total - average * average + EPSILON)
    return ((hidden - average) * inv_std * params[0] + params[1]) * channel

def conv_three(activations, weight, stride):
    kernel = weight.reshape(3, 3, weight.shape[1], weight.shape[1])
    return lax.conv_general_dilated(activations, kernel, (stride, stride), ((1, 1), (1, 1)), dimension_numbers=('NHWC', 'HWIO', 'NHWC'), precision=lax.Precision.HIGHEST)

def project(activations, weight):
    return jnp.einsum('nhwc,cd->nhwd', activations, weight, precision=lax.Precision.HIGHEST)

def reference(images, image_sides, widths, keep_gate, w_in_a, w_mid_a, w_out_a, w_proj_a, norm_in_a, norm_mid_a, norm_out_a, norm_proj_a, w_in_b, w_mid_b, w_out_b, norm_in_b, norm_mid_b, norm_out_b, cotangent):
    mask_in, mask_out, count_in, count_out = pixel_masks(image_sides)
    lane_ids = jnp.arange(MID, dtype=jnp.int32)
    chan_a = (lane_ids < widths[0]).astype(jnp.float32)
    chan_b = (lane_ids < widths[1]).astype(jnp.float32)
    depth_gate = keep_gate.astype(jnp.float32)[:, None, None, None]

    def forward(pixels, wia, wma, woa, wpa, nia, nma, noa, npa, wib, wmb, wob, nib, nmb, nob):
        inputs = pixels * mask_in
        conv_first = low_back(project(inputs, wia))
        act_first = low(jax.nn.silu(batch_norm(conv_first, mask_in, count_in, nia, chan_a)) * mask_in)
        conv_mid = low_back(conv_three(act_first, wma, 2))
        act_mid = low(jax.nn.silu(batch_norm(conv_mid, mask_out, count_out, nma, chan_a)) * mask_out)
        conv_out = low_back(project(act_mid, woa))
        conv_proj = low_back(project(inputs[:, ::2, ::2, :], wpa))
        pre_a = batch_norm(conv_out, mask_out, count_out, noa, 1.0) + batch_norm(conv_proj, mask_out, count_out, npa, 1.0)
        block_out = jax.nn.silu(pre_a) * mask_out
        feed_in = low(block_out)
        second_first = low_back(project(feed_in, wib))
        second_act = low(jax.nn.silu(batch_norm(second_first, mask_out, count_out, nib, chan_b)) * mask_out)
        second_mid = low_back(conv_three(second_act, wmb, 1))
        second_act_mid = low(jax.nn.silu(batch_norm(second_mid, mask_out, count_out, nmb, chan_b)) * mask_out)
        second_out = low_back(project(second_act_mid, wob))
        pre_b = block_out + depth_gate * batch_norm(second_out, mask_out, count_out, nob, 1.0)
        return jax.nn.silu(pre_b) * mask_out
    floats = [values.astype(jnp.float32) for values in (images, w_in_a, w_mid_a, w_out_a, w_proj_a, norm_in_a, norm_mid_a, norm_out_a, norm_proj_a, w_in_b, w_mid_b, w_out_b, norm_in_b, norm_mid_b, norm_out_b)]
    result, pullback = jax.vjp(forward, *floats)
    gradients = pullback(cotangent.astype(jnp.float32))
    return (result.astype(jnp.bfloat16), gradients[0].astype(jnp.bfloat16), gradients[1], gradients[2], gradients[3], gradients[4], gradients[5], gradients[6], gradients[7], gradients[8], gradients[9], gradients[10], gradients[11], gradients[12], gradients[13], gradients[14])
```

```python
import functools

import jax
import jax.numpy as jnp
from jax import lax
from jax.experimental import pallas as pl
from jax.experimental.pallas import tpu as pltpu
from jax.sharding import PartitionSpec as P

EPSILON = 1e-05
BY_MESH = pl.DeviceIdType.MESH


def flip(index, bits):
    out = index
    for bit in (1, 2, 4):
        if bits & bit:
            out = out + bit - 2 * bit * ((index // bit) % 2)
    return out


class Place:
    def __init__(self):
        self.f = lax.axis_index("fsdp")
        self.d = lax.axis_index("dp")
        self.y = self.f % 2
        self.z = self.f // 2
        self.c = self.d % 2
        self.x = self.d // 2

    def peer(self, f_bits, d_bits):
        return (flip(self.f, f_bits), flip(self.d, d_bits))


def enter(place, peers):
    barrier = pltpu.get_barrier_semaphore()
    for f_bits, d_bits in peers:
        pl.semaphore_signal(barrier, inc=1, device_id=place.peer(f_bits, d_bits), device_id_type=BY_MESH)
    pl.semaphore_wait(barrier, len(peers))


def push(source, target, send_sem, recv_sem, device):
    pltpu.make_async_remote_copy(
        src_ref=source,
        dst_ref=target,
        send_sem=send_sem,
        recv_sem=recv_sem,
        device_id=device,
        device_id_type=BY_MESH,
    ).start()


def await_bytes(view, sem):
    pltpu.make_async_copy(view, view, sem).wait()


def rows_of(start, size):
    return pl.ds(pl.multiple_of(start, 16), size)


def cols_of(start, size):
    return pl.ds(pl.multiple_of(start, 128), size)


LINK_PEERS = ((2, 0), (4, 0), (6, 0), (1, 0), (0, 2), (0, 1))


def split_of(columns):
    half = columns // 2
    return half // 2


def gather_steps(place, shard, whole, local_sem, send, recv):
    rows, columns = shard.shape
    half = columns // 2
    wide_a = split_of(columns)
    wide_b = half - wide_a
    part = rows // 2
    col_0 = place.c * half
    col_b = col_0 + wide_a
    row_q = place.x * part
    mine = place.f * rows
    pltpu.make_async_copy(
        shard.at[:, cols_of(col_0, half)], whole.at[rows_of(mine, rows), cols_of(col_0, half)], local_sem
    ).start()
    for bits in (2, 4, 6):
        push(
            shard.at[rows_of(row_q, part), cols_of(col_0, half)],
            whole.at[rows_of(mine + row_q, part), cols_of(col_0, half)],
            send.at[0],
            recv.at[0],
            place.peer(bits, 0),
        )
    yield
    await_bytes(whole.at[pl.ds(0, rows), pl.ds(0, half)], local_sem)
    await_bytes(whole.at[pl.ds(0, 3 * part), pl.ds(0, half)], recv.at[0])
    for bits in (0, 2, 4, 6):
        block = whole.at[rows_of(flip(place.f, bits) * rows + row_q, part), cols_of(col_0, wide_a)]
        push(block, block, send.at[1], recv.at[1], place.peer(1, 0))
    for bits in (2, 4, 6):
        block = whole.at[rows_of(flip(place.f, bits) * rows + row_q, part), cols_of(col_b, wide_b)]
        push(block, block, send.at[2], recv.at[2], place.peer(0, 2))
    yield
    await_bytes(whole.at[pl.ds(0, 4 * part), pl.ds(0, wide_a)], recv.at[1])
    await_bytes(whole.at[pl.ds(0, 3 * part), pl.ds(0, wide_b)], recv.at[2])
    for bits in range(1, 8):
        block = whole.at[rows_of(flip(place.f, bits) * rows + row_q, part), cols_of(col_0, wide_a)]
        push(block, block, send.at[3], recv.at[3], place.peer(0, 2))
    for bits in (0, 2, 4, 6):
        block = whole.at[rows_of(flip(place.f, bits) * rows, rows), cols_of(col_b, wide_b)]
        push(block, block, send.at[4], recv.at[4], place.peer(1, 0))
    yield
    await_bytes(whole.at[pl.ds(0, 7 * part), pl.ds(0, wide_a)], recv.at[3])
    await_bytes(whole.at[pl.ds(0, 4 * rows), pl.ds(0, wide_b)], recv.at[4])
    block = whole.at[:, cols_of(col_0, half)]
    push(block, block, send.at[5], recv.at[5], place.peer(0, 1))
    yield
    await_bytes(whole.at[:, pl.ds(0, half)], recv.at[5])


def gather_sent(shard, whole, send):
    rows, columns = shard.shape
    half = columns // 2
    wide_a = split_of(columns)
    wide_b = half - wide_a
    part = rows // 2
    await_bytes(whole.at[pl.ds(0, 3 * part), pl.ds(0, half)], send.at[0])
    await_bytes(whole.at[pl.ds(0, 4 * part), pl.ds(0, wide_a)], send.at[1])
    await_bytes(whole.at[pl.ds(0, 3 * part), pl.ds(0, wide_b)], send.at[2])
    await_bytes(whole.at[pl.ds(0, 7 * part), pl.ds(0, wide_a)], send.at[3])
    await_bytes(whole.at[pl.ds(0, 4 * rows), pl.ds(0, wide_b)], send.at[4])
    await_bytes(whole.at[:, pl.ds(0, half)], send.at[5])


def add_rows(target, source, total, chunk):
    def step(index, carry):
        start = pl.multiple_of(index * chunk, chunk)
        into = target(start, chunk)
        into[...] = (into[...].astype(jnp.float32) + source(start, chunk)[...].astype(jnp.float32)).astype(into.dtype)
        return carry

    lax.fori_loop(0, total // chunk, step, 0)


def scatter_steps(place, grad, room, out, send, recv):
    from_core, from_x, from_y, from_y2, from_x2, from_z = room
    total_rows, columns = grad.shape
    rows = total_rows // 8
    half = columns // 2
    wide_a = split_of(columns)
    wide_b = half - wide_a
    part = rows // 2
    col_0 = place.c * half
    col_1 = half - col_0
    row_q = place.x * part
    row_o = part - row_q
    chunk = 32 if part % 32 == 0 else 16
    push(grad.at[:, cols_of(col_1, half)], from_core, send.at[0], recv.at[0], place.peer(0, 1))
    yield
    await_bytes(from_core, recv.at[0])
    add_rows(
        lambda s, n: from_core.at[pl.ds(s, n)],
        lambda s, n: grad.at[pl.ds(s, n), cols_of(col_0, half)],
        total_rows,
        chunk,
    )
    for block in range(8):
        push(
            from_core.at[rows_of(block * rows + row_o, part), pl.ds(0, wide_a)],
            from_x.at[pl.ds(block * part, part)],
            send.at[1],
            recv.at[1],
            place.peer(0, 2),
        )
    for level in range(4):
        push(
            from_core.at[rows_of((2 * level + 1 - place.y) * rows, rows), pl.ds(wide_a, wide_b)],
            from_y.at[pl.ds(level * rows, rows)],
            send.at[2],
            recv.at[2],
            place.peer(1, 0),
        )
    yield
    await_bytes(from_x, recv.at[1])
    await_bytes(from_y, recv.at[2])

    def fold_x(block, carry):
        add_rows(
            lambda s, n: from_core.at[rows_of(block * rows + row_q + s, n), pl.ds(0, wide_a)],
            lambda s, n: from_x.at[rows_of(block * part + s, n)],
            part,
            chunk,
        )
        return carry

    lax.fori_loop(0, 8, fold_x, 0)

    def fold_y(level, carry):
        add_rows(
            lambda s, n: from_core.at[rows_of((2 * level + place.y) * rows + s, n), pl.ds(wide_a, wide_b)],
            lambda s, n: from_y.at[rows_of(level * rows + s, n)],
            rows,
            chunk,
        )
        return carry

    lax.fori_loop(0, 4, fold_y, 0)
    for level in range(4):
        push(
            from_core.at[rows_of((2 * level + 1 - place.y) * rows + row_q, part), pl.ds(0, wide_a)],
            from_y2.at[pl.ds(level * part, part)],
            send.at[3],
            recv.at[3],
            place.peer(1, 0),
        )
        push(
            from_core.at[rows_of((2 * level + place.y) * rows + row_o, part), pl.ds(wide_a, wide_b)],
            from_x2.at[pl.ds(level * part, part)],
            send.at[4],
            recv.at[4],
            place.peer(0, 2),
        )
    yield
    await_bytes(from_y2, recv.at[3])
    await_bytes(from_x2, recv.at[4])

    def fold_last(level, carry):
        own = (2 * level + place.y) * rows + row_q
        add_rows(
            lambda s, n: from_core.at[rows_of(own + s, n), pl.ds(0, wide_a)],
            lambda s, n: from_y2.at[rows_of(level * part + s, n)],
            part,
            chunk,
        )
        add_rows(
            lambda s, n: from_core.at[rows_of(own + s, n), pl.ds(wide_a, wide_b)],
            lambda s, n: from_x2.at[rows_of(level * part + s, n)],
            part,
            chunk,
        )
        return carry

    lax.fori_loop(0, 4, fold_last, 0)
    for slot, bits in enumerate((2, 4, 6)):
        push(
            from_core.at[rows_of(flip(place.f, bits) * rows + row_q, part)],
            from_z.at[pl.ds(slot * part, part)],
            send.at[5],
            recv.at[5],
            place.peer(bits, 0),
        )
    yield
    await_bytes(from_z, recv.at[5])

    def fold_z(index, carry):
        start = pl.multiple_of(index * chunk, chunk)
        total = from_core[rows_of(place.f * rows + row_q + start, chunk)].astype(jnp.float32)
        for slot in range(3):
            total = total + from_z[rows_of(slot * part + start, chunk)].astype(jnp.float32)
        out[rows_of(row_q + start, chunk), cols_of(col_0, half)] = total.astype(out.dtype)
        return carry

    lax.fori_loop(0, part // chunk, fold_z, 0)
    block = out.at[rows_of(row_q, part), cols_of(col_0, half)]
    push(block, block, send.at[6], recv.at[6], place.peer(0, 2))
    yield
    await_bytes(out.at[pl.ds(0, part), pl.ds(0, half)], recv.at[6])
    block = out.at[:, cols_of(col_0, half)]
    push(block, block, send.at[7], recv.at[7], place.peer(0, 1))
    yield
    await_bytes(out.at[:, pl.ds(0, half)], recv.at[7])


def scatter_sent(grad, room, out, send):
    from_core, from_x, from_y, from_y2, from_x2, from_z = room
    half = grad.shape[1] // 2
    for index, view in enumerate((from_core, from_x, from_y, from_y2, from_x2, from_z)):
        await_bytes(view, send.at[index])
    await_bytes(out.at[pl.ds(0, out.shape[0] // 2), pl.ds(0, half)], send.at[6])
    await_bytes(out.at[:, pl.ds(0, half)], send.at[7])


def room_shapes(total_rows, columns):
    rows = total_rows // 8
    half = columns // 2
    wide_a = split_of(columns)
    wide_b = half - wide_a
    part = rows // 2
    return [
        (8 * rows, half),
        (8 * part, wide_a),
        (4 * rows, wide_b),
        (4 * part, wide_a),
        (4 * part, wide_b),
        (3 * part, half),
    ]


def run_staggered(steps):
    alive = list(steps)
    for one in alive:
        next(one)
    begun = 0
    while any(one is not None for one in alive):
        begun += 1
        for index in range(min(begun, len(alive))):
            if alive[index] is not None and next(alive[index], "end") == "end":
                alive[index] = None


def gather_kernel(*refs):
    shards, wholes = refs[:7], refs[7:14]
    local_sem, send, recv = refs[14:]
    place = Place()
    enter(place, LINK_PEERS)
    run_staggered(
        [
            gather_steps(place, shards[i], wholes[i], local_sem.at[i], send.at[i], recv.at[i])
            for i in range(7)
        ]
    )
    for i in range(7):
        gather_sent(shards[i], wholes[i], send.at[i])


def gather_all(shards):
    shapes = [(8 * one.shape[0], one.shape[1]) for one in shards]
    return pl.pallas_call(
        gather_kernel,
        out_shape=[jax.ShapeDtypeStruct(shape, jnp.bfloat16) for shape in shapes],
        in_specs=[pl.BlockSpec(memory_space=pl.ANY)] * 7,
        out_specs=[pl.BlockSpec(memory_space=pltpu.VMEM)] * 7,
        scratch_shapes=[
            pltpu.SemaphoreType.DMA((7,)),
            pltpu.SemaphoreType.DMA((7, 6)),
            pltpu.SemaphoreType.DMA((7, 6)),
        ],
        compiler_params=pltpu.CompilerParams(
            collective_id=0, has_side_effects=True, vmem_limit_bytes=60 * 2**20
        ),
        name="gather_weights",
    )(*shards)


def scatter_kernel(*refs):
    grads, outs = refs[:7], refs[7:14]
    rooms = [refs[14 + 6 * i : 20 + 6 * i] for i in range(7)]
    send, recv = refs[14 + 42 :]
    place = Place()
    enter(place, LINK_PEERS)
    run_staggered(
        [scatter_steps(place, grads[i], rooms[i], outs[i], send.at[i], recv.at[i]) for i in range(7)]
    )
    for i in range(7):
        scatter_sent(grads[i], rooms[i], outs[i], send.at[i])


def scatter_all(grads):
    shapes = [(one.shape[0] // 8, one.shape[1]) for one in grads]
    return pl.pallas_call(
        scatter_kernel,
        out_shape=[jax.ShapeDtypeStruct(shape, jnp.bfloat16) for shape in shapes],
        in_specs=[pl.BlockSpec(memory_space=pltpu.VMEM)] * 7,
        out_specs=[pl.BlockSpec(memory_space=pltpu.VMEM)] * 7,
        scratch_shapes=[
            pltpu.VMEM(shape, jnp.bfloat16) for one in grads for shape in room_shapes(*one.shape)
        ]
        + [pltpu.SemaphoreType.DMA((7, 8)), pltpu.SemaphoreType.DMA((7, 8))],
        compiler_params=pltpu.CompilerParams(
            collective_id=1, has_side_effects=True, vmem_limit_bytes=62 * 2**20
        ),
        name="scatter_grads",
    )(*grads)


SUM_PEERS = ((0, 1), (0, 2), (0, 3), (1, 0), (2, 0), (3, 0), (4, 0), (5, 0), (6, 0), (7, 0))


def sum_everywhere(place, near, far, send, recv):
    own = near.at[place.d]
    for bits in (1, 2, 3):
        push(own, own, send.at[0], recv.at[0], place.peer(0, bits))
    await_bytes(near.at[pl.ds(0, 3)], recv.at[0])
    own_far = far.at[place.f]
    own_far[...] = (near[0] + near[1]) + (near[2] + near[3])
    for bits in range(1, 8):
        push(own_far, own_far, send.at[1], recv.at[1], place.peer(bits, 0))
    await_bytes(far.at[pl.ds(0, 7)], recv.at[1])
    total = far[0]
    for index in range(1, 8):
        total = total + far[index]
    await_bytes(near.at[pl.ds(0, 3)], send.at[0])
    await_bytes(far.at[pl.ds(0, 7)], send.at[1])
    return total


def sum_kernel(local, out, near, far, send, recv):
    place = Place()
    near[place.d] = local[...]
    enter(place, SUM_PEERS)
    out[...] = sum_everywhere(place, near, far, send, recv)


def sum_call(local, index):
    rows = local.shape[0]
    return pl.pallas_call(
        sum_kernel,
        out_shape=jax.ShapeDtypeStruct(local.shape, jnp.float32),
        in_specs=[pl.BlockSpec(memory_space=pltpu.VMEM)],
        out_specs=pl.BlockSpec(memory_space=pltpu.VMEM),
        scratch_shapes=[
            pltpu.VMEM((4, rows, 128), jnp.float32),
            pltpu.VMEM((8, rows, 128), jnp.float32),
            pltpu.SemaphoreType.DMA((2,)),
            pltpu.SemaphoreType.DMA((2,)),
        ],
        compiler_params=pltpu.CompilerParams(collective_id=2 + index, has_side_effects=True),
        name="sum_all",
    )(local)


def gather_plain(shards):
    return [lax.all_gather(one, "fsdp", axis=0, tiled=True) for one in shards]


def scatter_plain(grads):
    parts = [lax.psum_scatter(one, "fsdp", scatter_dimension=0, tiled=True) for one in grads]
    return lax.psum(tuple(parts), "dp")


MODE = {"fast": True, "calls": 0}


def sum_pair(first, second):
    width = first.shape[0]
    if not MODE["fast"]:
        return lax.psum((first, second), ("fsdp", "dp"))
    packed = jnp.concatenate([first, second]).reshape(2 * width // 128, 128)
    MODE["calls"] += 1
    total = sum_call(packed, MODE["calls"] - 1).reshape(2, width)
    return total[0], total[1]


def silu_slope(values):
    sigmoid_part = jax.nn.sigmoid(values)
    return sigmoid_part * (1.0 + values * (1.0 - sigmoid_part))


def pixel_masks(image_sides, side_in, side_out):
    half_sides = image_sides // 2
    rows_in = jnp.arange(side_in, dtype=jnp.int32)
    rows_out = jnp.arange(side_out, dtype=jnp.int32)
    inside_in = (rows_in[None, :, None] < image_sides[:, None, None]) & (
        rows_in[None, None, :] < image_sides[:, None, None]
    )
    inside_out = (rows_out[None, :, None] < half_sides[:, None, None]) & (
        rows_out[None, None, :] < half_sides[:, None, None]
    )
    local_counts = jnp.stack(
        [jnp.sum(image_sides * image_sides), jnp.sum(half_sides * half_sides)]
    ).astype(jnp.float32)
    return (
        inside_in.astype(jnp.float32)[..., None],
        inside_out.astype(jnp.float32)[..., None],
        local_counts,
    )


def norm_stats(hidden, pixel_mask, local_counts, count_slot):
    sum_values, sum_squares = sum_pair(
        jnp.sum(hidden * pixel_mask, axis=(0, 1, 2)),
        jnp.sum(hidden * hidden * pixel_mask, axis=(0, 1, 2)),
    )
    pixel_total = local_counts[count_slot]
    average = sum_values / pixel_total
    inv_std = lax.rsqrt(sum_squares / pixel_total - average * average + EPSILON)
    return (average, inv_std, pixel_total)


def normalize(hidden, stats_now, params, channel):
    average, inv_std, pixel_total = stats_now
    scaled = (hidden - average) * inv_std
    params_wide = params.astype(jnp.float32)
    return (scaled, (scaled * params_wide[0] + params_wide[1]) * channel)


def norm_backward(grad_norm, scaled, stats_now, params, pixel_mask):
    average, inv_std, pixel_total = stats_now
    shift_sum, gain_sum = sum_pair(
        jnp.sum(grad_norm, axis=(0, 1, 2)), jnp.sum(grad_norm * scaled, axis=(0, 1, 2))
    )
    gain_row = params[0].astype(jnp.float32)
    grad_hidden = (
        gain_row
        * inv_std
        * (grad_norm - shift_sum / pixel_total - scaled * gain_sum / pixel_total)
        * pixel_mask
    )
    return (grad_hidden.astype(jnp.bfloat16), gain_sum, shift_sum)


def taps_stride_two(activations):
    slot_count = activations.shape[0]
    half_side = activations.shape[1] // 2
    lane_count = activations.shape[3]
    padded = jnp.pad(activations, ((0, 0), (1, 1), (1, 1), (0, 0)))
    parity_grid = padded.reshape(slot_count, half_side + 1, 2, half_side + 1, 2, lane_count)
    pieces = [
        parity_grid[
            :,
            row_tap // 2 : row_tap // 2 + half_side,
            row_tap % 2,
            col_tap // 2 : col_tap // 2 + half_side,
            col_tap % 2,
            :,
        ]
        for row_tap in range(3)
        for col_tap in range(3)
    ]
    return jnp.concatenate(pieces, axis=-1)


def fold_stride_two(grad_cols, side_in):
    slot_count = grad_cols.shape[0]
    half_side = grad_cols.shape[1]
    lane_count = grad_cols.shape[3] // 9
    planes = [
        [
            jnp.zeros((slot_count, half_side + 1, half_side + 1, lane_count), jnp.float32)
            for col_par in range(2)
        ]
        for row_par in range(2)
    ]
    for row_tap in range(3):
        for col_tap in range(3):
            tap_index = row_tap * 3 + col_tap
            tap_piece = grad_cols[..., tap_index * lane_count : (tap_index + 1) * lane_count]
            placed = jnp.pad(
                tap_piece,
                (
                    (0, 0),
                    (row_tap // 2, 1 - row_tap // 2),
                    (col_tap // 2, 1 - col_tap // 2),
                    (0, 0),
                ),
            )
            planes[row_tap % 2][col_tap % 2] = planes[row_tap % 2][col_tap % 2] + placed
    parity_grid = jnp.stack([jnp.stack(planes[0], axis=3), jnp.stack(planes[1], axis=3)], axis=2)
    whole_grid = parity_grid.reshape(slot_count, side_in + 2, side_in + 2, lane_count)
    return whole_grid[:, 1:-1, 1:-1, :]


def taps_stride_one(activations):
    side_now = activations.shape[1]
    padded = jnp.pad(activations, ((0, 0), (1, 1), (1, 1), (0, 0)))
    pieces = [
        padded[:, row_tap : row_tap + side_now, col_tap : col_tap + side_now, :]
        for row_tap in range(3)
        for col_tap in range(3)
    ]
    return jnp.concatenate(pieces, axis=-1)


def fold_stride_one(grad_cols):
    lane_count = grad_cols.shape[3] // 9
    whole_grid = None
    for row_tap in range(3):
        for col_tap in range(3):
            tap_index = row_tap * 3 + col_tap
            tap_piece = grad_cols[..., tap_index * lane_count : (tap_index + 1) * lane_count]
            placed = jnp.pad(
                tap_piece, ((0, 0), (row_tap, 2 - row_tap), (col_tap, 2 - col_tap), (0, 0))
            )
            whole_grid = placed if whole_grid is None else whole_grid + placed
    return whole_grid[:, 1:-1, 1:-1, :]


def contract(left_side, right_side):
    return lax.dot_general(
        left_side,
        right_side,
        (((0, 1, 2), (0, 1, 2)), ((), ())),
        preferred_element_type=jnp.float32,
    )


def back_project(gradient, weight):
    return lax.dot_general(
        gradient, weight, (((3,), (1,)), ((), ())), preferred_element_type=jnp.float32
    )


def own_shard(pair_sums):
    gain_sum, shift_sum = pair_sums
    shard_width = gain_sum.shape[0] // lax.axis_size("fsdp")
    offset = lax.axis_index("fsdp") * shard_width
    return jnp.stack(
        [
            lax.dynamic_slice_in_dim(gain_sum, offset, shard_width, 0),
            lax.dynamic_slice_in_dim(shift_sum, offset, shard_width, 0),
        ]
    )


def block_a_forward(inputs, weights, mask_in, mask_out, local_counts, channel, saved_stats):
    w_in, w_mid, w_out, w_proj, norm_in, norm_mid, norm_out, norm_proj = weights
    conv_first = jnp.dot(inputs, w_in, preferred_element_type=jnp.float32)
    stats_first = (
        norm_stats(conv_first, mask_in, local_counts, 0) if saved_stats is None else saved_stats[0]
    )
    scaled_first, normed_first = normalize(conv_first, stats_first, norm_in, channel)
    act_first = (jax.nn.silu(normed_first) * mask_in).astype(jnp.bfloat16)
    cols_mid = taps_stride_two(act_first)
    conv_mid = jnp.dot(cols_mid, w_mid, preferred_element_type=jnp.float32)
    stats_mid = (
        norm_stats(conv_mid, mask_out, local_counts, 1) if saved_stats is None else saved_stats[1]
    )
    scaled_mid, normed_mid = normalize(conv_mid, stats_mid, norm_mid, channel)
    act_mid = (jax.nn.silu(normed_mid) * mask_out).astype(jnp.bfloat16)
    conv_out = jnp.dot(act_mid, w_out, preferred_element_type=jnp.float32)
    slot_count, side_in, lane_count = (inputs.shape[0], inputs.shape[1], inputs.shape[3])
    sampled = inputs.reshape(slot_count, side_in // 2, 2, side_in // 2, 2, lane_count)[
        :, :, 0, :, 0, :
    ]
    conv_proj = jnp.dot(sampled, w_proj, preferred_element_type=jnp.float32)
    conv_both = jnp.concatenate([conv_out, conv_proj], axis=-1)
    norm_both = jnp.concatenate([norm_out, norm_proj], axis=-1)
    stats_both = (
        norm_stats(conv_both, mask_out, local_counts, 1) if saved_stats is None else saved_stats[2]
    )
    scaled_both, normed_both = normalize(conv_both, stats_both, norm_both, 1.0)
    width_out = conv_out.shape[-1]
    pre_sum = normed_both[..., :width_out] + normed_both[..., width_out:]
    block_out = jax.nn.silu(pre_sum) * mask_out
    saved_values = (
        scaled_first,
        normed_first,
        act_first,
        cols_mid,
        scaled_mid,
        normed_mid,
        act_mid,
        sampled,
        scaled_both,
        pre_sum,
    )
    return (block_out, (stats_first, stats_mid, stats_both), saved_values)


def block_a_backward(
    grad_out, inputs, weights, stats_all, saved_values, mask_in, mask_out, channel
):
    w_in, w_mid, w_out, w_proj, norm_in, norm_mid, norm_out, norm_proj = weights
    stats_first, stats_mid, stats_both = stats_all
    (
        scaled_first,
        normed_first,
        act_first,
        cols_mid,
        scaled_mid,
        normed_mid,
        act_mid,
        sampled,
        scaled_both,
        pre_sum,
    ) = saved_values
    grad_pre = grad_out * mask_out * silu_slope(pre_sum)
    grad_both = jnp.concatenate([grad_pre, grad_pre], axis=-1)
    norm_both = jnp.concatenate([norm_out, norm_proj], axis=-1)
    low_both, gain_both, shift_both = norm_backward(
        grad_both, scaled_both, stats_both, norm_both, mask_out
    )
    width_out = grad_pre.shape[-1]
    low_out = low_both[..., :width_out]
    low_proj = low_both[..., width_out:]
    grad_w_out = contract(act_mid, low_out)
    grad_w_proj = contract(sampled, low_proj)
    grad_norm_mid = back_project(low_out, w_out) * mask_out * channel * silu_slope(normed_mid)
    low_mid, gain_mid, shift_mid = norm_backward(
        grad_norm_mid, scaled_mid, stats_mid, norm_mid, mask_out
    )
    grad_w_mid = contract(cols_mid, low_mid)
    grad_act_first = fold_stride_two(back_project(low_mid, w_mid), inputs.shape[1])
    grad_norm_first = grad_act_first * mask_in * channel * silu_slope(normed_first)
    low_first, gain_first, shift_first = norm_backward(
        grad_norm_first, scaled_first, stats_first, norm_in, mask_in
    )
    grad_w_in = contract(inputs, low_first)
    spread = lax.pad(
        back_project(low_proj, w_proj),
        jnp.float32(0.0),
        ((0, 0, 0), (0, 1, 1), (0, 1, 1), (0, 0, 0)),
    )
    grad_inputs = (back_project(low_first, w_in) + spread) * mask_in
    norm_grads = (
        (gain_first, shift_first),
        (gain_mid, shift_mid),
        (gain_both[:width_out], shift_both[:width_out]),
        (gain_both[width_out:], shift_both[width_out:]),
    )
    return (grad_inputs, (grad_w_in, grad_w_mid, grad_w_out, grad_w_proj), norm_grads)


def block_b_forward(block_in, weights, mask_out, local_counts, channel, depth_gate, saved_stats):
    w_in, w_mid, w_out, norm_in, norm_mid, norm_out = weights
    feed_in = block_in.astype(jnp.bfloat16)
    conv_first = jnp.dot(feed_in, w_in, preferred_element_type=jnp.float32)
    stats_first = (
        norm_stats(conv_first, mask_out, local_counts, 1) if saved_stats is None else saved_stats[0]
    )
    scaled_first, normed_first = normalize(conv_first, stats_first, norm_in, channel)
    act_first = (jax.nn.silu(normed_first) * mask_out).astype(jnp.bfloat16)
    cols_mid = taps_stride_one(act_first)
    conv_mid = jnp.dot(cols_mid, w_mid, preferred_element_type=jnp.float32)
    stats_mid = (
        norm_stats(conv_mid, mask_out, local_counts, 1) if saved_stats is None else saved_stats[1]
    )
    scaled_mid, normed_mid = normalize(conv_mid, stats_mid, norm_mid, channel)
    act_mid = (jax.nn.silu(normed_mid) * mask_out).astype(jnp.bfloat16)
    conv_out = jnp.dot(act_mid, w_out, preferred_element_type=jnp.float32)
    stats_out = (
        norm_stats(conv_out, mask_out, local_counts, 1) if saved_stats is None else saved_stats[2]
    )
    scaled_out, normed_out = normalize(conv_out, stats_out, norm_out, 1.0)
    pre_sum = block_in + depth_gate * normed_out
    result = jax.nn.silu(pre_sum) * mask_out
    saved_values = (
        feed_in,
        scaled_first,
        normed_first,
        act_first,
        cols_mid,
        scaled_mid,
        normed_mid,
        act_mid,
        scaled_out,
        pre_sum,
    )
    return (result, (stats_first, stats_mid, stats_out), saved_values)


def block_b_backward(grad_out, weights, stats_all, saved_values, mask_out, channel, depth_gate):
    w_in, w_mid, w_out, norm_in, norm_mid, norm_out = weights
    stats_first, stats_mid, stats_out = stats_all
    (
        feed_in,
        scaled_first,
        normed_first,
        act_first,
        cols_mid,
        scaled_mid,
        normed_mid,
        act_mid,
        scaled_out,
        pre_sum,
    ) = saved_values
    grad_pre = grad_out * mask_out * silu_slope(pre_sum)
    low_out, gain_out, shift_out = norm_backward(
        grad_pre * depth_gate, scaled_out, stats_out, norm_out, mask_out
    )
    grad_w_out = contract(act_mid, low_out)
    grad_norm_mid = back_project(low_out, w_out) * mask_out * channel * silu_slope(normed_mid)
    low_mid, gain_mid, shift_mid = norm_backward(
        grad_norm_mid, scaled_mid, stats_mid, norm_mid, mask_out
    )
    grad_w_mid = contract(cols_mid, low_mid)
    grad_norm_first = (
        fold_stride_one(back_project(low_mid, w_mid))
        * mask_out
        * channel
        * silu_slope(normed_first)
    )
    low_first, gain_first, shift_first = norm_backward(
        grad_norm_first, scaled_first, stats_first, norm_in, mask_out
    )
    grad_w_in = contract(feed_in, low_first)
    grad_in = grad_pre + back_project(low_first, w_in)
    norm_grads = ((gain_first, shift_first), (gain_mid, shift_mid), (gain_out, shift_out))
    return (grad_in, (grad_w_in, grad_w_mid, grad_w_out), norm_grads)


def body(
    images,
    image_sides,
    widths,
    keep_gate,
    w_in_a,
    w_mid_a,
    w_out_a,
    w_proj_a,
    norm_in_a,
    norm_mid_a,
    norm_out_a,
    norm_proj_a,
    w_in_b,
    w_mid_b,
    w_out_b,
    norm_in_b,
    norm_mid_b,
    norm_out_b,
    cotangent,
):
    mask_in, mask_out, local_counts = pixel_masks(image_sides, images.shape[1], cotangent.shape[1])
    lane_ids = jnp.arange(w_mid_a.shape[1], dtype=jnp.int32)
    channel_a = (lane_ids < widths[0]).astype(jnp.float32)
    channel_b = (lane_ids < widths[1]).astype(jnp.float32)
    depth_gate = keep_gate.astype(jnp.float32)[:, None, None, None]
    inputs = images * mask_in.astype(jnp.bfloat16)
    MODE["fast"] = lax.axis_size("fsdp") == 8 and lax.axis_size("dp") == 4
    MODE["calls"] = 0
    gather_now = gather_all if MODE["fast"] else gather_plain
    scatter_now = scatter_all if MODE["fast"] else scatter_plain
    total_counts = lax.psum(local_counts, ("fsdp", "dp"))
    gathered = gather_now((w_in_a, w_mid_a, w_out_a, w_proj_a, w_in_b, w_mid_b, w_out_b))
    norms = lax.all_gather(
        jnp.concatenate(
            [norm_in_a, norm_mid_a, norm_out_a, norm_proj_a, norm_in_b, norm_mid_b, norm_out_b], axis=1
        ),
        "fsdp",
        axis=0,
    )
    wide = []
    place = 0
    for one in (norm_in_a, norm_mid_a, norm_out_a, norm_proj_a, norm_in_b, norm_mid_b, norm_out_b):
        width = one.shape[1]
        wide.append(norms[:, :, place : place + width].transpose(1, 0, 2).reshape(2, -1))
        place += width
    weights_a = tuple(gathered[:4]) + tuple(wide[:4])
    weights_b = tuple(gathered[4:]) + tuple(wide[4:])
    block_out, stats_a, redone_a = block_a_forward(
        inputs, weights_a, mask_in, mask_out, total_counts, channel_a, None
    )
    result, stats_b, redone_b = block_b_forward(
        block_out, weights_b, mask_out, total_counts, channel_b, depth_gate, None
    )
    grad_block, grads_b, norms_b = block_b_backward(
        cotangent.astype(jnp.float32), weights_b, stats_b, redone_b, mask_out, channel_b, depth_gate
    )
    grad_inputs, grads_a, norms_a = block_a_backward(
        grad_block, inputs, weights_a, stats_a, redone_a, mask_in, mask_out, channel_a
    )
    finals = scatter_now(tuple(one.astype(jnp.bfloat16) for one in grads_a + grads_b))
    final_in_a, final_mid_a, final_out_a, final_proj_a, final_in_b, final_mid_b, final_out_b = (
        one.astype(jnp.float32) for one in finals
    )
    return (
        result.astype(jnp.bfloat16),
        grad_inputs.astype(jnp.bfloat16),
        final_in_a,
        final_mid_a,
        final_out_a,
        final_proj_a,
        own_shard(norms_a[0]),
        own_shard(norms_a[1]),
        own_shard(norms_a[2]),
        own_shard(norms_a[3]),
        final_in_b,
        final_mid_b,
        final_out_b,
        own_shard(norms_b[0]),
        own_shard(norms_b[1]),
        own_shard(norms_b[2]),
    )


def solution(mesh):
    in_specs = (
        P(("fsdp", "dp"), None, None, None),
        P(("fsdp", "dp")),
        P(),
        P(("fsdp", "dp")),
        P("fsdp", None),
        P("fsdp", None),
        P("fsdp", None),
        P("fsdp", None),
        P(None, "fsdp"),
        P(None, "fsdp"),
        P(None, "fsdp"),
        P(None, "fsdp"),
        P("fsdp", None),
        P("fsdp", None),
        P("fsdp", None),
        P(None, "fsdp"),
        P(None, "fsdp"),
        P(None, "fsdp"),
        P(("fsdp", "dp"), None, None, None),
    )
    out_specs = (
        P(("fsdp", "dp"), None, None, None),
        P(("fsdp", "dp"), None, None, None),
        P("fsdp", None),
        P("fsdp", None),
        P("fsdp", None),
        P("fsdp", None),
        P(None, "fsdp"),
        P(None, "fsdp"),
        P(None, "fsdp"),
        P(None, "fsdp"),
        P("fsdp", None),
        P("fsdp", None),
        P("fsdp", None),
        P(None, "fsdp"),
        P(None, "fsdp"),
        P(None, "fsdp"),
    )
    return jax.shard_map(body, mesh=mesh, in_specs=in_specs, out_specs=out_specs, check_vma=False)
```

```python
import functools

import jax
import jax.numpy as jnp
from jax import lax
from jax.experimental import pallas as pl
from jax.experimental.pallas import tpu as pltpu
from jax.sharding import PartitionSpec as P

EPSILON = 1e-05
BY_MESH = pl.DeviceIdType.MESH


def flip(index, bits):
    out = index
    for bit in (1, 2, 4):
        if bits & bit:
            out = out + bit - 2 * bit * ((index // bit) % 2)
    return out


class Place:
    def __init__(self):
        self.f = lax.axis_index("fsdp")
        self.d = lax.axis_index("dp")
        self.y = self.f % 2
        self.z = self.f // 2
        self.c = self.d % 2
        self.x = self.d // 2

    def peer(self, f_bits, d_bits):
        return (flip(self.f, f_bits), flip(self.d, d_bits))


def enter(place, peers):
    barrier = pltpu.get_barrier_semaphore()
    for f_bits, d_bits in peers:
        pl.semaphore_signal(barrier, inc=1, device_id=place.peer(f_bits, d_bits), device_id_type=BY_MESH)
    pl.semaphore_wait(barrier, len(peers))


def push(source, target, send_sem, recv_sem, device):
    pltpu.make_async_remote_copy(
        src_ref=source,
        dst_ref=target,
        send_sem=send_sem,
        recv_sem=recv_sem,
        device_id=device,
        device_id_type=BY_MESH,
    ).start()


def await_bytes(view, sem):
    pltpu.make_async_copy(view, view, sem).wait()


def rows_of(start, size):
    return pl.ds(pl.multiple_of(start, 16), size)


def cols_of(start, size):
    return pl.ds(pl.multiple_of(start, 128), size)


LINK_PEERS = ((2, 0), (4, 0), (6, 0), (1, 0), (0, 2), (0, 1))


def split_of(columns):
    half = columns // 2
    return half // 2


def gather_steps(place, shard, whole, local_sem, send, recv):
    rows, columns = shard.shape
    half = columns // 2
    wide_a = split_of(columns)
    wide_b = half - wide_a
    part = rows // 2
    col_0 = place.c * half
    col_b = col_0 + wide_a
    row_q = place.x * part
    mine = place.f * rows
    pltpu.make_async_copy(
        shard.at[:, cols_of(col_0, half)], whole.at[rows_of(mine, rows), cols_of(col_0, half)], local_sem
    ).start()
    for bits in (2, 4, 6):
        push(
            shard.at[rows_of(row_q, part), cols_of(col_0, half)],
            whole.at[rows_of(mine + row_q, part), cols_of(col_0, half)],
            send.at[0],
            recv.at[0],
            place.peer(bits, 0),
        )
    yield
    await_bytes(whole.at[pl.ds(0, rows), pl.ds(0, half)], local_sem)
    await_bytes(whole.at[pl.ds(0, 3 * part), pl.ds(0, half)], recv.at[0])
    for bits in (0, 2, 4, 6):
        block = whole.at[rows_of(flip(place.f, bits) * rows + row_q, part), cols_of(col_0, wide_a)]
        push(block, block, send.at[1], recv.at[1], place.peer(1, 0))
    for bits in (2, 4, 6):
        block = whole.at[rows_of(flip(place.f, bits) * rows + row_q, part), cols_of(col_b, wide_b)]
        push(block, block, send.at[2], recv.at[2], place.peer(0, 2))
    yield
    await_bytes(whole.at[pl.ds(0, 4 * part), pl.ds(0, wide_a)], recv.at[1])
    await_bytes(whole.at[pl.ds(0, 3 * part), pl.ds(0, wide_b)], recv.at[2])
    for bits in range(1, 8):
        block = whole.at[rows_of(flip(place.f, bits) * rows + row_q, part), cols_of(col_0, wide_a)]
        push(block, block, send.at[3], recv.at[3], place.peer(0, 2))
    for bits in (0, 2, 4, 6):
        block = whole.at[rows_of(flip(place.f, bits) * rows, rows), cols_of(col_b, wide_b)]
        push(block, block, send.at[4], recv.at[4], place.peer(1, 0))
    yield
    await_bytes(whole.at[pl.ds(0, 7 * part), pl.ds(0, wide_a)], recv.at[3])
    await_bytes(whole.at[pl.ds(0, 4 * rows), pl.ds(0, wide_b)], recv.at[4])
    block = whole.at[:, cols_of(col_0, half)]
    push(block, block, send.at[5], recv.at[5], place.peer(0, 1))
    yield
    await_bytes(whole.at[:, pl.ds(0, half)], recv.at[5])


def gather_sent(shard, whole, send):
    rows, columns = shard.shape
    half = columns // 2
    wide_a = split_of(columns)
    wide_b = half - wide_a
    part = rows // 2
    await_bytes(whole.at[pl.ds(0, 3 * part), pl.ds(0, half)], send.at[0])
    await_bytes(whole.at[pl.ds(0, 4 * part), pl.ds(0, wide_a)], send.at[1])
    await_bytes(whole.at[pl.ds(0, 3 * part), pl.ds(0, wide_b)], send.at[2])
    await_bytes(whole.at[pl.ds(0, 7 * part), pl.ds(0, wide_a)], send.at[3])
    await_bytes(whole.at[pl.ds(0, 4 * rows), pl.ds(0, wide_b)], send.at[4])
    await_bytes(whole.at[:, pl.ds(0, half)], send.at[5])


def add_rows(target, source, total, chunk):
    def step(index, carry):
        start = pl.multiple_of(index * chunk, chunk)
        into = target(start, chunk)
        into[...] = (into[...].astype(jnp.float32) + source(start, chunk)[...].astype(jnp.float32)).astype(into.dtype)
        return carry

    lax.fori_loop(0, total // chunk, step, 0)


def scatter_steps(place, grad, room, out, send, recv):
    from_core, from_x, from_y, from_y2, from_x2, from_z = room
    total_rows, columns = grad.shape
    rows = total_rows // 8
    half = columns // 2
    wide_a = split_of(columns)
    wide_b = half - wide_a
    part = rows // 2
    col_0 = place.c * half
    col_1 = half - col_0
    row_q = place.x * part
    row_o = part - row_q
    chunk = 32 if part % 32 == 0 else 16
    push(grad.at[:, cols_of(col_1, half)], from_core, send.at[0], recv.at[0], place.peer(0, 1))
    yield
    await_bytes(from_core, recv.at[0])
    add_rows(
        lambda s, n: from_core.at[pl.ds(s, n)],
        lambda s, n: grad.at[pl.ds(s, n), cols_of(col_0, half)],
        total_rows,
        chunk,
    )
    await_bytes(from_core, send.at[0])
    for block in range(8):
        push(
            from_core.at[rows_of(block * rows + row_o, part), pl.ds(0, wide_a)],
            from_x.at[pl.ds(block * part, part)],
            send.at[1],
            recv.at[1],
            place.peer(0, 2),
        )
    for level in range(4):
        push(
            from_core.at[rows_of((2 * level + 1 - place.y) * rows, rows), pl.ds(wide_a, wide_b)],
            from_y.at[pl.ds(level * rows, rows)],
            send.at[2],
            recv.at[2],
            place.peer(1, 0),
        )
    yield
    await_bytes(from_x, recv.at[1])
    await_bytes(from_y, recv.at[2])

    def fold_x(block, carry):
        add_rows(
            lambda s, n: from_core.at[rows_of(block * rows + row_q + s, n), pl.ds(0, wide_a)],
            lambda s, n: from_x.at[rows_of(block * part + s, n)],
            part,
            chunk,
        )
        return carry

    lax.fori_loop(0, 8, fold_x, 0)

    def fold_y(level, carry):
        add_rows(
            lambda s, n: from_core.at[rows_of((2 * level + place.y) * rows + s, n), pl.ds(wide_a, wide_b)],
            lambda s, n: from_y.at[rows_of(level * rows + s, n)],
            rows,
            chunk,
        )
        return carry

    lax.fori_loop(0, 4, fold_y, 0)
    for level in range(4):
        push(
            from_core.at[rows_of((2 * level + 1 - place.y) * rows + row_q, part), pl.ds(0, wide_a)],
            from_y2.at[pl.ds(level * part, part)],
            send.at[3],
            recv.at[3],
            place.peer(1, 0),
        )
        push(
            from_core.at[rows_of((2 * level + place.y) * rows + row_o, part), pl.ds(wide_a, wide_b)],
            from_x2.at[pl.ds(level * part, part)],
            send.at[4],
            recv.at[4],
            place.peer(0, 2),
        )
    yield
    await_bytes(from_y2, recv.at[3])
    await_bytes(from_x2, recv.at[4])

    def fold_last(level, carry):
        own = (2 * level + place.y) * rows + row_q
        add_rows(
            lambda s, n: from_core.at[rows_of(own + s, n), pl.ds(0, wide_a)],
            lambda s, n: from_y2.at[rows_of(level * part + s, n)],
            part,
            chunk,
        )
        add_rows(
            lambda s, n: from_core.at[rows_of(own + s, n), pl.ds(wide_a, wide_b)],
            lambda s, n: from_x2.at[rows_of(level * part + s, n)],
            part,
            chunk,
        )
        return carry

    lax.fori_loop(0, 4, fold_last, 0)
    for slot, bits in enumerate((2, 4, 6)):
        push(
            from_core.at[rows_of(flip(place.f, bits) * rows + row_q, part)],
            from_z.at[pl.ds(slot * part, part)],
            send.at[5],
            recv.at[5],
            place.peer(bits, 0),
        )
    yield
    await_bytes(from_z, recv.at[5])

    def fold_z(index, carry):
        start = pl.multiple_of(index * chunk, chunk)
        total = from_core[rows_of(place.f * rows + row_q + start, chunk)].astype(jnp.float32)
        for slot in range(3):
            total = total + from_z[rows_of(slot * part + start, chunk)].astype(jnp.float32)
        out[rows_of(row_q + start, chunk), cols_of(col_0, half)] = total.astype(out.dtype)
        return carry

    lax.fori_loop(0, part // chunk, fold_z, 0)
    block = out.at[rows_of(row_q, part), cols_of(col_0, half)]
    push(block, block, send.at[6], recv.at[6], place.peer(0, 2))
    yield
    await_bytes(out.at[pl.ds(0, part), pl.ds(0, half)], recv.at[6])
    block = out.at[:, cols_of(col_0, half)]
    push(block, block, send.at[7], recv.at[7], place.peer(0, 1))
    yield
    await_bytes(out.at[:, pl.ds(0, half)], recv.at[7])


def scatter_sent(grad, room, out, send):
    from_core, from_x, from_y, from_y2, from_x2, from_z = room
    half = grad.shape[1] // 2
    for index, view in enumerate((from_x, from_y, from_y2, from_x2, from_z)):
        await_bytes(view, send.at[index + 1])
    await_bytes(out.at[pl.ds(0, out.shape[0] // 2), pl.ds(0, half)], send.at[6])
    await_bytes(out.at[:, pl.ds(0, half)], send.at[7])


ORDER = ("in_a", "mid_a", "proj_a", "out_a", "in_b", "mid_b", "out_b")
BLOCK = 256
LANES = 512
CHUNK = 32
TAPS = [(u, v) for u in range(3) for v in range(3)]
EVERY_PEER = ((0, 1), (0, 2), (0, 3), (1, 0), (2, 0), (3, 0), (4, 0), (5, 0), (6, 0), (7, 0))
F32 = jnp.float32
BF16 = jnp.bfloat16


def mm(left, right):
    return jnp.dot(left, right, preferred_element_type=F32)


def mm_nt(left, right):
    return lax.dot_general(left, right, (((1,), (1,)), ((), ())), preferred_element_type=F32)


def mm_tn(left, right):
    return lax.dot_general(left, right, (((0,), (0,)), ((), ())), preferred_element_type=F32)


def loop(count, step):
    def body_of(index, carry):
        step(index)
        return carry

    lax.fori_loop(0, count, body_of, 0)


def at_block(index, size):
    return pl.ds(pl.multiple_of(index * size, size), size)


def slope_of(values):
    gate = jax.nn.sigmoid(values)
    return gate * (1.0 + values * (1.0 - gate))


def fold(values):
    total = values[0:8]
    for start in range(8, values.shape[0], 8):
        total = total + values[start : start + 8]
    return total


def column_sums(count, terms, chunk=CHUNK):
    def step(index, carry):
        start = pl.multiple_of(index * chunk, chunk)
        return tuple(total + fold(one) for total, one in zip(carry, terms(start)))

    width = len(jax.eval_shape(lambda: terms(0)))
    zero = jnp.zeros((8, LANES), F32)
    totals = lax.fori_loop(0, count, step, (zero,) * width)
    return [jnp.sum(one, axis=0, keepdims=True) for one in totals]


class Vectors:
    def __init__(self, ref):
        self.ref, self.used = ref, 0

    def put(self, row):
        at = self.used
        self.used += 1
        self.ref[at : at + 1, :] = row
        return at

    def get(self, at):
        return self.ref[at : at + 1, :]


class Totals:
    def __init__(self, place, near, far, tot, send, recv):
        self.place, self.near, self.far, self.tot, self.send, self.recv = place, near, far, tot, send, recv
        self.turn, self.rows = 1, 0

    def start(self, rows_of_values, extra=None):
        self.turn = 1 - self.turn
        turn, place = self.turn, self.place
        at = 0
        for row in rows_of_values:
            for lane in range(0, LANES, 128):
                self.near[turn, place.d, at : at + 1, :] = row[:, lane : lane + 128]
                at += 1
        if extra is not None:
            self.near[turn, place.d, at : at + 8, :] = extra
            at += 8
        self.rows = at
        own = self.near.at[turn, place.d, pl.ds(0, at)]
        for bits in (1, 2, 3):
            push(own, own, self.send.at[turn, 0], self.recv.at[turn, 0], place.peer(0, bits))

    def middle(self):
        turn, rows, place = self.turn, self.rows, self.place
        await_bytes(self.near.at[turn, pl.ds(0, 3), pl.ds(0, rows)], self.recv.at[turn, 0])
        near = self.near
        own = self.far.at[turn, place.f, pl.ds(0, rows)]
        own[...] = (near[turn, 0, 0:rows, :] + near[turn, 1, 0:rows, :]) + (
            near[turn, 2, 0:rows, :] + near[turn, 3, 0:rows, :]
        )
        for bits in range(1, 8):
            push(own, own, self.send.at[turn, 1], self.recv.at[turn, 1], place.peer(bits, 0))

    def end(self):
        turn, rows = self.turn, self.rows
        await_bytes(self.far.at[turn, pl.ds(0, 7), pl.ds(0, rows)], self.recv.at[turn, 1])
        total = self.far[turn, 0, 0:rows, :]
        for index in range(1, 8):
            total = total + self.far[turn, index, 0:rows, :]
        self.tot[0:rows, :] = total
        await_bytes(self.near.at[turn, pl.ds(0, 3), pl.ds(0, rows)], self.send.at[turn, 0])
        await_bytes(self.far.at[turn, pl.ds(0, 7), pl.ds(0, rows)], self.send.at[turn, 1])

    def whole(self, rows_of_values, extra=None):
        self.start(rows_of_values, extra)
        self.middle()
        self.end()

    def row(self, index):
        at = 4 * index
        return jnp.concatenate([self.tot[at + k : at + k + 1, :] for k in range(4)], axis=1)

    def wide(self, at):
        return jnp.concatenate([self.tot[at : at + 1, :]] * 4, axis=1)


def room_in(whole):
    total, columns = whole.shape
    rows = total // 8
    half = columns // 2
    wide_a = split_of(columns)
    wide_b = half - wide_a
    return (
        whole.at[:, pl.ds(0, half)],
        whole.at[pl.ds(0, 4 * rows), pl.ds(half, wide_a)],
        whole.at[pl.ds(0, 4 * rows), pl.ds(half + wide_a, wide_b)],
        whole.at[pl.ds(4 * rows, 2 * rows), pl.ds(half, wide_a)],
        whole.at[pl.ds(4 * rows, 2 * rows), pl.ds(half + wide_a, wide_b)],
        whole.at[pl.ds(6 * rows, 3 * rows // 2), pl.ds(half, half)],
    )


def step_kernel(
    x_hbm,
    cot_hbm,
    mask_ref,
    gate_ref,
    count_ref,
    chan_ref,
    norm_hbm,
    sh_in_a,
    sh_mid_a,
    sh_out_a,
    sh_proj_a,
    sh_in_b,
    sh_mid_b,
    sh_out_b,
    result_hbm,
    images_hbm,
    sums_out,
    out_in_a,
    out_mid_a,
    out_out_a,
    out_proj_a,
    out_in_b,
    out_mid_b,
    out_out_b,
    w_in_a,
    w_mid_a,
    w_out_a,
    w_proj_a,
    w_in_b,
    w_mid_b,
    w_out_b,
    room_a,
    x,
    cot,
    c1,
    cols_a,
    c2,
    a2,
    c3,
    cp,
    bo,
    feed,
    d1,
    cols_b,
    d2,
    b2,
    d3,
    dz,
    dm,
    df,
    dout,
    dproj,
    dfa,
    g_mid,
    g_out,
    g_in,
    g_proj,
    norms,
    vec_ref,
    near,
    far,
    tot,
    io_sem,
    ag_local,
    ag_send,
    ag_recv,
    rs_send,
    rs_recv,
    ar_send,
    ar_recv,
    nb_sem,
):
    place = Place()
    enter(place, EVERY_PEER)
    shards = dict(in_a=sh_in_a, mid_a=sh_mid_a, out_a=sh_out_a, proj_a=sh_proj_a, in_b=sh_in_b, mid_b=sh_mid_b, out_b=sh_out_b)
    wholes = dict(in_a=w_in_a, mid_a=w_mid_a, out_a=w_out_a, proj_a=w_proj_a, in_b=w_in_b, mid_b=w_mid_b, out_b=w_out_b)
    outs = dict(in_a=out_in_a, mid_a=out_mid_a, out_a=out_out_a, proj_a=out_proj_a, in_b=out_in_b, mid_b=out_mid_b, out_b=out_out_b)

    pltpu.make_async_copy(norm_hbm, norms.at[place.f], nb_sem.at[0]).start()
    for bits in range(1, 8):
        push(norm_hbm, norms.at[place.f], nb_sem.at[1], nb_sem.at[2], place.peer(bits, 0))
    pltpu.make_async_copy(x_hbm, x, io_sem.at[0]).start()
    legs = {}
    for i, name in enumerate(ORDER):
        legs[name] = gather_steps(place, shards[name], wholes[name], ag_local.at[i], ag_send.at[i], ag_recv.at[i])
        next(legs[name])
    pltpu.make_async_copy(cot_hbm, cot, io_sem.at[1]).start()
    ticks = [0]

    def tick():
        ticks[0] += 1
        now = ticks[0]
        due = [i for i in range(7) if 0 <= now - 1 - i < 4]
        for i in [j for j in due if now - 1 - j < 3] + [j for j in due if now - 1 - j == 3]:
            next(legs[ORDER[i]], None)

    vec = Vectors(vec_ref)
    totals = Totals(place, near, far, tot, ar_send, ar_recv)

    for _ in range(3):
        tick()

    pltpu.make_async_copy(norm_hbm, norms.at[place.f], nb_sem.at[0]).wait()
    await_bytes(norms.at[pl.ds(0, 7)], nb_sem.at[2])
    await_bytes(norms.at[pl.ds(0, 7)], nb_sem.at[1])

    def narrow_row(at):
        pieces = [norms[2 * k, at : at + 1, :] + norms[2 * k + 1, at : at + 1, :] for k in range(4)]
        return vec.put(jnp.concatenate(pieces, axis=1))

    def wide_rows(at):
        return [
            vec.put(
                jnp.concatenate(
                    [norms[2 * j + k // 2, at + k % 2 : at + k % 2 + 1, :] for k in range(4)], axis=1
                )
            )
            for j in range(4)
        ]

    params = dict(
        in_a=([narrow_row(0)], [narrow_row(10)]),
        mid_a=([narrow_row(1)], [narrow_row(11)]),
        out_a=(wide_rows(2), wide_rows(12)),
        proj_a=(wide_rows(4), wide_rows(14)),
        in_b=([narrow_row(6)], [narrow_row(16)]),
        mid_b=([narrow_row(7)], [narrow_row(17)]),
        out_b=(wide_rows(8), wide_rows(18)),
    )
    chan_a = vec.put(chan_ref[0:1, :])
    chan_b = vec.put(chan_ref[1:2, :])
    scales = {}

    def mask_at(start, size=CHUNK):
        return jnp.concatenate([mask_ref[pl.ds(start, size), :]] * 4, axis=1)

    def gate_at(start, size=CHUNK):
        return jnp.concatenate([gate_ref[pl.ds(start, size), :]] * 4, axis=1)

    def set_norm(name, block, sums, inverse, chan):
        total, squares = sums
        average = total * inverse
        rstd = lax.rsqrt(squares * inverse - average * average + EPSILON)
        gain, shift = (vec.get(rows[block]) for rows in params[name])
        keep = 1.0 if chan is None else vec.get(chan)
        by = gain * rstd
        scales[name, block] = dict(
            rstd=vec.put(rstd),
            off=vec.put(-average * rstd),
            by=vec.put(by),
            mul=vec.put(by * keep),
            add=vec.put((shift - average * by) * keep),
        )

    def normed(name, block, values):
        s = scales[name, block]
        return values * vec.get(s["mul"]) + vec.get(s["add"])

    def hat(name, block, values):
        s = scales[name, block]
        return values * vec.get(s["rstd"]) + vec.get(s["off"])

    def set_back(name, block, shift_sum, gain_sum):
        s = scales[name, block]
        inverse = vec.get(inv_in if name == "in_a" else inv_out)
        by = vec.get(s["by"])
        pull = by * gain_sum * inverse
        s["back_add"] = vec.put(by * shift_sum * inverse + pull * vec.get(s["off"]))
        s["back_mul"] = vec.put(pull * vec.get(s["rstd"]))

    def back(name, block, grad, values):
        s = scales[name, block]
        return grad * vec.get(s["by"]) - vec.get(s["back_add"]) - values * vec.get(s["back_mul"])

    pltpu.make_async_copy(x_hbm, x, io_sem.at[0]).wait()
    tick()

    def first_a(p):
        c1[at_block(p, BLOCK), :] = mm(x[at_block(p, BLOCK), :], w_in_a[...])

    loop(4, first_a)

    def square_terms(ref):
        def terms(start):
            values = ref[pl.ds(start, CHUNK), :]
            return values, values * values

        return terms

    totals.whole(column_sums(32, square_terms(c1)), count_ref[...])
    inv_in = vec.put(1.0 / totals.wide(8))
    inv_out = vec.put(1.0 / totals.wide(9))
    set_norm("in_a", 0, (totals.row(0), totals.row(1)), vec.get(inv_in), chan_a)

    def lane_row(at, lane):
        return vec_ref[at : at + 1, at_block(lane, 128)]

    def act_a(lane):
        s = scales["in_a", 0]
        for row_par in range(2):
            for col_par in range(2):
                p = 2 * row_par + col_par
                values = c1[p * BLOCK : (p + 1) * BLOCK, at_block(lane, 128)]
                scaled = values * lane_row(s["mul"], lane) + lane_row(s["add"], lane)
                act = scaled * jax.nn.sigmoid(scaled) * mask_ref[...]
                for t, (u, v) in enumerate(TAPS):
                    if (u != 1) != bool(row_par) or (v != 1) != bool(col_par):
                        continue
                    shift = (8 if u == 0 else 0) + (1 if v == 0 else 0)
                    moved = pltpu.roll(act, shift, 0) if shift else act
                    cols_a[:, pl.ds(pl.multiple_of(t * LANES + lane * 128, 128), 128)] = moved.astype(BF16)

    loop(4, act_a)
    tick()

    def conv_mid(out, cols, weight):
        out[...] = mm(cols[:, 0:1536], weight[0:1536, :])

        def more(k):
            at = at_block(k + 1, 1536)
            out[...] += mm(cols[:, at], weight[at, :])

        loop(2, more)

    def masked_terms(ref):
        def terms(start):
            values = ref[pl.ds(start, CHUNK), :]
            kept = values * mask_at(start)
            return kept, kept * values

        return terms

    conv_mid(c2, cols_a, w_mid_a)
    totals.start(column_sums(8, masked_terms(c2)))
    tick()

    def project(j):
        cp[at_block(j, BLOCK), :] = mm(x[0:BLOCK, :], w_proj_a[:, at_block(j, LANES)])

    loop(4, project)
    totals.middle()
    totals.end()
    set_norm("mid_a", 0, (totals.row(0), totals.row(1)), vec.get(inv_out), chan_a)

    def act_mid(act_ref, ref, name):
        def step(index):
            start = pl.multiple_of(index * CHUNK, CHUNK)
            scaled = normed(name, 0, ref[pl.ds(start, CHUNK), :])
            act_ref[pl.ds(start, CHUNK), :] = (scaled * jax.nn.sigmoid(scaled) * mask_at(start)).astype(BF16)

        loop(BLOCK // CHUNK, step)

    act_mid(a2, c2, "mid_a")
    tick()

    def expand_a(j):
        c3[at_block(j, BLOCK), :] = mm(a2[...], w_out_a[:, at_block(j, LANES)])

    loop(4, expand_a)

    def blocked(ref, j, terms_of=square_terms):
        return terms_of(ref.at[pl.ds(j * BLOCK, BLOCK)])

    values = []
    for ref in (c3, cp):
        for j in range(4):
            values += column_sums(8, blocked(ref, j))
    totals.whole(values)
    for n, name in enumerate(("out_a", "proj_a")):
        for j in range(4):
            at = 8 * n + 2 * j
            set_norm(name, j, (totals.row(at), totals.row(at + 1)), vec.get(inv_out), None)

    for j in range(4):

        def join_a(index, j=j):
            start = pl.multiple_of(index * CHUNK, CHUNK)
            rows = pl.ds(j * BLOCK + start, CHUNK)
            pre = normed("out_a", j, c3[rows, :]) + normed("proj_a", j, cp[rows, :])
            out = pre * jax.nn.sigmoid(pre) * mask_at(start)
            bo[rows, :] = out
            feed[pl.ds(start, CHUNK), pl.ds(j * LANES, LANES)] = out.astype(BF16)

        loop(BLOCK // CHUNK, join_a)

    tick()
    d1[...] = mm(feed[:, 0:LANES], w_in_b[0:LANES, :])

    def first_b(k):
        at = at_block(k + 1, LANES)
        d1[...] += mm(feed[:, at], w_in_b[at, :])

    loop(3, first_b)
    totals.whole(column_sums(8, square_terms(d1)))
    set_norm("in_b", 0, (totals.row(0), totals.row(1)), vec.get(inv_out), chan_b)

    def act_b(lane):
        s = scales["in_b", 0]
        scaled = d1[:, at_block(lane, 128)] * lane_row(s["mul"], lane) + lane_row(s["add"], lane)
        act = scaled * jax.nn.sigmoid(scaled) * mask_ref[...]
        for t, (u, v) in enumerate(TAPS):
            shift = (-(8 * (u - 1) + v - 1)) % BLOCK
            moved = pltpu.roll(act, shift, 0) if shift else act
            cols_b[:, pl.ds(pl.multiple_of(t * LANES + lane * 128, 128), 128)] = moved.astype(BF16)

    loop(4, act_b)
    tick()
    conv_mid(d2, cols_b, w_mid_b)
    totals.whole(column_sums(8, masked_terms(d2)))
    set_norm("mid_b", 0, (totals.row(0), totals.row(1)), vec.get(inv_out), chan_b)
    act_mid(b2, d2, "mid_b")
    tick()

    def expand_b(j):
        d3[at_block(j, BLOCK), :] = mm(b2[...], w_out_b[:, at_block(j, LANES)])

    loop(4, expand_b)
    values = []
    for j in range(4):
        values += column_sums(8, blocked(d3, j))
    totals.whole(values)
    for j in range(4):
        set_norm("out_b", j, (totals.row(2 * j), totals.row(2 * j + 1)), vec.get(inv_out), None)
    for i, name in enumerate(ORDER):
        gather_sent(shards[name], wholes[name], ag_send.at[i])

    pltpu.make_async_copy(cot_hbm, cot, io_sem.at[1]).wait()
    values = []
    for j in range(4):

        def finish(start, j=j):
            rows = pl.ds(j * BLOCK + start, CHUNK)
            near_rows, lanes = pl.ds(start, CHUNK), pl.ds(j * LANES, LANES)
            mask, gate, hidden = mask_at(start), gate_at(start), d3[rows, :]
            pre = bo[rows, :] + gate * normed("out_b", j, hidden)
            part = jax.nn.sigmoid(pre)
            grad = cot[near_rows, lanes].astype(F32) * mask * (part * (1.0 + pre * (1.0 - part)))
            cot[near_rows, lanes] = (pre * part * mask).astype(BF16)
            bo[rows, :] = grad
            grad = grad * gate
            return grad, grad * hat("out_b", j, hidden)

        values += column_sums(8, finish)
    result_copy = pltpu.make_async_copy(cot, result_hbm, io_sem.at[2])
    result_copy.start()
    totals.whole(values)
    sums_out[0:32, :] = tot[0:32, :]
    for j in range(4):
        set_back("out_b", j, totals.row(2 * j), totals.row(2 * j + 1))
    for j in range(4):

        def low_out_b(index, j=j):
            start = pl.multiple_of(index * CHUNK, CHUNK)
            rows = pl.ds(j * BLOCK + start, CHUNK)
            grad = back("out_b", j, bo[rows, :] * gate_at(start), d3[rows, :]) * mask_at(start)
            dout[pl.ds(start, CHUNK), pl.ds(j * LANES, LANES)] = grad.astype(BF16)

        loop(BLOCK // CHUNK, low_out_b)

    def through_out(weight):
        dz[...] = mm_nt(dout[:, 0:LANES], weight[:, 0:LANES])

        def more(k):
            at = at_block(k + 1, LANES)
            dz[...] += mm_nt(dout[:, at], weight[:, at])

        loop(3, more)

    def slope_terms(grad_ref, ref, name, chan):
        def terms(start):
            rows = pl.ds(start, CHUNK)
            hidden = ref[rows, :]
            mask = mask_at(start % BLOCK) if grad_ref.shape[0] > BLOCK else mask_at(start)
            grad = grad_ref[rows, :] * mask * vec.get(chan) * slope_of(normed(name, 0, hidden))
            grad_ref[rows, :] = grad
            return grad, grad * hat(name, 0, hidden)

        return terms

    through_out(w_out_b)
    totals.start(column_sums(8, slope_terms(dz, d2, "mid_b", chan_b)))

    def grad_out(act_ref, j):
        g_out[:, at_block(j, LANES)] = mm_tn(act_ref[...], dout[:, at_block(j, LANES)]).astype(BF16)

    loop(2, lambda j: grad_out(b2, j))
    totals.middle()
    loop(2, lambda j: grad_out(b2, j + 2))
    totals.end()
    sums_out[32:40, :] = tot[0:8, :]
    scatters = {}

    def scatter(name, grad, room):
        i = ORDER.index(name)
        scatters[name] = scatter_steps(place, grad, room, outs[name], rs_send.at[i], rs_recv.at[i])
        next(scatters[name])

    def go(*names):
        for name in names:
            next(scatters[name], None)

    scatter("out_b", g_out, room_in(w_out_b))
    set_back("mid_b", 0, totals.row(0), totals.row(1))

    def low_mid(name, ref, shifts):
        s = scales[name, 0]

        def step(lane):
            lanes = at_block(lane, 128)
            grad = (
                dz[:, lanes] * lane_row(s["by"], lane)
                - lane_row(s["back_add"], lane)
                - ref[:, lanes] * lane_row(s["back_mul"], lane)
            ) * mask_ref[...]
            dm[:, lanes] = grad.astype(BF16)
            for k, shift in enumerate(shifts):
                moved = pltpu.roll(grad, shift, 0) if shift else grad
                g_mid[k * BLOCK : (k + 1) * BLOCK, lanes] = moved.astype(BF16)

        loop(4, step)

    low_mid("mid_b", d2, [(8 * (u - 1) + v - 1) % BLOCK for u, v in TAPS])
    dz[...] = mm_nt(g_mid[0:BLOCK, :], w_mid_b[0:LANES, :])

    def back_mid_b(t):
        dz[...] += mm_nt(g_mid[at_block(t + 1, BLOCK), :], w_mid_b[at_block(t + 1, LANES), :])

    loop(8, back_mid_b)
    totals.start(column_sums(8, slope_terms(dz, d1, "in_b", chan_b)))
    go("out_b")

    def grad_mid(cols, t):
        g_mid[at_block(t, LANES), :] = mm_tn(cols[:, at_block(t, LANES)], dm[...]).astype(BF16)

    loop(3, lambda t: grad_mid(cols_b, t))
    totals.middle()
    loop(6, lambda t: grad_mid(cols_b, t + 3))
    totals.end()
    sums_out[40:48, :] = tot[0:8, :]
    scatter("mid_b", g_mid, room_in(w_mid_b))
    set_back("in_b", 0, totals.row(0), totals.row(1))

    def low_first_b(index):
        start = pl.multiple_of(index * CHUNK, CHUNK)
        rows = pl.ds(start, CHUNK)
        df[rows, :] = (back("in_b", 0, dz[rows, :], d1[rows, :]) * mask_at(start)).astype(BF16)

    loop(BLOCK // CHUNK, low_first_b)

    def back_in_b(j):
        bo[at_block(j, BLOCK), :] += mm_nt(df[...], w_in_b[at_block(j, LANES), :])

    loop(4, back_in_b)

    values = []
    for j in range(4):

        def join_back(start, j=j):
            rows = pl.ds(j * BLOCK + start, CHUNK)
            left, right = c3[rows, :], cp[rows, :]
            pre = normed("out_a", j, left) + normed("proj_a", j, right)
            grad = bo[rows, :] * mask_at(start) * slope_of(pre)
            bo[rows, :] = grad
            return grad, grad * hat("out_a", j, left), grad * hat("proj_a", j, right)

        values += column_sums(8, join_back)
    totals.start(values)
    go("out_b")

    def grad_in_b(j):
        g_in[at_block(j, LANES), :] = mm_tn(feed[:, at_block(j, LANES)], df[...]).astype(BF16)

    loop(4, grad_in_b)
    totals.middle()
    go("mid_b")
    totals.end()
    sums_out[48:96, :] = tot[0:48, :]
    scatter("in_b", g_in, room_in(w_in_b))
    for j in range(4):
        set_back("out_a", j, totals.row(3 * j), totals.row(3 * j + 1))
        set_back("proj_a", j, totals.row(3 * j), totals.row(3 * j + 2))
    for j in range(4):

        def low_both(index, j=j):
            start = pl.multiple_of(index * CHUNK, CHUNK)
            rows = pl.ds(j * BLOCK + start, CHUNK)
            near_rows, lanes = pl.ds(start, CHUNK), pl.ds(j * LANES, LANES)
            grad, mask = bo[rows, :], mask_at(start)
            dout[near_rows, lanes] = (back("out_a", j, grad, c3[rows, :]) * mask).astype(BF16)
            dproj[near_rows, lanes] = (back("proj_a", j, grad, cp[rows, :]) * mask).astype(BF16)

        loop(BLOCK // CHUNK, low_both)
    through_out(w_out_a)
    totals.start(column_sums(8, slope_terms(dz, c2, "mid_a", chan_a)))
    go("out_b", "mid_b")
    loop(4, lambda j: grad_out(a2, j))
    totals.middle()

    def grad_proj(n):
        i, j = n // 4, n % 4
        g_proj[at_block(i, LANES), at_block(j, LANES)] = mm_tn(
            x[0:BLOCK, at_block(i, LANES)], dproj[:, at_block(j, LANES)]
        ).astype(BF16)

    loop(8, grad_proj)

    def back_proj(n):
        rows = at_block(n, BLOCK)
        d3[rows, :] = mm_nt(dproj[:, 0:LANES], w_proj_a[at_block(n, LANES), 0:LANES])

        def more(k):
            at = at_block(k + 1, LANES)
            d3[rows, :] += mm_nt(dproj[:, at], w_proj_a[at_block(n, LANES), at])

        loop(3, more)

    loop(2, back_proj)
    go("in_b")
    totals.end()
    sums_out[96:104, :] = tot[0:8, :]
    scatter("out_a", g_out, room_in(w_out_a))
    set_back("mid_a", 0, totals.row(0), totals.row(1))
    go("out_b", "mid_b", "in_b")
    low_mid("mid_a", c2, [(-(8 * r + s)) % BLOCK for r in range(2) for s in range(2)])
    for row_par in range(2):
        for col_par in range(2):
            rows = pl.ds((2 * row_par + col_par) * BLOCK, BLOCK)
            grad = None
            for t, (u, v) in enumerate(TAPS):
                if (u != 1) != bool(row_par) or (v != 1) != bool(col_par):
                    continue
                moved = 2 * (1 if u == 0 else 0) + (1 if v == 0 else 0)
                term = mm_nt(g_mid[moved * BLOCK : (moved + 1) * BLOCK, :], w_mid_a[t * LANES : (t + 1) * LANES, :])
                grad = term if grad is None else grad + term
            bo[rows, :] = grad
    totals.start(column_sums(32, slope_terms(bo, c1, "in_a", chan_a)))
    go("out_b", "out_a")
    loop(3, lambda t: grad_mid(cols_a, t))
    totals.middle()
    loop(6, lambda t: grad_mid(cols_a, t + 3))
    go("mid_b", "in_b")
    totals.end()
    sums_out[104:112, :] = tot[0:8, :]
    scatter("mid_a", g_mid, room_in(w_mid_a))
    scatter("proj_a", g_proj, room_in(w_proj_a))
    go("out_b", "out_a")
    set_back("in_a", 0, totals.row(0), totals.row(1))

    def low_first_a(index):
        start = pl.multiple_of(index * CHUNK, CHUNK)
        rows = pl.ds(start, CHUNK)
        dfa[rows, :] = (back("in_a", 0, bo[rows, :], c1[rows, :]) * mask_at(start % BLOCK)).astype(BF16)

    loop(4 * BLOCK // CHUNK, low_first_a)

    def grad_in_a(i):
        g_in[at_block(i, 256), :] = mm_tn(x[:, at_block(i, 256)], dfa[...]).astype(BF16)

    loop(4, grad_in_a)
    scatter("in_a", g_in.at[pl.ds(0, 1024)], room_in(room_a))
    go("mid_b", "in_b", "out_a", "mid_a", "proj_a")

    def back_in_a(n):
        p, h = n // 2, n % 2
        grad = mm_nt(dfa[at_block(p, BLOCK), :], w_in_a[at_block(h, LANES), :])
        spread = jnp.where(p == 0, d3[at_block(h, BLOCK), :], 0.0)
        x[at_block(p, BLOCK), at_block(h, LANES)] = (grad + spread).astype(BF16)

    loop(8, back_in_a)
    images_copy = pltpu.make_async_copy(x, images_hbm, io_sem.at[3])
    images_copy.start()
    for _ in range(8):
        go("mid_b", "in_b", "out_a", "mid_a", "proj_a", "in_a")
    go("out_b")
    go("out_b")
    result_copy.wait()
    images_copy.wait()
    for name, grad, room in (
        ("in_a", g_in.at[pl.ds(0, 1024)], room_in(room_a)),
        ("mid_a", g_mid, room_in(w_mid_a)),
        ("out_a", g_out, room_in(w_out_a)),
        ("proj_a", g_proj, room_in(w_proj_a)),
        ("in_b", g_in, room_in(w_in_b)),
        ("mid_b", g_mid, room_in(w_mid_b)),
        ("out_b", g_out, room_in(w_out_b)),
    ):
        scatter_sent(grad, room, outs[name], rs_send.at[ORDER.index(name)])


def pieces_128(row, odd):
    width = row.shape[0]
    if width >= 128:
        return row.reshape(width // 128, 128)
    blank = jnp.zeros((width,), F32)
    return jnp.where(odd, jnp.concatenate([blank, row]), jnp.concatenate([row, blank]))[None]


def body_fast(
    images,
    image_sides,
    widths,
    keep_gate,
    w_in_a,
    w_mid_a,
    w_out_a,
    w_proj_a,
    norm_in_a,
    norm_mid_a,
    norm_out_a,
    norm_proj_a,
    w_in_b,
    w_mid_b,
    w_out_b,
    norm_in_b,
    norm_mid_b,
    norm_out_b,
    cotangent,
):
    slots, side_in, _, width_in = images.shape
    side, width_out = cotangent.shape[1], cotangent.shape[3]
    grid = side + 1
    half = image_sides // 2
    steps = jnp.arange(grid, dtype=jnp.int32)
    inside = (steps[None, :, None] < half[:, None, None]) & (steps[None, None, :] < half[:, None, None])
    mask = jnp.broadcast_to(inside.reshape(BLOCK, 1), (BLOCK, 128)).astype(F32)
    gate = jnp.broadcast_to(keep_gate[:, None, None], (slots, grid * grid, 128)).reshape(BLOCK, 128).astype(F32)
    counts = jnp.stack([jnp.sum(image_sides * image_sides), jnp.sum(half * half)]).astype(F32)
    counts = jnp.broadcast_to(jnp.concatenate([counts, jnp.zeros((6,), F32)])[:, None], (8, 128))
    lane_ids = jnp.arange(LANES, dtype=jnp.int32)
    chan = jnp.concatenate([lane_ids[None, :] < widths[:, None], jnp.zeros((6, LANES), bool)]).astype(F32)
    planes = images.reshape(slots, side, 2, side, 2, width_in).transpose(2, 4, 0, 1, 3, 5)
    planes = jnp.pad(planes, ((0, 0), (0, 0), (0, 0), (0, 1), (0, 1), (0, 0)))
    planes = planes * inside[None, None, :, :, :, None].astype(planes.dtype)
    planes = planes.reshape(4 * BLOCK, width_in)
    cot = jnp.pad(cotangent, ((0, 0), (0, 1), (0, 1), (0, 0))).reshape(BLOCK, width_out)
    norms = [norm_in_a, norm_mid_a, norm_out_a, norm_proj_a, norm_in_b, norm_mid_b, norm_out_b]
    odd = lax.axis_index("fsdp") % 2 == 1
    packed = [pieces_128(one[k].astype(F32), odd) for k in range(2) for one in norms]
    packed = jnp.concatenate(packed + [jnp.zeros((4, 128), F32)])
    shards = (w_in_a, w_mid_a, w_out_a, w_proj_a, w_in_b, w_mid_b, w_out_b)
    vmem = pl.BlockSpec(memory_space=pltpu.VMEM)
    anywhere = pl.BlockSpec(memory_space=pl.ANY)
    wholes = [(8 * one.shape[0], one.shape[1]) for one in shards]
    outs = pl.pallas_call(
        step_kernel,
        out_shape=[
            jax.ShapeDtypeStruct((BLOCK, width_out), BF16),
            jax.ShapeDtypeStruct((4 * BLOCK, width_in), BF16),
            jax.ShapeDtypeStruct((112, 128), F32),
        ]
        + [jax.ShapeDtypeStruct(one.shape, BF16) for one in shards],
        in_specs=[anywhere, anywhere, vmem, vmem, vmem, vmem, anywhere] + [anywhere] * 7,
        out_specs=[anywhere, anywhere, vmem] + [vmem] * 7,
        scratch_shapes=[pltpu.VMEM(shape, BF16) for shape in wholes]
        + [
            pltpu.VMEM(wholes[0], BF16),
            pltpu.VMEM((4 * BLOCK, width_in), BF16),
            pltpu.VMEM((BLOCK, width_out), BF16),
            pltpu.VMEM((4 * BLOCK, LANES), F32),
            pltpu.VMEM((BLOCK, 9 * LANES), BF16),
            pltpu.VMEM((BLOCK, LANES), F32),
            pltpu.VMEM((BLOCK, LANES), BF16),
            pltpu.VMEM((4 * BLOCK, LANES), F32),
            pltpu.VMEM((4 * BLOCK, LANES), F32),
            pltpu.VMEM((4 * BLOCK, LANES), F32),
            pltpu.VMEM((BLOCK, width_out), BF16),
            pltpu.VMEM((BLOCK, LANES), F32),
            pltpu.VMEM((BLOCK, 9 * LANES), BF16),
            pltpu.VMEM((BLOCK, LANES), F32),
            pltpu.VMEM((BLOCK, LANES), BF16),
            pltpu.VMEM((4 * BLOCK, LANES), F32),
            pltpu.VMEM((BLOCK, LANES), F32),
            pltpu.VMEM((BLOCK, LANES), BF16),
            pltpu.VMEM((BLOCK, LANES), BF16),
            pltpu.VMEM((BLOCK, width_out), BF16),
            pltpu.VMEM((BLOCK, width_out), BF16),
            pltpu.VMEM((4 * BLOCK, LANES), BF16),
            pltpu.VMEM(wholes[1], BF16),
            pltpu.VMEM(wholes[2], BF16),
            pltpu.VMEM(wholes[4], BF16),
            pltpu.VMEM(wholes[3], BF16),
            pltpu.VMEM((8, 24, 128), F32),
            pltpu.VMEM((160, LANES), F32),
            pltpu.VMEM((2, 4, 64, 128), F32),
            pltpu.VMEM((2, 8, 64, 128), F32),
            pltpu.VMEM((64, 128), F32),
            pltpu.SemaphoreType.DMA((4,)),
            pltpu.SemaphoreType.DMA((7,)),
            pltpu.SemaphoreType.DMA((7, 6)),
            pltpu.SemaphoreType.DMA((7, 6)),
            pltpu.SemaphoreType.DMA((7, 8)),
            pltpu.SemaphoreType.DMA((7, 8)),
            pltpu.SemaphoreType.DMA((2, 2)),
            pltpu.SemaphoreType.DMA((2, 2)),
            pltpu.SemaphoreType.DMA((3,)),
        ],
        compiler_params=pltpu.CompilerParams(
            collective_id=0, has_side_effects=True, vmem_limit_bytes=64 * 2**20
        ),
        name="whole_step",
    )(planes, cot, mask, gate, counts, chan, packed, *shards)
    result, grad_planes, sums = outs[:3]
    finals = [one.astype(F32) for one in outs[3:]]
    result = result.reshape(slots, grid, grid, width_out)[:, :side, :side]
    grad_images = grad_planes.reshape(2, 2, slots, grid, grid, width_in)[:, :, :, :side, :side]
    grad_images = grad_images.transpose(2, 3, 0, 4, 1, 5).reshape(images.shape)
    out_b = sums[0:32].reshape(4, 2, LANES)
    both = sums[48:96].reshape(4, 3, LANES)

    def narrow(at):
        pair = sums[at : at + 8].reshape(2, LANES)
        return own_shard((pair[1], pair[0]))

    def wide(array, gain):
        return own_shard((array[:, gain].reshape(-1), array[:, 0].reshape(-1)))

    return (
        result,
        grad_images,
        finals[0],
        finals[1],
        finals[2],
        finals[3],
        narrow(104),
        narrow(96),
        wide(both, 1),
        wide(both, 2),
        finals[4],
        finals[5],
        finals[6],
        narrow(40),
        narrow(32),
        wide(out_b, 1),
    )


def fits(mesh):
    return mesh.shape["fsdp"] == 8 and mesh.shape["dp"] == 4


def gather_plain(shards):
    return [lax.all_gather(one, "fsdp", axis=0, tiled=True) for one in shards]


def scatter_plain(grads):
    parts = [lax.psum_scatter(one, "fsdp", scatter_dimension=0, tiled=True) for one in grads]
    return lax.psum(tuple(parts), "dp")


def sum_pair(first, second):
    return lax.psum((first, second), ("fsdp", "dp"))


def silu_slope(values):
    sigmoid_part = jax.nn.sigmoid(values)
    return sigmoid_part * (1.0 + values * (1.0 - sigmoid_part))


def pixel_masks(image_sides, side_in, side_out):
    half_sides = image_sides // 2
    rows_in = jnp.arange(side_in, dtype=jnp.int32)
    rows_out = jnp.arange(side_out, dtype=jnp.int32)
    inside_in = (rows_in[None, :, None] < image_sides[:, None, None]) & (
        rows_in[None, None, :] < image_sides[:, None, None]
    )
    inside_out = (rows_out[None, :, None] < half_sides[:, None, None]) & (
        rows_out[None, None, :] < half_sides[:, None, None]
    )
    local_counts = jnp.stack(
        [jnp.sum(image_sides * image_sides), jnp.sum(half_sides * half_sides)]
    ).astype(jnp.float32)
    return (
        inside_in.astype(jnp.float32)[..., None],
        inside_out.astype(jnp.float32)[..., None],
        local_counts,
    )


def norm_stats(hidden, pixel_mask, local_counts, count_slot):
    sum_values, sum_squares = sum_pair(
        jnp.sum(hidden * pixel_mask, axis=(0, 1, 2)),
        jnp.sum(hidden * hidden * pixel_mask, axis=(0, 1, 2)),
    )
    pixel_total = local_counts[count_slot]
    average = sum_values / pixel_total
    inv_std = lax.rsqrt(sum_squares / pixel_total - average * average + EPSILON)
    return (average, inv_std, pixel_total)


def normalize(hidden, stats_now, params, channel):
    average, inv_std, pixel_total = stats_now
    scaled = (hidden - average) * inv_std
    params_wide = params.astype(jnp.float32)
    return (scaled, (scaled * params_wide[0] + params_wide[1]) * channel)


def norm_backward(grad_norm, scaled, stats_now, params, pixel_mask):
    average, inv_std, pixel_total = stats_now
    shift_sum, gain_sum = sum_pair(
        jnp.sum(grad_norm, axis=(0, 1, 2)), jnp.sum(grad_norm * scaled, axis=(0, 1, 2))
    )
    gain_row = params[0].astype(jnp.float32)
    grad_hidden = (
        gain_row
        * inv_std
        * (grad_norm - shift_sum / pixel_total - scaled * gain_sum / pixel_total)
        * pixel_mask
    )
    return (grad_hidden.astype(jnp.bfloat16), gain_sum, shift_sum)


def taps_stride_two(activations):
    slot_count = activations.shape[0]
    half_side = activations.shape[1] // 2
    lane_count = activations.shape[3]
    padded = jnp.pad(activations, ((0, 0), (1, 1), (1, 1), (0, 0)))
    parity_grid = padded.reshape(slot_count, half_side + 1, 2, half_side + 1, 2, lane_count)
    pieces = [
        parity_grid[
            :,
            row_tap // 2 : row_tap // 2 + half_side,
            row_tap % 2,
            col_tap // 2 : col_tap // 2 + half_side,
            col_tap % 2,
            :,
        ]
        for row_tap in range(3)
        for col_tap in range(3)
    ]
    return jnp.concatenate(pieces, axis=-1)


def fold_stride_two(grad_cols, side_in):
    slot_count = grad_cols.shape[0]
    half_side = grad_cols.shape[1]
    lane_count = grad_cols.shape[3] // 9
    planes = [
        [
            jnp.zeros((slot_count, half_side + 1, half_side + 1, lane_count), jnp.float32)
            for col_par in range(2)
        ]
        for row_par in range(2)
    ]
    for row_tap in range(3):
        for col_tap in range(3):
            tap_index = row_tap * 3 + col_tap
            tap_piece = grad_cols[..., tap_index * lane_count : (tap_index + 1) * lane_count]
            placed = jnp.pad(
                tap_piece,
                (
                    (0, 0),
                    (row_tap // 2, 1 - row_tap // 2),
                    (col_tap // 2, 1 - col_tap // 2),
                    (0, 0),
                ),
            )
            planes[row_tap % 2][col_tap % 2] = planes[row_tap % 2][col_tap % 2] + placed
    parity_grid = jnp.stack([jnp.stack(planes[0], axis=3), jnp.stack(planes[1], axis=3)], axis=2)
    whole_grid = parity_grid.reshape(slot_count, side_in + 2, side_in + 2, lane_count)
    return whole_grid[:, 1:-1, 1:-1, :]


def taps_stride_one(activations):
    side_now = activations.shape[1]
    padded = jnp.pad(activations, ((0, 0), (1, 1), (1, 1), (0, 0)))
    pieces = [
        padded[:, row_tap : row_tap + side_now, col_tap : col_tap + side_now, :]
        for row_tap in range(3)
        for col_tap in range(3)
    ]
    return jnp.concatenate(pieces, axis=-1)


def fold_stride_one(grad_cols):
    lane_count = grad_cols.shape[3] // 9
    whole_grid = None
    for row_tap in range(3):
        for col_tap in range(3):
            tap_index = row_tap * 3 + col_tap
            tap_piece = grad_cols[..., tap_index * lane_count : (tap_index + 1) * lane_count]
            placed = jnp.pad(
                tap_piece, ((0, 0), (row_tap, 2 - row_tap), (col_tap, 2 - col_tap), (0, 0))
            )
            whole_grid = placed if whole_grid is None else whole_grid + placed
    return whole_grid[:, 1:-1, 1:-1, :]


def contract(left_side, right_side):
    return lax.dot_general(
        left_side,
        right_side,
        (((0, 1, 2), (0, 1, 2)), ((), ())),
        preferred_element_type=jnp.float32,
    )


def back_project(gradient, weight):
    return lax.dot_general(
        gradient, weight, (((3,), (1,)), ((), ())), preferred_element_type=jnp.float32
    )


def own_shard(pair_sums):
    gain_sum, shift_sum = pair_sums
    shard_width = gain_sum.shape[0] // lax.axis_size("fsdp")
    offset = lax.axis_index("fsdp") * shard_width
    return jnp.stack(
        [
            lax.dynamic_slice_in_dim(gain_sum, offset, shard_width, 0),
            lax.dynamic_slice_in_dim(shift_sum, offset, shard_width, 0),
        ]
    )


def block_a_forward(inputs, weights, mask_in, mask_out, local_counts, channel, saved_stats):
    w_in, w_mid, w_out, w_proj, norm_in, norm_mid, norm_out, norm_proj = weights
    conv_first = jnp.dot(inputs, w_in, preferred_element_type=jnp.float32)
    stats_first = (
        norm_stats(conv_first, mask_in, local_counts, 0) if saved_stats is None else saved_stats[0]
    )
    scaled_first, normed_first = normalize(conv_first, stats_first, norm_in, channel)
    act_first = (jax.nn.silu(normed_first) * mask_in).astype(jnp.bfloat16)
    cols_mid = taps_stride_two(act_first)
    conv_mid = jnp.dot(cols_mid, w_mid, preferred_element_type=jnp.float32)
    stats_mid = (
        norm_stats(conv_mid, mask_out, local_counts, 1) if saved_stats is None else saved_stats[1]
    )
    scaled_mid, normed_mid = normalize(conv_mid, stats_mid, norm_mid, channel)
    act_mid = (jax.nn.silu(normed_mid) * mask_out).astype(jnp.bfloat16)
    conv_out = jnp.dot(act_mid, w_out, preferred_element_type=jnp.float32)
    slot_count, side_in, lane_count = (inputs.shape[0], inputs.shape[1], inputs.shape[3])
    sampled = inputs.reshape(slot_count, side_in // 2, 2, side_in // 2, 2, lane_count)[
        :, :, 0, :, 0, :
    ]
    conv_proj = jnp.dot(sampled, w_proj, preferred_element_type=jnp.float32)
    conv_both = jnp.concatenate([conv_out, conv_proj], axis=-1)
    norm_both = jnp.concatenate([norm_out, norm_proj], axis=-1)
    stats_both = (
        norm_stats(conv_both, mask_out, local_counts, 1) if saved_stats is None else saved_stats[2]
    )
    scaled_both, normed_both = normalize(conv_both, stats_both, norm_both, 1.0)
    width_out = conv_out.shape[-1]
    pre_sum = normed_both[..., :width_out] + normed_both[..., width_out:]
    block_out = jax.nn.silu(pre_sum) * mask_out
    saved_values = (
        scaled_first,
        normed_first,
        act_first,
        cols_mid,
        scaled_mid,
        normed_mid,
        act_mid,
        sampled,
        scaled_both,
        pre_sum,
    )
    return (block_out, (stats_first, stats_mid, stats_both), saved_values)


def block_a_backward(
    grad_out, inputs, weights, stats_all, saved_values, mask_in, mask_out, channel
):
    w_in, w_mid, w_out, w_proj, norm_in, norm_mid, norm_out, norm_proj = weights
    stats_first, stats_mid, stats_both = stats_all
    (
        scaled_first,
        normed_first,
        act_first,
        cols_mid,
        scaled_mid,
        normed_mid,
        act_mid,
        sampled,
        scaled_both,
        pre_sum,
    ) = saved_values
    grad_pre = grad_out * mask_out * silu_slope(pre_sum)
    grad_both = jnp.concatenate([grad_pre, grad_pre], axis=-1)
    norm_both = jnp.concatenate([norm_out, norm_proj], axis=-1)
    low_both, gain_both, shift_both = norm_backward(
        grad_both, scaled_both, stats_both, norm_both, mask_out
    )
    width_out = grad_pre.shape[-1]
    low_out = low_both[..., :width_out]
    low_proj = low_both[..., width_out:]
    grad_w_out = contract(act_mid, low_out)
    grad_w_proj = contract(sampled, low_proj)
    grad_norm_mid = back_project(low_out, w_out) * mask_out * channel * silu_slope(normed_mid)
    low_mid, gain_mid, shift_mid = norm_backward(
        grad_norm_mid, scaled_mid, stats_mid, norm_mid, mask_out
    )
    grad_w_mid = contract(cols_mid, low_mid)
    grad_act_first = fold_stride_two(back_project(low_mid, w_mid), inputs.shape[1])
    grad_norm_first = grad_act_first * mask_in * channel * silu_slope(normed_first)
    low_first, gain_first, shift_first = norm_backward(
        grad_norm_first, scaled_first, stats_first, norm_in, mask_in
    )
    grad_w_in = contract(inputs, low_first)
    spread = lax.pad(
        back_project(low_proj, w_proj),
        jnp.float32(0.0),
        ((0, 0, 0), (0, 1, 1), (0, 1, 1), (0, 0, 0)),
    )
    grad_inputs = (back_project(low_first, w_in) + spread) * mask_in
    norm_grads = (
        (gain_first, shift_first),
        (gain_mid, shift_mid),
        (gain_both[:width_out], shift_both[:width_out]),
        (gain_both[width_out:], shift_both[width_out:]),
    )
    return (grad_inputs, (grad_w_in, grad_w_mid, grad_w_out, grad_w_proj), norm_grads)


def block_b_forward(block_in, weights, mask_out, local_counts, channel, depth_gate, saved_stats):
    w_in, w_mid, w_out, norm_in, norm_mid, norm_out = weights
    feed_in = block_in.astype(jnp.bfloat16)
    conv_first = jnp.dot(feed_in, w_in, preferred_element_type=jnp.float32)
    stats_first = (
        norm_stats(conv_first, mask_out, local_counts, 1) if saved_stats is None else saved_stats[0]
    )
    scaled_first, normed_first = normalize(conv_first, stats_first, norm_in, channel)
    act_first = (jax.nn.silu(normed_first) * mask_out).astype(jnp.bfloat16)
    cols_mid = taps_stride_one(act_first)
    conv_mid = jnp.dot(cols_mid, w_mid, preferred_element_type=jnp.float32)
    stats_mid = (
        norm_stats(conv_mid, mask_out, local_counts, 1) if saved_stats is None else saved_stats[1]
    )
    scaled_mid, normed_mid = normalize(conv_mid, stats_mid, norm_mid, channel)
    act_mid = (jax.nn.silu(normed_mid) * mask_out).astype(jnp.bfloat16)
    conv_out = jnp.dot(act_mid, w_out, preferred_element_type=jnp.float32)
    stats_out = (
        norm_stats(conv_out, mask_out, local_counts, 1) if saved_stats is None else saved_stats[2]
    )
    scaled_out, normed_out = normalize(conv_out, stats_out, norm_out, 1.0)
    pre_sum = block_in + depth_gate * normed_out
    result = jax.nn.silu(pre_sum) * mask_out
    saved_values = (
        feed_in,
        scaled_first,
        normed_first,
        act_first,
        cols_mid,
        scaled_mid,
        normed_mid,
        act_mid,
        scaled_out,
        pre_sum,
    )
    return (result, (stats_first, stats_mid, stats_out), saved_values)


def block_b_backward(grad_out, weights, stats_all, saved_values, mask_out, channel, depth_gate):
    w_in, w_mid, w_out, norm_in, norm_mid, norm_out = weights
    stats_first, stats_mid, stats_out = stats_all
    (
        feed_in,
        scaled_first,
        normed_first,
        act_first,
        cols_mid,
        scaled_mid,
        normed_mid,
        act_mid,
        scaled_out,
        pre_sum,
    ) = saved_values
    grad_pre = grad_out * mask_out * silu_slope(pre_sum)
    low_out, gain_out, shift_out = norm_backward(
        grad_pre * depth_gate, scaled_out, stats_out, norm_out, mask_out
    )
    grad_w_out = contract(act_mid, low_out)
    grad_norm_mid = back_project(low_out, w_out) * mask_out * channel * silu_slope(normed_mid)
    low_mid, gain_mid, shift_mid = norm_backward(
        grad_norm_mid, scaled_mid, stats_mid, norm_mid, mask_out
    )
    grad_w_mid = contract(cols_mid, low_mid)
    grad_norm_first = (
        fold_stride_one(back_project(low_mid, w_mid))
        * mask_out
        * channel
        * silu_slope(normed_first)
    )
    low_first, gain_first, shift_first = norm_backward(
        grad_norm_first, scaled_first, stats_first, norm_in, mask_out
    )
    grad_w_in = contract(feed_in, low_first)
    grad_in = grad_pre + back_project(low_first, w_in)
    norm_grads = ((gain_first, shift_first), (gain_mid, shift_mid), (gain_out, shift_out))
    return (grad_in, (grad_w_in, grad_w_mid, grad_w_out), norm_grads)


def body(
    images,
    image_sides,
    widths,
    keep_gate,
    w_in_a,
    w_mid_a,
    w_out_a,
    w_proj_a,
    norm_in_a,
    norm_mid_a,
    norm_out_a,
    norm_proj_a,
    w_in_b,
    w_mid_b,
    w_out_b,
    norm_in_b,
    norm_mid_b,
    norm_out_b,
    cotangent,
):
    mask_in, mask_out, local_counts = pixel_masks(image_sides, images.shape[1], cotangent.shape[1])
    lane_ids = jnp.arange(w_mid_a.shape[1], dtype=jnp.int32)
    channel_a = (lane_ids < widths[0]).astype(jnp.float32)
    channel_b = (lane_ids < widths[1]).astype(jnp.float32)
    depth_gate = keep_gate.astype(jnp.float32)[:, None, None, None]
    inputs = images * mask_in.astype(jnp.bfloat16)
    total_counts = lax.psum(local_counts, ("fsdp", "dp"))
    gathered = gather_plain((w_in_a, w_mid_a, w_out_a, w_proj_a, w_in_b, w_mid_b, w_out_b))
    norms = lax.all_gather(
        jnp.concatenate(
            [norm_in_a, norm_mid_a, norm_out_a, norm_proj_a, norm_in_b, norm_mid_b, norm_out_b], axis=1
        ),
        "fsdp",
        axis=0,
    )
    wide = []
    place = 0
    for one in (norm_in_a, norm_mid_a, norm_out_a, norm_proj_a, norm_in_b, norm_mid_b, norm_out_b):
        width = one.shape[1]
        wide.append(norms[:, :, place : place + width].transpose(1, 0, 2).reshape(2, -1))
        place += width
    weights_a = tuple(gathered[:4]) + tuple(wide[:4])
    weights_b = tuple(gathered[4:]) + tuple(wide[4:])
    block_out, stats_a, redone_a = block_a_forward(
        inputs, weights_a, mask_in, mask_out, total_counts, channel_a, None
    )
    result, stats_b, redone_b = block_b_forward(
        block_out, weights_b, mask_out, total_counts, channel_b, depth_gate, None
    )
    grad_block, grads_b, norms_b = block_b_backward(
        cotangent.astype(jnp.float32), weights_b, stats_b, redone_b, mask_out, channel_b, depth_gate
    )
    grad_inputs, grads_a, norms_a = block_a_backward(
        grad_block, inputs, weights_a, stats_a, redone_a, mask_in, mask_out, channel_a
    )
    finals = scatter_plain(tuple(one.astype(jnp.bfloat16) for one in grads_a + grads_b))
    final_in_a, final_mid_a, final_out_a, final_proj_a, final_in_b, final_mid_b, final_out_b = (
        one.astype(jnp.float32) for one in finals
    )
    return (
        result.astype(jnp.bfloat16),
        grad_inputs.astype(jnp.bfloat16),
        final_in_a,
        final_mid_a,
        final_out_a,
        final_proj_a,
        own_shard(norms_a[0]),
        own_shard(norms_a[1]),
        own_shard(norms_a[2]),
        own_shard(norms_a[3]),
        final_in_b,
        final_mid_b,
        final_out_b,
        own_shard(norms_b[0]),
        own_shard(norms_b[1]),
        own_shard(norms_b[2]),
    )


def solution(mesh):
    in_specs = (
        P(("fsdp", "dp"), None, None, None),
        P(("fsdp", "dp")),
        P(),
        P(("fsdp", "dp")),
        P("fsdp", None),
        P("fsdp", None),
        P("fsdp", None),
        P("fsdp", None),
        P(None, "fsdp"),
        P(None, "fsdp"),
        P(None, "fsdp"),
        P(None, "fsdp"),
        P("fsdp", None),
        P("fsdp", None),
        P("fsdp", None),
        P(None, "fsdp"),
        P(None, "fsdp"),
        P(None, "fsdp"),
        P(("fsdp", "dp"), None, None, None),
    )
    out_specs = (
        P(("fsdp", "dp"), None, None, None),
        P(("fsdp", "dp"), None, None, None),
        P("fsdp", None),
        P("fsdp", None),
        P("fsdp", None),
        P("fsdp", None),
        P(None, "fsdp"),
        P(None, "fsdp"),
        P(None, "fsdp"),
        P(None, "fsdp"),
        P("fsdp", None),
        P("fsdp", None),
        P("fsdp", None),
        P(None, "fsdp"),
        P(None, "fsdp"),
        P(None, "fsdp"),
    )
    step = body_fast if fits(mesh) else body
    return jax.shard_map(step, mesh=mesh, in_specs=in_specs, out_specs=out_specs, check_vma=False)
```

```python
import functools

import jax
import jax.numpy as jnp
from jax import lax
from jax.experimental import pallas as pl
from jax.experimental.pallas import tpu as pltpu
from jax.sharding import PartitionSpec as P

EPSILON = 1e-05
BY_MESH = pl.DeviceIdType.MESH
F32 = jnp.float32
BF16 = jnp.bfloat16
NAMES = ("in_a", "mid_a", "out_a", "proj_a", "in_b", "mid_b", "out_b")
BLOCK = 256
LANES = 512
CHUNK = 32
SIDE = 7
TAPS = [(u, v) for u in range(3) for v in range(3)]
LINK_PEERS = ((1, 0), (2, 0), (4, 0), (6, 0), (0, 2), (0, 1))
CHIP_PEERS = tuple((a, b) for a in (7, 6, 5, 4, 3, 2, 1, 0) for b in (2, 0) if a or b)
PIECES = {
    "in_a": [(0, 128, 4, 4)],
    "mid_a": [(0, 96, 4, 4), (96, 96, 4, 4), (192, 96, 4, 4), (288, 96, 4, 4), (384, 96, 4, 4), (480, 96, 8, 4)],
    "out_a": [(0, 32, 6, 5), (32, 32, 4, 5)],
    "proj_a": [(0, 64, 6, 5), (64, 64, 4, 5)],
    "in_b": [(0, 128, 4, 4), (128, 128, 4, 4)],
    "mid_b": [(0, 96, 4, 4), (96, 96, 4, 4), (192, 96, 4, 4), (288, 96, 4, 4), (384, 96, 4, 4), (480, 96, 8, 4)],
    "out_b": [(0, 32, 6, 5), (32, 32, 4, 5)],
}
RUN = [
    253, 297, 300, 301, 295, 272, 273, 302, 276, 277, 278, 303, 279, 48, 304, 280, 51, 305, 281, 52, 316, 292,
    53, 69, 54, 72, 55, 317, 73, 56, 74, 293, 90, 312, 75, 93, 67, 244, 15, 94, 14, 13, 313, 95, 298, 76, 77,
    68, 96, 299, 288, 306, 63, 307, 88, 97, 98, 12, 289, 64, 308, 309, 246, 19, 18, 17, 89, 310, 274, 84, 311,
    109, 275, 49, 314, 85, 50, 315, 110, 282, 16, 57, 105, 283, 58, 250, 296, 70, 106, 284, 59, 71, 248, 23,
    22, 78, 285, 79, 60, 91, 286, 61, 92, 80, 287, 21, 62, 99, 245, 290, 100, 65, 81, 291, 20, 27, 101, 26,
    25, 82, 83, 66, 86, 102, 103, 104, 24, 87, 247, 31, 107, 30, 29, 108, 249, 28, 35, 34, 33, 32, 39, 38, 37,
    36, 43, 266, 267, 42, 41, 40, 47, 116, 261, 46, 45, 262, 263, 135, 136, 44, 3, 114, 256, 2, 156, 257, 157,
    127, 1, 128, 129, 130, 131, 132, 177, 178, 148, 0, 7, 112, 251, 6, 5, 149, 150, 252, 119, 120, 151, 268,
    152, 269, 198, 199, 153, 117, 169, 264, 265, 170, 4, 11, 219, 115, 258, 10, 9, 140, 137, 138, 141, 133,
    220, 134, 171, 172, 190, 191, 259, 173, 260, 174, 240, 241, 161, 8, 113, 254, 255, 270, 158, 121, 122,
    123, 124, 125, 126, 271, 111, 294, 162, 159, 118, 154, 179, 155, 192, 193, 211, 212, 194, 195, 232, 182,
    233, 142, 143, 144, 145, 146, 147, 183, 180, 139, 200, 213, 214, 175, 215, 234, 216, 235, 236, 203, 237,
    176, 204, 224, 163, 225, 201, 164, 221, 165, 242, 166, 167, 222, 168, 196, 243, 160, 197, 184, 217, 185,
    238, 218, 186, 205, 239, 187, 206, 226, 188, 207, 227, 189, 208, 228, 181, 209, 229, 210, 230, 231, 202,
    223,
]


def flip(index, bits):
    out = index
    for bit in (1, 2, 4):
        if bits & bit:
            out = out + bit - 2 * bit * ((index // bit) % 2)
    return out


class Place:
    def __init__(self):
        self.f = lax.axis_index("fsdp")
        self.d = lax.axis_index("dp")
        self.y = self.f % 2
        self.z = self.f // 2
        self.c = self.d % 2
        self.x = self.d // 2

    def peer(self, f_bits, d_bits):
        return (flip(self.f, f_bits), flip(self.d, d_bits))


def enter(place, peers):
    barrier = pltpu.get_barrier_semaphore()
    for f_bits, d_bits in peers:
        pl.semaphore_signal(barrier, inc=1, device_id=place.peer(f_bits, d_bits), device_id_type=BY_MESH)
    pl.semaphore_wait(barrier, len(peers))


def push(source, target, send_sem, recv_sem, device):
    pltpu.make_async_remote_copy(
        src_ref=source,
        dst_ref=target,
        send_sem=send_sem,
        recv_sem=recv_sem,
        device_id=device,
        device_id_type=BY_MESH,
    ).start()


def await_bytes(view, sem):
    pltpu.make_async_copy(view, view, sem).wait()


def await_count(ref, count, sem):
    if not count:
        return
    rows_most, columns_most = ref.shape
    for columns in range(columns_most, 0, -128):
        rows = count // columns
        if count % columns == 0 and rows % 16 == 0 and rows <= rows_most:
            await_bytes(ref.at[pl.ds(0, rows), pl.ds(0, columns)], sem)
            return
    raise ValueError(count)


def rows_of(start, size):
    return pl.ds(pl.multiple_of(start, 16), size)


def cols_of(start, size):
    return pl.ds(pl.multiple_of(start, 128), size)


class Gather:
    def __init__(self, place, shard, whole, start, rows, wide_a, send, recv):
        self.place, self.shard, self.whole = place, shard, whole
        self.start, self.rows, self.wide_a = start, rows, wide_a
        self.local, self.send, self.recv = recv.at[6], send, recv
        self.total, columns = shard.shape
        self.half = columns // 2
        self.wide_b = self.half - wide_a
        self.part = rows // 2
        self.col_0 = place.c * self.half
        self.row_q = start + place.x * self.part
        self.row_o = start + self.part - place.x * self.part
        self.near_count = self.part * wide_a + rows * self.wide_b + 3 * self.part * self.half

    def view(self, bits, row, rows, from_col, columns):
        block = flip(self.place.f, bits) * self.total
        return self.whole.at[rows_of(block + row, rows), cols_of(self.col_0 + from_col, columns)]

    def pass_on(self, bits, row, rows, from_col, columns, leg, device):
        view = self.view(bits, row, rows, from_col, columns)
        push(view, view, self.send, self.recv.at[leg], device)

    def first(self):
        half, part, place = self.half, self.part, self.place
        pltpu.make_async_copy(
            self.shard.at[pl.ds(self.start, self.rows), cols_of(self.col_0, half)],
            self.view(0, self.start, self.rows, 0, half),
            self.local,
        ).start()
        for bits in (6, 4, 2):
            push(
                self.shard.at[rows_of(self.row_q, part), cols_of(self.col_0, half)],
                self.view(0, self.row_q, part, 0, half),
                self.send,
                self.recv.at[0],
                place.peer(bits, 0),
            )

    def own(self):
        place = self.place
        for row, rows, col, columns in (
            (self.row_q, self.part, 0, self.wide_a),
            (self.start, self.rows, self.wide_a, self.wide_b),
        ):
            if columns:
                push(
                    self.shard.at[rows_of(row, rows), cols_of(self.col_0 + col, columns)],
                    self.view(0, row, rows, col, columns),
                    self.send,
                    self.recv.at[1],
                    place.peer(1, 0),
                )

    def one(self):
        place = self.place
        await_count(self.whole, self.rows * self.half, self.local)
        await_count(self.whole, 3 * self.part * self.half, self.recv.at[0])
        for bits in (2, 4, 6):
            self.pass_on(bits, self.row_q, self.part, 0, self.half, 1, place.peer(1, 0))
            self.pass_on(bits, self.row_q, self.part, 0, self.half, 2, place.peer(0, 2))

    def two(self):
        place = self.place
        await_count(self.whole, self.near_count, self.recv.at[1])
        await_count(self.whole, 3 * self.part * self.half, self.recv.at[2])
        if self.wide_a:
            for bits in (1, 3, 5, 7):
                self.pass_on(bits, self.row_q, self.part, 0, self.wide_a, 3, place.peer(0, 2))
        if self.wide_b:
            for bits in (2, 4, 6):
                self.pass_on(bits, self.row_o, self.part, self.wide_a, self.wide_b, 4, place.peer(1, 0))

    def three(self):
        place = self.place
        await_count(self.whole, 4 * self.part * self.wide_a, self.recv.at[3])
        await_count(self.whole, 3 * self.part * self.wide_b, self.recv.at[4])
        for bits in range(8):
            self.pass_on(bits, self.start, self.rows, 0, self.half, 5, place.peer(0, 1))

    def four(self):
        await_count(self.whole, 8 * self.rows * self.half, self.recv.at[5])

    def sent(self):
        count = 6 * self.part * self.half + self.near_count + 8 * self.rows * self.half
        count += 4 * self.part * self.wide_a + 3 * self.part * self.wide_b
        await_count(self.whole, count, self.send)


def chunk_of(rows, columns):
    best = 16
    for chunk in range(16, rows + 1, 16):
        if rows % chunk == 0 and chunk * columns <= 16384:
            best = chunk
    return best


def add_blocks(blocks, rows, columns, target, source):
    chunk = chunk_of(rows, columns)
    each = rows // chunk

    def step(index, carry):
        block, start = index // each, pl.multiple_of((index % each) * chunk, 16)
        into, more = target(block, start, chunk), source(block, start, chunk)
        into[...] = (into[...].astype(F32) + more[...].astype(F32)).astype(BF16)
        return carry

    lax.fori_loop(0, blocks * each, step, 0)


class Scatter:
    def __init__(self, place, grad, room, out, start, rows, wide_a, first, send, recv):
        self.place, self.grad, self.out = place, grad, out
        self.start, self.rows, self.wide_a = start, rows, wide_a
        self.first, self.send, self.recv = first, send, recv
        total, columns = room.shape
        self.total = total = total // 8
        self.half = half = columns // 2
        self.wide_b = wide_b = half - wide_a
        self.part = part = rows // 2
        self.room = room
        self.from_core = room.at[:, pl.ds(0, half)]

        def landing(row, count, col, width):
            return room.at[pl.ds(row, count), pl.ds(half + col, width)] if width else None

        self.a_x = landing(4 * start, 4 * rows, 0, wide_a)
        self.a_y = landing(4 * total + 2 * start, 2 * rows, 0, wide_a)
        self.a_z = landing(6 * total + 3 * start // 2, 3 * part, 0, wide_a)
        self.b_y = landing(4 * start, 4 * rows, wide_a, wide_b)
        self.b_z = landing(4 * total + 3 * start, 3 * rows, wide_a, wide_b)
        self.b_x = landing(7 * total + start // 2, part, wide_a, wide_b)
        self.col_0 = place.c * half
        self.row_q = start + place.x * part
        self.row_o = start + part - place.x * part

    def push(self, source, target, leg, device):
        push(source, target, self.send, self.recv.at[leg - 1], device)

    def zero(self):
        other = self.half - self.col_0
        source = self.grad.at[:, cols_of(other, self.half)]
        push(source, self.from_core, self.first.at[0], self.first.at[1], self.place.peer(0, 1))

    def core(self, row, rows, from_col, columns):
        return self.from_core.at[rows_of(row, rows), pl.ds(from_col, columns)]

    def mine(self, row, rows, from_col, columns):
        return self.core(self.place.f * self.total + row, rows, from_col, columns)

    def one(self, first, last):
        place, total, part, rows = self.place, self.total, self.part, self.rows
        if first:
            await_bytes(self.from_core, self.first.at[1])
        add_blocks(
            8,
            rows,
            self.half,
            lambda b, s, n: self.core(b * total + self.start + s, n, 0, self.half),
            lambda b, s, n: self.grad.at[rows_of(b * total + self.start + s, n), cols_of(self.col_0, self.half)],
        )
        if last:
            await_bytes(self.from_core, self.first.at[0])
        if self.wide_a:
            for block in range(8):
                self.push(
                    self.core(block * total + self.row_o, part, 0, self.wide_a),
                    self.a_x.at[pl.ds(block * part, part)],
                    1,
                    place.peer(0, 2),
                )
        if self.wide_b:
            for level in range(4):
                self.push(
                    self.core((2 * level + 1 - place.y) * total + self.start, rows, self.wide_a, self.wide_b),
                    self.b_y.at[pl.ds(level * rows, rows)],
                    2,
                    place.peer(1, 0),
                )

    def two(self):
        place, total, part, rows = self.place, self.total, self.part, self.rows
        if self.wide_a:
            await_bytes(self.a_x, self.recv.at[0])
            add_blocks(
                8,
                part,
                self.wide_a,
                lambda b, s, n: self.core(b * total + self.row_q + s, n, 0, self.wide_a),
                lambda b, s, n: self.a_x.at[rows_of(b * part + s, n)],
            )
            for level in range(4):
                self.push(
                    self.core((2 * level + 1 - place.y) * total + self.row_q, part, 0, self.wide_a),
                    self.a_y.at[pl.ds(level * part, part)],
                    3,
                    place.peer(1, 0),
                )
        if self.wide_b:
            await_bytes(self.b_y, self.recv.at[1])
            add_blocks(
                4,
                rows,
                self.wide_b,
                lambda b, s, n: self.core((2 * b + place.y) * total + self.start + s, n, self.wide_a, self.wide_b),
                lambda b, s, n: self.b_y.at[rows_of(b * rows + s, n)],
            )
            for slot, bits in enumerate((6, 4, 2)):
                self.push(
                    self.core(flip(place.f, bits) * total + self.start, rows, self.wide_a, self.wide_b),
                    self.b_z.at[pl.ds(slot * rows, rows)],
                    4,
                    place.peer(bits, 0),
                )

    def sum_four(self, row, rows, col, wide, landed, store):
        chunk = chunk_of(rows, wide)

        def step(index, carry):
            start = pl.multiple_of(index * chunk, 16)
            total = self.mine(row + start, chunk, col, wide)[...].astype(F32)
            for slot in range(3):
                total = total + landed[rows_of(slot * rows + start, chunk)].astype(F32)
            store(start, chunk, total.astype(BF16))
            return carry

        lax.fori_loop(0, rows // chunk, step, 0)

    def three(self):
        place, total, part, rows = self.place, self.total, self.part, self.rows
        if self.wide_a:
            await_bytes(self.a_y, self.recv.at[2])
            add_blocks(
                4,
                part,
                self.wide_a,
                lambda b, s, n: self.core((2 * b + place.y) * total + self.row_q + s, n, 0, self.wide_a),
                lambda b, s, n: self.a_y.at[rows_of(b * part + s, n)],
            )
            for slot, bits in enumerate((6, 4, 2)):
                self.push(
                    self.core(flip(place.f, bits) * total + self.row_q, part, 0, self.wide_a),
                    self.a_z.at[pl.ds(slot * part, part)],
                    5,
                    place.peer(bits, 0),
                )
        if self.wide_b:
            await_bytes(self.b_z, self.recv.at[3])

            def keep(start, chunk, value):
                self.mine(self.start + start, chunk, self.wide_a, self.wide_b)[...] = value

            self.sum_four(self.start, rows, self.wide_a, self.wide_b, self.b_z, keep)
            self.push(self.mine(self.row_o, part, self.wide_a, self.wide_b), self.b_x, 6, place.peer(0, 2))

    def four(self):
        place, part = self.place, self.part
        if self.wide_a:
            await_bytes(self.a_z, self.recv.at[4])

            def keep(start, chunk, value):
                self.out[rows_of(self.row_q + start, chunk), cols_of(self.col_0, self.wide_a)] = value

            self.sum_four(self.row_q, part, 0, self.wide_a, self.a_z, keep)
        if self.wide_b:
            await_bytes(self.b_x, self.recv.at[5])
            chunk = chunk_of(part, self.wide_b)

            def step(index, carry):
                start = pl.multiple_of(index * chunk, 16)
                total = self.mine(self.row_q + start, chunk, self.wide_a, self.wide_b)[...].astype(F32)
                total = total + self.b_x[rows_of(start, chunk)].astype(F32)
                columns = cols_of(self.col_0 + self.wide_a, self.wide_b)
                self.out[rows_of(self.row_q + start, chunk), columns] = total.astype(BF16)
                return carry

            lax.fori_loop(0, part // chunk, step, 0)
        block = self.out.at[rows_of(self.row_q, part), cols_of(self.col_0, self.half)]
        self.push(block, block, 7, place.peer(0, 2))

    def five(self):
        await_bytes(self.out.at[pl.ds(0, self.part), pl.ds(0, self.half)], self.recv.at[6])
        block = self.out.at[pl.ds(self.start, self.rows), cols_of(self.col_0, self.half)]
        self.push(block, block, 8, self.place.peer(0, 1))

    def six(self):
        await_bytes(self.out.at[pl.ds(0, self.rows), pl.ds(0, self.half)], self.recv.at[7])

    def sent(self):
        await_count(self.room, 18 * self.part * self.half, self.send)


def mm(left, right):
    return jnp.dot(left, right, preferred_element_type=F32)


def mm_nt(left, right):
    return lax.dot_general(left, right, (((1,), (1,)), ((), ())), preferred_element_type=F32)


def mm_tn(left, right):
    return lax.dot_general(left, right, (((0,), (0,)), ((), ())), preferred_element_type=F32)


def loop(count, step):
    def body_of(index, carry):
        step(index)
        return carry

    lax.fori_loop(0, count, body_of, 0)


def at_block(index, size):
    return pl.ds(pl.multiple_of(index * size, size), size)


def slope_of(values):
    gate = jax.nn.sigmoid(values)
    return gate * (1.0 + values * (1.0 - gate))


def fold(values):
    total = values[0:8]
    for start in range(8, values.shape[0], 8):
        total = total + values[start : start + 8]
    return total


def column_sums(count, width, terms):
    def step(index, carry):
        start = pl.multiple_of(index * CHUNK, CHUNK)
        return tuple(total + fold(one) for total, one in zip(carry, terms(start)))

    zero = jnp.zeros((8, LANES), F32)
    totals = lax.fori_loop(0, count, step, (zero,) * width)
    return [jnp.sum(one, axis=0, keepdims=True) for one in totals]


class Vectors:
    def __init__(self, ref):
        self.ref, self.used = ref, 0

    def put(self, row):
        at = self.used
        self.used += 1
        self.ref[at : at + 1, :] = row
        return at

    def get(self, at):
        return self.ref[at : at + 1, :]


class Totals:
    def __init__(self, place, short, long, tot, send, recv):
        self.place, self.short, self.long, self.tot, self.send, self.recv = place, short, long, tot, send, recv
        self.turns, self.is_long, self.rows = [1, 1], 0, 0

    def slot(self, at):
        ref = self.long if self.is_long else self.short
        return ref.at[self.turn, at, pl.ds(0, self.rows)]

    def slots(self, at, count):
        ref = self.long if self.is_long else self.short
        return ref.at[self.turn, pl.ds(at, count), pl.ds(0, self.rows)]

    def spread(self, at, peers, phase):
        own = self.slot(at)
        for bits in peers:
            push(own, own, self.sem(self.send, phase), self.sem(self.recv, phase), self.place.peer(*bits))

    def sem(self, sems, phase):
        return sems.at[self.is_long, self.turn, phase]

    def gather(self, at, count, peers, phase):
        await_bytes(self.slots(at, peers), self.sem(self.recv, phase))
        ref = self.long if self.is_long else self.short
        total = ref[self.turn, at, 0 : self.rows, :]
        for index in range(at + 1, at + count):
            total = total + ref[self.turn, index, 0 : self.rows, :]
        return total

    def start(self, rows_of_values, extra=None):
        count = 4 * len(rows_of_values) + (8 if extra is not None else 0)
        self.is_long = 1 if count > 16 else 0
        self.turns[self.is_long] = self.turn = 1 - self.turns[self.is_long]
        self.rows = count
        own = self.slot(self.place.c)
        at = 0
        for row in rows_of_values:
            for lane in range(0, LANES, 128):
                own[at : at + 1, :] = row[:, lane : lane + 128]
                at += 1
        if extra is not None:
            own[at : at + 8, :] = extra
        self.spread(self.place.c, ((0, 1),), 0)

    def middle(self):
        place = self.place
        total = self.gather(0, 2, 1, 0)
        if self.is_long:
            self.slot(2 + 2 * place.y + place.x)[...] = total
            self.spread(2 + 2 * place.y + place.x, ((1, 2), (1, 0), (0, 2)), 1)
        else:
            self.slot(2 + 2 * place.f + place.x)[...] = total
            self.spread(2 + 2 * place.f + place.x, CHIP_PEERS, 1)

    def late(self):
        if self.is_long:
            self.slot(6 + self.place.z)[...] = self.gather(2, 4, 3, 1)
            self.spread(6 + self.place.z, ((6, 0), (4, 0), (2, 0)), 2)

    def end(self):
        if self.is_long:
            self.tot[0 : self.rows, :] = self.gather(6, 4, 3, 2)
        else:
            self.tot[0 : self.rows, :] = self.gather(2, 16, 15, 1)
        for phase, count in enumerate((1, 3, 3) if self.is_long else (1, 15)):
            await_bytes(self.slots(0, count), self.sem(self.send, phase))

    def row(self, index):
        at = 4 * index
        return jnp.concatenate([self.tot[at + k : at + k + 1, :] for k in range(4)], axis=1)

    def wide(self, at):
        return jnp.concatenate([self.tot[at : at + 1, :]] * 4, axis=1)


def step_kernel(
    img_hbm,
    cot_hbm,
    sides,
    keep,
    widths,
    norm_in_a,
    norm_mid_a,
    norm_out_a,
    norm_proj_a,
    norm_in_b,
    norm_mid_b,
    norm_out_b,
    sh_in_a,
    sh_mid_a,
    sh_out_a,
    sh_proj_a,
    sh_in_b,
    sh_mid_b,
    sh_out_b,
    result_hbm,
    images_hbm,
    own_hbm_in_a,
    own_hbm_mid_a,
    own_hbm_out_a,
    own_hbm_proj_a,
    own_hbm_in_b,
    own_hbm_mid_b,
    own_hbm_out_b,
    out_hbm_in_a,
    out_hbm_mid_a,
    out_hbm_out_a,
    out_hbm_proj_a,
    out_hbm_in_b,
    out_hbm_mid_b,
    out_hbm_out_b,
    own_in_a,
    own_mid_a,
    own_out_a,
    own_proj_a,
    own_in_b,
    own_mid_b,
    own_out_b,
    out_in_a,
    out_mid_a,
    out_out_a,
    out_proj_a,
    out_in_b,
    out_mid_b,
    out_out_b,
    w_in_a,
    w_mid_a,
    w_out_a,
    w_proj_a,
    w_in_b,
    w_mid_b,
    w_out_b,
    raw,
    cot,
    x,
    c1,
    cols_a,
    c2,
    a2,
    c3,
    cp,
    bo,
    feed,
    d1,
    cols_b,
    d2,
    b2,
    d3,
    dz,
    dm,
    df,
    dout,
    dproj,
    g_mid,
    g_out,
    g_in,
    g_proj,
    mask_ref,
    gate_ref,
    move,
    norms,
    block_ref,
    vec_ref,
    short,
    long,
    tot,
    sums,
    io_sem,
    link_send,
    link_recv,
    core_sem,
    ar_send,
    ar_recv,
    nb_sem,
    out_sem,
    free_sem,
):
    place = Place()
    shards = dict(zip(NAMES, (sh_in_a, sh_mid_a, sh_out_a, sh_proj_a, sh_in_b, sh_mid_b, sh_out_b)))
    wholes = dict(zip(NAMES, (w_in_a, w_mid_a, w_out_a, w_proj_a, w_in_b, w_mid_b, w_out_b)))
    outs = dict(zip(NAMES, (out_in_a, out_mid_a, out_out_a, out_proj_a, out_in_b, out_mid_b, out_out_b)))
    owned = dict(zip(NAMES, (own_in_a, own_mid_a, own_out_a, own_proj_a, own_in_b, own_mid_b, own_out_b)))
    own_hbm = (own_hbm_in_a, own_hbm_mid_a, own_hbm_out_a, own_hbm_proj_a, own_hbm_in_b, own_hbm_mid_b, own_hbm_out_b)
    out_hbm = (out_hbm_in_a, out_hbm_mid_a, out_hbm_out_a, out_hbm_proj_a, out_hbm_in_b, out_hbm_mid_b, out_hbm_out_b)
    own_copies = [pltpu.make_async_copy(owned[n], own_hbm[i], out_sem.at[0, i]) for i, n in enumerate(NAMES)]
    out_copies = [pltpu.make_async_copy(outs[n], out_hbm[i], out_sem.at[1, i]) for i, n in enumerate(NAMES)]
    small = dict(zip(NAMES, (norm_in_a, norm_mid_a, norm_out_a, norm_proj_a, norm_in_b, norm_mid_b, norm_out_b)))
    grads = dict(mid_a=g_mid, mid_b=g_mid, out_a=g_out, out_b=g_out, in_b=g_in, proj_a=g_proj)
    grads["in_a"] = g_in.at[pl.ds(0, wholes["in_a"].shape[0])]
    todo = {}

    def token(name):
        def keep_it(function):
            todo[name] = function
            return function

        return keep_it

    def tokens(name, count, each, step):
        for part in range(count):
            todo[f"{name}.{part}"] = functools.partial(loop, each, lambda k, first=part * each: step(first + k))

    gathers, scatters, at = {}, {}, 0
    left = {name: len(PIECES[name]) for name in NAMES}

    def finish_piece(name, piece):
        piece.six()
        left[name] -= 1
        if not left[name]:
            out_copies[NAMES.index(name)].start()

    for name in NAMES:
        eighth = shards[name].shape[1] // 16
        for n, (start, rows, way_in, way_out) in enumerate(PIECES[name]):
            sems = link_send.at[at], link_recv.at[at]
            g = Gather(place, shards[name], wholes[name], start, rows, way_in * eighth, *sems)
            first_sem = core_sem.at[NAMES.index(name)]
            s = Scatter(
                place, grads[name], wholes[name], outs[name], start, rows, way_out * eighth, first_sem, *sems
            )
            gathers[name, n], scatters[name, n] = g, s
            at += 1
            key = f"{name}.{n}"
            todo["z." + key], todo["o." + key], todo["L1." + key] = g.first, g.own, g.one
            todo["L2." + key], todo["L3." + key] = g.two, g.three
            if n == 0:
                todo["S0." + name] = s.zero
            todo["S1." + key] = functools.partial(s.one, n == 0, n == len(PIECES[name]) - 1)
            todo["S2." + key], todo["S3." + key], todo["S4." + key] = s.two, s.three, s.four
            todo["S5." + key] = s.five
            todo["S6." + key] = functools.partial(finish_piece, name, s)

        def arrived(name=name):
            for n in range(len(PIECES[name])):
                gathers[name, n].four()

        todo["W." + name] = arrived

    vec = Vectors(vec_ref)
    totals = Totals(place, short, long, tot, ar_send, ar_recv)
    state, scales, params = {}, {}, {}
    for n in range(1, 13):
        todo[f"A{n}m"] = totals.middle
        todo[f"A{n}l"] = totals.late

    image_copy = pltpu.make_async_copy(img_hbm, raw, io_sem.at[0])
    cot_copy = pltpu.make_async_copy(cot_hbm, cot, io_sem.at[1])
    result_copy = pltpu.make_async_copy(cot, result_hbm, io_sem.at[2])
    grad_copy = pltpu.make_async_copy(raw, images_hbm, io_sem.at[3])

    @token("enter")
    def _():
        image_copy.start()
        cot_copy.start()
        odd = (place.f % 2).astype(F32)
        block_ref[...] = jnp.zeros_like(block_ref)
        at = 0
        for name in NAMES:
            values = small[name][...].astype(F32)
            if values.shape[1] < 128:
                move[0:8, 0:128] = jnp.zeros((8, 128), F32)
                move[0:2, 0 : values.shape[1]] = values
                plain = move[0:8, 0:128]
                values = (plain + (pltpu.roll(plain, 64, 1) - plain) * odd)[0:2]
            for lane in range(0, values.shape[1], 128):
                block_ref[at : at + 1, :] = values[0:1, lane : lane + 128]
                block_ref[at + 10 : at + 11, :] = values[1:2, lane : lane + 128]
                at += 1
        norms[place.f] = block_ref[...]
        enter(place, ((0, 1),) + CHIP_PEERS)
        for bits in (7, 6, 5, 4, 3, 2, 1):
            push(block_ref, norms.at[place.f], nb_sem.at[0], nb_sem.at[1], place.peer(bits, 0))

    @token("prep")
    def _():
        pixel = lax.broadcasted_iota(jnp.int32, (BLOCK, 128), 0)
        slot = pixel % 4

        def by_slot(values):
            return jnp.where(slot == 0, values[0], jnp.where(slot == 1, values[1], jnp.where(slot == 2, values[2], values[3])))

        half = by_slot([sides[i] // 2 for i in range(4)])
        inside = ((pixel // 4) % 8 < half) & (pixel // 32 < half)
        mask_ref[...] = jnp.where(inside, 1.0, 0.0).astype(F32)
        gate_ref[...] = by_slot([keep[i] for i in range(4)]).astype(F32)
        move[...] = jnp.zeros_like(move)
        image_copy.wait()

        def plane_rows(row):
            mask = jnp.concatenate([mask_ref[at_block(row, CHUNK), :]] * (x.shape[1] // 128), axis=1)
            for row_par in range(2):
                for col_par in range(2):
                    for col in range(SIDE):
                        move[4 * col : 4 * col + 4, :] = raw[2 * row + row_par, 2 * col + col_par].astype(F32)
                    start = (2 * row_par + col_par) * BLOCK + row * CHUNK
                    x[pl.ds(pl.multiple_of(start, CHUNK), CHUNK), :] = (move[...] * mask).astype(BF16)

        loop(SIDE, plane_rows)
        for p in range(4):
            x[(p + 1) * BLOCK - CHUNK : (p + 1) * BLOCK, :] = jnp.zeros((CHUNK, x.shape[1]), BF16)

    @token("norms")
    def _():
        await_bytes(norms.at[pl.ds(0, 7)], nb_sem.at[1])
        await_bytes(norms.at[pl.ds(0, 7)], nb_sem.at[0])

        def narrow_row(at):
            pieces = [norms[2 * k, at : at + 1, :] + norms[2 * k + 1, at : at + 1, :] for k in range(4)]
            return vec.put(jnp.concatenate(pieces, axis=1))

        def wide_rows(at):
            return [
                vec.put(
                    jnp.concatenate(
                        [norms[2 * j + k // 2, at + k % 2 : at + k % 2 + 1, :] for k in range(4)], axis=1
                    )
                )
                for j in range(4)
            ]

        params["in_a"] = ([narrow_row(0)], [narrow_row(10)])
        params["mid_a"] = ([narrow_row(1)], [narrow_row(11)])
        params["out_a"] = (wide_rows(2), wide_rows(12))
        params["proj_a"] = (wide_rows(4), wide_rows(14))
        params["in_b"] = ([narrow_row(6)], [narrow_row(16)])
        params["mid_b"] = ([narrow_row(7)], [narrow_row(17)])
        params["out_b"] = (wide_rows(8), wide_rows(18))
        lanes = lax.broadcasted_iota(jnp.int32, (1, LANES), 1)
        state["chan_a"] = vec.put(jnp.where(lanes < widths[0], 1.0, 0.0).astype(F32))
        state["chan_b"] = vec.put(jnp.where(lanes < widths[1], 1.0, 0.0).astype(F32))

    def wide_of(ref, start, size=CHUNK):
        return jnp.concatenate([ref[pl.ds(start, size), :]] * 4, axis=1)

    def mask_at(start):
        return wide_of(mask_ref, start)

    def gate_at(start):
        return wide_of(gate_ref, start)

    def set_norm(name, block, first_row, inverse, chan):
        inverse = vec.get(state[inverse])
        average = totals.row(first_row) * inverse
        rstd = lax.rsqrt(totals.row(first_row + 1) * inverse - average * average + EPSILON)
        gain, shift = (vec.get(rows[block]) for rows in params[name])
        keep_lanes = 1.0 if chan is None else vec.get(state[chan])
        by = gain * rstd
        scales[name, block] = dict(
            rstd=vec.put(rstd),
            off=vec.put(-average * rstd),
            by=vec.put(by),
            mul=vec.put(by * keep_lanes),
            add=vec.put((shift - average * by) * keep_lanes),
        )

    def normed(name, block, values):
        s = scales[name, block]
        return values * vec.get(s["mul"]) + vec.get(s["add"])

    def hat(name, block, values):
        s = scales[name, block]
        return values * vec.get(s["rstd"]) + vec.get(s["off"])

    def set_back(name, block, shift_row, gain_row):
        s = scales[name, block]
        inverse = vec.get(state["inv_in" if name == "in_a" else "inv_out"])
        by = vec.get(s["by"])
        pull = by * totals.row(gain_row) * inverse
        s["back_add"] = vec.put(by * totals.row(shift_row) * inverse + pull * vec.get(s["off"]))
        s["back_mul"] = vec.put(pull * vec.get(s["rstd"]))

    def back(name, block, grad, values):
        s = scales[name, block]
        return grad * vec.get(s["by"]) - vec.get(s["back_add"]) - values * vec.get(s["back_mul"])

    def square_terms(ref):
        def terms(start):
            values = ref[pl.ds(start, CHUNK), :]
            return values, values * values

        return terms

    def masked_terms(ref):
        def terms(start):
            values = ref[pl.ds(start, CHUNK), :]
            kept = values * mask_at(start)
            return kept, kept * values

        return terms

    def lane_row(at, lane):
        return vec_ref[at : at + 1, at_block(lane, 128)]

    def add_up(out, count, left, right, product=mm):
        out[...] = product(left(0), right(0))

        def more(k):
            out[...] += product(left(k + 1), right(k + 1))

        loop(count - 1, more)

    @token("A1s")
    def _():
        def first_a(p):
            c1[at_block(p, BLOCK), :] = mm(x[at_block(p, BLOCK), :], w_in_a[...])

        loop(4, first_a)
        side = [sides[i] for i in range(4)]
        count_in = sum(s * s for s in side).astype(F32)
        count_out = sum((s // 2) * (s // 2) for s in side).astype(F32)
        at = lax.broadcasted_iota(jnp.int32, (8, 128), 0)
        counts = jnp.where(at == 0, count_in, jnp.where(at == 1, count_out, 0.0))
        totals.start(column_sums(32, 2, square_terms(c1)), counts)

    @token("A1e")
    def _():
        totals.end()
        state["inv_in"] = vec.put(1.0 / totals.wide(8))
        state["inv_out"] = vec.put(1.0 / totals.wide(9))
        set_norm("in_a", 0, 0, "inv_in", "chan_a")
        s = scales["in_a", 0]

        def act_a(lane):
            for row_par in range(2):
                for col_par in range(2):
                    p = 2 * row_par + col_par
                    values = c1[p * BLOCK : (p + 1) * BLOCK, at_block(lane, 128)]
                    scaled = values * lane_row(s["mul"], lane) + lane_row(s["add"], lane)
                    act = scaled * jax.nn.sigmoid(scaled) * mask_ref[...]
                    for t, (u, v) in enumerate(TAPS):
                        if (u != 1) != bool(row_par) or (v != 1) != bool(col_par):
                            continue
                        shift = (32 if u == 0 else 0) + (4 if v == 0 else 0)
                        moved = pltpu.roll(act, shift, 0) if shift else act
                        cols_a[:, pl.ds(pl.multiple_of(t * LANES + lane * 128, 128), 128)] = moved.astype(BF16)

        loop(4, act_a)

    def conv_mid(out, cols, weight):
        def at(k):
            return pl.ds(pl.multiple_of(k * 1536, 512), 1536)

        add_up(out, 3, lambda k: cols[:, at(k)], lambda k: weight[at(k), :])

    def act_mid(act_ref, ref, name):
        def step(index):
            start = pl.multiple_of(index * CHUNK, CHUNK)
            scaled = normed(name, 0, ref[pl.ds(start, CHUNK), :])
            act_ref[pl.ds(start, CHUNK), :] = (scaled * jax.nn.sigmoid(scaled) * mask_at(start)).astype(BF16)

        loop(BLOCK // CHUNK, step)

    @token("A2s")
    def _():
        conv_mid(c2, cols_a, w_mid_a)
        totals.start(column_sums(8, 2, masked_terms(c2)))

    @token("A2e")
    def _():
        totals.end()
        set_norm("mid_a", 0, 0, "inv_out", "chan_a")
        act_mid(a2, c2, "mid_a")

    @token("proj")
    def _():
        def project(j):
            cp[at_block(j, BLOCK), :] = mm(x[0:BLOCK, :], w_proj_a[:, at_block(j, LANES)])

        loop(4, project)

    def blocked(ref, j):
        return square_terms(ref.at[pl.ds(j * BLOCK, BLOCK)])

    @token("A3s")
    def _():
        def expand_a(j):
            c3[at_block(j, BLOCK), :] = mm(a2[...], w_out_a[:, at_block(j, LANES)])

        loop(4, expand_a)
        totals.start([row for ref in (c3, cp) for j in range(4) for row in column_sums(8, 2, blocked(ref, j))])

    @token("A3e")
    def _():
        totals.end()
        for j in range(4):
            set_norm("out_a", j, 2 * j, "inv_out", None)
            set_norm("proj_a", j, 8 + 2 * j, "inv_out", None)
        for j in range(4):

            def join_a(index, j=j):
                start = pl.multiple_of(index * CHUNK, CHUNK)
                rows = pl.ds(j * BLOCK + start, CHUNK)
                pre = normed("out_a", j, c3[rows, :]) + normed("proj_a", j, cp[rows, :])
                out = pre * jax.nn.sigmoid(pre) * mask_at(start)
                bo[rows, :] = out
                feed[pl.ds(start, CHUNK), pl.ds(j * LANES, LANES)] = out.astype(BF16)

            loop(BLOCK // CHUNK, join_a)

    @token("A4s")
    def _():
        add_up(d1, 4, lambda k: feed[:, at_block(k, LANES)], lambda k: w_in_b[at_block(k, LANES), :])
        totals.start(column_sums(8, 2, square_terms(d1)))

    @token("A4e")
    def _():
        totals.end()
        set_norm("in_b", 0, 0, "inv_out", "chan_b")
        s = scales["in_b", 0]

        def act_b(lane):
            scaled = d1[:, at_block(lane, 128)] * lane_row(s["mul"], lane) + lane_row(s["add"], lane)
            act = scaled * jax.nn.sigmoid(scaled) * mask_ref[...]
            for t, (u, v) in enumerate(TAPS):
                shift = (-(32 * (u - 1) + 4 * (v - 1))) % BLOCK
                moved = pltpu.roll(act, shift, 0) if shift else act
                cols_b[:, pl.ds(pl.multiple_of(t * LANES + lane * 128, 128), 128)] = moved.astype(BF16)

        loop(4, act_b)

    @token("A5s")
    def _():
        conv_mid(d2, cols_b, w_mid_b)
        totals.start(column_sums(8, 2, masked_terms(d2)))

    @token("A5e")
    def _():
        totals.end()
        set_norm("mid_b", 0, 0, "inv_out", "chan_b")
        act_mid(b2, d2, "mid_b")

    @token("A6s")
    def _():
        def expand_b(j):
            d3[at_block(j, BLOCK), :] = mm(b2[...], w_out_b[:, at_block(j, LANES)])

        loop(4, expand_b)
        totals.start([row for j in range(4) for row in column_sums(8, 2, blocked(d3, j))])

    @token("A6e")
    def _():
        totals.end()
        for j in range(4):
            set_norm("out_b", j, 2 * j, "inv_out", None)

    @token("A7s")
    def _():
        for one in gathers.values():
            one.sent()
        cot_copy.wait()
        values = []
        for j in range(4):
            lanes = pl.ds(j * LANES, LANES)

            def finish(start, j=j, lanes=lanes):
                rows = pl.ds(j * BLOCK + start, CHUNK)
                row = start // CHUNK
                for col in range(SIDE):
                    move[4 * col : 4 * col + 4, 0:LANES] = cot[row, col, :, lanes].astype(F32)
                mask, gate, hidden = mask_at(start), gate_at(start), d3[rows, :]
                pre = bo[rows, :] + gate * normed("out_b", j, hidden)
                part = jax.nn.sigmoid(pre)
                grad = move[:, 0:LANES] * mask * (part * (1.0 + pre * (1.0 - part)))
                move[:, LANES : 2 * LANES] = pre * part * mask
                for col in range(SIDE):
                    cot[row, col, :, lanes] = move[4 * col : 4 * col + 4, LANES : 2 * LANES].astype(BF16)
                bo[rows, :] = grad
                grad = grad * gate
                return grad, grad * hat("out_b", j, hidden)

            values += column_sums(SIDE, 2, finish)
            bo[(j + 1) * BLOCK - CHUNK : (j + 1) * BLOCK, :] = jnp.zeros((CHUNK, LANES), F32)
        result_copy.start()
        totals.start(values)

    def keep_sums(at):
        rows = totals.rows
        sums[at : at + rows, :] = tot[0:rows, :]

    @token("A7e")
    def _():
        totals.end()
        keep_sums(0)
        for j in range(4):
            set_back("out_b", j, 2 * j, 2 * j + 1)

    def through_out(weight):
        add_up(dz, 4, lambda k: dout[:, at_block(k, LANES)], lambda k: weight[:, at_block(k, LANES)], mm_nt)

    def slope_terms(grad_ref, ref, name, chan):
        def terms(start):
            rows = pl.ds(start, CHUNK)
            hidden = ref[rows, :]
            mask = mask_at(pl.multiple_of(start % BLOCK, CHUNK) if grad_ref.shape[0] > BLOCK else start)
            grad = grad_ref[rows, :] * mask * vec.get(state[chan]) * slope_of(normed(name, 0, hidden))
            grad_ref[rows, :] = grad
            return grad, grad * hat(name, 0, hidden)

        return terms

    @token("A8s")
    def _():
        for j in range(4):

            def low_out_b(index, j=j):
                start = pl.multiple_of(index * CHUNK, CHUNK)
                rows = pl.ds(j * BLOCK + start, CHUNK)
                grad = back("out_b", j, bo[rows, :] * gate_at(start), d3[rows, :]) * mask_at(start)
                dout[pl.ds(start, CHUNK), pl.ds(j * LANES, LANES)] = grad.astype(BF16)

            loop(BLOCK // CHUNK, low_out_b)
        through_out(w_out_b)
        totals.start(column_sums(8, 2, slope_terms(dz, d2, "mid_b", "chan_b")))

    def grad_out(act_ref, j):
        g_out[:, at_block(j, LANES)] = mm_tn(act_ref[...], dout[:, at_block(j, LANES)]).astype(BF16)

    tokens("g.out_b", 2, 2, lambda j: grad_out(b2, j))

    @token("A8e")
    def _():
        totals.end()
        keep_sums(32)
        set_back("mid_b", 0, 0, 1)

    def low_mid(name, ref, shifts):
        s = scales[name, 0]

        def step(lane):
            lanes = at_block(lane, 128)
            grad = (
                dz[:, lanes] * lane_row(s["by"], lane)
                - lane_row(s["back_add"], lane)
                - ref[:, lanes] * lane_row(s["back_mul"], lane)
            ) * mask_ref[...]
            dm[:, lanes] = grad.astype(BF16)
            for k, shift in enumerate(shifts):
                moved = pltpu.roll(grad, shift, 0) if shift else grad
                g_mid[k * BLOCK : (k + 1) * BLOCK, lanes] = moved.astype(BF16)

        loop(4, step)

    @token("A9s")
    def _():
        low_mid("mid_b", d2, [(32 * (u - 1) + 4 * (v - 1)) % BLOCK for u, v in TAPS])
        add_up(dz, 9, lambda t: g_mid[at_block(t, BLOCK), :], lambda t: w_mid_b[at_block(t, LANES), :], mm_nt)
        totals.start(column_sums(8, 2, slope_terms(dz, d1, "in_b", "chan_b")))

    def grad_mid(cols, t):
        g_mid[at_block(t, LANES), :] = mm_tn(cols[:, at_block(t, LANES)], dm[...]).astype(BF16)

    tokens("g.mid_b", 3, 3, lambda t: grad_mid(cols_b, t))

    @token("A9e")
    def _():
        totals.end()
        keep_sums(40)
        set_back("in_b", 0, 0, 1)

    @token("A10s")
    def _():
        def low_first_b(index):
            start = pl.multiple_of(index * CHUNK, CHUNK)
            rows = pl.ds(start, CHUNK)
            df[rows, :] = (back("in_b", 0, dz[rows, :], d1[rows, :]) * mask_at(start)).astype(BF16)

        loop(BLOCK // CHUNK, low_first_b)

        def back_in_b(j):
            bo[at_block(j, BLOCK), :] += mm_nt(df[...], w_in_b[at_block(j, LANES), :])

        loop(4, back_in_b)
        values = []
        for j in range(4):

            def join_back(start, j=j):
                rows = pl.ds(j * BLOCK + start, CHUNK)
                left, right = c3[rows, :], cp[rows, :]
                pre = normed("out_a", j, left) + normed("proj_a", j, right)
                grad = bo[rows, :] * mask_at(start) * slope_of(pre)
                bo[rows, :] = grad
                return grad, grad * hat("out_a", j, left), grad * hat("proj_a", j, right)

            values += column_sums(8, 3, join_back)
        totals.start(values)

    def grad_in_b(j):
        g_in[at_block(j, LANES), :] = mm_tn(feed[:, at_block(j, LANES)], df[...]).astype(BF16)

    tokens("g.in_b", 2, 2, grad_in_b)

    @token("A10e")
    def _():
        totals.end()
        keep_sums(48)
        for j in range(4):
            set_back("out_a", j, 3 * j, 3 * j + 1)
            set_back("proj_a", j, 3 * j, 3 * j + 2)

    @token("A11s")
    def _():
        for j in range(4):

            def low_both(index, j=j):
                start = pl.multiple_of(index * CHUNK, CHUNK)
                rows = pl.ds(j * BLOCK + start, CHUNK)
                near_rows, lanes = pl.ds(start, CHUNK), pl.ds(j * LANES, LANES)
                grad, mask = bo[rows, :], mask_at(start)
                dout[near_rows, lanes] = (back("out_a", j, grad, c3[rows, :]) * mask).astype(BF16)
                dproj[near_rows, lanes] = (back("proj_a", j, grad, cp[rows, :]) * mask).astype(BF16)

            loop(BLOCK // CHUNK, low_both)
        through_out(w_out_a)
        totals.start(column_sums(8, 2, slope_terms(dz, c2, "mid_a", "chan_a")))

    tokens("g.out_a", 2, 2, lambda j: grad_out(a2, j))

    def grad_proj(n):
        i, j = n // 4, n % 4
        g_proj[at_block(i, LANES), at_block(j, LANES)] = mm_tn(
            x[0:BLOCK, at_block(i, LANES)], dproj[:, at_block(j, LANES)]
        ).astype(BF16)

    tokens("g.proj_a", 2, 4, grad_proj)

    def tell(at):
        for bits in LINK_PEERS:
            pl.semaphore_signal(free_sem.at[at], inc=1, device_id=place.peer(*bits), device_id_type=BY_MESH)

    def told(at, name):
        def go():
            pl.semaphore_wait(free_sem.at[at], len(LINK_PEERS))
            scatters[name, 0].zero()

        todo["S0." + name] = go

    def back_proj(n):
        out, rows = d3.at[pl.ds(n * BLOCK, BLOCK)], pl.ds(n * LANES, LANES)
        add_up(out, 4, lambda k: dproj[:, at_block(k, LANES)], lambda k: w_proj_a[rows, at_block(k, LANES)], mm_nt)

    @token("dproj.0")
    def _():
        back_proj(0)

    @token("dproj.1")
    def _():
        back_proj(1)
        tell(0)

    told(0, "proj_a")

    @token("A11e")
    def _():
        totals.end()
        keep_sums(96)
        set_back("mid_a", 0, 0, 1)

    @token("A12s")
    def _():
        low_mid("mid_a", c2, [(-(32 * r + 4 * s)) % BLOCK for r in range(2) for s in range(2)])
        for row_par in range(2):
            for col_par in range(2):
                grad = None
                for t, (u, v) in enumerate(TAPS):
                    if (u != 1) != bool(row_par) or (v != 1) != bool(col_par):
                        continue
                    moved = 2 * (1 if u == 0 else 0) + (1 if v == 0 else 0)
                    term = mm_nt(g_mid[moved * BLOCK : (moved + 1) * BLOCK, :], w_mid_a[t * LANES : (t + 1) * LANES, :])
                    grad = term if grad is None else grad + term
                bo[pl.ds((2 * row_par + col_par) * BLOCK, BLOCK), :] = grad
        totals.start(column_sums(32, 2, slope_terms(bo, c1, "in_a", "chan_a")))

    tokens("g.mid_a", 3, 3, lambda t: grad_mid(cols_a, t))

    @token("A12e")
    def _():
        totals.end()
        keep_sums(104)
        set_back("in_a", 0, 0, 1)
        for p in range(4):

            def low_first_a(index, p=p):
                start = pl.multiple_of(index * CHUNK, CHUNK)
                rows = pl.ds(p * BLOCK + start, CHUNK)
                grad = back("in_a", 0, bo[rows, :], c1[rows, :]) * mask_at(start)
                cols_b[pl.ds(start, CHUNK), p * LANES : (p + 1) * LANES] = grad.astype(BF16)

            loop(BLOCK // CHUNK, low_first_a)

    def first_grad(p):
        return cols_b[:, p * LANES : (p + 1) * LANES]

    def grad_in_a(i):
        lanes = at_block(i, 256)
        total = mm_tn(x[0:BLOCK, lanes], first_grad(0))
        for p in range(1, 4):
            total = total + mm_tn(x[p * BLOCK : (p + 1) * BLOCK, lanes], first_grad(p))
        g_in[at_block(i, 256), :] = total.astype(BF16)

    tokens("g.in_a", 2, 2, grad_in_a)

    def image_grad(planes):
        for p in planes:
            for h in range(2):
                lanes = pl.ds(h * LANES, LANES)
                grad = mm_nt(first_grad(p), w_in_a[h * LANES : (h + 1) * LANES, :])
                dz[...] = grad + d3[h * BLOCK : (h + 1) * BLOCK, :] if p == 0 else grad

                def pixels(row, p=p, lanes=lanes):
                    move[:, 0:LANES] = dz[at_block(row, CHUNK), :]
                    for col in range(SIDE):
                        raw[2 * row + p // 2, 2 * col + p % 2, :, lanes] = move[4 * col : 4 * col + 4, 0:LANES].astype(BF16)

                loop(SIDE, pixels)

    @token("img.0")
    def _():
        image_grad((0, 1))

    @token("img.1")
    def _():
        image_grad((2, 3))
        grad_copy.start()
        tell(1)

    told(1, "in_a")

    @token("own")
    def _():
        def own_row(at, out, k):
            if out.shape[1] >= 128:
                for lane in range(2):
                    line = sums[pl.ds(at + 2 * (place.f % 2) + lane, 1), :]
                    out[k : k + 1, lane * 128 : (lane + 1) * 128] = line
            else:
                odd = (place.f % 2).astype(F32)
                move[0:1, 0:128] = sums[pl.ds(at + place.f // 2, 1), :]
                line = move[0:8, 0:128]
                line = line + (pltpu.roll(line, 64, 1) - line) * odd
                out[k : k + 1, :] = line[0:1, 0 : out.shape[1]]

        for name, at in (("mid_b", 32), ("in_b", 40), ("mid_a", 96), ("in_a", 104)):
            own_row(at + 4, owned[name], 0)
            own_row(at, owned[name], 1)
        block = place.f // 2
        for name, at, step, gain in (("out_b", 0, 8, 4), ("out_a", 48, 12, 4), ("proj_a", 48, 12, 8)):
            own_row(at + step * block + gain, owned[name], 0)
            own_row(at + step * block, owned[name], 1)
        for one in own_copies:
            one.start()

    steps = sorted(todo)
    if sorted(RUN) != list(range(len(steps))):
        raise ValueError(len(steps))
    for index in RUN:
        todo[steps[index]]()
    result_copy.wait()
    grad_copy.wait()
    for one in scatters.values():
        one.sent()
    for one in own_copies + out_copies:
        one.wait()


def finish_kernel(*refs):
    arrays_in, arrays_out, held, wide = refs[:16], refs[16:32], refs[32:48], refs[48:55]
    in_sem, out_sem = refs[55:]
    loads = [pltpu.make_async_copy(a, b, in_sem.at[i]) for i, (a, b) in enumerate(zip(arrays_in, held))]
    leaving = held[:9] + wide
    stores = [pltpu.make_async_copy(a, b, out_sem.at[i]) for i, (a, b) in enumerate(zip(leaving, arrays_out))]
    order = list(range(9, 16)) + list(range(9))
    for i in order:
        loads[i].start()
    for i in order:
        loads[i].wait()
        if i >= 9:
            narrow, target = held[i], wide[i - 9]
            rows, columns = narrow.shape
            chunk = chunk_of(rows, columns)

            def step(index, carry, narrow=narrow, target=target, chunk=chunk):
                at = pl.ds(pl.multiple_of(index * chunk, 16), chunk)
                target[at, :] = narrow[at, :].astype(F32)
                return carry

            lax.fori_loop(0, rows // chunk, step, 0)
        stores[i].start()
    for i in order:
        stores[i].wait()


def finish_call(plain, grads):
    anywhere = pl.BlockSpec(memory_space=pl.ANY)
    return pl.pallas_call(
        finish_kernel,
        out_shape=[jax.ShapeDtypeStruct(one.shape, one.dtype) for one in plain]
        + [jax.ShapeDtypeStruct(one.shape, F32) for one in grads],
        in_specs=[anywhere] * 16,
        out_specs=[anywhere] * 16,
        scratch_shapes=[pltpu.VMEM(one.shape, one.dtype) for one in (*plain, *grads)]
        + [pltpu.VMEM(one.shape, F32) for one in grads]
        + [pltpu.SemaphoreType.DMA((16,)), pltpu.SemaphoreType.DMA((16,))],
        compiler_params=pltpu.CompilerParams(vmem_limit_bytes=64 * 2**20),
        name="finish_step",
    )(*plain, *grads)


def body_fast(
    images,
    image_sides,
    widths,
    keep_gate,
    w_in_a,
    w_mid_a,
    w_out_a,
    w_proj_a,
    norm_in_a,
    norm_mid_a,
    norm_out_a,
    norm_proj_a,
    w_in_b,
    w_mid_b,
    w_out_b,
    norm_in_b,
    norm_mid_b,
    norm_out_b,
    cotangent,
):
    width_in, width_out = images.shape[3], cotangent.shape[3]
    turned = (1, 2, 0, 3)
    images, cotangent = images.transpose(turned), cotangent.transpose(turned)
    norms = (norm_in_a, norm_mid_a, norm_out_a, norm_proj_a, norm_in_b, norm_mid_b, norm_out_b)
    shards = (w_in_a, w_mid_a, w_out_a, w_proj_a, w_in_b, w_mid_b, w_out_b)
    vmem = pl.BlockSpec(memory_space=pltpu.VMEM)
    smem = pl.BlockSpec(memory_space=pltpu.SMEM)
    anywhere = pl.BlockSpec(memory_space=pl.ANY)
    wholes = [(8 * one.shape[0], one.shape[1]) for one in shards]
    pieces = sum(len(one) for one in PIECES.values())
    outs = pl.pallas_call(
        step_kernel,
        out_shape=[jax.ShapeDtypeStruct(cotangent.shape, BF16), jax.ShapeDtypeStruct(images.shape, BF16)]
        + [jax.ShapeDtypeStruct(one.shape, F32) for one in norms]
        + [jax.ShapeDtypeStruct(one.shape, BF16) for one in shards],
        in_specs=[anywhere, anywhere, smem, smem, smem] + [vmem] * 7 + [anywhere] * 7,
        out_specs=[anywhere] * 16,
        scratch_shapes=[pltpu.VMEM(one.shape, F32) for one in norms]
        + [pltpu.VMEM(one.shape, BF16) for one in shards]
        + [pltpu.VMEM(shape, BF16) for shape in wholes]
        + [
            pltpu.VMEM(images.shape, BF16),
            pltpu.VMEM(cotangent.shape, BF16),
            pltpu.VMEM((4 * BLOCK, width_in), BF16),
            pltpu.VMEM((4 * BLOCK, LANES), F32),
            pltpu.VMEM((BLOCK, 9 * LANES), BF16),
            pltpu.VMEM((BLOCK, LANES), F32),
            pltpu.VMEM((BLOCK, LANES), BF16),
            pltpu.VMEM((4 * BLOCK, LANES), F32),
            pltpu.VMEM((4 * BLOCK, LANES), F32),
            pltpu.VMEM((4 * BLOCK, LANES), F32),
            pltpu.VMEM((BLOCK, width_out), BF16),
            pltpu.VMEM((BLOCK, LANES), F32),
            pltpu.VMEM((BLOCK, 9 * LANES), BF16),
            pltpu.VMEM((BLOCK, LANES), F32),
            pltpu.VMEM((BLOCK, LANES), BF16),
            pltpu.VMEM((4 * BLOCK, LANES), F32),
            pltpu.VMEM((BLOCK, LANES), F32),
            pltpu.VMEM((BLOCK, LANES), BF16),
            pltpu.VMEM((BLOCK, LANES), BF16),
            pltpu.VMEM((BLOCK, width_out), BF16),
            pltpu.VMEM((BLOCK, width_out), BF16),
            pltpu.VMEM(wholes[1], BF16),
            pltpu.VMEM(wholes[2], BF16),
            pltpu.VMEM(wholes[4], BF16),
            pltpu.VMEM(wholes[3], BF16),
            pltpu.VMEM((BLOCK, 128), F32),
            pltpu.VMEM((BLOCK, 128), F32),
            pltpu.VMEM((CHUNK, width_in), F32),
            pltpu.VMEM((8, 24, 128), F32),
            pltpu.VMEM((24, 128), F32),
            pltpu.VMEM((160, LANES), F32),
            pltpu.VMEM((2, 18, 16, 128), F32),
            pltpu.VMEM((2, 10, 64, 128), F32),
            pltpu.VMEM((64, 128), F32),
            pltpu.VMEM((112, 128), F32),
            pltpu.SemaphoreType.DMA((4,)),
            pltpu.SemaphoreType.DMA((pieces,)),
            pltpu.SemaphoreType.DMA((pieces, 8)),
            pltpu.SemaphoreType.DMA((7, 2)),
            pltpu.SemaphoreType.DMA((2, 2, 3)),
            pltpu.SemaphoreType.DMA((2, 2, 3)),
            pltpu.SemaphoreType.DMA((2,)),
            pltpu.SemaphoreType.DMA((2, 7)),
            pltpu.SemaphoreType.REGULAR((2,)),
        ],
        compiler_params=pltpu.CompilerParams(
            collective_id=0, has_side_effects=True, vmem_limit_bytes=64 * 2**20
        ),
        name="whole_step",
    )(images, cotangent, image_sides, keep_gate, widths, *norms, *shards)
    back_turned = (2, 0, 1, 3)
    outs = finish_call(outs[:9], outs[9:])
    own, finals = outs[2:9], outs[9:]
    return (
        outs[0].transpose(back_turned),
        outs[1].transpose(back_turned),
        *finals[:4],
        *own[:4],
        *finals[4:],
        *own[4:],
    )


def fits(mesh):
    return mesh.shape["fsdp"] == 8 and mesh.shape["dp"] == 4


def gather_plain(shards):
    return [lax.all_gather(one, "fsdp", axis=0, tiled=True) for one in shards]


def scatter_plain(grads):
    parts = [lax.psum_scatter(one, "fsdp", scatter_dimension=0, tiled=True) for one in grads]
    return lax.psum(tuple(parts), "dp")


def sum_pair(first, second):
    return lax.psum((first, second), ("fsdp", "dp"))


def silu_slope(values):
    sigmoid_part = jax.nn.sigmoid(values)
    return sigmoid_part * (1.0 + values * (1.0 - sigmoid_part))


def pixel_masks(image_sides, side_in, side_out):
    half_sides = image_sides // 2
    rows_in = jnp.arange(side_in, dtype=jnp.int32)
    rows_out = jnp.arange(side_out, dtype=jnp.int32)
    inside_in = (rows_in[None, :, None] < image_sides[:, None, None]) & (
        rows_in[None, None, :] < image_sides[:, None, None]
    )
    inside_out = (rows_out[None, :, None] < half_sides[:, None, None]) & (
        rows_out[None, None, :] < half_sides[:, None, None]
    )
    local_counts = jnp.stack(
        [jnp.sum(image_sides * image_sides), jnp.sum(half_sides * half_sides)]
    ).astype(jnp.float32)
    return (
        inside_in.astype(jnp.float32)[..., None],
        inside_out.astype(jnp.float32)[..., None],
        local_counts,
    )


def norm_stats(hidden, pixel_mask, local_counts, count_slot):
    sum_values, sum_squares = sum_pair(
        jnp.sum(hidden * pixel_mask, axis=(0, 1, 2)),
        jnp.sum(hidden * hidden * pixel_mask, axis=(0, 1, 2)),
    )
    pixel_total = local_counts[count_slot]
    average = sum_values / pixel_total
    inv_std = lax.rsqrt(sum_squares / pixel_total - average * average + EPSILON)
    return (average, inv_std, pixel_total)


def normalize(hidden, stats_now, params, channel):
    average, inv_std, pixel_total = stats_now
    scaled = (hidden - average) * inv_std
    params_wide = params.astype(jnp.float32)
    return (scaled, (scaled * params_wide[0] + params_wide[1]) * channel)


def norm_backward(grad_norm, scaled, stats_now, params, pixel_mask):
    average, inv_std, pixel_total = stats_now
    shift_sum, gain_sum = sum_pair(
        jnp.sum(grad_norm, axis=(0, 1, 2)), jnp.sum(grad_norm * scaled, axis=(0, 1, 2))
    )
    gain_row = params[0].astype(jnp.float32)
    grad_hidden = (
        gain_row
        * inv_std
        * (grad_norm - shift_sum / pixel_total - scaled * gain_sum / pixel_total)
        * pixel_mask
    )
    return (grad_hidden.astype(jnp.bfloat16), gain_sum, shift_sum)


def taps_stride_two(activations):
    slot_count = activations.shape[0]
    half_side = activations.shape[1] // 2
    lane_count = activations.shape[3]
    padded = jnp.pad(activations, ((0, 0), (1, 1), (1, 1), (0, 0)))
    parity_grid = padded.reshape(slot_count, half_side + 1, 2, half_side + 1, 2, lane_count)
    pieces = [
        parity_grid[
            :,
            row_tap // 2 : row_tap // 2 + half_side,
            row_tap % 2,
            col_tap // 2 : col_tap // 2 + half_side,
            col_tap % 2,
            :,
        ]
        for row_tap in range(3)
        for col_tap in range(3)
    ]
    return jnp.concatenate(pieces, axis=-1)


def fold_stride_two(grad_cols, side_in):
    slot_count = grad_cols.shape[0]
    half_side = grad_cols.shape[1]
    lane_count = grad_cols.shape[3] // 9
    planes = [
        [
            jnp.zeros((slot_count, half_side + 1, half_side + 1, lane_count), jnp.float32)
            for col_par in range(2)
        ]
        for row_par in range(2)
    ]
    for row_tap in range(3):
        for col_tap in range(3):
            tap_index = row_tap * 3 + col_tap
            tap_piece = grad_cols[..., tap_index * lane_count : (tap_index + 1) * lane_count]
            placed = jnp.pad(
                tap_piece,
                (
                    (0, 0),
                    (row_tap // 2, 1 - row_tap // 2),
                    (col_tap // 2, 1 - col_tap // 2),
                    (0, 0),
                ),
            )
            planes[row_tap % 2][col_tap % 2] = planes[row_tap % 2][col_tap % 2] + placed
    parity_grid = jnp.stack([jnp.stack(planes[0], axis=3), jnp.stack(planes[1], axis=3)], axis=2)
    whole_grid = parity_grid.reshape(slot_count, side_in + 2, side_in + 2, lane_count)
    return whole_grid[:, 1:-1, 1:-1, :]


def taps_stride_one(activations):
    side_now = activations.shape[1]
    padded = jnp.pad(activations, ((0, 0), (1, 1), (1, 1), (0, 0)))
    pieces = [
        padded[:, row_tap : row_tap + side_now, col_tap : col_tap + side_now, :]
        for row_tap in range(3)
        for col_tap in range(3)
    ]
    return jnp.concatenate(pieces, axis=-1)


def fold_stride_one(grad_cols):
    lane_count = grad_cols.shape[3] // 9
    whole_grid = None
    for row_tap in range(3):
        for col_tap in range(3):
            tap_index = row_tap * 3 + col_tap
            tap_piece = grad_cols[..., tap_index * lane_count : (tap_index + 1) * lane_count]
            placed = jnp.pad(
                tap_piece, ((0, 0), (row_tap, 2 - row_tap), (col_tap, 2 - col_tap), (0, 0))
            )
            whole_grid = placed if whole_grid is None else whole_grid + placed
    return whole_grid[:, 1:-1, 1:-1, :]


def contract(left_side, right_side):
    return lax.dot_general(
        left_side,
        right_side,
        (((0, 1, 2), (0, 1, 2)), ((), ())),
        preferred_element_type=jnp.float32,
    )


def back_project(gradient, weight):
    return lax.dot_general(
        gradient, weight, (((3,), (1,)), ((), ())), preferred_element_type=jnp.float32
    )


def own_shard(pair_sums):
    gain_sum, shift_sum = pair_sums
    shard_width = gain_sum.shape[0] // lax.axis_size("fsdp")
    offset = lax.axis_index("fsdp") * shard_width
    return jnp.stack(
        [
            lax.dynamic_slice_in_dim(gain_sum, offset, shard_width, 0),
            lax.dynamic_slice_in_dim(shift_sum, offset, shard_width, 0),
        ]
    )


def block_a_forward(inputs, weights, mask_in, mask_out, local_counts, channel, saved_stats):
    w_in, w_mid, w_out, w_proj, norm_in, norm_mid, norm_out, norm_proj = weights
    conv_first = jnp.dot(inputs, w_in, preferred_element_type=jnp.float32)
    stats_first = (
        norm_stats(conv_first, mask_in, local_counts, 0) if saved_stats is None else saved_stats[0]
    )
    scaled_first, normed_first = normalize(conv_first, stats_first, norm_in, channel)
    act_first = (jax.nn.silu(normed_first) * mask_in).astype(jnp.bfloat16)
    cols_mid = taps_stride_two(act_first)
    conv_mid = jnp.dot(cols_mid, w_mid, preferred_element_type=jnp.float32)
    stats_mid = (
        norm_stats(conv_mid, mask_out, local_counts, 1) if saved_stats is None else saved_stats[1]
    )
    scaled_mid, normed_mid = normalize(conv_mid, stats_mid, norm_mid, channel)
    act_mid = (jax.nn.silu(normed_mid) * mask_out).astype(jnp.bfloat16)
    conv_out = jnp.dot(act_mid, w_out, preferred_element_type=jnp.float32)
    slot_count, side_in, lane_count = (inputs.shape[0], inputs.shape[1], inputs.shape[3])
    sampled = inputs.reshape(slot_count, side_in // 2, 2, side_in // 2, 2, lane_count)[
        :, :, 0, :, 0, :
    ]
    conv_proj = jnp.dot(sampled, w_proj, preferred_element_type=jnp.float32)
    conv_both = jnp.concatenate([conv_out, conv_proj], axis=-1)
    norm_both = jnp.concatenate([norm_out, norm_proj], axis=-1)
    stats_both = (
        norm_stats(conv_both, mask_out, local_counts, 1) if saved_stats is None else saved_stats[2]
    )
    scaled_both, normed_both = normalize(conv_both, stats_both, norm_both, 1.0)
    width_out = conv_out.shape[-1]
    pre_sum = normed_both[..., :width_out] + normed_both[..., width_out:]
    block_out = jax.nn.silu(pre_sum) * mask_out
    saved_values = (
        scaled_first,
        normed_first,
        act_first,
        cols_mid,
        scaled_mid,
        normed_mid,
        act_mid,
        sampled,
        scaled_both,
        pre_sum,
    )
    return (block_out, (stats_first, stats_mid, stats_both), saved_values)


def block_a_backward(
    grad_out, inputs, weights, stats_all, saved_values, mask_in, mask_out, channel
):
    w_in, w_mid, w_out, w_proj, norm_in, norm_mid, norm_out, norm_proj = weights
    stats_first, stats_mid, stats_both = stats_all
    (
        scaled_first,
        normed_first,
        act_first,
        cols_mid,
        scaled_mid,
        normed_mid,
        act_mid,
        sampled,
        scaled_both,
        pre_sum,
    ) = saved_values
    grad_pre = grad_out * mask_out * silu_slope(pre_sum)
    grad_both = jnp.concatenate([grad_pre, grad_pre], axis=-1)
    norm_both = jnp.concatenate([norm_out, norm_proj], axis=-1)
    low_both, gain_both, shift_both = norm_backward(
        grad_both, scaled_both, stats_both, norm_both, mask_out
    )
    width_out = grad_pre.shape[-1]
    low_out = low_both[..., :width_out]
    low_proj = low_both[..., width_out:]
    grad_w_out = contract(act_mid, low_out)
    grad_w_proj = contract(sampled, low_proj)
    grad_norm_mid = back_project(low_out, w_out) * mask_out * channel * silu_slope(normed_mid)
    low_mid, gain_mid, shift_mid = norm_backward(
        grad_norm_mid, scaled_mid, stats_mid, norm_mid, mask_out
    )
    grad_w_mid = contract(cols_mid, low_mid)
    grad_act_first = fold_stride_two(back_project(low_mid, w_mid), inputs.shape[1])
    grad_norm_first = grad_act_first * mask_in * channel * silu_slope(normed_first)
    low_first, gain_first, shift_first = norm_backward(
        grad_norm_first, scaled_first, stats_first, norm_in, mask_in
    )
    grad_w_in = contract(inputs, low_first)
    spread = lax.pad(
        back_project(low_proj, w_proj),
        jnp.float32(0.0),
        ((0, 0, 0), (0, 1, 1), (0, 1, 1), (0, 0, 0)),
    )
    grad_inputs = (back_project(low_first, w_in) + spread) * mask_in
    norm_grads = (
        (gain_first, shift_first),
        (gain_mid, shift_mid),
        (gain_both[:width_out], shift_both[:width_out]),
        (gain_both[width_out:], shift_both[width_out:]),
    )
    return (grad_inputs, (grad_w_in, grad_w_mid, grad_w_out, grad_w_proj), norm_grads)


def block_b_forward(block_in, weights, mask_out, local_counts, channel, depth_gate, saved_stats):
    w_in, w_mid, w_out, norm_in, norm_mid, norm_out = weights
    feed_in = block_in.astype(jnp.bfloat16)
    conv_first = jnp.dot(feed_in, w_in, preferred_element_type=jnp.float32)
    stats_first = (
        norm_stats(conv_first, mask_out, local_counts, 1) if saved_stats is None else saved_stats[0]
    )
    scaled_first, normed_first = normalize(conv_first, stats_first, norm_in, channel)
    act_first = (jax.nn.silu(normed_first) * mask_out).astype(jnp.bfloat16)
    cols_mid = taps_stride_one(act_first)
    conv_mid = jnp.dot(cols_mid, w_mid, preferred_element_type=jnp.float32)
    stats_mid = (
        norm_stats(conv_mid, mask_out, local_counts, 1) if saved_stats is None else saved_stats[1]
    )
    scaled_mid, normed_mid = normalize(conv_mid, stats_mid, norm_mid, channel)
    act_mid = (jax.nn.silu(normed_mid) * mask_out).astype(jnp.bfloat16)
    conv_out = jnp.dot(act_mid, w_out, preferred_element_type=jnp.float32)
    stats_out = (
        norm_stats(conv_out, mask_out, local_counts, 1) if saved_stats is None else saved_stats[2]
    )
    scaled_out, normed_out = normalize(conv_out, stats_out, norm_out, 1.0)
    pre_sum = block_in + depth_gate * normed_out
    result = jax.nn.silu(pre_sum) * mask_out
    saved_values = (
        feed_in,
        scaled_first,
        normed_first,
        act_first,
        cols_mid,
        scaled_mid,
        normed_mid,
        act_mid,
        scaled_out,
        pre_sum,
    )
    return (result, (stats_first, stats_mid, stats_out), saved_values)


def block_b_backward(grad_out, weights, stats_all, saved_values, mask_out, channel, depth_gate):
    w_in, w_mid, w_out, norm_in, norm_mid, norm_out = weights
    stats_first, stats_mid, stats_out = stats_all
    (
        feed_in,
        scaled_first,
        normed_first,
        act_first,
        cols_mid,
        scaled_mid,
        normed_mid,
        act_mid,
        scaled_out,
        pre_sum,
    ) = saved_values
    grad_pre = grad_out * mask_out * silu_slope(pre_sum)
    low_out, gain_out, shift_out = norm_backward(
        grad_pre * depth_gate, scaled_out, stats_out, norm_out, mask_out
    )
    grad_w_out = contract(act_mid, low_out)
    grad_norm_mid = back_project(low_out, w_out) * mask_out * channel * silu_slope(normed_mid)
    low_mid, gain_mid, shift_mid = norm_backward(
        grad_norm_mid, scaled_mid, stats_mid, norm_mid, mask_out
    )
    grad_w_mid = contract(cols_mid, low_mid)
    grad_norm_first = (
        fold_stride_one(back_project(low_mid, w_mid))
        * mask_out
        * channel
        * silu_slope(normed_first)
    )
    low_first, gain_first, shift_first = norm_backward(
        grad_norm_first, scaled_first, stats_first, norm_in, mask_out
    )
    grad_w_in = contract(feed_in, low_first)
    grad_in = grad_pre + back_project(low_first, w_in)
    norm_grads = ((gain_first, shift_first), (gain_mid, shift_mid), (gain_out, shift_out))
    return (grad_in, (grad_w_in, grad_w_mid, grad_w_out), norm_grads)


def body(
    images,
    image_sides,
    widths,
    keep_gate,
    w_in_a,
    w_mid_a,
    w_out_a,
    w_proj_a,
    norm_in_a,
    norm_mid_a,
    norm_out_a,
    norm_proj_a,
    w_in_b,
    w_mid_b,
    w_out_b,
    norm_in_b,
    norm_mid_b,
    norm_out_b,
    cotangent,
):
    mask_in, mask_out, local_counts = pixel_masks(image_sides, images.shape[1], cotangent.shape[1])
    lane_ids = jnp.arange(w_mid_a.shape[1], dtype=jnp.int32)
    channel_a = (lane_ids < widths[0]).astype(jnp.float32)
    channel_b = (lane_ids < widths[1]).astype(jnp.float32)
    depth_gate = keep_gate.astype(jnp.float32)[:, None, None, None]
    inputs = images * mask_in.astype(jnp.bfloat16)
    total_counts = lax.psum(local_counts, ("fsdp", "dp"))
    gathered = gather_plain((w_in_a, w_mid_a, w_out_a, w_proj_a, w_in_b, w_mid_b, w_out_b))
    norms = lax.all_gather(
        jnp.concatenate(
            [norm_in_a, norm_mid_a, norm_out_a, norm_proj_a, norm_in_b, norm_mid_b, norm_out_b], axis=1
        ),
        "fsdp",
        axis=0,
    )
    wide = []
    place = 0
    for one in (norm_in_a, norm_mid_a, norm_out_a, norm_proj_a, norm_in_b, norm_mid_b, norm_out_b):
        width = one.shape[1]
        wide.append(norms[:, :, place : place + width].transpose(1, 0, 2).reshape(2, -1))
        place += width
    weights_a = tuple(gathered[:4]) + tuple(wide[:4])
    weights_b = tuple(gathered[4:]) + tuple(wide[4:])
    block_out, stats_a, redone_a = block_a_forward(
        inputs, weights_a, mask_in, mask_out, total_counts, channel_a, None
    )
    result, stats_b, redone_b = block_b_forward(
        block_out, weights_b, mask_out, total_counts, channel_b, depth_gate, None
    )
    grad_block, grads_b, norms_b = block_b_backward(
        cotangent.astype(jnp.float32), weights_b, stats_b, redone_b, mask_out, channel_b, depth_gate
    )
    grad_inputs, grads_a, norms_a = block_a_backward(
        grad_block, inputs, weights_a, stats_a, redone_a, mask_in, mask_out, channel_a
    )
    finals = scatter_plain(tuple(one.astype(jnp.bfloat16) for one in grads_a + grads_b))
    final_in_a, final_mid_a, final_out_a, final_proj_a, final_in_b, final_mid_b, final_out_b = (
        one.astype(jnp.float32) for one in finals
    )
    return (
        result.astype(jnp.bfloat16),
        grad_inputs.astype(jnp.bfloat16),
        final_in_a,
        final_mid_a,
        final_out_a,
        final_proj_a,
        own_shard(norms_a[0]),
        own_shard(norms_a[1]),
        own_shard(norms_a[2]),
        own_shard(norms_a[3]),
        final_in_b,
        final_mid_b,
        final_out_b,
        own_shard(norms_b[0]),
        own_shard(norms_b[1]),
        own_shard(norms_b[2]),
    )


def solution(mesh):
    in_specs = (
        P(("fsdp", "dp"), None, None, None),
        P(("fsdp", "dp")),
        P(),
        P(("fsdp", "dp")),
        P("fsdp", None),
        P("fsdp", None),
        P("fsdp", None),
        P("fsdp", None),
        P(None, "fsdp"),
        P(None, "fsdp"),
        P(None, "fsdp"),
        P(None, "fsdp"),
        P("fsdp", None),
        P("fsdp", None),
        P("fsdp", None),
        P(None, "fsdp"),
        P(None, "fsdp"),
        P(None, "fsdp"),
        P(("fsdp", "dp"), None, None, None),
    )
    out_specs = (
        P(("fsdp", "dp"), None, None, None),
        P(("fsdp", "dp"), None, None, None),
        P("fsdp", None),
        P("fsdp", None),
        P("fsdp", None),
        P("fsdp", None),
        P(None, "fsdp"),
        P(None, "fsdp"),
        P(None, "fsdp"),
        P(None, "fsdp"),
        P("fsdp", None),
        P("fsdp", None),
        P("fsdp", None),
        P(None, "fsdp"),
        P(None, "fsdp"),
        P(None, "fsdp"),
    )
    step = body_fast if fits(mesh) else body
    return jax.shard_map(step, mesh=mesh, in_specs=in_specs, out_specs=out_specs, check_vma=False)
```

```python
import functools

import jax
import jax.numpy as jnp
from jax import lax
from jax.experimental import pallas as pl
from jax.experimental.pallas import tpu as pltpu
from jax.sharding import PartitionSpec as P

EPSILON = 1e-05
BY_MESH = pl.DeviceIdType.MESH
FSDP, DP = "fsdp", "dp"
F32 = jnp.float32
BF16 = jnp.bfloat16
NAMES = ("in_a", "mid_a", "out_a", "proj_a", "in_b", "mid_b", "out_b")
BLOCK = 256
LANES = 512
CHUNK = 32
SIDE = 7
ZYX, ZXY, YZX = range(3)
TAPS = [(u, v) for u in range(3) for v in range(3)]
LINK_PEERS = ((1, 0), (2, 0), (4, 0), (6, 0), (0, 2), (0, 1))
CHIP_PEERS = tuple((a, b) for a in (7, 6, 5, 4, 3, 2, 1, 0) for b in (2, 0) if a or b)
WAYS_IN = {
    "in_a": ((0, 64, ((ZYX, 4), (ZXY, 4))), (64, 64, ((YZX, 4), (ZXY, 4)))),
    "mid_a": ((0, 192, ((ZYX, 4), (ZXY, 4))), (192, 192, ((YZX, 4), (ZXY, 4))), (384, 192, ((ZYX, 4), (ZXY, 4)))),
    "out_a": ((0, 32, ((ZYX, 2), (ZXY, 4), (YZX, 2))), (32, 32, ((ZYX, 2), (ZXY, 4), (YZX, 2)))),
    "proj_a": ((0, 64, ((ZYX, 2), (ZXY, 4), (YZX, 2))), (64, 64, ((ZYX, 2), (ZXY, 4), (YZX, 2)))),
    "in_b": ((0, 256, ((ZYX, 4), (ZXY, 4))),),
    "mid_b": ((0, 96, ((ZYX, 4), (ZXY, 4))), (96, 96, ((YZX, 4), (ZXY, 4))), (192, 96, ((ZYX, 4), (ZXY, 4))), (288, 96, ((YZX, 4), (ZXY, 4))), (384, 96, ((ZYX, 4), (ZXY, 4))), (480, 96, ((YZX, 4), (ZXY, 4)))),
    "out_b": ((0, 32, ((ZYX, 2), (ZXY, 4), (YZX, 2))), (32, 32, ((ZYX, 2), (ZXY, 4), (YZX, 2)))),
}
WAYS_OUT = {
    "in_a": ((0, 64, 4), (64, 64, 4)),
    "mid_a": ((0, 96, 4), (96, 96, 4), (192, 96, 4), (288, 96, 4), (384, 96, 4), (480, 96, 4)),
    "out_a": ((0, 32, 5), (32, 32, 5)),
    "proj_a": ((0, 32, 5), (32, 32, 5), (64, 32, 5), (96, 32, 5)),
    "in_b": ((0, 128, 4), (128, 128, 4)),
    "mid_b": ((0, 96, 4), (96, 96, 4), (192, 96, 4), (288, 96, 4), (384, 96, 4), (480, 96, 4)),
    "out_b": ((0, 32, 5), (32, 32, 5)),
}
RUN = [
    262, 303, 282, 304, 306, 283, 301, 285, 48, 49, 307, 308, 319, 320, 299, 286, 66, 67, 51, 287, 52, 298,
    85, 315, 294, 84, 253, 69, 316, 53, 295, 15, 14, 64, 71, 65, 70, 60, 61, 305, 13, 89, 284, 281, 87, 88,
    82, 83, 12, 255, 309, 19, 18, 310, 288, 79, 311, 100, 312, 78, 313, 291, 289, 290, 101, 50, 97, 314, 17,
    292, 54, 259, 96, 302, 16, 257, 55, 23, 317, 22, 293, 68, 58, 73, 21, 57, 56, 296, 72, 86, 59, 318, 91,
    76, 20, 254, 75, 27, 297, 74, 26, 77, 25, 62, 93, 94, 63, 90, 92, 95, 24, 80, 256, 31, 81, 30, 29, 98, 99,
    28, 258, 35, 34, 33, 32, 39, 38, 37, 36, 43, 275, 42, 41, 276, 107, 127, 128, 40, 47, 270, 271, 46, 272,
    105, 151, 152, 45, 119, 120, 44, 175, 3, 176, 143, 2, 121, 122, 265, 144, 266, 1, 123, 145, 200, 199, 124,
    146, 103, 167, 0, 111, 147, 168, 7, 169, 273, 274, 6, 260, 148, 106, 170, 112, 277, 125, 171, 5, 135, 126,
    261, 278, 172, 191, 136, 108, 4, 193, 11, 149, 10, 9, 159, 129, 194, 267, 223, 268, 150, 269, 160, 104,
    173, 130, 153, 113, 174, 183, 114, 218, 247, 8, 300, 154, 131, 192, 177, 137, 196, 263, 115, 138, 132,
    178, 264, 155, 279, 161, 198, 116, 139, 162, 280, 117, 156, 102, 220, 197, 118, 179, 207, 163, 109, 222,
    140, 180, 186, 184, 110, 244, 246, 202, 216, 141, 221, 142, 195, 201, 240, 185, 133, 203, 134, 217, 226,
    204, 209, 165, 225, 210, 166, 187, 227, 157, 224, 164, 158, 215, 189, 219, 190, 181, 188, 208, 249, 233,
    211, 234, 228, 182, 232, 239, 213, 245, 214, 205, 212, 206, 248, 229, 235, 242, 237, 252, 250, 241, 251,
    231, 238, 236, 243, 230,
]


def flip(index, bits):
    out = index
    for bit in (1, 2, 4):
        if bits & bit:
            out = out + bit - 2 * bit * ((index // bit) % 2)
    return out


class Place:
    def __init__(self):
        self.f = lax.axis_index(FSDP)
        self.d = lax.axis_index(DP)
        self.y = self.f % 2
        self.z = self.f // 2
        self.c = self.d % 2
        self.x = self.d // 2

    def peer(self, f_bits, d_bits):
        return (flip(self.f, f_bits), flip(self.d, d_bits))


def enter(place, peers):
    barrier = pltpu.get_barrier_semaphore()
    for f_bits, d_bits in peers:
        pl.semaphore_signal(barrier, inc=1, device_id=place.peer(f_bits, d_bits), device_id_type=BY_MESH)
    pl.semaphore_wait(barrier, len(peers))


def push(source, target, send_sem, recv_sem, device):
    pltpu.make_async_remote_copy(
        src_ref=source,
        dst_ref=target,
        send_sem=send_sem,
        recv_sem=recv_sem,
        device_id=device,
        device_id_type=BY_MESH,
    ).start()


def await_bytes(view, sem):
    pltpu.make_async_copy(view, view, sem).wait()


def await_count(ref, count, sem):
    if not count:
        return
    rows_most, columns_most = ref.shape
    for columns in range(columns_most, 0, -128):
        rows = count // columns
        if count % columns == 0 and rows % 16 == 0 and rows <= rows_most:
            await_bytes(ref.at[pl.ds(0, rows), pl.ds(0, columns)], sem)
            return
    raise ValueError(count)


def rows_of(start, size):
    return pl.ds(pl.multiple_of(start, 16), size)


def cols_of(start, size):
    return pl.ds(pl.multiple_of(start, 128), size)


class Gather:
    def __init__(self, place, shard, whole, start, rows, groups, send, recv):
        self.place, self.shard, self.whole = place, shard, whole
        self.start, self.rows, self.send, self.recv = start, rows, send, recv
        self.total, columns = shard.shape
        self.half = half = columns // 2
        self.part = part = rows // 2
        self.col_0 = place.c * half
        self.row_q = start + place.x * part
        self.row_o = start + part - place.x * part
        self.arriving, self.leaving = [0] * 4, 0
        self.groups, at = {}, 0
        for way, eighths in groups:
            self.groups[way] = (at, half * eighths // 8)
            at += half * eighths // 8

    def view(self, bits, row, rows, from_col, columns):
        block = flip(self.place.f, bits) * self.total
        return self.whole.at[rows_of(block + row, rows), cols_of(self.col_0 + from_col, columns)]

    def pass_on(self, bits, row, rows, group, leg, peer):
        from_col, columns = group
        view = self.view(bits, row, rows, from_col, columns)
        push(view, view, self.send, self.recv.at[leg], self.place.peer(*peer))
        self.arriving[leg] += rows * columns
        self.leaving += rows * columns

    def pass_own(self, row, rows, group, leg, peer):
        from_col, columns = group
        source = self.shard.at[rows_of(row, rows), cols_of(self.col_0 + from_col, columns)]
        push(source, self.view(0, row, rows, from_col, columns), self.send, self.recv.at[leg], self.place.peer(*peer))
        self.arriving[leg] += rows * columns
        self.leaving += rows * columns

    def arrive(self, leg):
        await_count(self.whole, self.arriving[leg], self.recv.at[leg])

    def first(self):
        pltpu.make_async_copy(
            self.shard.at[pl.ds(self.start, self.rows), cols_of(self.col_0, self.half)],
            self.view(0, self.start, self.rows, 0, self.half),
            self.recv.at[0],
        ).start()
        self.arriving[0] += self.rows * self.half
        for bits in (6, 4, 2):
            self.pass_own(self.row_q, self.part, (0, self.half), 0, (bits, 0))

    def own(self):
        for way, group in self.groups.items():
            if way == ZXY:
                self.pass_own(self.start, self.rows, group, 0, (1, 0))
            else:
                self.pass_own(self.row_q, self.part, group, 0, (1, 0))

    def one(self):
        self.arrive(0)
        if YZX in self.groups:
            for bits in (6, 4, 2):
                self.pass_on(1, self.row_q, self.part, self.groups[YZX], 1, (bits, 0))
        for way, group in self.groups.items():
            for bits in (2, 4, 6):
                if way != YZX:
                    self.pass_on(bits, self.row_q, self.part, group, 1, (1, 0))
                self.pass_on(bits, self.row_q, self.part, group, 1, (0, 2))
            if way == YZX:
                self.pass_on(1, self.row_q, self.part, group, 1, (0, 2))

    def two(self):
        self.arrive(1)
        for way, group in self.groups.items():
            if way == ZXY:
                for bits in (2, 4, 6):
                    self.pass_on(bits, self.row_o, self.part, group, 2, (1, 0))
            else:
                for bits in (1, 3, 5, 7) if way == ZYX else (3, 5, 7):
                    self.pass_on(bits, self.row_q, self.part, group, 2, (0, 2))

    def three(self):
        self.arrive(2)
        for bits in range(8):
            self.pass_on(bits, self.start, self.rows, (0, self.half), 3, (0, 1))

    def four(self):
        self.arrive(3)

    def sent(self):
        await_count(self.whole, self.leaving, self.send)


def chunk_of(rows, columns):
    best = 16
    for chunk in range(16, rows + 1, 16):
        if rows % chunk == 0 and chunk * columns <= 16384:
            best = chunk
    return best


def add_blocks(blocks, rows, columns, target, source):
    chunk = chunk_of(rows, columns)
    each = rows // chunk

    def step(index, carry):
        block, start = index // each, pl.multiple_of((index % each) * chunk, 16)
        into, more = target(block, start, chunk), source(block, start, chunk)
        into[...] = (into[...].astype(F32) + more[...].astype(F32)).astype(BF16)
        return carry

    lax.fori_loop(0, blocks * each, step, 0)


class Scatter:
    def __init__(self, place, grad, room, out, start, rows, wide_a, first, send, recv):
        self.place, self.grad, self.out = place, grad, out
        self.start, self.rows, self.wide_a = start, rows, wide_a
        self.first, self.send, self.recv = first, send, recv
        total, columns = room.shape
        self.total = total = total // 8
        self.half = half = columns // 2
        self.wide_b = wide_b = half - wide_a
        self.part = part = rows // 2
        self.room = room
        self.from_core = room.at[:, pl.ds(0, half)]

        def landing(row, count, col, width):
            return room.at[pl.ds(row, count), pl.ds(half + col, width)] if width else None

        self.a_x = landing(4 * start, 4 * rows, 0, wide_a)
        self.a_y = landing(4 * total + 2 * start, 2 * rows, 0, wide_a)
        self.a_z = landing(6 * total + 3 * start // 2, 3 * part, 0, wide_a)
        self.b_y = landing(4 * start, 4 * rows, wide_a, wide_b)
        self.b_z = landing(4 * total + 3 * start, 3 * rows, wide_a, wide_b)
        self.b_x = landing(7 * total + start // 2, part, wide_a, wide_b)
        self.col_0 = place.c * half
        self.row_q = start + place.x * part
        self.row_o = start + part - place.x * part

    def push(self, source, target, leg, device):
        push(source, target, self.send, self.recv.at[leg], device)

    def zero(self):
        other = self.half - self.col_0
        source = self.grad.at[:, cols_of(other, self.half)]
        push(source, self.from_core, self.first.at[0], self.first.at[1], self.place.peer(0, 1))

    def core(self, row, rows, from_col, columns):
        return self.from_core.at[rows_of(row, rows), pl.ds(from_col, columns)]

    def mine(self, row, rows, from_col, columns):
        return self.core(self.place.f * self.total + row, rows, from_col, columns)

    def one(self, first, last):
        place, total, part, rows = self.place, self.total, self.part, self.rows
        if first:
            await_bytes(self.from_core, self.first.at[1])
        add_blocks(
            8,
            rows,
            self.half,
            lambda b, s, n: self.core(b * total + self.start + s, n, 0, self.half),
            lambda b, s, n: self.grad.at[rows_of(b * total + self.start + s, n), cols_of(self.col_0, self.half)],
        )
        if last:
            await_bytes(self.from_core, self.first.at[0])
        if self.wide_a:
            for block in range(8):
                self.push(
                    self.core(block * total + self.row_o, part, 0, self.wide_a),
                    self.a_x.at[pl.ds(block * part, part)],
                    0,
                    place.peer(0, 2),
                )
        if self.wide_b:
            for level in range(4):
                self.push(
                    self.core((2 * level + 1 - place.y) * total + self.start, rows, self.wide_a, self.wide_b),
                    self.b_y.at[pl.ds(level * rows, rows)],
                    0,
                    place.peer(1, 0),
                )

    def two(self):
        place, total, part, rows = self.place, self.total, self.part, self.rows
        await_count(self.room, 4 * rows * self.half, self.recv.at[0])
        if self.wide_a:
            add_blocks(
                8,
                part,
                self.wide_a,
                lambda b, s, n: self.core(b * total + self.row_q + s, n, 0, self.wide_a),
                lambda b, s, n: self.a_x.at[rows_of(b * part + s, n)],
            )
            for level in range(4):
                self.push(
                    self.core((2 * level + 1 - place.y) * total + self.row_q, part, 0, self.wide_a),
                    self.a_y.at[pl.ds(level * part, part)],
                    1,
                    place.peer(1, 0),
                )
        if self.wide_b:
            add_blocks(
                4,
                rows,
                self.wide_b,
                lambda b, s, n: self.core((2 * b + place.y) * total + self.start + s, n, self.wide_a, self.wide_b),
                lambda b, s, n: self.b_y.at[rows_of(b * rows + s, n)],
            )
            for slot, bits in enumerate((6, 4, 2)):
                self.push(
                    self.core(flip(place.f, bits) * total + self.start, rows, self.wide_a, self.wide_b),
                    self.b_z.at[pl.ds(slot * rows, rows)],
                    1,
                    place.peer(bits, 0),
                )

    def sum_four(self, row, rows, col, wide, landed, store):
        chunk = chunk_of(rows, wide)

        def step(index, carry):
            start = pl.multiple_of(index * chunk, 16)
            total = self.mine(row + start, chunk, col, wide)[...].astype(F32)
            for slot in range(3):
                total = total + landed[rows_of(slot * rows + start, chunk)].astype(F32)
            store(start, chunk, total.astype(BF16))
            return carry

        lax.fori_loop(0, rows // chunk, step, 0)

    def three(self):
        place, total, part, rows = self.place, self.total, self.part, self.rows
        await_count(self.room, 2 * rows * self.wide_a + 3 * rows * self.wide_b, self.recv.at[1])
        if self.wide_a:
            add_blocks(
                4,
                part,
                self.wide_a,
                lambda b, s, n: self.core((2 * b + place.y) * total + self.row_q + s, n, 0, self.wide_a),
                lambda b, s, n: self.a_y.at[rows_of(b * part + s, n)],
            )
            for slot, bits in enumerate((6, 4, 2)):
                self.push(
                    self.core(flip(place.f, bits) * total + self.row_q, part, 0, self.wide_a),
                    self.a_z.at[pl.ds(slot * part, part)],
                    2,
                    place.peer(bits, 0),
                )
        if self.wide_b:

            def keep(start, chunk, value):
                self.mine(self.start + start, chunk, self.wide_a, self.wide_b)[...] = value

            self.sum_four(self.start, rows, self.wide_a, self.wide_b, self.b_z, keep)
            self.push(self.mine(self.row_o, part, self.wide_a, self.wide_b), self.b_x, 2, place.peer(0, 2))

    def four(self):
        place, part = self.place, self.part
        await_count(self.room, 3 * part * self.wide_a + part * self.wide_b, self.recv.at[2])
        if self.wide_a:

            def keep(start, chunk, value):
                self.out[rows_of(self.row_q + start, chunk), cols_of(self.col_0, self.wide_a)] = value

            self.sum_four(self.row_q, part, 0, self.wide_a, self.a_z, keep)
        if self.wide_b:
            chunk = chunk_of(part, self.wide_b)

            def step(index, carry):
                start = pl.multiple_of(index * chunk, 16)
                total = self.mine(self.row_q + start, chunk, self.wide_a, self.wide_b)[...].astype(F32)
                total = total + self.b_x[rows_of(start, chunk)].astype(F32)
                columns = cols_of(self.col_0 + self.wide_a, self.wide_b)
                self.out[rows_of(self.row_q + start, chunk), columns] = total.astype(BF16)
                return carry

            lax.fori_loop(0, part // chunk, step, 0)
        block = self.out.at[rows_of(self.row_q, part), cols_of(self.col_0, self.half)]
        self.push(block, block, 3, place.peer(0, 2))

    def five(self):
        await_bytes(self.out.at[pl.ds(0, self.part), pl.ds(0, self.half)], self.recv.at[3])
        block = self.out.at[pl.ds(self.start, self.rows), cols_of(self.col_0, self.half)]
        self.push(block, block, 4, self.place.peer(0, 1))

    def six(self):
        await_bytes(self.out.at[pl.ds(0, self.rows), pl.ds(0, self.half)], self.recv.at[4])

    def sent(self):
        await_count(self.room, 18 * self.part * self.half, self.send)


def mm(left, right):
    return jnp.dot(left, right, preferred_element_type=F32)


def mm_nt(left, right):
    return lax.dot_general(left, right, (((1,), (1,)), ((), ())), preferred_element_type=F32)


def mm_tn(left, right):
    return lax.dot_general(left, right, (((0,), (0,)), ((), ())), preferred_element_type=F32)


def loop(count, step):
    def body_of(index, carry):
        step(index)
        return carry

    lax.fori_loop(0, count, body_of, 0)


def at_block(index, size):
    if isinstance(index, int):
        return pl.ds(index * size, size)
    return pl.ds(pl.multiple_of(index * size, size), size)


def slope_of(values):
    gate = jax.nn.sigmoid(values)
    return gate * (1.0 + values * (1.0 - gate))


def fold(values):
    total = values[0:8]
    for start in range(8, values.shape[0], 8):
        total = total + values[start : start + 8]
    return total


def column_sums(count, width, terms):
    def step(index, carry):
        start = pl.multiple_of(index * CHUNK, CHUNK)
        return tuple(total + fold(one) for total, one in zip(carry, terms(start)))

    zero = jnp.zeros((8, LANES), F32)
    totals = lax.fori_loop(0, count, step, (zero,) * width)
    return [jnp.sum(one, axis=0, keepdims=True) for one in totals]


class Vectors:
    def __init__(self, ref):
        self.ref, self.used = ref, 0

    def put(self, row):
        at = self.used
        self.used += 1
        self.ref[at : at + 1, :] = row
        return at

    def get(self, at):
        return self.ref[at : at + 1, :]


class Totals:
    def __init__(self, place, short, long, tot, send, recv):
        self.place, self.short, self.long, self.tot, self.send, self.recv = place, short, long, tot, send, recv
        self.turns, self.is_long, self.rows = [1, 1], 0, 0

    def slot(self, at):
        ref = self.long if self.is_long else self.short
        return ref.at[self.turn, at, pl.ds(0, self.rows)]

    def slots(self, at, count):
        ref = self.long if self.is_long else self.short
        return ref.at[self.turn, pl.ds(at, count), pl.ds(0, self.rows)]

    def spread(self, at, peers, phase):
        own = self.slot(at)
        for bits in peers:
            push(own, own, self.sem(self.send, phase), self.sem(self.recv, phase), self.place.peer(*bits))

    def sem(self, sems, phase):
        return sems.at[self.is_long, self.turn, phase]

    def gather(self, at, count, peers, phase):
        await_bytes(self.slots(at, peers), self.sem(self.recv, phase))
        ref = self.long if self.is_long else self.short
        total = ref[self.turn, at, 0 : self.rows, :]
        for index in range(at + 1, at + count):
            total = total + ref[self.turn, index, 0 : self.rows, :]
        return total

    def start(self, rows_of_values, extra=None):
        count = 4 * len(rows_of_values) + (8 if extra is not None else 0)
        self.is_long = 1 if count > 16 else 0
        self.turns[self.is_long] = self.turn = 1 - self.turns[self.is_long]
        self.rows = count
        own = self.slot(self.place.c)
        at = 0
        for row in rows_of_values:
            for lane in range(0, LANES, 128):
                own[at : at + 1, :] = row[:, lane : lane + 128]
                at += 1
        if extra is not None:
            own[at : at + 8, :] = extra
        self.spread(self.place.c, ((0, 1),), 0)

    def middle(self):
        place = self.place
        total = self.gather(0, 2, 1, 0)
        if self.is_long:
            self.slot(2 + 2 * place.y + place.x)[...] = total
            self.spread(2 + 2 * place.y + place.x, ((1, 2), (1, 0), (0, 2)), 1)
        else:
            self.slot(2 + 2 * place.f + place.x)[...] = total
            self.spread(2 + 2 * place.f + place.x, CHIP_PEERS, 1)

    def late(self):
        if self.is_long:
            self.slot(6 + self.place.z)[...] = self.gather(2, 4, 3, 1)
            self.spread(6 + self.place.z, ((6, 0), (4, 0), (2, 0)), 2)

    def end(self):
        if self.is_long:
            self.tot[0 : self.rows, :] = self.gather(6, 4, 3, 2)
        else:
            self.tot[0 : self.rows, :] = self.gather(2, 16, 15, 1)
        for phase, count in enumerate((1, 3, 3) if self.is_long else (1, 15)):
            await_bytes(self.slots(0, count), self.sem(self.send, phase))

    def row(self, index):
        at = 4 * index
        return jnp.concatenate([self.tot[at + k : at + k + 1, :] for k in range(4)], axis=1)

    def wide(self, at):
        return jnp.concatenate([self.tot[at : at + 1, :]] * 4, axis=1)


def step_kernel(
    img_hbm,
    cot_hbm,
    sides,
    keep,
    widths,
    norm_in_a,
    norm_mid_a,
    norm_out_a,
    norm_proj_a,
    norm_in_b,
    norm_mid_b,
    norm_out_b,
    sh_in_a,
    sh_mid_a,
    sh_out_a,
    sh_proj_a,
    sh_in_b,
    sh_mid_b,
    sh_out_b,
    result_hbm,
    images_hbm,
    own_hbm_in_a,
    own_hbm_mid_a,
    own_hbm_out_a,
    own_hbm_proj_a,
    own_hbm_in_b,
    own_hbm_mid_b,
    own_hbm_out_b,
    out_hbm_in_a,
    out_hbm_mid_a,
    out_hbm_out_a,
    out_hbm_proj_a,
    out_hbm_in_b,
    out_hbm_mid_b,
    out_hbm_out_b,
    own_in_a,
    own_mid_a,
    own_out_a,
    own_proj_a,
    own_in_b,
    own_mid_b,
    own_out_b,
    out_in_a,
    out_mid_a,
    out_out_a,
    out_proj_a,
    out_in_b,
    out_mid_b,
    out_out_b,
    w_in_a,
    w_mid_a,
    w_out_a,
    w_proj_a,
    w_in_b,
    w_mid_b,
    w_out_b,
    raw,
    cot,
    x,
    c1,
    cols_a,
    c2,
    a2,
    c3,
    cp,
    bo,
    feed,
    d1,
    cols_b,
    d2,
    b2,
    d3,
    dz,
    dm,
    df,
    dout,
    dproj,
    g_mid,
    g_out,
    g_in,
    g_proj,
    mask_ref,
    gate_ref,
    move,
    norms,
    block_ref,
    vec_ref,
    short,
    long,
    tot,
    sums,
    io_sem,
    link_send,
    link_recv,
    core_sem,
    ar_send,
    ar_recv,
    nb_sem,
    out_sem,
    free_sem,
):
    place = Place()
    shards = dict(zip(NAMES, (sh_in_a, sh_mid_a, sh_out_a, sh_proj_a, sh_in_b, sh_mid_b, sh_out_b)))
    wholes = dict(zip(NAMES, (w_in_a, w_mid_a, w_out_a, w_proj_a, w_in_b, w_mid_b, w_out_b)))
    outs = dict(zip(NAMES, (out_in_a, out_mid_a, out_out_a, out_proj_a, out_in_b, out_mid_b, out_out_b)))
    owned = dict(zip(NAMES, (own_in_a, own_mid_a, own_out_a, own_proj_a, own_in_b, own_mid_b, own_out_b)))
    own_hbm = (own_hbm_in_a, own_hbm_mid_a, own_hbm_out_a, own_hbm_proj_a, own_hbm_in_b, own_hbm_mid_b, own_hbm_out_b)
    out_hbm = (out_hbm_in_a, out_hbm_mid_a, out_hbm_out_a, out_hbm_proj_a, out_hbm_in_b, out_hbm_mid_b, out_hbm_out_b)
    own_copies = [pltpu.make_async_copy(owned[n], own_hbm[i], out_sem.at[0, i]) for i, n in enumerate(NAMES)]
    out_copies = [pltpu.make_async_copy(outs[n], out_hbm[i], out_sem.at[1, i]) for i, n in enumerate(NAMES)]
    small = dict(zip(NAMES, (norm_in_a, norm_mid_a, norm_out_a, norm_proj_a, norm_in_b, norm_mid_b, norm_out_b)))
    grads = dict(mid_a=g_mid, mid_b=g_mid, out_a=g_out, out_b=g_out, in_b=g_in, proj_a=g_proj)
    grads["in_a"] = g_in.at[pl.ds(0, wholes["in_a"].shape[0])]
    todo = {}

    def token(name):
        def keep_it(function):
            todo[name] = function
            return function

        return keep_it

    def tokens(name, count, each, step):
        for part in range(count):
            todo[f"{name}.{part}"] = functools.partial(loop, each, lambda k, first=part * each: step(first + k))

    gathers, scatters, at, going = {}, {}, 0, 0
    left = {name: len(WAYS_OUT[name]) for name in NAMES}

    def finish_piece(name, piece):
        piece.six()
        left[name] -= 1
        if not left[name]:
            out_copies[NAMES.index(name)].start()

    def tell(name):
        for bits in LINK_PEERS:
            sem = free_sem.at[NAMES.index(name)]
            pl.semaphore_signal(sem, inc=1, device_id=place.peer(*bits), device_id_type=BY_MESH)

    def send_core(name):
        pl.semaphore_wait(free_sem.at[NAMES.index(name)], len(LINK_PEERS))
        scatters[name, 0].zero()

    for name in NAMES:
        for n, (start, rows, ways) in enumerate(WAYS_IN[name]):
            sems = link_send.at[at], link_recv.at[at]
            g = gathers[name, n] = Gather(place, shards[name], wholes[name], start, rows, ways, *sems)
            at += 1
            key = f"{name}.{n}"
            todo["z." + key], todo["o." + key], todo["L1." + key] = g.first, g.own, g.one
            todo["L2." + key], todo["L3." + key] = g.two, g.three
        eighth = shards[name].shape[1] // 16
        for n, (start, rows, wide) in enumerate(WAYS_OUT[name]):
            sems = core_sem.at[NAMES.index(name)], link_send.at[going], link_recv.at[going]
            s = Scatter(place, grads[name], wholes[name], outs[name], start, rows, wide * eighth, *sems)
            scatters[name, n] = s
            going += 1
            key = f"{name}.{n}"
            todo["S1." + key] = functools.partial(s.one, n == 0, n == len(WAYS_OUT[name]) - 1)
            todo["S2." + key], todo["S3." + key], todo["S4." + key] = s.two, s.three, s.four
            todo["S5." + key] = s.five
            todo["S6." + key] = functools.partial(finish_piece, name, s)
        todo["S0." + name] = functools.partial(send_core, name)

        def arrived(name=name):
            for n in range(len(WAYS_IN[name])):
                gathers[name, n].four()

        todo["W." + name] = arrived

    vec = Vectors(vec_ref)
    totals = Totals(place, short, long, tot, ar_send, ar_recv)
    state, scales, params = {}, {}, {}
    for n in range(1, 13):
        todo[f"A{n}m"] = totals.middle
        todo[f"A{n}l"] = totals.late

    image_copy = pltpu.make_async_copy(img_hbm, raw, io_sem.at[0])
    cot_copy = pltpu.make_async_copy(cot_hbm, cot, io_sem.at[1])
    result_copy = pltpu.make_async_copy(cot, result_hbm, io_sem.at[2])
    grad_copy = pltpu.make_async_copy(raw, images_hbm, io_sem.at[3])

    @token("enter")
    def _():
        image_copy.start()
        cot_copy.start()
        odd = (place.f % 2).astype(F32)
        block_ref[...] = jnp.zeros_like(block_ref)
        at = 0
        for name in NAMES:
            values = small[name][...].astype(F32)
            if values.shape[1] < 128:
                move[0:8, 0:128] = jnp.zeros((8, 128), F32)
                move[0:2, 0 : values.shape[1]] = values
                plain = move[0:8, 0:128]
                values = (plain + (pltpu.roll(plain, 64, 1) - plain) * odd)[0:2]
            for lane in range(0, values.shape[1], 128):
                block_ref[at : at + 1, :] = values[0:1, lane : lane + 128]
                block_ref[at + 10 : at + 11, :] = values[1:2, lane : lane + 128]
                at += 1
        norms[place.f] = block_ref[...]
        enter(place, ((0, 1),) + CHIP_PEERS)
        for bits in (7, 6, 5, 4, 3, 2, 1):
            push(block_ref, norms.at[place.f], nb_sem.at[0], nb_sem.at[1], place.peer(bits, 0))

    @token("prep")
    def _():
        pixel = lax.broadcasted_iota(jnp.int32, (BLOCK, 128), 0)
        slot = pixel % 4

        def by_slot(values):
            return jnp.where(slot == 0, values[0], jnp.where(slot == 1, values[1], jnp.where(slot == 2, values[2], values[3])))

        half = by_slot([sides[i] // 2 for i in range(4)])
        inside = ((pixel // 4) % 8 < half) & (pixel // 32 < half)
        mask_ref[...] = jnp.where(inside, 1.0, 0.0).astype(F32)
        gate_ref[...] = by_slot([keep[i] for i in range(4)]).astype(F32)
        move[...] = jnp.zeros_like(move)
        image_copy.wait()

        def plane_rows(row):
            mask = jnp.concatenate([mask_ref[at_block(row, CHUNK), :]] * (x.shape[1] // 128), axis=1)
            for row_par in range(2):
                for col_par in range(2):
                    for col in range(SIDE):
                        move[4 * col : 4 * col + 4, :] = raw[2 * row + row_par, 2 * col + col_par].astype(F32)
                    start = (2 * row_par + col_par) * BLOCK + row * CHUNK
                    x[pl.ds(pl.multiple_of(start, CHUNK), CHUNK), :] = (move[...] * mask).astype(BF16)

        loop(SIDE, plane_rows)
        for p in range(4):
            x[(p + 1) * BLOCK - CHUNK : (p + 1) * BLOCK, :] = jnp.zeros((CHUNK, x.shape[1]), BF16)

    @token("norms")
    def _():
        await_bytes(norms.at[pl.ds(0, 7)], nb_sem.at[1])
        await_bytes(norms.at[pl.ds(0, 7)], nb_sem.at[0])

        def narrow_row(at):
            pieces = [norms[2 * k, at : at + 1, :] + norms[2 * k + 1, at : at + 1, :] for k in range(4)]
            return vec.put(jnp.concatenate(pieces, axis=1))

        def wide_rows(at):
            return [
                vec.put(
                    jnp.concatenate(
                        [norms[2 * j + k // 2, at + k % 2 : at + k % 2 + 1, :] for k in range(4)], axis=1
                    )
                )
                for j in range(4)
            ]

        params["in_a"] = ([narrow_row(0)], [narrow_row(10)])
        params["mid_a"] = ([narrow_row(1)], [narrow_row(11)])
        params["out_a"] = (wide_rows(2), wide_rows(12))
        params["proj_a"] = (wide_rows(4), wide_rows(14))
        params["in_b"] = ([narrow_row(6)], [narrow_row(16)])
        params["mid_b"] = ([narrow_row(7)], [narrow_row(17)])
        params["out_b"] = (wide_rows(8), wide_rows(18))
        lanes = lax.broadcasted_iota(jnp.int32, (1, LANES), 1)
        state["chan_a"] = vec.put(jnp.where(lanes < widths[0], 1.0, 0.0).astype(F32))
        state["chan_b"] = vec.put(jnp.where(lanes < widths[1], 1.0, 0.0).astype(F32))

    def wide_of(ref, start, size=CHUNK):
        return jnp.concatenate([ref[pl.ds(start, size), :]] * 4, axis=1)

    def mask_at(start):
        return wide_of(mask_ref, start)

    def gate_at(start):
        return wide_of(gate_ref, start)

    def set_norm(name, block, first_row, inverse, chan):
        inverse = vec.get(state[inverse])
        average = totals.row(first_row) * inverse
        rstd = lax.rsqrt(totals.row(first_row + 1) * inverse - average * average + EPSILON)
        gain, shift = (vec.get(rows[block]) for rows in params[name])
        keep_lanes = 1.0 if chan is None else vec.get(state[chan])
        by = gain * rstd
        scales[name, block] = dict(
            rstd=vec.put(rstd),
            off=vec.put(-average * rstd),
            by=vec.put(by),
            mul=vec.put(by * keep_lanes),
            add=vec.put((shift - average * by) * keep_lanes),
        )

    def normed(name, block, values):
        s = scales[name, block]
        return values * vec.get(s["mul"]) + vec.get(s["add"])

    def hat(name, block, values):
        s = scales[name, block]
        return values * vec.get(s["rstd"]) + vec.get(s["off"])

    def set_back(name, block, shift_row, gain_row):
        s = scales[name, block]
        inverse = vec.get(state["inv_in" if name == "in_a" else "inv_out"])
        by = vec.get(s["by"])
        pull = by * totals.row(gain_row) * inverse
        s["back_add"] = vec.put(by * totals.row(shift_row) * inverse + pull * vec.get(s["off"]))
        s["back_mul"] = vec.put(pull * vec.get(s["rstd"]))

    def back(name, block, grad, values):
        s = scales[name, block]
        return grad * vec.get(s["by"]) - vec.get(s["back_add"]) - values * vec.get(s["back_mul"])

    def square_terms(ref):
        def terms(start):
            values = ref[pl.ds(start, CHUNK), :]
            return values, values * values

        return terms

    def masked_terms(ref):
        def terms(start):
            values = ref[pl.ds(start, CHUNK), :]
            kept = values * mask_at(start)
            return kept, kept * values

        return terms

    def lane_row(at, lane):
        return vec_ref[at : at + 1, at_block(lane, 128)]

    def add_up(out, count, left, right, product=mm):
        total = product(left(0), right(0))
        for k in range(1, count):
            total = total + product(left(k), right(k))
        out[...] = total

    @token("A1s")
    def _():
        for p in range(4):
            c1[at_block(p, BLOCK), :] = mm(x[at_block(p, BLOCK), :], w_in_a[...])
        side = [sides[i] for i in range(4)]
        count_in = sum(s * s for s in side).astype(F32)
        count_out = sum((s // 2) * (s // 2) for s in side).astype(F32)
        at = lax.broadcasted_iota(jnp.int32, (8, 128), 0)
        counts = jnp.where(at == 0, count_in, jnp.where(at == 1, count_out, 0.0))
        totals.start(column_sums(32, 2, square_terms(c1)), counts)

    @token("A1e")
    def _():
        totals.end()
        state["inv_in"] = vec.put(1.0 / totals.wide(8))
        state["inv_out"] = vec.put(1.0 / totals.wide(9))
        set_norm("in_a", 0, 0, "inv_in", "chan_a")
        s = scales["in_a", 0]

        def act_a(lane):
            for row_par in range(2):
                for col_par in range(2):
                    p = 2 * row_par + col_par
                    values = c1[p * BLOCK : (p + 1) * BLOCK, at_block(lane, 128)]
                    scaled = values * lane_row(s["mul"], lane) + lane_row(s["add"], lane)
                    act = scaled * jax.nn.sigmoid(scaled) * mask_ref[...]
                    for t, (u, v) in enumerate(TAPS):
                        if (u != 1) != bool(row_par) or (v != 1) != bool(col_par):
                            continue
                        shift = (32 if u == 0 else 0) + (4 if v == 0 else 0)
                        moved = pltpu.roll(act, shift, 0) if shift else act
                        cols_a[:, pl.ds(pl.multiple_of(t * LANES + lane * 128, 128), 128)] = moved.astype(BF16)

        loop(4, act_a)

    def conv_mid(out, cols, weight):
        add_up(out, 3, lambda k: cols[:, at_block(k, 1536)], lambda k: weight[at_block(k, 1536), :])

    def act_mid(act_ref, ref, name):
        def step(index):
            start = pl.multiple_of(index * CHUNK, CHUNK)
            scaled = normed(name, 0, ref[pl.ds(start, CHUNK), :])
            act_ref[pl.ds(start, CHUNK), :] = (scaled * jax.nn.sigmoid(scaled) * mask_at(start)).astype(BF16)

        loop(BLOCK // CHUNK, step)

    @token("A2s")
    def _():
        conv_mid(c2, cols_a, w_mid_a)
        totals.start(column_sums(8, 2, masked_terms(c2)))

    @token("A2e")
    def _():
        totals.end()
        set_norm("mid_a", 0, 0, "inv_out", "chan_a")
        act_mid(a2, c2, "mid_a")

    @token("proj")
    def _():
        def project(j):
            cp[at_block(j, BLOCK), :] = mm(x[0:BLOCK, :], w_proj_a[:, at_block(j, LANES)])

        loop(4, project)

    def blocked(ref, j):
        return square_terms(ref.at[pl.ds(j * BLOCK, BLOCK)])

    @token("A3s")
    def _():
        for j in range(4):
            c3[at_block(j, BLOCK), :] = mm(a2[...], w_out_a[:, at_block(j, LANES)])
        totals.start([row for ref in (c3, cp) for j in range(4) for row in column_sums(8, 2, blocked(ref, j))])

    @token("A3e")
    def _():
        totals.end()
        for j in range(4):
            set_norm("out_a", j, 2 * j, "inv_out", None)
            set_norm("proj_a", j, 8 + 2 * j, "inv_out", None)
        for j in range(4):

            def join_a(index, j=j):
                start = pl.multiple_of(index * CHUNK, CHUNK)
                rows = pl.ds(j * BLOCK + start, CHUNK)
                pre = normed("out_a", j, c3[rows, :]) + normed("proj_a", j, cp[rows, :])
                out = pre * jax.nn.sigmoid(pre) * mask_at(start)
                bo[rows, :] = out
                feed[pl.ds(start, CHUNK), pl.ds(j * LANES, LANES)] = out.astype(BF16)

            loop(BLOCK // CHUNK, join_a)

    @token("A4s")
    def _():
        add_up(d1, 4, lambda k: feed[:, at_block(k, LANES)], lambda k: w_in_b[at_block(k, LANES), :])
        totals.start(column_sums(8, 2, square_terms(d1)))

    @token("A4e")
    def _():
        totals.end()
        set_norm("in_b", 0, 0, "inv_out", "chan_b")
        s = scales["in_b", 0]

        def act_b(lane):
            scaled = d1[:, at_block(lane, 128)] * lane_row(s["mul"], lane) + lane_row(s["add"], lane)
            act = scaled * jax.nn.sigmoid(scaled) * mask_ref[...]
            for t, (u, v) in enumerate(TAPS):
                shift = (-(32 * (u - 1) + 4 * (v - 1))) % BLOCK
                moved = pltpu.roll(act, shift, 0) if shift else act
                cols_b[:, pl.ds(pl.multiple_of(t * LANES + lane * 128, 128), 128)] = moved.astype(BF16)

        loop(4, act_b)

    @token("A5s")
    def _():
        conv_mid(d2, cols_b, w_mid_b)
        totals.start(column_sums(8, 2, masked_terms(d2)))

    @token("A5e")
    def _():
        totals.end()
        set_norm("mid_b", 0, 0, "inv_out", "chan_b")
        act_mid(b2, d2, "mid_b")

    @token("A6s")
    def _():
        for j in range(4):
            d3[at_block(j, BLOCK), :] = mm(b2[...], w_out_b[:, at_block(j, LANES)])
        totals.start([row for j in range(4) for row in column_sums(8, 2, blocked(d3, j))])

    @token("A6e")
    def _():
        totals.end()
        for j in range(4):
            set_norm("out_b", j, 2 * j, "inv_out", None)

    @token("A7s")
    def _():
        for one in gathers.values():
            one.sent()
        cot_copy.wait()
        values = []
        for j in range(4):
            lanes = pl.ds(j * LANES, LANES)

            def finish(start, j=j, lanes=lanes):
                rows = pl.ds(j * BLOCK + start, CHUNK)
                row = start // CHUNK
                for col in range(SIDE):
                    move[4 * col : 4 * col + 4, 0:LANES] = cot[row, col, :, lanes].astype(F32)
                mask, gate, hidden = mask_at(start), gate_at(start), d3[rows, :]
                pre = bo[rows, :] + gate * normed("out_b", j, hidden)
                part = jax.nn.sigmoid(pre)
                grad = move[:, 0:LANES] * mask * (part * (1.0 + pre * (1.0 - part)))
                move[:, LANES : 2 * LANES] = pre * part * mask
                for col in range(SIDE):
                    cot[row, col, :, lanes] = move[4 * col : 4 * col + 4, LANES : 2 * LANES].astype(BF16)
                bo[rows, :] = grad
                grad = grad * gate
                return grad, grad * hat("out_b", j, hidden)

            values += column_sums(SIDE, 2, finish)
            bo[(j + 1) * BLOCK - CHUNK : (j + 1) * BLOCK, :] = jnp.zeros((CHUNK, LANES), F32)
        result_copy.start()
        totals.start(values)

    def keep_sums(at):
        rows = totals.rows
        sums[at : at + rows, :] = tot[0:rows, :]

    @token("A7e")
    def _():
        totals.end()
        keep_sums(0)
        for j in range(4):
            set_back("out_b", j, 2 * j, 2 * j + 1)

    def through_out(weight):
        add_up(dz, 4, lambda k: dout[:, at_block(k, LANES)], lambda k: weight[:, at_block(k, LANES)], mm_nt)

    def slope_terms(grad_ref, ref, name, chan):
        def terms(start):
            rows = pl.ds(start, CHUNK)
            hidden = ref[rows, :]
            mask = mask_at(pl.multiple_of(start % BLOCK, CHUNK) if grad_ref.shape[0] > BLOCK else start)
            grad = grad_ref[rows, :] * mask * vec.get(state[chan]) * slope_of(normed(name, 0, hidden))
            grad_ref[rows, :] = grad
            return grad, grad * hat(name, 0, hidden)

        return terms

    @token("A8s")
    def _():
        for j in range(4):

            def low_out_b(index, j=j):
                start = pl.multiple_of(index * CHUNK, CHUNK)
                rows = pl.ds(j * BLOCK + start, CHUNK)
                grad = back("out_b", j, bo[rows, :] * gate_at(start), d3[rows, :]) * mask_at(start)
                dout[pl.ds(start, CHUNK), pl.ds(j * LANES, LANES)] = grad.astype(BF16)

            loop(BLOCK // CHUNK, low_out_b)
        through_out(w_out_b)
        tell("out_b")
        totals.start(column_sums(8, 2, slope_terms(dz, d2, "mid_b", "chan_b")))

    def grad_out(act_ref, j):
        g_out[:, at_block(j, LANES)] = mm_tn(act_ref[...], dout[:, at_block(j, LANES)]).astype(BF16)

    tokens("g.out_b", 2, 2, lambda j: grad_out(b2, j))

    @token("A8e")
    def _():
        totals.end()
        keep_sums(32)
        set_back("mid_b", 0, 0, 1)

    def low_mid(name, ref, shifts):
        s = scales[name, 0]

        def step(lane):
            lanes = at_block(lane, 128)
            grad = (
                dz[:, lanes] * lane_row(s["by"], lane)
                - lane_row(s["back_add"], lane)
                - ref[:, lanes] * lane_row(s["back_mul"], lane)
            ) * mask_ref[...]
            dm[:, lanes] = grad.astype(BF16)
            for k, shift in enumerate(shifts):
                moved = pltpu.roll(grad, shift, 0) if shift else grad
                g_mid[k * BLOCK : (k + 1) * BLOCK, lanes] = moved.astype(BF16)

        loop(4, step)

    @token("A9s")
    def _():
        low_mid("mid_b", d2, [(32 * (u - 1) + 4 * (v - 1)) % BLOCK for u, v in TAPS])
        add_up(dz, 9, lambda t: g_mid[at_block(t, BLOCK), :], lambda t: w_mid_b[at_block(t, LANES), :], mm_nt)
        tell("mid_b")
        totals.start(column_sums(8, 2, slope_terms(dz, d1, "in_b", "chan_b")))

    def grad_mid(cols, t):
        g_mid[at_block(t, LANES), :] = mm_tn(cols[:, at_block(t, LANES)], dm[...]).astype(BF16)

    tokens("g.mid_b", 3, 3, lambda t: grad_mid(cols_b, t))

    @token("A9e")
    def _():
        totals.end()
        keep_sums(40)
        set_back("in_b", 0, 0, 1)

    @token("A10s")
    def _():
        def low_first_b(index):
            start = pl.multiple_of(index * CHUNK, CHUNK)
            rows = pl.ds(start, CHUNK)
            df[rows, :] = (back("in_b", 0, dz[rows, :], d1[rows, :]) * mask_at(start)).astype(BF16)

        loop(BLOCK // CHUNK, low_first_b)

        for j in range(4):
            bo[at_block(j, BLOCK), :] += mm_nt(df[...], w_in_b[at_block(j, LANES), :])
        tell("in_b")
        values = []
        for j in range(4):

            def join_back(start, j=j):
                rows = pl.ds(j * BLOCK + start, CHUNK)
                left, right = c3[rows, :], cp[rows, :]
                pre = normed("out_a", j, left) + normed("proj_a", j, right)
                grad = bo[rows, :] * mask_at(start) * slope_of(pre)
                bo[rows, :] = grad
                return grad, grad * hat("out_a", j, left), grad * hat("proj_a", j, right)

            values += column_sums(8, 3, join_back)
        totals.start(values)

    def grad_in_b(j):
        g_in[at_block(j, LANES), :] = mm_tn(feed[:, at_block(j, LANES)], df[...]).astype(BF16)

    tokens("g.in_b", 2, 2, grad_in_b)

    @token("A10e")
    def _():
        totals.end()
        keep_sums(48)
        for j in range(4):
            set_back("out_a", j, 3 * j, 3 * j + 1)
            set_back("proj_a", j, 3 * j, 3 * j + 2)

    @token("A11s")
    def _():
        for j in range(4):

            def low_both(index, j=j):
                start = pl.multiple_of(index * CHUNK, CHUNK)
                rows = pl.ds(j * BLOCK + start, CHUNK)
                near_rows, lanes = pl.ds(start, CHUNK), pl.ds(j * LANES, LANES)
                grad, mask = bo[rows, :], mask_at(start)
                dout[near_rows, lanes] = (back("out_a", j, grad, c3[rows, :]) * mask).astype(BF16)
                dproj[near_rows, lanes] = (back("proj_a", j, grad, cp[rows, :]) * mask).astype(BF16)

            loop(BLOCK // CHUNK, low_both)
        through_out(w_out_a)
        tell("out_a")
        totals.start(column_sums(8, 2, slope_terms(dz, c2, "mid_a", "chan_a")))

    tokens("g.out_a", 2, 2, lambda j: grad_out(a2, j))

    def grad_proj(n):
        i, j = n // 4, n % 4
        g_proj[at_block(i, LANES), at_block(j, LANES)] = mm_tn(
            x[0:BLOCK, at_block(i, LANES)], dproj[:, at_block(j, LANES)]
        ).astype(BF16)

    tokens("g.proj_a", 2, 4, grad_proj)

    def back_proj(n):
        out, rows = d3.at[pl.ds(n * BLOCK, BLOCK)], pl.ds(n * LANES, LANES)
        add_up(out, 4, lambda k: dproj[:, at_block(k, LANES)], lambda k: w_proj_a[rows, at_block(k, LANES)], mm_nt)

    @token("dproj.0")
    def _():
        back_proj(0)

    @token("dproj.1")
    def _():
        back_proj(1)
        tell("proj_a")

    @token("A11e")
    def _():
        totals.end()
        keep_sums(96)
        set_back("mid_a", 0, 0, 1)

    @token("A12s")
    def _():
        low_mid("mid_a", c2, [(-(32 * r + 4 * s)) % BLOCK for r in range(2) for s in range(2)])
        for row_par in range(2):
            for col_par in range(2):
                grad = None
                for t, (u, v) in enumerate(TAPS):
                    if (u != 1) != bool(row_par) or (v != 1) != bool(col_par):
                        continue
                    moved = 2 * (1 if u == 0 else 0) + (1 if v == 0 else 0)
                    term = mm_nt(g_mid[moved * BLOCK : (moved + 1) * BLOCK, :], w_mid_a[t * LANES : (t + 1) * LANES, :])
                    grad = term if grad is None else grad + term
                bo[pl.ds((2 * row_par + col_par) * BLOCK, BLOCK), :] = grad
        tell("mid_a")
        totals.start(column_sums(32, 2, slope_terms(bo, c1, "in_a", "chan_a")))

    tokens("g.mid_a", 3, 3, lambda t: grad_mid(cols_a, t))

    @token("A12e")
    def _():
        totals.end()
        keep_sums(104)
        set_back("in_a", 0, 0, 1)
        for p in range(4):

            def low_first_a(index, p=p):
                start = pl.multiple_of(index * CHUNK, CHUNK)
                rows = pl.ds(p * BLOCK + start, CHUNK)
                grad = back("in_a", 0, bo[rows, :], c1[rows, :]) * mask_at(start)
                cols_b[pl.ds(start, CHUNK), p * LANES : (p + 1) * LANES] = grad.astype(BF16)

            loop(BLOCK // CHUNK, low_first_a)

    def first_grad(p):
        return cols_b[:, p * LANES : (p + 1) * LANES]

    def grad_in_a(i):
        lanes = at_block(i, 256)
        total = mm_tn(x[0:BLOCK, lanes], first_grad(0))
        for p in range(1, 4):
            total = total + mm_tn(x[p * BLOCK : (p + 1) * BLOCK, lanes], first_grad(p))
        g_in[at_block(i, 256), :] = total.astype(BF16)

    tokens("g.in_a", 2, 2, grad_in_a)

    def image_grad(planes):
        for p in planes:
            for h in range(2):
                lanes = pl.ds(h * LANES, LANES)
                grad = mm_nt(first_grad(p), w_in_a[h * LANES : (h + 1) * LANES, :])
                dz[...] = grad + d3[h * BLOCK : (h + 1) * BLOCK, :] if p == 0 else grad

                def pixels(row, p=p, lanes=lanes):
                    move[:, 0:LANES] = dz[at_block(row, CHUNK), :]
                    for col in range(SIDE):
                        raw[2 * row + p // 2, 2 * col + p % 2, :, lanes] = move[4 * col : 4 * col + 4, 0:LANES].astype(BF16)

                loop(SIDE, pixels)

    @token("img.0")
    def _():
        image_grad((0, 1))

    @token("img.1")
    def _():
        image_grad((2, 3))
        grad_copy.start()
        tell("in_a")

    @token("own")
    def _():
        def own_row(at, out, k):
            if out.shape[1] >= 128:
                for lane in range(2):
                    line = sums[pl.ds(at + 2 * (place.f % 2) + lane, 1), :]
                    out[k : k + 1, lane * 128 : (lane + 1) * 128] = line
            else:
                odd = (place.f % 2).astype(F32)
                move[0:1, 0:128] = sums[pl.ds(at + place.f // 2, 1), :]
                line = move[0:8, 0:128]
                line = line + (pltpu.roll(line, 64, 1) - line) * odd
                out[k : k + 1, :] = line[0:1, 0 : out.shape[1]]

        for name, at in (("mid_b", 32), ("in_b", 40), ("mid_a", 96), ("in_a", 104)):
            own_row(at + 4, owned[name], 0)
            own_row(at, owned[name], 1)
        block = place.f // 2
        for name, at, step, gain in (("out_b", 0, 8, 4), ("out_a", 48, 12, 4), ("proj_a", 48, 12, 8)):
            own_row(at + step * block + gain, owned[name], 0)
            own_row(at + step * block, owned[name], 1)
        for one in own_copies:
            one.start()

    steps = sorted(todo)
    if sorted(RUN) != list(range(len(steps))):
        raise ValueError(len(steps))
    for index in RUN:
        todo[steps[index]]()
    result_copy.wait()
    grad_copy.wait()
    for one in scatters.values():
        one.sent()
    for one in own_copies + out_copies:
        one.wait()


def finish_kernel(*refs):
    arrays_in, arrays_out, held, wide = refs[:16], refs[16:32], refs[32:48], refs[48:55]
    in_sem, out_sem = refs[55:]
    loads = [pltpu.make_async_copy(a, b, in_sem.at[i]) for i, (a, b) in enumerate(zip(arrays_in, held))]
    leaving = held[:9] + wide
    stores = [pltpu.make_async_copy(a, b, out_sem.at[i]) for i, (a, b) in enumerate(zip(leaving, arrays_out))]
    order = list(range(9, 16)) + list(range(9))
    for i in order:
        loads[i].start()
    for i in order:
        loads[i].wait()
        if i >= 9:
            narrow, target = held[i], wide[i - 9]
            rows, columns = narrow.shape
            chunk = chunk_of(rows, columns)

            def step(index, carry, narrow=narrow, target=target, chunk=chunk):
                at = pl.ds(pl.multiple_of(index * chunk, 16), chunk)
                target[at, :] = narrow[at, :].astype(F32)
                return carry

            lax.fori_loop(0, rows // chunk, step, 0)
        stores[i].start()
    for i in order:
        stores[i].wait()


def finish_call(plain, grads):
    anywhere = pl.BlockSpec(memory_space=pl.ANY)
    return pl.pallas_call(
        finish_kernel,
        out_shape=[jax.ShapeDtypeStruct(one.shape, one.dtype) for one in plain]
        + [jax.ShapeDtypeStruct(one.shape, F32) for one in grads],
        in_specs=[anywhere] * 16,
        out_specs=[anywhere] * 16,
        scratch_shapes=[pltpu.VMEM(one.shape, one.dtype) for one in (*plain, *grads)]
        + [pltpu.VMEM(one.shape, F32) for one in grads]
        + [pltpu.SemaphoreType.DMA((16,)), pltpu.SemaphoreType.DMA((16,))],
        compiler_params=pltpu.CompilerParams(vmem_limit_bytes=64 * 2**20),
        name="finish_step",
    )(*plain, *grads)


def body_fast(
    images,
    image_sides,
    widths,
    keep_gate,
    w_in_a,
    w_mid_a,
    w_out_a,
    w_proj_a,
    norm_in_a,
    norm_mid_a,
    norm_out_a,
    norm_proj_a,
    w_in_b,
    w_mid_b,
    w_out_b,
    norm_in_b,
    norm_mid_b,
    norm_out_b,
    cotangent,
):
    width_in, width_out = images.shape[3], cotangent.shape[3]
    turned = (1, 2, 0, 3)
    images, cotangent = images.transpose(turned), cotangent.transpose(turned)
    norms = (norm_in_a, norm_mid_a, norm_out_a, norm_proj_a, norm_in_b, norm_mid_b, norm_out_b)
    shards = (w_in_a, w_mid_a, w_out_a, w_proj_a, w_in_b, w_mid_b, w_out_b)
    vmem = pl.BlockSpec(memory_space=pltpu.VMEM)
    smem = pl.BlockSpec(memory_space=pltpu.SMEM)
    anywhere = pl.BlockSpec(memory_space=pl.ANY)
    wholes = [(8 * one.shape[0], one.shape[1]) for one in shards]
    pieces = max(sum(len(one) for one in ways.values()) for ways in (WAYS_IN, WAYS_OUT))
    outs = pl.pallas_call(
        step_kernel,
        out_shape=[jax.ShapeDtypeStruct(cotangent.shape, BF16), jax.ShapeDtypeStruct(images.shape, BF16)]
        + [jax.ShapeDtypeStruct(one.shape, F32) for one in norms]
        + [jax.ShapeDtypeStruct(one.shape, BF16) for one in shards],
        in_specs=[anywhere, anywhere, smem, smem, smem] + [vmem] * 7 + [anywhere] * 7,
        out_specs=[anywhere] * 16,
        scratch_shapes=[pltpu.VMEM(one.shape, F32) for one in norms]
        + [pltpu.VMEM(one.shape, BF16) for one in shards]
        + [pltpu.VMEM(shape, BF16) for shape in wholes]
        + [
            pltpu.VMEM(images.shape, BF16),
            pltpu.VMEM(cotangent.shape, BF16),
            pltpu.VMEM((4 * BLOCK, width_in), BF16),
            pltpu.VMEM((4 * BLOCK, LANES), F32),
            pltpu.VMEM((BLOCK, 9 * LANES), BF16),
            pltpu.VMEM((BLOCK, LANES), F32),
            pltpu.VMEM((BLOCK, LANES), BF16),
            pltpu.VMEM((4 * BLOCK, LANES), F32),
            pltpu.VMEM((4 * BLOCK, LANES), F32),
            pltpu.VMEM((4 * BLOCK, LANES), F32),
            pltpu.VMEM((BLOCK, width_out), BF16),
            pltpu.VMEM((BLOCK, LANES), F32),
            pltpu.VMEM((BLOCK, 9 * LANES), BF16),
            pltpu.VMEM((BLOCK, LANES), F32),
            pltpu.VMEM((BLOCK, LANES), BF16),
            pltpu.VMEM((4 * BLOCK, LANES), F32),
            pltpu.VMEM((BLOCK, LANES), F32),
            pltpu.VMEM((BLOCK, LANES), BF16),
            pltpu.VMEM((BLOCK, LANES), BF16),
            pltpu.VMEM((BLOCK, width_out), BF16),
            pltpu.VMEM((BLOCK, width_out), BF16),
            pltpu.VMEM(wholes[1], BF16),
            pltpu.VMEM(wholes[2], BF16),
            pltpu.VMEM(wholes[4], BF16),
            pltpu.VMEM(wholes[3], BF16),
            pltpu.VMEM((BLOCK, 128), F32),
            pltpu.VMEM((BLOCK, 128), F32),
            pltpu.VMEM((CHUNK, width_in), F32),
            pltpu.VMEM((8, 24, 128), F32),
            pltpu.VMEM((24, 128), F32),
            pltpu.VMEM((160, LANES), F32),
            pltpu.VMEM((2, 18, 16, 128), F32),
            pltpu.VMEM((2, 10, 64, 128), F32),
            pltpu.VMEM((64, 128), F32),
            pltpu.VMEM((112, 128), F32),
            pltpu.SemaphoreType.DMA((4,)),
            pltpu.SemaphoreType.DMA((pieces,)),
            pltpu.SemaphoreType.DMA((pieces, 5)),
            pltpu.SemaphoreType.DMA((7, 2)),
            pltpu.SemaphoreType.DMA((2, 2, 3)),
            pltpu.SemaphoreType.DMA((2, 2, 3)),
            pltpu.SemaphoreType.DMA((2,)),
            pltpu.SemaphoreType.DMA((2, 7)),
            pltpu.SemaphoreType.REGULAR((7,)),
        ],
        compiler_params=pltpu.CompilerParams(
            collective_id=0, has_side_effects=True, vmem_limit_bytes=64 * 2**20
        ),
        name="whole_step",
    )(images, cotangent, image_sides, keep_gate, widths, *norms, *shards)
    back_turned = (2, 0, 1, 3)
    outs = finish_call(outs[:9], outs[9:])
    own, finals = outs[2:9], outs[9:]
    return (
        outs[0].transpose(back_turned),
        outs[1].transpose(back_turned),
        *finals[:4],
        *own[:4],
        *finals[4:],
        *own[4:],
    )


def fits(mesh):
    return mesh.shape[FSDP] == 8 and mesh.shape[DP] == 4


def gather_plain(shards):
    return [lax.all_gather(one, FSDP, axis=0, tiled=True) for one in shards]


def scatter_plain(grads):
    parts = [lax.psum_scatter(one, FSDP, scatter_dimension=0, tiled=True) for one in grads]
    return lax.psum(tuple(parts), DP)


def sum_pair(first, second):
    return lax.psum((first, second), (FSDP, DP))


def silu_slope(values):
    sigmoid_part = jax.nn.sigmoid(values)
    return sigmoid_part * (1.0 + values * (1.0 - sigmoid_part))


def pixel_masks(image_sides, side_in, side_out):
    half_sides = image_sides // 2
    rows_in = jnp.arange(side_in, dtype=jnp.int32)
    rows_out = jnp.arange(side_out, dtype=jnp.int32)
    inside_in = (rows_in[None, :, None] < image_sides[:, None, None]) & (
        rows_in[None, None, :] < image_sides[:, None, None]
    )
    inside_out = (rows_out[None, :, None] < half_sides[:, None, None]) & (
        rows_out[None, None, :] < half_sides[:, None, None]
    )
    local_counts = jnp.stack(
        [jnp.sum(image_sides * image_sides), jnp.sum(half_sides * half_sides)]
    ).astype(jnp.float32)
    return (
        inside_in.astype(jnp.float32)[..., None],
        inside_out.astype(jnp.float32)[..., None],
        local_counts,
    )


def norm_stats(hidden, pixel_mask, local_counts, count_slot):
    sum_values, sum_squares = sum_pair(
        jnp.sum(hidden * pixel_mask, axis=(0, 1, 2)),
        jnp.sum(hidden * hidden * pixel_mask, axis=(0, 1, 2)),
    )
    pixel_total = local_counts[count_slot]
    average = sum_values / pixel_total
    inv_std = lax.rsqrt(sum_squares / pixel_total - average * average + EPSILON)
    return (average, inv_std, pixel_total)


def normalize(hidden, stats_now, params, channel):
    average, inv_std, pixel_total = stats_now
    scaled = (hidden - average) * inv_std
    params_wide = params.astype(jnp.float32)
    return (scaled, (scaled * params_wide[0] + params_wide[1]) * channel)


def norm_backward(grad_norm, scaled, stats_now, params, pixel_mask):
    average, inv_std, pixel_total = stats_now
    shift_sum, gain_sum = sum_pair(
        jnp.sum(grad_norm, axis=(0, 1, 2)), jnp.sum(grad_norm * scaled, axis=(0, 1, 2))
    )
    gain_row = params[0].astype(jnp.float32)
    grad_hidden = (
        gain_row
        * inv_std
        * (grad_norm - shift_sum / pixel_total - scaled * gain_sum / pixel_total)
        * pixel_mask
    )
    return (grad_hidden.astype(jnp.bfloat16), gain_sum, shift_sum)


def taps_stride_two(activations):
    slot_count = activations.shape[0]
    half_side = activations.shape[1] // 2
    lane_count = activations.shape[3]
    padded = jnp.pad(activations, ((0, 0), (1, 1), (1, 1), (0, 0)))
    parity_grid = padded.reshape(slot_count, half_side + 1, 2, half_side + 1, 2, lane_count)
    pieces = [
        parity_grid[
            :,
            row_tap // 2 : row_tap // 2 + half_side,
            row_tap % 2,
            col_tap // 2 : col_tap // 2 + half_side,
            col_tap % 2,
            :,
        ]
        for row_tap in range(3)
        for col_tap in range(3)
    ]
    return jnp.concatenate(pieces, axis=-1)


def fold_stride_two(grad_cols, side_in):
    slot_count = grad_cols.shape[0]
    half_side = grad_cols.shape[1]
    lane_count = grad_cols.shape[3] // 9
    planes = [
        [
            jnp.zeros((slot_count, half_side + 1, half_side + 1, lane_count), jnp.float32)
            for col_par in range(2)
        ]
        for row_par in range(2)
    ]
    for row_tap in range(3):
        for col_tap in range(3):
            tap_index = row_tap * 3 + col_tap
            tap_piece = grad_cols[..., tap_index * lane_count : (tap_index + 1) * lane_count]
            placed = jnp.pad(
                tap_piece,
                (
                    (0, 0),
                    (row_tap // 2, 1 - row_tap // 2),
                    (col_tap // 2, 1 - col_tap // 2),
                    (0, 0),
                ),
            )
            planes[row_tap % 2][col_tap % 2] = planes[row_tap % 2][col_tap % 2] + placed
    parity_grid = jnp.stack([jnp.stack(planes[0], axis=3), jnp.stack(planes[1], axis=3)], axis=2)
    whole_grid = parity_grid.reshape(slot_count, side_in + 2, side_in + 2, lane_count)
    return whole_grid[:, 1:-1, 1:-1, :]


def taps_stride_one(activations):
    side_now = activations.shape[1]
    padded = jnp.pad(activations, ((0, 0), (1, 1), (1, 1), (0, 0)))
    pieces = [
        padded[:, row_tap : row_tap + side_now, col_tap : col_tap + side_now, :]
        for row_tap in range(3)
        for col_tap in range(3)
    ]
    return jnp.concatenate(pieces, axis=-1)


def fold_stride_one(grad_cols):
    lane_count = grad_cols.shape[3] // 9
    whole_grid = None
    for row_tap in range(3):
        for col_tap in range(3):
            tap_index = row_tap * 3 + col_tap
            tap_piece = grad_cols[..., tap_index * lane_count : (tap_index + 1) * lane_count]
            placed = jnp.pad(
                tap_piece, ((0, 0), (row_tap, 2 - row_tap), (col_tap, 2 - col_tap), (0, 0))
            )
            whole_grid = placed if whole_grid is None else whole_grid + placed
    return whole_grid[:, 1:-1, 1:-1, :]


def contract(left_side, right_side):
    return lax.dot_general(
        left_side,
        right_side,
        (((0, 1, 2), (0, 1, 2)), ((), ())),
        preferred_element_type=jnp.float32,
    )


def back_project(gradient, weight):
    return lax.dot_general(
        gradient, weight, (((3,), (1,)), ((), ())), preferred_element_type=jnp.float32
    )


def own_shard(pair_sums):
    gain_sum, shift_sum = pair_sums
    shard_width = gain_sum.shape[0] // lax.axis_size(FSDP)
    offset = lax.axis_index(FSDP) * shard_width
    return jnp.stack(
        [
            lax.dynamic_slice_in_dim(gain_sum, offset, shard_width, 0),
            lax.dynamic_slice_in_dim(shift_sum, offset, shard_width, 0),
        ]
    )


def block_a_forward(inputs, weights, mask_in, mask_out, local_counts, channel, saved_stats):
    w_in, w_mid, w_out, w_proj, norm_in, norm_mid, norm_out, norm_proj = weights
    conv_first = jnp.dot(inputs, w_in, preferred_element_type=jnp.float32)
    stats_first = (
        norm_stats(conv_first, mask_in, local_counts, 0) if saved_stats is None else saved_stats[0]
    )
    scaled_first, normed_first = normalize(conv_first, stats_first, norm_in, channel)
    act_first = (jax.nn.silu(normed_first) * mask_in).astype(jnp.bfloat16)
    cols_mid = taps_stride_two(act_first)
    conv_mid = jnp.dot(cols_mid, w_mid, preferred_element_type=jnp.float32)
    stats_mid = (
        norm_stats(conv_mid, mask_out, local_counts, 1) if saved_stats is None else saved_stats[1]
    )
    scaled_mid, normed_mid = normalize(conv_mid, stats_mid, norm_mid, channel)
    act_mid = (jax.nn.silu(normed_mid) * mask_out).astype(jnp.bfloat16)
    conv_out = jnp.dot(act_mid, w_out, preferred_element_type=jnp.float32)
    slot_count, side_in, lane_count = (inputs.shape[0], inputs.shape[1], inputs.shape[3])
    sampled = inputs.reshape(slot_count, side_in // 2, 2, side_in // 2, 2, lane_count)[
        :, :, 0, :, 0, :
    ]
    conv_proj = jnp.dot(sampled, w_proj, preferred_element_type=jnp.float32)
    conv_both = jnp.concatenate([conv_out, conv_proj], axis=-1)
    norm_both = jnp.concatenate([norm_out, norm_proj], axis=-1)
    stats_both = (
        norm_stats(conv_both, mask_out, local_counts, 1) if saved_stats is None else saved_stats[2]
    )
    scaled_both, normed_both = normalize(conv_both, stats_both, norm_both, 1.0)
    width_out = conv_out.shape[-1]
    pre_sum = normed_both[..., :width_out] + normed_both[..., width_out:]
    block_out = jax.nn.silu(pre_sum) * mask_out
    saved_values = (
        scaled_first,
        normed_first,
        act_first,
        cols_mid,
        scaled_mid,
        normed_mid,
        act_mid,
        sampled,
        scaled_both,
        pre_sum,
    )
    return (block_out, (stats_first, stats_mid, stats_both), saved_values)


def block_a_backward(
    grad_out, inputs, weights, stats_all, saved_values, mask_in, mask_out, channel
):
    w_in, w_mid, w_out, w_proj, norm_in, norm_mid, norm_out, norm_proj = weights
    stats_first, stats_mid, stats_both = stats_all
    (
        scaled_first,
        normed_first,
        act_first,
        cols_mid,
        scaled_mid,
        normed_mid,
        act_mid,
        sampled,
        scaled_both,
        pre_sum,
    ) = saved_values
    grad_pre = grad_out * mask_out * silu_slope(pre_sum)
    grad_both = jnp.concatenate([grad_pre, grad_pre], axis=-1)
    norm_both = jnp.concatenate([norm_out, norm_proj], axis=-1)
    low_both, gain_both, shift_both = norm_backward(
        grad_both, scaled_both, stats_both, norm_both, mask_out
    )
    width_out = grad_pre.shape[-1]
    low_out = low_both[..., :width_out]
    low_proj = low_both[..., width_out:]
    grad_w_out = contract(act_mid, low_out)
    grad_w_proj = contract(sampled, low_proj)
    grad_norm_mid = back_project(low_out, w_out) * mask_out * channel * silu_slope(normed_mid)
    low_mid, gain_mid, shift_mid = norm_backward(
        grad_norm_mid, scaled_mid, stats_mid, norm_mid, mask_out
    )
    grad_w_mid = contract(cols_mid, low_mid)
    grad_act_first = fold_stride_two(back_project(low_mid, w_mid), inputs.shape[1])
    grad_norm_first = grad_act_first * mask_in * channel * silu_slope(normed_first)
    low_first, gain_first, shift_first = norm_backward(
        grad_norm_first, scaled_first, stats_first, norm_in, mask_in
    )
    grad_w_in = contract(inputs, low_first)
    spread = lax.pad(
        back_project(low_proj, w_proj),
        jnp.float32(0.0),
        ((0, 0, 0), (0, 1, 1), (0, 1, 1), (0, 0, 0)),
    )
    grad_inputs = (back_project(low_first, w_in) + spread) * mask_in
    norm_grads = (
        (gain_first, shift_first),
        (gain_mid, shift_mid),
        (gain_both[:width_out], shift_both[:width_out]),
        (gain_both[width_out:], shift_both[width_out:]),
    )
    return (grad_inputs, (grad_w_in, grad_w_mid, grad_w_out, grad_w_proj), norm_grads)


def block_b_forward(block_in, weights, mask_out, local_counts, channel, depth_gate, saved_stats):
    w_in, w_mid, w_out, norm_in, norm_mid, norm_out = weights
    feed_in = block_in.astype(jnp.bfloat16)
    conv_first = jnp.dot(feed_in, w_in, preferred_element_type=jnp.float32)
    stats_first = (
        norm_stats(conv_first, mask_out, local_counts, 1) if saved_stats is None else saved_stats[0]
    )
    scaled_first, normed_first = normalize(conv_first, stats_first, norm_in, channel)
    act_first = (jax.nn.silu(normed_first) * mask_out).astype(jnp.bfloat16)
    cols_mid = taps_stride_one(act_first)
    conv_mid = jnp.dot(cols_mid, w_mid, preferred_element_type=jnp.float32)
    stats_mid = (
        norm_stats(conv_mid, mask_out, local_counts, 1) if saved_stats is None else saved_stats[1]
    )
    scaled_mid, normed_mid = normalize(conv_mid, stats_mid, norm_mid, channel)
    act_mid = (jax.nn.silu(normed_mid) * mask_out).astype(jnp.bfloat16)
    conv_out = jnp.dot(act_mid, w_out, preferred_element_type=jnp.float32)
    stats_out = (
        norm_stats(conv_out, mask_out, local_counts, 1) if saved_stats is None else saved_stats[2]
    )
    scaled_out, normed_out = normalize(conv_out, stats_out, norm_out, 1.0)
    pre_sum = block_in + depth_gate * normed_out
    result = jax.nn.silu(pre_sum) * mask_out
    saved_values = (
        feed_in,
        scaled_first,
        normed_first,
        act_first,
        cols_mid,
        scaled_mid,
        normed_mid,
        act_mid,
        scaled_out,
        pre_sum,
    )
    return (result, (stats_first, stats_mid, stats_out), saved_values)


def block_b_backward(grad_out, weights, stats_all, saved_values, mask_out, channel, depth_gate):
    w_in, w_mid, w_out, norm_in, norm_mid, norm_out = weights
    stats_first, stats_mid, stats_out = stats_all
    (
        feed_in,
        scaled_first,
        normed_first,
        act_first,
        cols_mid,
        scaled_mid,
        normed_mid,
        act_mid,
        scaled_out,
        pre_sum,
    ) = saved_values
    grad_pre = grad_out * mask_out * silu_slope(pre_sum)
    low_out, gain_out, shift_out = norm_backward(
        grad_pre * depth_gate, scaled_out, stats_out, norm_out, mask_out
    )
    grad_w_out = contract(act_mid, low_out)
    grad_norm_mid = back_project(low_out, w_out) * mask_out * channel * silu_slope(normed_mid)
    low_mid, gain_mid, shift_mid = norm_backward(
        grad_norm_mid, scaled_mid, stats_mid, norm_mid, mask_out
    )
    grad_w_mid = contract(cols_mid, low_mid)
    grad_norm_first = (
        fold_stride_one(back_project(low_mid, w_mid))
        * mask_out
        * channel
        * silu_slope(normed_first)
    )
    low_first, gain_first, shift_first = norm_backward(
        grad_norm_first, scaled_first, stats_first, norm_in, mask_out
    )
    grad_w_in = contract(feed_in, low_first)
    grad_in = grad_pre + back_project(low_first, w_in)
    norm_grads = ((gain_first, shift_first), (gain_mid, shift_mid), (gain_out, shift_out))
    return (grad_in, (grad_w_in, grad_w_mid, grad_w_out), norm_grads)


def body(
    images,
    image_sides,
    widths,
    keep_gate,
    w_in_a,
    w_mid_a,
    w_out_a,
    w_proj_a,
    norm_in_a,
    norm_mid_a,
    norm_out_a,
    norm_proj_a,
    w_in_b,
    w_mid_b,
    w_out_b,
    norm_in_b,
    norm_mid_b,
    norm_out_b,
    cotangent,
):
    mask_in, mask_out, local_counts = pixel_masks(image_sides, images.shape[1], cotangent.shape[1])
    lane_ids = jnp.arange(w_mid_a.shape[1], dtype=jnp.int32)
    channel_a = (lane_ids < widths[0]).astype(jnp.float32)
    channel_b = (lane_ids < widths[1]).astype(jnp.float32)
    depth_gate = keep_gate.astype(jnp.float32)[:, None, None, None]
    inputs = images * mask_in.astype(jnp.bfloat16)
    total_counts = lax.psum(local_counts, (FSDP, DP))
    gathered = gather_plain((w_in_a, w_mid_a, w_out_a, w_proj_a, w_in_b, w_mid_b, w_out_b))
    norms = lax.all_gather(
        jnp.concatenate(
            [norm_in_a, norm_mid_a, norm_out_a, norm_proj_a, norm_in_b, norm_mid_b, norm_out_b], axis=1
        ),
        FSDP,
        axis=0,
    )
    wide = []
    place = 0
    for one in (norm_in_a, norm_mid_a, norm_out_a, norm_proj_a, norm_in_b, norm_mid_b, norm_out_b):
        width = one.shape[1]
        wide.append(norms[:, :, place : place + width].transpose(1, 0, 2).reshape(2, -1))
        place += width
    weights_a = tuple(gathered[:4]) + tuple(wide[:4])
    weights_b = tuple(gathered[4:]) + tuple(wide[4:])
    block_out, stats_a, redone_a = block_a_forward(
        inputs, weights_a, mask_in, mask_out, total_counts, channel_a, None
    )
    result, stats_b, redone_b = block_b_forward(
        block_out, weights_b, mask_out, total_counts, channel_b, depth_gate, None
    )
    grad_block, grads_b, norms_b = block_b_backward(
        cotangent.astype(jnp.float32), weights_b, stats_b, redone_b, mask_out, channel_b, depth_gate
    )
    grad_inputs, grads_a, norms_a = block_a_backward(
        grad_block, inputs, weights_a, stats_a, redone_a, mask_in, mask_out, channel_a
    )
    finals = scatter_plain(tuple(one.astype(jnp.bfloat16) for one in grads_a + grads_b))
    final_in_a, final_mid_a, final_out_a, final_proj_a, final_in_b, final_mid_b, final_out_b = (
        one.astype(jnp.float32) for one in finals
    )
    return (
        result.astype(jnp.bfloat16),
        grad_inputs.astype(jnp.bfloat16),
        final_in_a,
        final_mid_a,
        final_out_a,
        final_proj_a,
        own_shard(norms_a[0]),
        own_shard(norms_a[1]),
        own_shard(norms_a[2]),
        own_shard(norms_a[3]),
        final_in_b,
        final_mid_b,
        final_out_b,
        own_shard(norms_b[0]),
        own_shard(norms_b[1]),
        own_shard(norms_b[2]),
    )


def solution(mesh):
    in_specs = (
        P((FSDP, DP), None, None, None),
        P((FSDP, DP)),
        P(),
        P((FSDP, DP)),
        P(FSDP, None),
        P(FSDP, None),
        P(FSDP, None),
        P(FSDP, None),
        P(None, FSDP),
        P(None, FSDP),
        P(None, FSDP),
        P(None, FSDP),
        P(FSDP, None),
        P(FSDP, None),
        P(FSDP, None),
        P(None, FSDP),
        P(None, FSDP),
        P(None, FSDP),
        P((FSDP, DP), None, None, None),
    )
    out_specs = (
        P((FSDP, DP), None, None, None),
        P((FSDP, DP), None, None, None),
        P(FSDP, None),
        P(FSDP, None),
        P(FSDP, None),
        P(FSDP, None),
        P(None, FSDP),
        P(None, FSDP),
        P(None, FSDP),
        P(None, FSDP),
        P(FSDP, None),
        P(FSDP, None),
        P(FSDP, None),
        P(None, FSDP),
        P(None, FSDP),
        P(None, FSDP),
    )
    step = body_fast if fits(mesh) else body
    return jax.shard_map(step, mesh=mesh, in_specs=in_specs, out_specs=out_specs, check_vma=False)
```

```python
import functools

import jax
import jax.numpy as jnp
from jax import lax
from jax.experimental import pallas as pl
from jax.experimental.pallas import tpu as pltpu
from jax.sharding import PartitionSpec as P

EPSILON = 1e-05
BY_MESH = pl.DeviceIdType.MESH
FSDP, DP = "fsdp", "dp"
F32 = jnp.float32
BF16 = jnp.bfloat16
NAMES = ("in_a", "mid_a", "out_a", "proj_a", "in_b", "mid_b", "out_b")
BLOCK = 256
LANES = 512
CHUNK = 32
SIDE = 7
ZYX, ZXY, YZX = range(3)
SHORT_SETS = 4
TAPS = [(u, v) for u in range(3) for v in range(3)]
LINK_PEERS = ((1, 0), (2, 0), (4, 0), (6, 0), (0, 2), (0, 1))
CHIP_PEERS = tuple((a, b) for a in (7, 6, 5, 4, 3, 2, 1, 0) for b in (2, 0) if a or b)
WAYS_IN = {
    "in_a": ((0, 64, 0, ((YZX, 4), (ZXY, 4))), (64, 64, 0, ((YZX, 4), (ZXY, 4)))),
    "mid_a": ((0, 96, 0, ((YZX, 4), (ZXY, 4))), (96, 96, 0, ((YZX, 4), (ZXY, 4))), (192, 96, 0, ((ZYX, 4), (ZXY, 4))), (288, 96, 0, ((YZX, 4), (ZXY, 4))), (384, 96, 0, ((YZX, 4), (ZXY, 4))), (480, 96, 0, ((ZYX, 4), (ZXY, 4)))),
    "out_a": ((0, 32, 0, ((ZXY, 5), (YZX, 3))), (32, 32, 0, ((ZXY, 5), (YZX, 3)))),
    "proj_a": ((0, 64, 0, ((ZXY, 5), (YZX, 3))), (64, 64, 0, ((ZXY, 5), (YZX, 3)))),
    "in_b": ((0, 64, 0, ((YZX, 4), (ZXY, 4))), (64, 64, 0, ((YZX, 4), (ZXY, 4))), (128, 64, 0, ((ZYX, 4), (ZXY, 4))), (192, 64, 0, ((YZX, 4), (ZXY, 4)))),
    "mid_b": ((0, 96, 0, ((YZX, 4), (ZXY, 4))), (96, 96, 0, ((YZX, 4), (ZXY, 4))), (192, 96, 0, ((ZYX, 4), (ZXY, 4))), (288, 96, 0, ((YZX, 4), (ZXY, 4))), (384, 96, 0, ((YZX, 4), (ZXY, 4))), (480, 96, 0, ((ZYX, 4), (ZXY, 4)))),
    "out_b": ((0, 64, 0, ((ZXY, 2), (YZX, 2))), (0, 64, 4, ((ZXY, 2), (YZX, 2)))),
}
WAYS_OUT = {
    "in_a": ((0, 64, 4), (64, 64, 4)),
    "mid_a": ((0, 96, 4), (96, 96, 4), (192, 96, 4), (288, 96, 4), (384, 96, 4), (480, 96, 4)),
    "out_a": ((0, 32, 5), (32, 32, 5)),
    "proj_a": ((0, 32, 5), (32, 32, 5), (64, 32, 5), (96, 32, 5)),
    "in_b": ((0, 128, 4), (128, 128, 4)),
    "mid_b": ((0, 96, 4), (96, 96, 4), (192, 96, 4), (288, 96, 4), (384, 96, 4), (480, 96, 4)),
    "out_b": ((0, 32, 5), (32, 32, 5)),
}
RUN = [
    331, 379, 380, 385, 386, 357, 358, 351, 129, 387, 130, 352, 388, 360, 359, 135, 389, 361, 57, 137, 390,
    362, 58, 138, 136, 401, 373, 63, 139, 81, 65, 140, 82, 66, 64, 402, 374, 376, 89, 106, 151, 397, 87, 68,
    105, 67, 398, 88, 321, 90, 23, 369, 111, 152, 22, 92, 350, 79, 91, 370, 114, 147, 148, 21, 381, 382, 80,
    383, 354, 384, 353, 391, 356, 75, 20, 76, 115, 116, 103, 113, 132, 112, 355, 392, 393, 104, 134, 323, 27,
    26, 99, 133, 394, 364, 100, 395, 142, 363, 366, 131, 127, 60, 61, 128, 141, 25, 62, 123, 143, 396, 24, 70,
    59, 124, 145, 328, 367, 377, 365, 69, 325, 31, 368, 85, 146, 30, 86, 84, 144, 83, 399, 73, 74, 93, 109,
    29, 72, 371, 108, 110, 71, 107, 94, 322, 149, 97, 98, 400, 28, 35, 96, 34, 95, 372, 150, 118, 122, 121,
    33, 77, 117, 120, 119, 78, 32, 324, 39, 101, 38, 102, 125, 326, 126, 37, 36, 43, 327, 15, 42, 14, 41, 13,
    40, 47, 12, 19, 46, 378, 18, 17, 45, 44, 56, 16, 51, 344, 345, 50, 171, 195, 49, 172, 196, 48, 55, 339,
    54, 340, 219, 53, 341, 163, 164, 165, 166, 220, 188, 187, 189, 243, 52, 3, 244, 167, 2, 212, 334, 190,
    211, 168, 335, 191, 192, 1, 155, 156, 213, 179, 214, 180, 215, 0, 236, 267, 235, 7, 237, 329, 330, 6, 216,
    346, 347, 173, 342, 203, 174, 268, 259, 238, 198, 5, 239, 204, 343, 169, 193, 197, 227, 261, 240, 175, 4,
    11, 222, 336, 170, 10, 228, 217, 337, 338, 199, 157, 158, 159, 160, 246, 221, 184, 194, 241, 9, 223, 8,
    260, 161, 245, 183, 262, 332, 333, 208, 348, 218, 182, 162, 247, 265, 181, 349, 207, 291, 286, 292, 185,
    242, 176, 153, 232, 270, 206, 263, 154, 178, 205, 200, 209, 177, 230, 271, 229, 231, 186, 252, 287, 266,
    264, 315, 251, 224, 295, 202, 269, 375, 201, 210, 233, 255, 294, 254, 288, 256, 283, 248, 275, 276, 226,
    316, 289, 253, 280, 225, 319, 285, 234, 310, 311, 312, 284, 293, 299, 257, 272, 309, 300, 318, 290, 250,
    281, 279, 278, 307, 249, 277, 317, 258, 302, 305, 304, 274, 313, 296, 273, 282, 320, 308, 297, 301, 303,
    298, 314, 306,
]


def flip(index, bits):
    out = index
    for bit in (1, 2, 4):
        if bits & bit:
            out = out + bit - 2 * bit * ((index // bit) % 2)
    return out


class Place:
    def __init__(self):
        self.f = lax.axis_index(FSDP)
        self.d = lax.axis_index(DP)
        self.y = self.f % 2
        self.z = self.f // 2
        self.c = self.d % 2
        self.x = self.d // 2
        self.inner = self.z * (3 - self.z) > 0

    def peer(self, f_bits, d_bits):
        return (flip(self.f, f_bits), flip(self.d, d_bits))


def enter(place, peers):
    barrier = pltpu.get_barrier_semaphore()
    for f_bits, d_bits in peers:
        pl.semaphore_signal(barrier, inc=1, device_id=place.peer(f_bits, d_bits), device_id_type=BY_MESH)
    pl.semaphore_wait(barrier, len(peers))


def push(source, target, send_sem, recv_sem, device):
    pltpu.make_async_remote_copy(
        src_ref=source,
        dst_ref=target,
        send_sem=send_sem,
        recv_sem=recv_sem,
        device_id=device,
        device_id_type=BY_MESH,
    ).start()


def await_bytes(view, sem):
    pltpu.make_async_copy(view, view, sem).wait()


def await_count(ref, count, sem):
    if not count:
        return
    rows_most, columns_most = ref.shape
    for columns in range(columns_most, 0, -128):
        rows = count // columns
        if count % columns == 0 and rows % 16 == 0 and rows <= rows_most:
            await_bytes(ref.at[pl.ds(0, rows), pl.ds(0, columns)], sem)
            return
    raise ValueError(count)


def rows_of(start, size):
    return pl.ds(pl.multiple_of(start, 16), size)


def cols_of(start, size):
    return pl.ds(pl.multiple_of(start, 128), size)


class Gather:
    def __init__(self, place, shard, whole, start, rows, from_eighth, groups, send, recv):
        self.place, self.shard, self.whole = place, shard, whole
        self.start, self.rows, self.send, self.recv = start, rows, send, recv
        self.total, columns = shard.shape
        half = columns // 2
        self.part = part = rows // 2
        self.col_0 = place.c * half + half * from_eighth // 8
        self.row_q = start + place.x * part
        self.row_o = start + part - place.x * part
        self.arriving, self.leaving = [0] * 5, 0
        self.groups, at = {}, 0
        for way, eighths in groups:
            self.groups[way] = (at, half * eighths // 8)
            at += half * eighths // 8
        self.wide = at

    def view(self, bits, row, rows, from_col, columns):
        block = flip(self.place.f, bits) * self.total
        return self.whole.at[rows_of(block + row, rows), cols_of(self.col_0 + from_col, columns)]

    def pass_on(self, bits, row, rows, group, leg, peer):
        from_col, columns = group
        view = self.view(bits, row, rows, from_col, columns)
        push(view, view, self.send, self.recv.at[leg or 0], self.place.peer(*peer))
        if leg is not None:
            self.arriving[leg] += rows * columns
            self.leaving += rows * columns

    def pass_own(self, row, rows, group, leg, peer):
        from_col, columns = group
        source = self.shard.at[rows_of(row, rows), cols_of(self.col_0 + from_col, columns)]
        push(source, self.view(0, row, rows, from_col, columns), self.send, self.recv.at[leg], self.place.peer(*peer))
        self.arriving[leg] += rows * columns
        self.leaving += rows * columns

    def arrive(self, leg):
        await_count(self.whole, self.arriving[leg], self.recv.at[leg])

    def first(self):
        pltpu.make_async_copy(
            self.shard.at[pl.ds(self.start, self.rows), cols_of(self.col_0, self.wide)],
            self.view(0, self.start, self.rows, 0, self.wide),
            self.recv.at[0],
        ).start()
        self.arriving[0] += self.rows * self.wide
        everything = (0, self.wide)

        @pl.when(self.place.inner)
        def _():
            self.pass_own(self.row_q, self.part, everything, 0, (6, 0))

        self.pass_own(self.row_q, self.part, everything, 4, (4, 0))
        self.pass_own(self.row_q, self.part, everything, 0, (2, 0))

    def relay(self):
        self.arrive(4)

        @pl.when(self.place.inner)
        def _():
            self.pass_on(4, self.row_q, self.part, (0, self.wide), None, (2, 0))

    def own(self):
        for way, group in self.groups.items():
            if way == ZXY:
                self.pass_own(self.start, self.rows, group, 0, (1, 0))
            else:
                self.pass_own(self.row_q, self.part, group, 0, (1, 0))

    def one(self):
        self.arrive(0)
        if YZX in self.groups:
            for bits in (6, 4, 2):
                self.pass_on(1, self.row_q, self.part, self.groups[YZX], 1, (bits, 0))
        for way, group in self.groups.items():
            for bits in (2, 4, 6):
                if way != YZX:
                    self.pass_on(bits, self.row_q, self.part, group, 1, (1, 0))
                self.pass_on(bits, self.row_q, self.part, group, 1, (0, 2))
            if way == YZX:
                self.pass_on(1, self.row_q, self.part, group, 1, (0, 2))

    def two(self):
        self.arrive(1)
        for way, group in self.groups.items():
            if way == ZXY:
                for bits in (2, 4, 6):
                    self.pass_on(bits, self.row_o, self.part, group, 2, (1, 0))
            else:
                for bits in (1, 3, 5, 7) if way == ZYX else (3, 5, 7):
                    self.pass_on(bits, self.row_q, self.part, group, 2, (0, 2))

    def three(self):
        self.arrive(2)
        for bits in range(8):
            self.pass_on(bits, self.start, self.rows, (0, self.wide), 3, (0, 1))

    def four(self):
        self.arrive(3)

    def sent(self):
        block = self.part * self.wide

        @pl.when(self.place.inner)
        def _():
            await_count(self.whole, self.leaving + block, self.send)

        @pl.when(jnp.logical_not(self.place.inner))
        def _():
            await_count(self.whole, self.leaving - block, self.send)


def chunk_of(rows, columns):
    best = 16
    for chunk in range(16, rows + 1, 16):
        if rows % chunk == 0 and chunk * columns <= 16384:
            best = chunk
    return best


def add_blocks(blocks, rows, columns, target, source):
    chunk = chunk_of(rows, columns)
    each = rows // chunk

    def step(index, carry):
        block, start = index // each, pl.multiple_of((index % each) * chunk, 16)
        into, more = target(block, start, chunk), source(block, start, chunk)
        into[...] = into[...] + more[...]
        return carry

    lax.fori_loop(0, blocks * each, step, 0)


class Scatter:
    def __init__(self, place, grad, room, out, start, rows, wide_a, send, recv):
        self.place, self.grad, self.out = place, grad, out
        self.start, self.rows, self.wide_a = start, rows, wide_a
        self.send, self.recv = send, recv
        total, columns = room.shape
        self.total = total = total // 8
        self.half = half = columns // 2
        self.wide_b = wide_b = half - wide_a
        self.part = part = rows // 2
        self.room = room
        self.from_core = room.at[:, pl.ds(0, half)]

        def landing(row, count, col, width):
            return room.at[pl.ds(row, count), pl.ds(half + col, width)] if width else None

        self.a_x = landing(4 * start, 4 * rows, 0, wide_a)
        self.a_y = landing(4 * total + 2 * start, 2 * rows, 0, wide_a)
        self.a_z = landing(6 * total + 3 * start // 2, 3 * part, 0, wide_a)
        self.b_y = landing(4 * start, 4 * rows, wide_a, wide_b)
        self.b_z = landing(4 * total + 3 * start, 3 * rows, wide_a, wide_b)
        self.b_x = landing(7 * total + start // 2, part, wide_a, wide_b)
        self.col_0 = place.c * half
        self.row_q = start + place.x * part
        self.row_o = start + part - place.x * part

    def push(self, source, target, leg, device):
        push(source, target, self.send, self.recv.at[leg], device)

    def zero(self):
        other = cols_of(self.half - self.col_0, self.half)
        for block in range(8):
            rows = pl.ds(block * self.total + self.start, self.rows)
            self.push(self.grad.at[rows, other], self.from_core.at[rows], 5, self.place.peer(0, 1))

    def core(self, row, rows, from_col, columns):
        return self.from_core.at[rows_of(row, rows), pl.ds(from_col, columns)]

    def mine(self, row, rows, from_col, columns):
        return self.core(self.place.f * self.total + row, rows, from_col, columns)

    def one(self):
        place, total, part, rows = self.place, self.total, self.part, self.rows
        await_count(self.room, 8 * rows * self.half, self.recv.at[5])
        add_blocks(
            8,
            rows,
            self.half,
            lambda b, s, n: self.core(b * total + self.start + s, n, 0, self.half),
            lambda b, s, n: self.grad.at[rows_of(b * total + self.start + s, n), cols_of(self.col_0, self.half)],
        )
        await_count(self.room, 8 * rows * self.half, self.send)
        if self.wide_a:
            for block in range(8):
                self.push(
                    self.core(block * total + self.row_o, part, 0, self.wide_a),
                    self.a_x.at[pl.ds(block * part, part)],
                    0,
                    place.peer(0, 2),
                )
        if self.wide_b:
            for level in range(4):
                self.push(
                    self.core((2 * level + 1 - place.y) * total + self.start, rows, self.wide_a, self.wide_b),
                    self.b_y.at[pl.ds(level * rows, rows)],
                    0,
                    place.peer(1, 0),
                )

    def two(self):
        place, total, part, rows = self.place, self.total, self.part, self.rows
        await_count(self.room, 4 * rows * self.half, self.recv.at[0])
        if self.wide_a:
            add_blocks(
                8,
                part,
                self.wide_a,
                lambda b, s, n: self.core(b * total + self.row_q + s, n, 0, self.wide_a),
                lambda b, s, n: self.a_x.at[rows_of(b * part + s, n)],
            )
            for level in range(4):
                self.push(
                    self.core((2 * level + 1 - place.y) * total + self.row_q, part, 0, self.wide_a),
                    self.a_y.at[pl.ds(level * part, part)],
                    1,
                    place.peer(1, 0),
                )
        if self.wide_b:
            add_blocks(
                4,
                rows,
                self.wide_b,
                lambda b, s, n: self.core((2 * b + place.y) * total + self.start + s, n, self.wide_a, self.wide_b),
                lambda b, s, n: self.b_y.at[rows_of(b * rows + s, n)],
            )
            for slot, bits in enumerate((6, 4, 2)):
                self.push(
                    self.core(flip(place.f, bits) * total + self.start, rows, self.wide_a, self.wide_b),
                    self.b_z.at[pl.ds(slot * rows, rows)],
                    1,
                    place.peer(bits, 0),
                )

    def sum_four(self, row, rows, col, wide, landed, store):
        chunk = chunk_of(rows, wide)

        def step(index, carry):
            start = pl.multiple_of(index * chunk, 16)
            total = self.mine(row + start, chunk, col, wide)[...].astype(F32)
            for slot in range(3):
                total = total + landed[rows_of(slot * rows + start, chunk)].astype(F32)
            store(start, chunk, total.astype(BF16))
            return carry

        lax.fori_loop(0, rows // chunk, step, 0)

    def three(self):
        place, total, part, rows = self.place, self.total, self.part, self.rows
        await_count(self.room, 2 * rows * self.wide_a + 3 * rows * self.wide_b, self.recv.at[1])
        if self.wide_a:
            add_blocks(
                4,
                part,
                self.wide_a,
                lambda b, s, n: self.core((2 * b + place.y) * total + self.row_q + s, n, 0, self.wide_a),
                lambda b, s, n: self.a_y.at[rows_of(b * part + s, n)],
            )
            for slot, bits in enumerate((6, 4, 2)):
                self.push(
                    self.core(flip(place.f, bits) * total + self.row_q, part, 0, self.wide_a),
                    self.a_z.at[pl.ds(slot * part, part)],
                    2,
                    place.peer(bits, 0),
                )
        if self.wide_b:

            def keep(start, chunk, value):
                self.mine(self.start + start, chunk, self.wide_a, self.wide_b)[...] = value

            self.sum_four(self.start, rows, self.wide_a, self.wide_b, self.b_z, keep)
            self.push(self.mine(self.row_o, part, self.wide_a, self.wide_b), self.b_x, 2, place.peer(0, 2))

    def four(self):
        place, part = self.place, self.part
        await_count(self.room, 3 * part * self.wide_a + part * self.wide_b, self.recv.at[2])
        if self.wide_a:

            def keep(start, chunk, value):
                self.out[rows_of(self.row_q + start, chunk), cols_of(self.col_0, self.wide_a)] = value

            self.sum_four(self.row_q, part, 0, self.wide_a, self.a_z, keep)
        if self.wide_b:
            chunk = chunk_of(part, self.wide_b)

            def step(index, carry):
                start = pl.multiple_of(index * chunk, 16)
                total = self.mine(self.row_q + start, chunk, self.wide_a, self.wide_b)[...].astype(F32)
                total = total + self.b_x[rows_of(start, chunk)].astype(F32)
                columns = cols_of(self.col_0 + self.wide_a, self.wide_b)
                self.out[rows_of(self.row_q + start, chunk), columns] = total.astype(BF16)
                return carry

            lax.fori_loop(0, part // chunk, step, 0)
        block = self.out.at[rows_of(self.row_q, part), cols_of(self.col_0, self.half)]
        self.push(block, block, 3, place.peer(0, 2))

    def five(self):
        await_bytes(self.out.at[pl.ds(0, self.part), pl.ds(0, self.half)], self.recv.at[3])
        block = self.out.at[pl.ds(self.start, self.rows), cols_of(self.col_0, self.half)]
        self.push(block, block, 4, self.place.peer(0, 1))

    def six(self):
        await_bytes(self.out.at[pl.ds(0, self.rows), pl.ds(0, self.half)], self.recv.at[4])

    def sent(self):
        await_count(self.room, 18 * self.part * self.half, self.send)


def mm(left, right):
    return jnp.dot(left, right, preferred_element_type=F32)


def mm_nt(left, right):
    return lax.dot_general(left, right, (((1,), (1,)), ((), ())), preferred_element_type=F32)


def mm_tn(left, right):
    return lax.dot_general(left, right, (((0,), (0,)), ((), ())), preferred_element_type=F32)


def loop(count, step):
    def body_of(index, carry):
        step(index)
        return carry

    lax.fori_loop(0, count, body_of, 0)


def at_block(index, size):
    if isinstance(index, int):
        return pl.ds(index * size, size)
    return pl.ds(pl.multiple_of(index * size, size), size)


def slope_of(values):
    gate = jax.nn.sigmoid(values)
    return gate * (1.0 + values * (1.0 - gate))


def fold(values):
    total = values[0:8]
    for start in range(8, values.shape[0], 8):
        total = total + values[start : start + 8]
    return total


def column_sums(count, width, terms):
    def step(index, carry):
        start = pl.multiple_of(index * CHUNK, CHUNK)
        return tuple(total + fold(one) for total, one in zip(carry, terms(start)))

    zero = jnp.zeros((8, LANES), F32)
    totals = lax.fori_loop(0, count, step, (zero,) * width)
    return [jnp.sum(one, axis=0, keepdims=True) for one in totals]


class Vectors:
    def __init__(self, ref):
        self.ref, self.used = ref, 0

    def put(self, row):
        at = self.used
        self.used += 1
        self.ref[at : at + 1, :] = row
        return at

    def get(self, at):
        return self.ref[at : at + 1, :]


class Totals:
    def __init__(self, place, short, long, tot, send, recv):
        self.place, self.short, self.long, self.tot, self.send, self.recv = place, short, long, tot, send, recv
        self.began = 0

    def start(self, rows_of_values, extra=None):
        one = Total(self, 4 * len(rows_of_values) + (8 if extra is not None else 0))
        own = one.slot(self.place.c)
        at = 0
        for row in rows_of_values:
            for lane in range(0, LANES, 128):
                own[at : at + 1, :] = row[:, lane : lane + 128]
                at += 1
        if extra is not None:
            own[at : at + 8, :] = extra
        one.spread(self.place.c, ((0, 1),), 0)
        return one

    def row(self, index):
        at = 4 * index
        return jnp.concatenate([self.tot[at + k : at + k + 1, :] for k in range(4)], axis=1)

    def wide(self, at):
        return jnp.concatenate([self.tot[at : at + 1, :]] * 4, axis=1)


class Total:
    def __init__(self, all_of_them, rows):
        self.all, self.place, self.rows = all_of_them, all_of_them.place, rows
        self.is_long = rows > 16
        self.set = SHORT_SETS
        if not self.is_long:
            self.set = all_of_them.began % SHORT_SETS
            all_of_them.began += 1

    def slots(self, at, count):
        if self.is_long:
            return self.all.long.at[pl.ds(at, count), pl.ds(0, self.rows)]
        return self.all.short.at[self.set, pl.ds(at, count), pl.ds(0, self.rows)]

    def slot(self, at):
        if self.is_long:
            return self.all.long.at[at, pl.ds(0, self.rows)]
        return self.all.short.at[self.set, at, pl.ds(0, self.rows)]

    def spread(self, at, peers, phase):
        own = self.slot(at)
        for bits in peers:
            push(own, own, self.all.send.at[self.set, phase], self.all.recv.at[self.set, phase], self.place.peer(*bits))

    def gather(self, at, count, peers, phase):
        await_bytes(self.slots(at, peers), self.all.recv.at[self.set, phase])
        total = self.slot(at)[...]
        for index in range(at + 1, at + count):
            total = total + self.slot(index)[...]
        return total

    def middle(self):
        place = self.place
        total = self.gather(0, 2, 1, 0)
        if self.is_long:
            self.slot(2 + 2 * place.y + place.x)[...] = total
            self.spread(2 + 2 * place.y + place.x, ((1, 2), (1, 0), (0, 2)), 1)
        else:
            self.slot(2 + 2 * place.f + place.x)[...] = total
            self.spread(2 + 2 * place.f + place.x, CHIP_PEERS, 1)

    def late(self):
        if self.is_long:
            self.slot(6 + self.place.z)[...] = self.gather(2, 4, 3, 1)
            self.spread(6 + self.place.z, ((6, 0), (4, 0), (2, 0)), 2)

    def end(self):
        if self.is_long:
            self.all.tot[0 : self.rows, :] = self.gather(6, 4, 3, 2)
        else:
            self.all.tot[0 : self.rows, :] = self.gather(2, 16, 15, 1)
        for phase, count in enumerate((1, 3, 3) if self.is_long else (1, 15)):
            await_bytes(self.slots(0, count), self.all.send.at[self.set, phase])


def step_kernel(
    img_hbm,
    cot_hbm,
    sides,
    keep,
    widths,
    norm_in_a,
    norm_mid_a,
    norm_out_a,
    norm_proj_a,
    norm_in_b,
    norm_mid_b,
    norm_out_b,
    sh_in_a,
    sh_mid_a,
    sh_out_a,
    sh_proj_a,
    sh_in_b,
    sh_mid_b,
    sh_out_b,
    result_hbm,
    images_hbm,
    own_hbm_in_a,
    own_hbm_mid_a,
    own_hbm_out_a,
    own_hbm_proj_a,
    own_hbm_in_b,
    own_hbm_mid_b,
    own_hbm_out_b,
    out_hbm_in_a,
    out_hbm_mid_a,
    out_hbm_out_a,
    out_hbm_proj_a,
    out_hbm_in_b,
    out_hbm_mid_b,
    out_hbm_out_b,
    own_in_a,
    own_mid_a,
    own_out_a,
    own_proj_a,
    own_in_b,
    own_mid_b,
    own_out_b,
    out_in_a,
    out_mid_a,
    out_out_a,
    out_proj_a,
    out_in_b,
    out_mid_b,
    out_out_b,
    w_in_a,
    w_mid_a,
    w_out_a,
    w_proj_a,
    w_in_b,
    w_mid_b,
    w_out_b,
    raw,
    cot,
    x,
    c1,
    cols_a,
    c2,
    a2,
    c3,
    cp,
    bo,
    feed,
    d1,
    cols_b,
    d2,
    b2,
    d3,
    dz,
    dm,
    df,
    dout,
    dproj,
    g_mid,
    g_out,
    g_in,
    g_proj,
    mask_ref,
    gate_ref,
    move,
    norms,
    block_ref,
    vec_ref,
    short,
    long,
    tot,
    sums,
    io_sem,
    link_send,
    link_recv,
    ar_send,
    ar_recv,
    nb_sem,
    out_sem,
    free_sem,
):
    place = Place()
    shards = dict(zip(NAMES, (sh_in_a, sh_mid_a, sh_out_a, sh_proj_a, sh_in_b, sh_mid_b, sh_out_b)))
    wholes = dict(zip(NAMES, (w_in_a, w_mid_a, w_out_a, w_proj_a, w_in_b, w_mid_b, w_out_b)))
    outs = dict(zip(NAMES, (out_in_a, out_mid_a, out_out_a, out_proj_a, out_in_b, out_mid_b, out_out_b)))
    owned = dict(zip(NAMES, (own_in_a, own_mid_a, own_out_a, own_proj_a, own_in_b, own_mid_b, own_out_b)))
    own_hbm = (own_hbm_in_a, own_hbm_mid_a, own_hbm_out_a, own_hbm_proj_a, own_hbm_in_b, own_hbm_mid_b, own_hbm_out_b)
    out_hbm = (out_hbm_in_a, out_hbm_mid_a, out_hbm_out_a, out_hbm_proj_a, out_hbm_in_b, out_hbm_mid_b, out_hbm_out_b)
    own_copies = [pltpu.make_async_copy(owned[n], own_hbm[i], out_sem.at[0, i]) for i, n in enumerate(NAMES)]
    out_copies = [pltpu.make_async_copy(outs[n], out_hbm[i], out_sem.at[1, i]) for i, n in enumerate(NAMES)]
    small = dict(zip(NAMES, (norm_in_a, norm_mid_a, norm_out_a, norm_proj_a, norm_in_b, norm_mid_b, norm_out_b)))
    grads = dict(mid_a=g_mid, mid_b=g_mid, out_a=g_out, out_b=g_out, in_b=g_in, proj_a=g_proj)
    grads["in_a"] = g_in.at[pl.ds(0, wholes["in_a"].shape[0])]
    todo = {}

    def token(name):
        def keep_it(function):
            todo[name] = function
            return function

        return keep_it

    def tokens(name, count, each, step):
        def some(first):
            for k in range(each):
                step(first + k)

        for part in range(count):
            todo[f"{name}.{part}"] = functools.partial(some, part * each)

    gathers, scatters, at, going = {}, {}, 0, 0
    left = {name: len(WAYS_OUT[name]) for name in NAMES}

    def finish_piece(name, piece):
        piece.six()
        left[name] -= 1
        if not left[name]:
            out_copies[NAMES.index(name)].start()

    def tell(name):
        for bits in LINK_PEERS:
            sem = free_sem.at[NAMES.index(name)]
            pl.semaphore_signal(sem, inc=1, device_id=place.peer(*bits), device_id_type=BY_MESH)

    def send_core(name, n):
        if n == 0:
            pl.semaphore_wait(free_sem.at[NAMES.index(name)], len(LINK_PEERS))
        scatters[name, n].zero()

    for name in NAMES:
        for n, (start, rows, from_eighth, ways) in enumerate(WAYS_IN[name]):
            sems = link_send.at[at], link_recv.at[at]
            g = gathers[name, n] = Gather(
                place, shards[name], wholes[name], start, rows, from_eighth, ways, *sems
            )
            at += 1
            key = f"{name}.{n}"
            todo["z." + key], todo["o." + key], todo["L1." + key] = g.first, g.own, g.one
            todo["R." + key] = g.relay
            todo["L2." + key], todo["L3." + key] = g.two, g.three
        eighth = shards[name].shape[1] // 16
        for n, (start, rows, wide) in enumerate(WAYS_OUT[name]):
            sems = link_send.at[going], link_recv.at[going]
            s = Scatter(place, grads[name], wholes[name], outs[name], start, rows, wide * eighth, *sems)
            scatters[name, n] = s
            going += 1
            key = f"{name}.{n}"
            todo["S0." + key], todo["S1." + key] = functools.partial(send_core, name, n), s.one
            todo["S2." + key], todo["S3." + key], todo["S4." + key] = s.two, s.three, s.four
            todo["S5." + key] = s.five
            todo["S6." + key] = functools.partial(finish_piece, name, s)
        def arrived(some):
            for one in some:
                one.four()

        mine = [gathers[name, n] for n in range(len(WAYS_IN[name]))]
        if name == "out_b":
            for n, one in enumerate(mine):
                todo[f"W.{name}.{n}"] = one.four
        else:
            todo["W." + name] = functools.partial(arrived, mine)

    vec = Vectors(vec_ref)
    totals = Totals(place, short, long, tot, ar_send, ar_recv)
    state, scales, params = {}, {}, {}
    sums_of = {}

    def begin(n, values, extra=None):
        sums_of[n] = totals.start(values, extra)

    for n in range(1, 15):
        todo[f"A{n}m"] = lambda n=n: sums_of[n].middle()
        todo[f"A{n}l"] = lambda n=n: sums_of[n].late()

    image_copy = pltpu.make_async_copy(img_hbm, raw, io_sem.at[0])
    cot_copy = pltpu.make_async_copy(cot_hbm, cot, io_sem.at[1])
    result_copy = pltpu.make_async_copy(cot, result_hbm, io_sem.at[2])
    grad_copy = pltpu.make_async_copy(raw, images_hbm, io_sem.at[3])

    @token("enter")
    def _():
        image_copy.start()
        cot_copy.start()
        odd = (place.f % 2).astype(F32)
        block_ref[...] = jnp.zeros_like(block_ref)
        at = 0
        for name in NAMES:
            values = small[name][...].astype(F32)
            if values.shape[1] < 128:
                move[0:8, 0:128] = jnp.zeros((8, 128), F32)
                move[0:2, 0 : values.shape[1]] = values
                plain = move[0:8, 0:128]
                values = (plain + (pltpu.roll(plain, 64, 1) - plain) * odd)[0:2]
            for lane in range(0, values.shape[1], 128):
                block_ref[at : at + 1, :] = values[0:1, lane : lane + 128]
                block_ref[at + 10 : at + 11, :] = values[1:2, lane : lane + 128]
                at += 1
        norms[place.f] = block_ref[...]
        enter(place, ((0, 1),) + CHIP_PEERS)
        for bits in (7, 6, 5, 4, 3, 2, 1):
            push(block_ref, norms.at[place.f], nb_sem.at[0], nb_sem.at[1], place.peer(bits, 0))

    @token("prep")
    def _():
        pixel = lax.broadcasted_iota(jnp.int32, (BLOCK, 128), 0)
        slot = pixel % 4

        def by_slot(values):
            return jnp.where(slot == 0, values[0], jnp.where(slot == 1, values[1], jnp.where(slot == 2, values[2], values[3])))

        half = by_slot([sides[i] // 2 for i in range(4)])
        inside = ((pixel // 4) % 8 < half) & (pixel // 32 < half)
        mask_ref[...] = jnp.where(inside, 1.0, 0.0).astype(F32)
        gate_ref[...] = by_slot([keep[i] for i in range(4)]).astype(F32)
        move[...] = jnp.zeros_like(move)
        image_copy.wait()

        def plane_rows(row):
            mask = jnp.concatenate([mask_ref[at_block(row, CHUNK), :]] * (x.shape[1] // 128), axis=1)
            for row_par in range(2):
                for col_par in range(2):
                    for col in range(SIDE):
                        move[4 * col : 4 * col + 4, :] = raw[2 * row + row_par, 2 * col + col_par].astype(F32)
                    start = (2 * row_par + col_par) * BLOCK + row * CHUNK
                    x[pl.ds(pl.multiple_of(start, CHUNK), CHUNK), :] = (move[...] * mask).astype(BF16)

        loop(SIDE, plane_rows)
        for p in range(4):
            x[(p + 1) * BLOCK - CHUNK : (p + 1) * BLOCK, :] = jnp.zeros((CHUNK, x.shape[1]), BF16)

    @token("norms")
    def _():
        await_bytes(norms.at[pl.ds(0, 7)], nb_sem.at[1])
        await_bytes(norms.at[pl.ds(0, 7)], nb_sem.at[0])

        def narrow_row(at):
            pieces = [norms[2 * k, at : at + 1, :] + norms[2 * k + 1, at : at + 1, :] for k in range(4)]
            return vec.put(jnp.concatenate(pieces, axis=1))

        def wide_rows(at):
            return [
                vec.put(
                    jnp.concatenate(
                        [norms[2 * j + k // 2, at + k % 2 : at + k % 2 + 1, :] for k in range(4)], axis=1
                    )
                )
                for j in range(4)
            ]

        params["in_a"] = ([narrow_row(0)], [narrow_row(10)])
        params["mid_a"] = ([narrow_row(1)], [narrow_row(11)])
        params["out_a"] = (wide_rows(2), wide_rows(12))
        params["proj_a"] = (wide_rows(4), wide_rows(14))
        params["in_b"] = ([narrow_row(6)], [narrow_row(16)])
        params["mid_b"] = ([narrow_row(7)], [narrow_row(17)])
        params["out_b"] = (wide_rows(8), wide_rows(18))
        lanes = lax.broadcasted_iota(jnp.int32, (1, LANES), 1)
        state["chan_a"] = vec.put(jnp.where(lanes < widths[0], 1.0, 0.0).astype(F32))
        state["chan_b"] = vec.put(jnp.where(lanes < widths[1], 1.0, 0.0).astype(F32))

    def wide_of(ref, start, size=CHUNK):
        return jnp.concatenate([ref[pl.ds(start, size), :]] * 4, axis=1)

    def mask_at(start):
        return wide_of(mask_ref, start)

    def gate_at(start):
        return wide_of(gate_ref, start)

    def set_norm(name, block, first_row, inverse, chan):
        inverse = vec.get(state[inverse])
        average = totals.row(first_row) * inverse
        rstd = lax.rsqrt(totals.row(first_row + 1) * inverse - average * average + EPSILON)
        gain, shift = (vec.get(rows[block]) for rows in params[name])
        keep_lanes = 1.0 if chan is None else vec.get(state[chan])
        by = gain * rstd
        scales[name, block] = dict(
            rstd=vec.put(rstd),
            off=vec.put(-average * rstd),
            by=vec.put(by),
            mul=vec.put(by * keep_lanes),
            add=vec.put((shift - average * by) * keep_lanes),
        )

    def normed(name, block, values):
        s = scales[name, block]
        return values * vec.get(s["mul"]) + vec.get(s["add"])

    def hat(name, block, values):
        s = scales[name, block]
        return values * vec.get(s["rstd"]) + vec.get(s["off"])

    def set_back(name, block, shift_row, gain_row):
        s = scales[name, block]
        inverse = vec.get(state["inv_in" if name == "in_a" else "inv_out"])
        by = vec.get(s["by"])
        pull = by * totals.row(gain_row) * inverse
        s["back_add"] = vec.put(by * totals.row(shift_row) * inverse + pull * vec.get(s["off"]))
        s["back_mul"] = vec.put(pull * vec.get(s["rstd"]))

    def back(name, block, grad, values):
        s = scales[name, block]
        return grad * vec.get(s["by"]) - vec.get(s["back_add"]) - values * vec.get(s["back_mul"])

    def square_terms(ref):
        def terms(start):
            values = ref[pl.ds(start, CHUNK), :]
            return values, values * values

        return terms

    def masked_terms(ref):
        def terms(start):
            values = ref[pl.ds(start, CHUNK), :]
            kept = values * mask_at(start)
            return kept, kept * values

        return terms

    def lane_row(at, lane):
        return vec_ref[at : at + 1, at_block(lane, 128)]

    def add_up(out, count, left, right, product=mm):
        total = product(left(0), right(0))
        for k in range(1, count):
            total = total + product(left(k), right(k))
        out[...] = total

    @token("A1s")
    def _():
        for p in range(4):
            c1[at_block(p, BLOCK), :] = mm(x[at_block(p, BLOCK), :], w_in_a[...])
        side = [sides[i] for i in range(4)]
        count_in = sum(s * s for s in side).astype(F32)
        count_out = sum((s // 2) * (s // 2) for s in side).astype(F32)
        at = lax.broadcasted_iota(jnp.int32, (8, 128), 0)
        counts = jnp.where(at == 0, count_in, jnp.where(at == 1, count_out, 0.0))
        begin(1, column_sums(32, 2, square_terms(c1)), counts)

    @token("A1e")
    def _():
        sums_of[1].end()
        state["inv_in"] = vec.put(1.0 / totals.wide(8))
        state["inv_out"] = vec.put(1.0 / totals.wide(9))
        set_norm("in_a", 0, 0, "inv_in", "chan_a")
        s = scales["in_a", 0]

        def act_a(lane):
            for row_par in range(2):
                for col_par in range(2):
                    p = 2 * row_par + col_par
                    values = c1[p * BLOCK : (p + 1) * BLOCK, at_block(lane, 128)]
                    scaled = values * lane_row(s["mul"], lane) + lane_row(s["add"], lane)
                    act = scaled * jax.nn.sigmoid(scaled) * mask_ref[...]
                    for t, (u, v) in enumerate(TAPS):
                        if (u != 1) != bool(row_par) or (v != 1) != bool(col_par):
                            continue
                        shift = (32 if u == 0 else 0) + (4 if v == 0 else 0)
                        moved = pltpu.roll(act, shift, 0) if shift else act
                        cols_a[:, pl.ds(pl.multiple_of(t * LANES + lane * 128, 128), 128)] = moved.astype(BF16)

        loop(4, act_a)

    def conv_mid(out, cols, weight):
        add_up(out, 3, lambda k: cols[:, at_block(k, 1536)], lambda k: weight[at_block(k, 1536), :])

    def act_mid(act_ref, ref, name):
        def step(index):
            start = pl.multiple_of(index * CHUNK, CHUNK)
            scaled = normed(name, 0, ref[pl.ds(start, CHUNK), :])
            act_ref[pl.ds(start, CHUNK), :] = (scaled * jax.nn.sigmoid(scaled) * mask_at(start)).astype(BF16)

        loop(BLOCK // CHUNK, step)

    @token("A2s")
    def _():
        conv_mid(c2, cols_a, w_mid_a)
        begin(2, column_sums(8, 2, masked_terms(c2)))

    @token("A2e")
    def _():
        sums_of[2].end()
        set_norm("mid_a", 0, 0, "inv_out", "chan_a")
        act_mid(a2, c2, "mid_a")

    @token("proj")
    def _():
        def project(j):
            cp[at_block(j, BLOCK), :] = mm(x[0:BLOCK, :], w_proj_a[:, at_block(j, LANES)])

        loop(4, project)

    def blocked(ref, j):
        return square_terms(ref.at[pl.ds(j * BLOCK, BLOCK)])

    @token("A3s")
    def _():
        for j in range(4):
            c3[at_block(j, BLOCK), :] = mm(a2[...], w_out_a[:, at_block(j, LANES)])
        begin(3, [row for ref in (c3, cp) for j in range(4) for row in column_sums(8, 2, blocked(ref, j))])

    @token("A3e")
    def _():
        sums_of[3].end()
        for j in range(4):
            set_norm("out_a", j, 2 * j, "inv_out", None)
            set_norm("proj_a", j, 8 + 2 * j, "inv_out", None)
        for j in range(4):

            def join_a(index, j=j):
                start = pl.multiple_of(index * CHUNK, CHUNK)
                rows = pl.ds(j * BLOCK + start, CHUNK)
                pre = normed("out_a", j, c3[rows, :]) + normed("proj_a", j, cp[rows, :])
                out = pre * jax.nn.sigmoid(pre) * mask_at(start)
                bo[rows, :] = out
                feed[pl.ds(start, CHUNK), pl.ds(j * LANES, LANES)] = out.astype(BF16)

            loop(BLOCK // CHUNK, join_a)

    @token("A4s")
    def _():
        add_up(d1, 4, lambda k: feed[:, at_block(k, LANES)], lambda k: w_in_b[at_block(k, LANES), :])
        begin(4, column_sums(8, 2, square_terms(d1)))

    @token("A4e")
    def _():
        sums_of[4].end()
        set_norm("in_b", 0, 0, "inv_out", "chan_b")
        s = scales["in_b", 0]

        def act_b(lane):
            scaled = d1[:, at_block(lane, 128)] * lane_row(s["mul"], lane) + lane_row(s["add"], lane)
            act = scaled * jax.nn.sigmoid(scaled) * mask_ref[...]
            for t, (u, v) in enumerate(TAPS):
                shift = (-(32 * (u - 1) + 4 * (v - 1))) % BLOCK
                moved = pltpu.roll(act, shift, 0) if shift else act
                cols_b[:, pl.ds(pl.multiple_of(t * LANES + lane * 128, 128), 128)] = moved.astype(BF16)

        loop(4, act_b)

    @token("A5s")
    def _():
        conv_mid(d2, cols_b, w_mid_b)
        begin(5, column_sums(8, 2, masked_terms(d2)))

    @token("A5e")
    def _():
        sums_of[5].end()
        set_norm("mid_b", 0, 0, "inv_out", "chan_b")
        act_mid(b2, d2, "mid_b")

    PAIRS = ((0, 2), (1, 3))

    def expand_b(n, pair):
        for j in pair:
            d3[at_block(j, BLOCK), :] = mm(b2[...], w_out_b[:, at_block(j, LANES)])
        begin(n, [row for j in pair for row in column_sums(8, 2, blocked(d3, j))])

    def set_out_b(n, pair):
        sums_of[n].end()
        for k, j in enumerate(pair):
            set_norm("out_b", j, 2 * k, "inv_out", None)

    def finish_b(n, pair):
        values = []
        for j in pair:
            lanes = pl.ds(j * LANES, LANES)

            def finish(start, j=j, lanes=lanes):
                rows = pl.ds(j * BLOCK + start, CHUNK)
                row = start // CHUNK
                for col in range(SIDE):
                    move[4 * col : 4 * col + 4, 0:LANES] = cot[row, col, :, lanes].astype(F32)
                mask, gate, hidden = mask_at(start), gate_at(start), d3[rows, :]
                pre = bo[rows, :] + gate * normed("out_b", j, hidden)
                part = jax.nn.sigmoid(pre)
                grad = move[:, 0:LANES] * mask * (part * (1.0 + pre * (1.0 - part)))
                move[:, LANES : 2 * LANES] = pre * part * mask
                for col in range(SIDE):
                    cot[row, col, :, lanes] = move[4 * col : 4 * col + 4, LANES : 2 * LANES].astype(BF16)
                bo[rows, :] = grad
                grad = grad * gate
                return grad, grad * hat("out_b", j, hidden)

            values += column_sums(SIDE, 2, finish)
            bo[(j + 1) * BLOCK - CHUNK : (j + 1) * BLOCK, :] = jnp.zeros((CHUNK, LANES), F32)
        begin(n, values)

    todo["A6s"], todo["A13s"] = (functools.partial(expand_b, n, pair) for n, pair in zip((6, 13), PAIRS))
    todo["A6e"], todo["A13e"] = (functools.partial(set_out_b, n, pair) for n, pair in zip((6, 13), PAIRS))

    @token("A7s")
    def _():
        cot_copy.wait()
        finish_b(7, PAIRS[0])

    @token("A14s")
    def _():
        finish_b(14, PAIRS[1])
        result_copy.start()

    @token("sent")
    def _():
        for one in gathers.values():
            one.sent()

    def keep_sums(n, at):
        rows = sums_of[n].rows
        sums[at : at + rows, :] = tot[0:rows, :]

    def low_out_b(n, at, pair):
        sums_of[n].end()
        keep_sums(n, at)
        for k, j in enumerate(pair):
            set_back("out_b", j, 2 * k, 2 * k + 1)

            def step(index, j=j):
                start = pl.multiple_of(index * CHUNK, CHUNK)
                rows = pl.ds(j * BLOCK + start, CHUNK)
                grad = back("out_b", j, bo[rows, :] * gate_at(start), d3[rows, :]) * mask_at(start)
                dout[pl.ds(start, CHUNK), pl.ds(j * LANES, LANES)] = grad.astype(BF16)

            loop(BLOCK // CHUNK, step)

    todo["A7e"] = functools.partial(low_out_b, 7, 0, PAIRS[0])
    todo["A14e"] = functools.partial(low_out_b, 14, 16, PAIRS[1])

    def through_out(weight):
        add_up(dz, 4, lambda k: dout[:, at_block(k, LANES)], lambda k: weight[:, at_block(k, LANES)], mm_nt)

    def slope_terms(grad_ref, ref, name, chan):
        def terms(start):
            rows = pl.ds(start, CHUNK)
            hidden = ref[rows, :]
            mask = mask_at(pl.multiple_of(start % BLOCK, CHUNK) if grad_ref.shape[0] > BLOCK else start)
            grad = grad_ref[rows, :] * mask * vec.get(state[chan]) * slope_of(normed(name, 0, hidden))
            grad_ref[rows, :] = grad
            return grad, grad * hat(name, 0, hidden)

        return terms

    def through_pair(pair):
        return [mm_nt(dout[:, at_block(j, LANES)], w_out_b[:, at_block(j, LANES)]) for j in pair]

    @token("D8")
    def _():
        first, second = through_pair(PAIRS[0])
        dz[...] = first + second

    @token("A8s")
    def _():
        first, second = through_pair(PAIRS[1])
        dz[...] += first + second
        tell("out_b")
        begin(8, column_sums(8, 2, slope_terms(dz, d2, "mid_b", "chan_b")))

    def grad_out(act_ref, j):
        g_out[:, at_block(j, LANES)] = mm_tn(act_ref[...], dout[:, at_block(j, LANES)]).astype(BF16)

    tokens("g.out_b", 2, 2, lambda k: grad_out(b2, 2 * (k % 2) + k // 2))

    @token("A8e")
    def _():
        sums_of[8].end()
        keep_sums(8, 32)
        set_back("mid_b", 0, 0, 1)

    def low_mid(name, ref, shifts):
        s = scales[name, 0]

        def step(lane):
            lanes = at_block(lane, 128)
            grad = (
                dz[:, lanes] * lane_row(s["by"], lane)
                - lane_row(s["back_add"], lane)
                - ref[:, lanes] * lane_row(s["back_mul"], lane)
            ) * mask_ref[...]
            dm[:, lanes] = grad.astype(BF16)
            for k, shift in enumerate(shifts):
                moved = pltpu.roll(grad, shift, 0) if shift else grad
                g_mid[k * BLOCK : (k + 1) * BLOCK, lanes] = moved.astype(BF16)

        loop(4, step)

    @token("A9s")
    def _():
        low_mid("mid_b", d2, [(32 * (u - 1) + 4 * (v - 1)) % BLOCK for u, v in TAPS])
        add_up(dz, 9, lambda t: g_mid[at_block(t, BLOCK), :], lambda t: w_mid_b[at_block(t, LANES), :], mm_nt)
        tell("mid_b")
        begin(9, column_sums(8, 2, slope_terms(dz, d1, "in_b", "chan_b")))

    def grad_mid(cols, t):
        g_mid[at_block(t, LANES), :] = mm_tn(cols[:, at_block(t, LANES)], dm[...]).astype(BF16)

    tokens("g.mid_b", 3, 3, lambda t: grad_mid(cols_b, t))

    @token("A9e")
    def _():
        sums_of[9].end()
        keep_sums(9, 40)
        set_back("in_b", 0, 0, 1)

    @token("A10s")
    def _():
        def low_first_b(index):
            start = pl.multiple_of(index * CHUNK, CHUNK)
            rows = pl.ds(start, CHUNK)
            df[rows, :] = (back("in_b", 0, dz[rows, :], d1[rows, :]) * mask_at(start)).astype(BF16)

        loop(BLOCK // CHUNK, low_first_b)

        for j in range(4):
            bo[at_block(j, BLOCK), :] += mm_nt(df[...], w_in_b[at_block(j, LANES), :])
        tell("in_b")
        values = []
        for j in range(4):

            def join_back(start, j=j):
                rows = pl.ds(j * BLOCK + start, CHUNK)
                left, right = c3[rows, :], cp[rows, :]
                pre = normed("out_a", j, left) + normed("proj_a", j, right)
                grad = bo[rows, :] * mask_at(start) * slope_of(pre)
                bo[rows, :] = grad
                return grad, grad * hat("out_a", j, left), grad * hat("proj_a", j, right)

            values += column_sums(8, 3, join_back)
        begin(10, values)

    def grad_in_b(j):
        g_in[at_block(j, LANES), :] = mm_tn(feed[:, at_block(j, LANES)], df[...]).astype(BF16)

    tokens("g.in_b", 2, 2, grad_in_b)

    @token("A10e")
    def _():
        sums_of[10].end()
        keep_sums(10, 48)
        for j in range(4):
            set_back("out_a", j, 3 * j, 3 * j + 1)
            set_back("proj_a", j, 3 * j, 3 * j + 2)

    @token("A11s")
    def _():
        for j in range(4):

            def low_both(index, j=j):
                start = pl.multiple_of(index * CHUNK, CHUNK)
                rows = pl.ds(j * BLOCK + start, CHUNK)
                near_rows, lanes = pl.ds(start, CHUNK), pl.ds(j * LANES, LANES)
                grad, mask = bo[rows, :], mask_at(start)
                dout[near_rows, lanes] = (back("out_a", j, grad, c3[rows, :]) * mask).astype(BF16)
                dproj[near_rows, lanes] = (back("proj_a", j, grad, cp[rows, :]) * mask).astype(BF16)

            loop(BLOCK // CHUNK, low_both)
        through_out(w_out_a)
        tell("out_a")
        begin(11, column_sums(8, 2, slope_terms(dz, c2, "mid_a", "chan_a")))

    tokens("g.out_a", 2, 2, lambda j: grad_out(a2, j))

    def grad_proj(n):
        i, j = n // 4, n % 4
        g_proj[at_block(i, LANES), at_block(j, LANES)] = mm_tn(
            x[0:BLOCK, at_block(i, LANES)], dproj[:, at_block(j, LANES)]
        ).astype(BF16)

    tokens("g.proj_a", 2, 4, grad_proj)

    def back_proj(n):
        out, rows = d3.at[pl.ds(n * BLOCK, BLOCK)], pl.ds(n * LANES, LANES)
        add_up(out, 4, lambda k: dproj[:, at_block(k, LANES)], lambda k: w_proj_a[rows, at_block(k, LANES)], mm_nt)

    @token("dproj.0")
    def _():
        back_proj(0)

    @token("dproj.1")
    def _():
        back_proj(1)
        tell("proj_a")

    @token("A11e")
    def _():
        sums_of[11].end()
        keep_sums(11, 96)
        set_back("mid_a", 0, 0, 1)

    @token("A12s")
    def _():
        low_mid("mid_a", c2, [(-(32 * r + 4 * s)) % BLOCK for r in range(2) for s in range(2)])
        for row_par in range(2):
            for col_par in range(2):
                grad = None
                for t, (u, v) in enumerate(TAPS):
                    if (u != 1) != bool(row_par) or (v != 1) != bool(col_par):
                        continue
                    moved = 2 * (1 if u == 0 else 0) + (1 if v == 0 else 0)
                    term = mm_nt(g_mid[moved * BLOCK : (moved + 1) * BLOCK, :], w_mid_a[t * LANES : (t + 1) * LANES, :])
                    grad = term if grad is None else grad + term
                bo[pl.ds((2 * row_par + col_par) * BLOCK, BLOCK), :] = grad
        tell("mid_a")
        begin(12, column_sums(32, 2, slope_terms(bo, c1, "in_a", "chan_a")))

    tokens("g.mid_a", 3, 3, lambda t: grad_mid(cols_a, t))

    @token("A12e")
    def _():
        sums_of[12].end()
        keep_sums(12, 104)
        set_back("in_a", 0, 0, 1)
        for p in range(4):

            def low_first_a(index, p=p):
                start = pl.multiple_of(index * CHUNK, CHUNK)
                rows = pl.ds(p * BLOCK + start, CHUNK)
                grad = back("in_a", 0, bo[rows, :], c1[rows, :]) * mask_at(start)
                cols_b[pl.ds(start, CHUNK), p * LANES : (p + 1) * LANES] = grad.astype(BF16)

            loop(BLOCK // CHUNK, low_first_a)

    def first_grad(p):
        return cols_b[:, p * LANES : (p + 1) * LANES]

    def grad_in_a(i):
        lanes = at_block(i, 256)
        total = mm_tn(x[0:BLOCK, lanes], first_grad(0))
        for p in range(1, 4):
            total = total + mm_tn(x[p * BLOCK : (p + 1) * BLOCK, lanes], first_grad(p))
        g_in[at_block(i, 256), :] = total.astype(BF16)

    tokens("g.in_a", 2, 2, grad_in_a)

    def image_grad(planes):
        for p in planes:
            for h in range(2):
                lanes = pl.ds(h * LANES, LANES)
                grad = mm_nt(first_grad(p), w_in_a[h * LANES : (h + 1) * LANES, :])
                dz[...] = grad + d3[h * BLOCK : (h + 1) * BLOCK, :] if p == 0 else grad

                def pixels(row, p=p, lanes=lanes):
                    move[:, 0:LANES] = dz[at_block(row, CHUNK), :]
                    for col in range(SIDE):
                        raw[2 * row + p // 2, 2 * col + p % 2, :, lanes] = move[4 * col : 4 * col + 4, 0:LANES].astype(BF16)

                loop(SIDE, pixels)

    @token("img.0")
    def _():
        image_grad((0, 1))

    @token("img.1")
    def _():
        image_grad((2, 3))
        grad_copy.start()
        tell("in_a")

    @token("own")
    def _():
        def own_row(at, out, k):
            if out.shape[1] >= 128:
                for lane in range(2):
                    line = sums[pl.ds(at + 2 * (place.f % 2) + lane, 1), :]
                    out[k : k + 1, lane * 128 : (lane + 1) * 128] = line
            else:
                odd = (place.f % 2).astype(F32)
                move[0:1, 0:128] = sums[pl.ds(at + place.f // 2, 1), :]
                line = move[0:8, 0:128]
                line = line + (pltpu.roll(line, 64, 1) - line) * odd
                out[k : k + 1, :] = line[0:1, 0 : out.shape[1]]

        for name, at in (("mid_b", 32), ("in_b", 40), ("mid_a", 96), ("in_a", 104)):
            own_row(at + 4, owned[name], 0)
            own_row(at, owned[name], 1)
        block = place.f // 2
        pair_at = 16 * (block % 2) + 8 * (block // 2)
        for name, at, gain in (("out_b", pair_at, 4), ("out_a", 48 + 12 * block, 4), ("proj_a", 48 + 12 * block, 8)):
            own_row(at + gain, owned[name], 0)
            own_row(at, owned[name], 1)
        for one in own_copies:
            one.start()

    steps = sorted(todo)
    if sorted(RUN) != list(range(len(steps))):
        raise ValueError(len(steps))
    for index in RUN:
        todo[steps[index]]()
    result_copy.wait()
    grad_copy.wait()
    for one in scatters.values():
        one.sent()
    for one in own_copies + out_copies:
        one.wait()


def finish_kernel(*refs):
    arrays_in, arrays_out, held, wide = refs[:16], refs[16:32], refs[32:48], refs[48:55]
    in_sem, out_sem = refs[55:]
    loads = [pltpu.make_async_copy(a, b, in_sem.at[i]) for i, (a, b) in enumerate(zip(arrays_in, held))]
    leaving = held[:9] + wide
    stores = [pltpu.make_async_copy(a, b, out_sem.at[i]) for i, (a, b) in enumerate(zip(leaving, arrays_out))]
    order = list(range(9, 16)) + list(range(9))
    for i in order:
        loads[i].start()
    for i in order:
        loads[i].wait()
        if i >= 9:
            narrow, target = held[i], wide[i - 9]
            rows, columns = narrow.shape
            chunk = chunk_of(rows, columns)

            def step(index, carry, narrow=narrow, target=target, chunk=chunk):
                at = pl.ds(pl.multiple_of(index * chunk, 16), chunk)
                target[at, :] = narrow[at, :].astype(F32)
                return carry

            lax.fori_loop(0, rows // chunk, step, 0)
        stores[i].start()
    for i in order:
        stores[i].wait()


def finish_call(plain, grads):
    anywhere = pl.BlockSpec(memory_space=pl.ANY)
    return pl.pallas_call(
        finish_kernel,
        out_shape=[jax.ShapeDtypeStruct(one.shape, one.dtype) for one in plain]
        + [jax.ShapeDtypeStruct(one.shape, F32) for one in grads],
        in_specs=[anywhere] * 16,
        out_specs=[anywhere] * 16,
        scratch_shapes=[pltpu.VMEM(one.shape, one.dtype) for one in (*plain, *grads)]
        + [pltpu.VMEM(one.shape, F32) for one in grads]
        + [pltpu.SemaphoreType.DMA((16,)), pltpu.SemaphoreType.DMA((16,))],
        compiler_params=pltpu.CompilerParams(vmem_limit_bytes=64 * 2**20),
        name="finish_step",
    )(*plain, *grads)


def body_fast(
    images,
    image_sides,
    widths,
    keep_gate,
    w_in_a,
    w_mid_a,
    w_out_a,
    w_proj_a,
    norm_in_a,
    norm_mid_a,
    norm_out_a,
    norm_proj_a,
    w_in_b,
    w_mid_b,
    w_out_b,
    norm_in_b,
    norm_mid_b,
    norm_out_b,
    cotangent,
):
    width_in, width_out = images.shape[3], cotangent.shape[3]
    turned = (1, 2, 0, 3)
    images, cotangent = images.transpose(turned), cotangent.transpose(turned)
    norms = (norm_in_a, norm_mid_a, norm_out_a, norm_proj_a, norm_in_b, norm_mid_b, norm_out_b)
    shards = (w_in_a, w_mid_a, w_out_a, w_proj_a, w_in_b, w_mid_b, w_out_b)
    vmem = pl.BlockSpec(memory_space=pltpu.VMEM)
    smem = pl.BlockSpec(memory_space=pltpu.SMEM)
    anywhere = pl.BlockSpec(memory_space=pl.ANY)
    wholes = [(8 * one.shape[0], one.shape[1]) for one in shards]
    pieces = max(sum(len(one) for one in ways.values()) for ways in (WAYS_IN, WAYS_OUT))
    outs = pl.pallas_call(
        step_kernel,
        out_shape=[jax.ShapeDtypeStruct(cotangent.shape, BF16), jax.ShapeDtypeStruct(images.shape, BF16)]
        + [jax.ShapeDtypeStruct(one.shape, F32) for one in norms]
        + [jax.ShapeDtypeStruct(one.shape, BF16) for one in shards],
        in_specs=[anywhere, anywhere, smem, smem, smem] + [vmem] * 7 + [anywhere] * 7,
        out_specs=[anywhere] * 16,
        scratch_shapes=[pltpu.VMEM(one.shape, F32) for one in norms]
        + [pltpu.VMEM(one.shape, BF16) for one in shards]
        + [pltpu.VMEM(shape, BF16) for shape in wholes]
        + [
            pltpu.VMEM(images.shape, BF16),
            pltpu.VMEM(cotangent.shape, BF16),
            pltpu.VMEM((4 * BLOCK, width_in), BF16),
            pltpu.VMEM((4 * BLOCK, LANES), F32),
            pltpu.VMEM((BLOCK, 9 * LANES), BF16),
            pltpu.VMEM((BLOCK, LANES), F32),
            pltpu.VMEM((BLOCK, LANES), BF16),
            pltpu.VMEM((4 * BLOCK, LANES), F32),
            pltpu.VMEM((4 * BLOCK, LANES), F32),
            pltpu.VMEM((4 * BLOCK, LANES), F32),
            pltpu.VMEM((BLOCK, width_out), BF16),
            pltpu.VMEM((BLOCK, LANES), F32),
            pltpu.VMEM((BLOCK, 9 * LANES), BF16),
            pltpu.VMEM((BLOCK, LANES), F32),
            pltpu.VMEM((BLOCK, LANES), BF16),
            pltpu.VMEM((4 * BLOCK, LANES), F32),
            pltpu.VMEM((BLOCK, LANES), F32),
            pltpu.VMEM((BLOCK, LANES), BF16),
            pltpu.VMEM((BLOCK, LANES), BF16),
            pltpu.VMEM((BLOCK, width_out), BF16),
            pltpu.VMEM((BLOCK, width_out), BF16),
            pltpu.VMEM(wholes[1], BF16),
            pltpu.VMEM(wholes[2], BF16),
            pltpu.VMEM(wholes[4], BF16),
            pltpu.VMEM(wholes[3], BF16),
            pltpu.VMEM((BLOCK, 128), F32),
            pltpu.VMEM((BLOCK, 128), F32),
            pltpu.VMEM((CHUNK, width_in), F32),
            pltpu.VMEM((8, 24, 128), F32),
            pltpu.VMEM((24, 128), F32),
            pltpu.VMEM((160, LANES), F32),
            pltpu.VMEM((SHORT_SETS, 18, 16, 128), F32),
            pltpu.VMEM((10, 64, 128), F32),
            pltpu.VMEM((64, 128), F32),
            pltpu.VMEM((112, 128), F32),
            pltpu.SemaphoreType.DMA((4,)),
            pltpu.SemaphoreType.DMA((pieces,)),
            pltpu.SemaphoreType.DMA((pieces, 6)),
            pltpu.SemaphoreType.DMA((SHORT_SETS + 1, 3)),
            pltpu.SemaphoreType.DMA((SHORT_SETS + 1, 3)),
            pltpu.SemaphoreType.DMA((2,)),
            pltpu.SemaphoreType.DMA((2, 7)),
            pltpu.SemaphoreType.REGULAR((7,)),
        ],
        compiler_params=pltpu.CompilerParams(
            collective_id=0, has_side_effects=True, vmem_limit_bytes=64 * 2**20
        ),
        name="whole_step",
    )(images, cotangent, image_sides, keep_gate, widths, *norms, *shards)
    back_turned = (2, 0, 1, 3)
    outs = finish_call(outs[:9], outs[9:])
    own, finals = outs[2:9], outs[9:]
    return (
        outs[0].transpose(back_turned),
        outs[1].transpose(back_turned),
        *finals[:4],
        *own[:4],
        *finals[4:],
        *own[4:],
    )


def fits(mesh):
    return mesh.shape[FSDP] == 8 and mesh.shape[DP] == 4


def gather_plain(shards):
    return [lax.all_gather(one, FSDP, axis=0, tiled=True) for one in shards]


def scatter_plain(grads):
    parts = [lax.psum_scatter(one, FSDP, scatter_dimension=0, tiled=True) for one in grads]
    return lax.psum(tuple(parts), DP)


def sum_pair(first, second):
    return lax.psum((first, second), (FSDP, DP))


def silu_slope(values):
    sigmoid_part = jax.nn.sigmoid(values)
    return sigmoid_part * (1.0 + values * (1.0 - sigmoid_part))


def pixel_masks(image_sides, side_in, side_out):
    half_sides = image_sides // 2
    rows_in = jnp.arange(side_in, dtype=jnp.int32)
    rows_out = jnp.arange(side_out, dtype=jnp.int32)
    inside_in = (rows_in[None, :, None] < image_sides[:, None, None]) & (
        rows_in[None, None, :] < image_sides[:, None, None]
    )
    inside_out = (rows_out[None, :, None] < half_sides[:, None, None]) & (
        rows_out[None, None, :] < half_sides[:, None, None]
    )
    local_counts = jnp.stack(
        [jnp.sum(image_sides * image_sides), jnp.sum(half_sides * half_sides)]
    ).astype(jnp.float32)
    return (
        inside_in.astype(jnp.float32)[..., None],
        inside_out.astype(jnp.float32)[..., None],
        local_counts,
    )


def norm_stats(hidden, pixel_mask, local_counts, count_slot):
    sum_values, sum_squares = sum_pair(
        jnp.sum(hidden * pixel_mask, axis=(0, 1, 2)),
        jnp.sum(hidden * hidden * pixel_mask, axis=(0, 1, 2)),
    )
    pixel_total = local_counts[count_slot]
    average = sum_values / pixel_total
    inv_std = lax.rsqrt(sum_squares / pixel_total - average * average + EPSILON)
    return (average, inv_std, pixel_total)


def normalize(hidden, stats_now, params, channel):
    average, inv_std, pixel_total = stats_now
    scaled = (hidden - average) * inv_std
    params_wide = params.astype(jnp.float32)
    return (scaled, (scaled * params_wide[0] + params_wide[1]) * channel)


def norm_backward(grad_norm, scaled, stats_now, params, pixel_mask):
    average, inv_std, pixel_total = stats_now
    shift_sum, gain_sum = sum_pair(
        jnp.sum(grad_norm, axis=(0, 1, 2)), jnp.sum(grad_norm * scaled, axis=(0, 1, 2))
    )
    gain_row = params[0].astype(jnp.float32)
    grad_hidden = (
        gain_row
        * inv_std
        * (grad_norm - shift_sum / pixel_total - scaled * gain_sum / pixel_total)
        * pixel_mask
    )
    return (grad_hidden.astype(jnp.bfloat16), gain_sum, shift_sum)


def taps_stride_two(activations):
    slot_count = activations.shape[0]
    half_side = activations.shape[1] // 2
    lane_count = activations.shape[3]
    padded = jnp.pad(activations, ((0, 0), (1, 1), (1, 1), (0, 0)))
    parity_grid = padded.reshape(slot_count, half_side + 1, 2, half_side + 1, 2, lane_count)
    pieces = [
        parity_grid[
            :,
            row_tap // 2 : row_tap // 2 + half_side,
            row_tap % 2,
            col_tap // 2 : col_tap // 2 + half_side,
            col_tap % 2,
            :,
        ]
        for row_tap in range(3)
        for col_tap in range(3)
    ]
    return jnp.concatenate(pieces, axis=-1)


def fold_stride_two(grad_cols, side_in):
    slot_count = grad_cols.shape[0]
    half_side = grad_cols.shape[1]
    lane_count = grad_cols.shape[3] // 9
    planes = [
        [
            jnp.zeros((slot_count, half_side + 1, half_side + 1, lane_count), jnp.float32)
            for col_par in range(2)
        ]
        for row_par in range(2)
    ]
    for row_tap in range(3):
        for col_tap in range(3):
            tap_index = row_tap * 3 + col_tap
            tap_piece = grad_cols[..., tap_index * lane_count : (tap_index + 1) * lane_count]
            placed = jnp.pad(
                tap_piece,
                (
                    (0, 0),
                    (row_tap // 2, 1 - row_tap // 2),
                    (col_tap // 2, 1 - col_tap // 2),
                    (0, 0),
                ),
            )
            planes[row_tap % 2][col_tap % 2] = planes[row_tap % 2][col_tap % 2] + placed
    parity_grid = jnp.stack([jnp.stack(planes[0], axis=3), jnp.stack(planes[1], axis=3)], axis=2)
    whole_grid = parity_grid.reshape(slot_count, side_in + 2, side_in + 2, lane_count)
    return whole_grid[:, 1:-1, 1:-1, :]


def taps_stride_one(activations):
    side_now = activations.shape[1]
    padded = jnp.pad(activations, ((0, 0), (1, 1), (1, 1), (0, 0)))
    pieces = [
        padded[:, row_tap : row_tap + side_now, col_tap : col_tap + side_now, :]
        for row_tap in range(3)
        for col_tap in range(3)
    ]
    return jnp.concatenate(pieces, axis=-1)


def fold_stride_one(grad_cols):
    lane_count = grad_cols.shape[3] // 9
    whole_grid = None
    for row_tap in range(3):
        for col_tap in range(3):
            tap_index = row_tap * 3 + col_tap
            tap_piece = grad_cols[..., tap_index * lane_count : (tap_index + 1) * lane_count]
            placed = jnp.pad(
                tap_piece, ((0, 0), (row_tap, 2 - row_tap), (col_tap, 2 - col_tap), (0, 0))
            )
            whole_grid = placed if whole_grid is None else whole_grid + placed
    return whole_grid[:, 1:-1, 1:-1, :]


def contract(left_side, right_side):
    return lax.dot_general(
        left_side,
        right_side,
        (((0, 1, 2), (0, 1, 2)), ((), ())),
        preferred_element_type=jnp.float32,
    )


def back_project(gradient, weight):
    return lax.dot_general(
        gradient, weight, (((3,), (1,)), ((), ())), preferred_element_type=jnp.float32
    )


def own_shard(pair_sums):
    gain_sum, shift_sum = pair_sums
    shard_width = gain_sum.shape[0] // lax.axis_size(FSDP)
    offset = lax.axis_index(FSDP) * shard_width
    return jnp.stack(
        [
            lax.dynamic_slice_in_dim(gain_sum, offset, shard_width, 0),
            lax.dynamic_slice_in_dim(shift_sum, offset, shard_width, 0),
        ]
    )


def block_a_forward(inputs, weights, mask_in, mask_out, local_counts, channel, saved_stats):
    w_in, w_mid, w_out, w_proj, norm_in, norm_mid, norm_out, norm_proj = weights
    conv_first = jnp.dot(inputs, w_in, preferred_element_type=jnp.float32)
    stats_first = (
        norm_stats(conv_first, mask_in, local_counts, 0) if saved_stats is None else saved_stats[0]
    )
    scaled_first, normed_first = normalize(conv_first, stats_first, norm_in, channel)
    act_first = (jax.nn.silu(normed_first) * mask_in).astype(jnp.bfloat16)
    cols_mid = taps_stride_two(act_first)
    conv_mid = jnp.dot(cols_mid, w_mid, preferred_element_type=jnp.float32)
    stats_mid = (
        norm_stats(conv_mid, mask_out, local_counts, 1) if saved_stats is None else saved_stats[1]
    )
    scaled_mid, normed_mid = normalize(conv_mid, stats_mid, norm_mid, channel)
    act_mid = (jax.nn.silu(normed_mid) * mask_out).astype(jnp.bfloat16)
    conv_out = jnp.dot(act_mid, w_out, preferred_element_type=jnp.float32)
    slot_count, side_in, lane_count = (inputs.shape[0], inputs.shape[1], inputs.shape[3])
    sampled = inputs.reshape(slot_count, side_in // 2, 2, side_in // 2, 2, lane_count)[
        :, :, 0, :, 0, :
    ]
    conv_proj = jnp.dot(sampled, w_proj, preferred_element_type=jnp.float32)
    conv_both = jnp.concatenate([conv_out, conv_proj], axis=-1)
    norm_both = jnp.concatenate([norm_out, norm_proj], axis=-1)
    stats_both = (
        norm_stats(conv_both, mask_out, local_counts, 1) if saved_stats is None else saved_stats[2]
    )
    scaled_both, normed_both = normalize(conv_both, stats_both, norm_both, 1.0)
    width_out = conv_out.shape[-1]
    pre_sum = normed_both[..., :width_out] + normed_both[..., width_out:]
    block_out = jax.nn.silu(pre_sum) * mask_out
    saved_values = (
        scaled_first,
        normed_first,
        act_first,
        cols_mid,
        scaled_mid,
        normed_mid,
        act_mid,
        sampled,
        scaled_both,
        pre_sum,
    )
    return (block_out, (stats_first, stats_mid, stats_both), saved_values)


def block_a_backward(
    grad_out, inputs, weights, stats_all, saved_values, mask_in, mask_out, channel
):
    w_in, w_mid, w_out, w_proj, norm_in, norm_mid, norm_out, norm_proj = weights
    stats_first, stats_mid, stats_both = stats_all
    (
        scaled_first,
        normed_first,
        act_first,
        cols_mid,
        scaled_mid,
        normed_mid,
        act_mid,
        sampled,
        scaled_both,
        pre_sum,
    ) = saved_values
    grad_pre = grad_out * mask_out * silu_slope(pre_sum)
    grad_both = jnp.concatenate([grad_pre, grad_pre], axis=-1)
    norm_both = jnp.concatenate([norm_out, norm_proj], axis=-1)
    low_both, gain_both, shift_both = norm_backward(
        grad_both, scaled_both, stats_both, norm_both, mask_out
    )
    width_out = grad_pre.shape[-1]
    low_out = low_both[..., :width_out]
    low_proj = low_both[..., width_out:]
    grad_w_out = contract(act_mid, low_out)
    grad_w_proj = contract(sampled, low_proj)
    grad_norm_mid = back_project(low_out, w_out) * mask_out * channel * silu_slope(normed_mid)
    low_mid, gain_mid, shift_mid = norm_backward(
        grad_norm_mid, scaled_mid, stats_mid, norm_mid, mask_out
    )
    grad_w_mid = contract(cols_mid, low_mid)
    grad_act_first = fold_stride_two(back_project(low_mid, w_mid), inputs.shape[1])
    grad_norm_first = grad_act_first * mask_in * channel * silu_slope(normed_first)
    low_first, gain_first, shift_first = norm_backward(
        grad_norm_first, scaled_first, stats_first, norm_in, mask_in
    )
    grad_w_in = contract(inputs, low_first)
    spread = lax.pad(
        back_project(low_proj, w_proj),
        jnp.float32(0.0),
        ((0, 0, 0), (0, 1, 1), (0, 1, 1), (0, 0, 0)),
    )
    grad_inputs = (back_project(low_first, w_in) + spread) * mask_in
    norm_grads = (
        (gain_first, shift_first),
        (gain_mid, shift_mid),
        (gain_both[:width_out], shift_both[:width_out]),
        (gain_both[width_out:], shift_both[width_out:]),
    )
    return (grad_inputs, (grad_w_in, grad_w_mid, grad_w_out, grad_w_proj), norm_grads)


def block_b_forward(block_in, weights, mask_out, local_counts, channel, depth_gate, saved_stats):
    w_in, w_mid, w_out, norm_in, norm_mid, norm_out = weights
    feed_in = block_in.astype(jnp.bfloat16)
    conv_first = jnp.dot(feed_in, w_in, preferred_element_type=jnp.float32)
    stats_first = (
        norm_stats(conv_first, mask_out, local_counts, 1) if saved_stats is None else saved_stats[0]
    )
    scaled_first, normed_first = normalize(conv_first, stats_first, norm_in, channel)
    act_first = (jax.nn.silu(normed_first) * mask_out).astype(jnp.bfloat16)
    cols_mid = taps_stride_one(act_first)
    conv_mid = jnp.dot(cols_mid, w_mid, preferred_element_type=jnp.float32)
    stats_mid = (
        norm_stats(conv_mid, mask_out, local_counts, 1) if saved_stats is None else saved_stats[1]
    )
    scaled_mid, normed_mid = normalize(conv_mid, stats_mid, norm_mid, channel)
    act_mid = (jax.nn.silu(normed_mid) * mask_out).astype(jnp.bfloat16)
    conv_out = jnp.dot(act_mid, w_out, preferred_element_type=jnp.float32)
    stats_out = (
        norm_stats(conv_out, mask_out, local_counts, 1) if saved_stats is None else saved_stats[2]
    )
    scaled_out, normed_out = normalize(conv_out, stats_out, norm_out, 1.0)
    pre_sum = block_in + depth_gate * normed_out
    result = jax.nn.silu(pre_sum) * mask_out
    saved_values = (
        feed_in,
        scaled_first,
        normed_first,
        act_first,
        cols_mid,
        scaled_mid,
        normed_mid,
        act_mid,
        scaled_out,
        pre_sum,
    )
    return (result, (stats_first, stats_mid, stats_out), saved_values)


def block_b_backward(grad_out, weights, stats_all, saved_values, mask_out, channel, depth_gate):
    w_in, w_mid, w_out, norm_in, norm_mid, norm_out = weights
    stats_first, stats_mid, stats_out = stats_all
    (
        feed_in,
        scaled_first,
        normed_first,
        act_first,
        cols_mid,
        scaled_mid,
        normed_mid,
        act_mid,
        scaled_out,
        pre_sum,
    ) = saved_values
    grad_pre = grad_out * mask_out * silu_slope(pre_sum)
    low_out, gain_out, shift_out = norm_backward(
        grad_pre * depth_gate, scaled_out, stats_out, norm_out, mask_out
    )
    grad_w_out = contract(act_mid, low_out)
    grad_norm_mid = back_project(low_out, w_out) * mask_out * channel * silu_slope(normed_mid)
    low_mid, gain_mid, shift_mid = norm_backward(
        grad_norm_mid, scaled_mid, stats_mid, norm_mid, mask_out
    )
    grad_w_mid = contract(cols_mid, low_mid)
    grad_norm_first = (
        fold_stride_one(back_project(low_mid, w_mid))
        * mask_out
        * channel
        * silu_slope(normed_first)
    )
    low_first, gain_first, shift_first = norm_backward(
        grad_norm_first, scaled_first, stats_first, norm_in, mask_out
    )
    grad_w_in = contract(feed_in, low_first)
    grad_in = grad_pre + back_project(low_first, w_in)
    norm_grads = ((gain_first, shift_first), (gain_mid, shift_mid), (gain_out, shift_out))
    return (grad_in, (grad_w_in, grad_w_mid, grad_w_out), norm_grads)


def body(
    images,
    image_sides,
    widths,
    keep_gate,
    w_in_a,
    w_mid_a,
    w_out_a,
    w_proj_a,
    norm_in_a,
    norm_mid_a,
    norm_out_a,
    norm_proj_a,
    w_in_b,
    w_mid_b,
    w_out_b,
    norm_in_b,
    norm_mid_b,
    norm_out_b,
    cotangent,
):
    mask_in, mask_out, local_counts = pixel_masks(image_sides, images.shape[1], cotangent.shape[1])
    lane_ids = jnp.arange(w_mid_a.shape[1], dtype=jnp.int32)
    channel_a = (lane_ids < widths[0]).astype(jnp.float32)
    channel_b = (lane_ids < widths[1]).astype(jnp.float32)
    depth_gate = keep_gate.astype(jnp.float32)[:, None, None, None]
    inputs = images * mask_in.astype(jnp.bfloat16)
    total_counts = lax.psum(local_counts, (FSDP, DP))
    gathered = gather_plain((w_in_a, w_mid_a, w_out_a, w_proj_a, w_in_b, w_mid_b, w_out_b))
    norms = lax.all_gather(
        jnp.concatenate(
            [norm_in_a, norm_mid_a, norm_out_a, norm_proj_a, norm_in_b, norm_mid_b, norm_out_b], axis=1
        ),
        FSDP,
        axis=0,
    )
    wide = []
    place = 0
    for one in (norm_in_a, norm_mid_a, norm_out_a, norm_proj_a, norm_in_b, norm_mid_b, norm_out_b):
        width = one.shape[1]
        wide.append(norms[:, :, place : place + width].transpose(1, 0, 2).reshape(2, -1))
        place += width
    weights_a = tuple(gathered[:4]) + tuple(wide[:4])
    weights_b = tuple(gathered[4:]) + tuple(wide[4:])
    block_out, stats_a, redone_a = block_a_forward(
        inputs, weights_a, mask_in, mask_out, total_counts, channel_a, None
    )
    result, stats_b, redone_b = block_b_forward(
        block_out, weights_b, mask_out, total_counts, channel_b, depth_gate, None
    )
    grad_block, grads_b, norms_b = block_b_backward(
        cotangent.astype(jnp.float32), weights_b, stats_b, redone_b, mask_out, channel_b, depth_gate
    )
    grad_inputs, grads_a, norms_a = block_a_backward(
        grad_block, inputs, weights_a, stats_a, redone_a, mask_in, mask_out, channel_a
    )
    finals = scatter_plain(tuple(one.astype(jnp.bfloat16) for one in grads_a + grads_b))
    final_in_a, final_mid_a, final_out_a, final_proj_a, final_in_b, final_mid_b, final_out_b = (
        one.astype(jnp.float32) for one in finals
    )
    return (
        result.astype(jnp.bfloat16),
        grad_inputs.astype(jnp.bfloat16),
        final_in_a,
        final_mid_a,
        final_out_a,
        final_proj_a,
        own_shard(norms_a[0]),
        own_shard(norms_a[1]),
        own_shard(norms_a[2]),
        own_shard(norms_a[3]),
        final_in_b,
        final_mid_b,
        final_out_b,
        own_shard(norms_b[0]),
        own_shard(norms_b[1]),
        own_shard(norms_b[2]),
    )


def solution(mesh):
    in_specs = (
        P((FSDP, DP), None, None, None),
        P((FSDP, DP)),
        P(),
        P((FSDP, DP)),
        P(FSDP, None),
        P(FSDP, None),
        P(FSDP, None),
        P(FSDP, None),
        P(None, FSDP),
        P(None, FSDP),
        P(None, FSDP),
        P(None, FSDP),
        P(FSDP, None),
        P(FSDP, None),
        P(FSDP, None),
        P(None, FSDP),
        P(None, FSDP),
        P(None, FSDP),
        P((FSDP, DP), None, None, None),
    )
    out_specs = (
        P((FSDP, DP), None, None, None),
        P((FSDP, DP), None, None, None),
        P(FSDP, None),
        P(FSDP, None),
        P(FSDP, None),
        P(FSDP, None),
        P(None, FSDP),
        P(None, FSDP),
        P(None, FSDP),
        P(None, FSDP),
        P(FSDP, None),
        P(FSDP, None),
        P(FSDP, None),
        P(None, FSDP),
        P(None, FSDP),
        P(None, FSDP),
    )
    step = body_fast if fits(mesh) else body
    return jax.shard_map(step, mesh=mesh, in_specs=in_specs, out_specs=out_specs, check_vma=False)
```

```python
import functools

import jax
import jax.numpy as jnp
from jax import lax
from jax.experimental import pallas as pl
from jax.experimental.pallas import tpu as pltpu
from jax.sharding import PartitionSpec as P

EPSILON = 1e-05
BY_MESH = pl.DeviceIdType.MESH
FSDP, DP = "fsdp", "dp"
F32 = jnp.float32
BF16 = jnp.bfloat16
NAMES = ("in_a", "mid_a", "out_a", "proj_a", "in_b", "mid_b", "out_b")
BLOCK = 256
LANES = 512
CHUNK = 32
SIDE = 7
ZYX, ZXY, YZX = range(3)
SHORT_SETS = 8
TAPS = [(u, v) for u in range(3) for v in range(3)]
LINK_PEERS = ((1, 0), (2, 0), (4, 0), (6, 0), (0, 2), (0, 1))
CHIP_PEERS = tuple((a, b) for a in (7, 6, 5, 4, 3, 2, 1, 0) for b in (2, 0) if a or b)
WAYS_IN = {
    "in_a": ((0, 64, 0, ((YZX, 4), (ZXY, 4))), (64, 64, 0, ((YZX, 4), (ZXY, 4)))),
    "mid_a": ((0, 96, 0, ((YZX, 4), (ZXY, 4))), (96, 96, 0, ((YZX, 4), (ZXY, 4))), (192, 96, 0, ((ZYX, 4), (ZXY, 4))), (288, 96, 0, ((YZX, 4), (ZXY, 4))), (384, 96, 0, ((YZX, 4), (ZXY, 4))), (480, 96, 0, ((ZYX, 4), (ZXY, 4)))),
    "out_a": ((0, 32, 0, ((ZXY, 5), (YZX, 3))), (32, 32, 0, ((ZXY, 5), (YZX, 3)))),
    "proj_a": ((0, 64, 0, ((ZXY, 5), (YZX, 3))), (64, 64, 0, ((ZXY, 5), (YZX, 3)))),
    "in_b": ((0, 128, 0, ((YZX, 4), (ZXY, 4))), (128, 128, 0, ((YZX, 4), (ZXY, 4)))),
    "mid_b": ((0, 96, 0, ((YZX, 4), (ZXY, 4))), (96, 96, 0, ((YZX, 4), (ZXY, 4))), (192, 96, 0, ((ZYX, 4), (ZXY, 4))), (288, 96, 0, ((YZX, 4), (ZXY, 4))), (384, 96, 0, ((YZX, 4), (ZXY, 4))), (480, 96, 0, ((ZYX, 4), (ZXY, 4)))),
    "out_b": ((0, 64, 0, ((ZXY, 2), (YZX, 2))), (0, 64, 4, ((ZXY, 2), (YZX, 2)))),
}
WAYS_OUT = {
    "in_a": ((0, 64, 4), (64, 64, 4)),
    "mid_a": ((0, 96, 4), (96, 96, 4), (192, 96, 4), (288, 96, 4), (384, 96, 4), (480, 96, 4)),
    "out_a": ((0, 32, 5), (32, 32, 5)),
    "proj_a": ((0, 32, 5), (32, 32, 5), (64, 32, 5), (96, 32, 5)),
    "in_b": ((0, 128, 4), (128, 128, 4)),
    "mid_b": ((0, 96, 4), (96, 96, 4), (192, 96, 4), (288, 96, 4), (384, 96, 4), (480, 96, 4)),
    "out_b": ((0, 32, 5), (32, 32, 5)),
}
RUN = [
    365, 411, 412, 385, 415, 386, 416, 408, 390, 39, 165, 417, 391, 166, 389, 169, 418, 392, 38, 76, 99, 171,
    419, 393, 100, 170, 420, 77, 82, 103, 394, 172, 121, 105, 173, 431, 80, 104, 405, 122, 174, 84, 107, 81,
    127, 106, 185, 432, 406, 143, 144, 125, 108, 37, 149, 129, 427, 36, 126, 428, 83, 85, 355, 119, 43, 151,
    401, 186, 181, 96, 130, 148, 42, 402, 413, 182, 384, 97, 128, 147, 120, 92, 152, 41, 115, 387, 141, 414,
    421, 150, 116, 40, 357, 93, 167, 47, 46, 422, 423, 142, 424, 163, 175, 137, 138, 168, 395, 45, 425, 388,
    396, 101, 164, 178, 426, 177, 78, 159, 109, 44, 160, 176, 102, 400, 362, 409, 112, 359, 51, 179, 399, 87,
    79, 180, 50, 86, 110, 398, 90, 123, 91, 124, 397, 49, 113, 429, 114, 145, 131, 430, 89, 111, 403, 132, 88,
    146, 135, 48, 136, 356, 183, 55, 184, 153, 54, 134, 133, 94, 404, 117, 157, 53, 154, 158, 118, 156, 155,
    52, 95, 358, 59, 139, 58, 140, 161, 57, 162, 360, 56, 63, 361, 15, 62, 23, 14, 27, 22, 61, 26, 60, 13, 67,
    12, 19, 25, 21, 66, 65, 20, 31, 18, 24, 17, 35, 30, 34, 64, 16, 33, 98, 410, 29, 378, 28, 32, 71, 70, 69,
    379, 205, 206, 229, 230, 68, 75, 373, 374, 74, 253, 375, 197, 198, 199, 221, 200, 201, 254, 223, 202, 277,
    225, 73, 72, 245, 3, 278, 2, 247, 301, 368, 226, 222, 224, 369, 189, 269, 1, 271, 250, 249, 190, 213, 0,
    246, 214, 7, 376, 248, 363, 6, 377, 203, 364, 273, 237, 274, 227, 204, 228, 380, 238, 381, 5, 272, 207,
    298, 261, 208, 209, 210, 231, 4, 251, 325, 11, 262, 370, 270, 233, 371, 252, 10, 372, 295, 322, 286, 255,
    234, 191, 346, 192, 275, 257, 216, 276, 9, 193, 8, 285, 310, 194, 232, 258, 366, 297, 294, 367, 195, 279,
    240, 319, 281, 382, 296, 219, 217, 256, 282, 196, 218, 383, 220, 334, 187, 188, 243, 320, 349, 241, 212,
    302, 280, 264, 306, 244, 215, 265, 299, 242, 305, 236, 304, 211, 268, 323, 239, 309, 300, 330, 266, 289,
    318, 326, 288, 293, 292, 235, 303, 263, 342, 260, 328, 312, 347, 407, 290, 329, 316, 333, 313, 324, 317,
    267, 340, 259, 327, 336, 287, 343, 344, 314, 284, 337, 354, 291, 321, 283, 352, 315, 308, 351, 341, 353,
    311, 307, 350, 345, 339, 348, 335, 338, 332, 331,
]


def flip(index, bits):
    out = index
    for bit in (1, 2, 4):
        if bits & bit:
            out = out + bit - 2 * bit * ((index // bit) % 2)
    return out


class Place:
    def __init__(self):
        self.f = lax.axis_index(FSDP)
        self.d = lax.axis_index(DP)
        self.y = self.f % 2
        self.z = self.f // 2
        self.c = self.d % 2
        self.x = self.d // 2
        self.inner = self.z * (3 - self.z) > 0

    def peer(self, f_bits, d_bits):
        return (flip(self.f, f_bits), flip(self.d, d_bits))


def enter(place, peers):
    barrier = pltpu.get_barrier_semaphore()
    for f_bits, d_bits in peers:
        pl.semaphore_signal(barrier, inc=1, device_id=place.peer(f_bits, d_bits), device_id_type=BY_MESH)
    pl.semaphore_wait(barrier, len(peers))


def push(source, target, send_sem, recv_sem, device):
    pltpu.make_async_remote_copy(
        src_ref=source,
        dst_ref=target,
        send_sem=send_sem,
        recv_sem=recv_sem,
        device_id=device,
        device_id_type=BY_MESH,
    ).start()


def await_bytes(view, sem):
    pltpu.make_async_copy(view, view, sem).wait()


def await_count(ref, count, sem):
    if not count:
        return
    rows_most, columns_most = ref.shape
    for columns in range(columns_most, 0, -128):
        rows = count // columns
        if count % columns == 0 and rows % 16 == 0 and rows <= rows_most:
            await_bytes(ref.at[pl.ds(0, rows), pl.ds(0, columns)], sem)
            return
    raise ValueError(count)


def rows_of(start, size):
    return pl.ds(pl.multiple_of(start, 16), size)


def cols_of(start, size):
    return pl.ds(pl.multiple_of(start, 128), size)


class Gather:
    def __init__(self, place, shard, whole, start, rows, from_eighth, groups, send, recv):
        self.place, self.shard, self.whole = place, shard, whole
        self.start, self.rows, self.send, self.recv = start, rows, send, recv
        self.total, columns = shard.shape
        half = columns // 2
        self.part = part = rows // 2
        self.col_0 = place.c * half + half * from_eighth // 8
        self.row_q = start + place.x * part
        self.row_o = start + part - place.x * part
        self.arriving, self.leaving = [0] * 6, 0
        self.groups, at = {}, 0
        for way, eighths in groups:
            self.groups[way] = (at, half * eighths // 8)
            at += half * eighths // 8
        self.wide = at

    def view(self, bits, row, rows, from_col, columns):
        block = flip(self.place.f, bits) * self.total
        return self.whole.at[rows_of(block + row, rows), cols_of(self.col_0 + from_col, columns)]

    def pass_on(self, bits, row, rows, group, leg, peer):
        from_col, columns = group
        view = self.view(bits, row, rows, from_col, columns)
        push(view, view, self.send, self.recv.at[leg or 0], self.place.peer(*peer))
        if leg is not None:
            self.arriving[leg] += rows * columns
            self.leaving += rows * columns

    def pass_own(self, row, rows, group, leg, peer):
        from_col, columns = group
        source = self.shard.at[rows_of(row, rows), cols_of(self.col_0 + from_col, columns)]
        push(source, self.view(0, row, rows, from_col, columns), self.send, self.recv.at[leg], self.place.peer(*peer))
        self.arriving[leg] += rows * columns
        self.leaving += rows * columns

    def arrive(self, leg):
        await_count(self.whole, self.arriving[leg], self.recv.at[leg])

    def first(self):
        pltpu.make_async_copy(
            self.shard.at[pl.ds(self.start, self.rows), cols_of(self.col_0, self.wide)],
            self.view(0, self.start, self.rows, 0, self.wide),
            self.recv.at[0],
        ).start()
        self.arriving[0] += self.rows * self.wide
        everything = (0, self.wide)

        @pl.when(self.place.inner)
        def _():
            self.pass_own(self.row_q, self.part, everything, 0, (6, 0))

        self.pass_own(self.row_q, self.part, everything, 4, (4, 0))
        self.pass_own(self.row_q, self.part, everything, 0, (2, 0))

    def relay(self):
        self.arrive(4)

        @pl.when(self.place.inner)
        def _():
            self.pass_on(4, self.row_q, self.part, (0, self.wide), None, (2, 0))

    def own(self):
        for way, group in self.groups.items():
            if way == ZXY:
                self.pass_own(self.start, self.rows, group, 5, (1, 0))
            else:
                self.pass_own(self.row_q, self.part, group, 5, (1, 0))

    def beside(self):
        self.arrive(5)
        if YZX in self.groups:
            for bits in (6, 4, 2):
                self.pass_on(1, self.row_q, self.part, self.groups[YZX], 1, (bits, 0))
            self.pass_on(1, self.row_q, self.part, self.groups[YZX], 1, (0, 2))

    def one(self):
        self.arrive(0)
        for way, group in self.groups.items():
            for bits in (2, 4, 6):
                if way != YZX:
                    self.pass_on(bits, self.row_q, self.part, group, 1, (1, 0))
                self.pass_on(bits, self.row_q, self.part, group, 1, (0, 2))

    def two(self):
        self.arrive(1)
        for way, group in self.groups.items():
            if way == ZXY:
                for bits in (2, 4, 6):
                    self.pass_on(bits, self.row_o, self.part, group, 2, (1, 0))
            else:
                for bits in (1, 3, 5, 7) if way == ZYX else (3, 5, 7):
                    self.pass_on(bits, self.row_q, self.part, group, 2, (0, 2))

    def three(self):
        self.arrive(2)
        for bits in range(8):
            self.pass_on(bits, self.start, self.rows, (0, self.wide), 3, (0, 1))

    def four(self):
        self.arrive(3)

    def sent(self):
        block = self.part * self.wide

        @pl.when(self.place.inner)
        def _():
            await_count(self.whole, self.leaving + block, self.send)

        @pl.when(jnp.logical_not(self.place.inner))
        def _():
            await_count(self.whole, self.leaving - block, self.send)


def chunk_of(rows, columns):
    best = 16
    for chunk in range(16, rows + 1, 16):
        if rows % chunk == 0 and chunk * columns <= 16384:
            best = chunk
    return best


def add_blocks(blocks, rows, columns, target, source):
    chunk = chunk_of(rows, columns)
    each = rows // chunk

    def step(index, carry):
        block, start = index // each, pl.multiple_of((index % each) * chunk, 16)
        into, more = target(block, start, chunk), source(block, start, chunk)
        into[...] = into[...] + more[...]
        return carry

    lax.fori_loop(0, blocks * each, step, 0)


class Scatter:
    def __init__(self, place, grad, room, out, start, rows, wide_a, send, recv):
        self.place, self.grad, self.out = place, grad, out
        self.start, self.rows, self.wide_a = start, rows, wide_a
        self.send, self.recv = send, recv
        total, columns = room.shape
        self.total = total = total // 8
        self.half = half = columns // 2
        self.wide_b = wide_b = half - wide_a
        self.part = part = rows // 2
        self.room = room
        self.from_core = room.at[:, pl.ds(0, half)]

        def landing(row, count, col, width):
            return room.at[pl.ds(row, count), pl.ds(half + col, width)] if width else None

        self.a_x = landing(4 * start, 4 * rows, 0, wide_a)
        self.a_y = landing(4 * total + 2 * start, 2 * rows, 0, wide_a)
        self.a_z = landing(6 * total + 3 * start // 2, 3 * part, 0, wide_a)
        self.b_y = landing(4 * start, 4 * rows, wide_a, wide_b)
        self.b_z = landing(4 * total + 3 * start, 3 * rows, wide_a, wide_b)
        self.b_x = landing(7 * total + start // 2, part, wide_a, wide_b)
        self.col_0 = place.c * half
        self.row_q = start + place.x * part
        self.row_o = start + part - place.x * part

    def push(self, source, target, leg, device):
        push(source, target, self.send, self.recv.at[leg], device)

    def zero(self):
        other = cols_of(self.half - self.col_0, self.half)
        for block in range(8):
            rows = pl.ds(block * self.total + self.start, self.rows)
            self.push(self.grad.at[rows, other], self.from_core.at[rows], 5, self.place.peer(0, 1))

    def core(self, row, rows, from_col, columns):
        return self.from_core.at[rows_of(row, rows), pl.ds(from_col, columns)]

    def mine(self, row, rows, from_col, columns):
        return self.core(self.place.f * self.total + row, rows, from_col, columns)

    def one(self):
        place, total, part, rows = self.place, self.total, self.part, self.rows
        await_count(self.room, 8 * rows * self.half, self.recv.at[5])
        add_blocks(
            8,
            rows,
            self.half,
            lambda b, s, n: self.core(b * total + self.start + s, n, 0, self.half),
            lambda b, s, n: self.grad.at[rows_of(b * total + self.start + s, n), cols_of(self.col_0, self.half)],
        )
        await_count(self.room, 8 * rows * self.half, self.send)
        if self.wide_a:
            for block in range(8):
                self.push(
                    self.core(block * total + self.row_o, part, 0, self.wide_a),
                    self.a_x.at[pl.ds(block * part, part)],
                    0,
                    place.peer(0, 2),
                )
        if self.wide_b:
            for level in range(4):
                self.push(
                    self.core((2 * level + 1 - place.y) * total + self.start, rows, self.wide_a, self.wide_b),
                    self.b_y.at[pl.ds(level * rows, rows)],
                    0,
                    place.peer(1, 0),
                )

    def two(self):
        place, total, part, rows = self.place, self.total, self.part, self.rows
        await_count(self.room, 4 * rows * self.half, self.recv.at[0])
        if self.wide_a:
            add_blocks(
                8,
                part,
                self.wide_a,
                lambda b, s, n: self.core(b * total + self.row_q + s, n, 0, self.wide_a),
                lambda b, s, n: self.a_x.at[rows_of(b * part + s, n)],
            )
            for level in range(4):
                self.push(
                    self.core((2 * level + 1 - place.y) * total + self.row_q, part, 0, self.wide_a),
                    self.a_y.at[pl.ds(level * part, part)],
                    1,
                    place.peer(1, 0),
                )
        if self.wide_b:
            add_blocks(
                4,
                rows,
                self.wide_b,
                lambda b, s, n: self.core((2 * b + place.y) * total + self.start + s, n, self.wide_a, self.wide_b),
                lambda b, s, n: self.b_y.at[rows_of(b * rows + s, n)],
            )
            for slot, bits in enumerate((6, 4, 2)):
                self.push(
                    self.core(flip(place.f, bits) * total + self.start, rows, self.wide_a, self.wide_b),
                    self.b_z.at[pl.ds(slot * rows, rows)],
                    1,
                    place.peer(bits, 0),
                )

    def sum_four(self, row, rows, col, wide, landed, store):
        chunk = chunk_of(rows, wide)

        def step(index, carry):
            start = pl.multiple_of(index * chunk, 16)
            total = self.mine(row + start, chunk, col, wide)[...].astype(F32)
            for slot in range(3):
                total = total + landed[rows_of(slot * rows + start, chunk)].astype(F32)
            store(start, chunk, total.astype(BF16))
            return carry

        lax.fori_loop(0, rows // chunk, step, 0)

    def three(self):
        place, total, part, rows = self.place, self.total, self.part, self.rows
        await_count(self.room, 2 * rows * self.wide_a + 3 * rows * self.wide_b, self.recv.at[1])
        if self.wide_a:
            add_blocks(
                4,
                part,
                self.wide_a,
                lambda b, s, n: self.core((2 * b + place.y) * total + self.row_q + s, n, 0, self.wide_a),
                lambda b, s, n: self.a_y.at[rows_of(b * part + s, n)],
            )
            for slot, bits in enumerate((6, 4, 2)):
                self.push(
                    self.core(flip(place.f, bits) * total + self.row_q, part, 0, self.wide_a),
                    self.a_z.at[pl.ds(slot * part, part)],
                    2,
                    place.peer(bits, 0),
                )
        if self.wide_b:

            def keep(start, chunk, value):
                self.mine(self.start + start, chunk, self.wide_a, self.wide_b)[...] = value

            self.sum_four(self.start, rows, self.wide_a, self.wide_b, self.b_z, keep)
            self.push(self.mine(self.row_o, part, self.wide_a, self.wide_b), self.b_x, 2, place.peer(0, 2))

    def four(self):
        place, part = self.place, self.part
        await_count(self.room, 3 * part * self.wide_a + part * self.wide_b, self.recv.at[2])
        if self.wide_a:

            def keep(start, chunk, value):
                self.out[rows_of(self.row_q + start, chunk), cols_of(self.col_0, self.wide_a)] = value

            self.sum_four(self.row_q, part, 0, self.wide_a, self.a_z, keep)
        if self.wide_b:
            chunk = chunk_of(part, self.wide_b)

            def step(index, carry):
                start = pl.multiple_of(index * chunk, 16)
                total = self.mine(self.row_q + start, chunk, self.wide_a, self.wide_b)[...].astype(F32)
                total = total + self.b_x[rows_of(start, chunk)].astype(F32)
                columns = cols_of(self.col_0 + self.wide_a, self.wide_b)
                self.out[rows_of(self.row_q + start, chunk), columns] = total.astype(BF16)
                return carry

            lax.fori_loop(0, part // chunk, step, 0)
        block = self.out.at[rows_of(self.row_q, part), cols_of(self.col_0, self.half)]
        self.push(block, block, 3, place.peer(0, 2))

    def five(self):
        await_bytes(self.out.at[pl.ds(0, self.part), pl.ds(0, self.half)], self.recv.at[3])
        block = self.out.at[pl.ds(self.start, self.rows), cols_of(self.col_0, self.half)]
        self.push(block, block, 4, self.place.peer(0, 1))

    def six(self):
        await_bytes(self.out.at[pl.ds(0, self.rows), pl.ds(0, self.half)], self.recv.at[4])

    def sent(self):
        await_count(self.room, 18 * self.part * self.half, self.send)


def mm(left, right):
    return jnp.dot(left, right, preferred_element_type=F32)


def mm_nt(left, right):
    return lax.dot_general(left, right, (((1,), (1,)), ((), ())), preferred_element_type=F32)


def mm_tn(left, right):
    return lax.dot_general(left, right, (((0,), (0,)), ((), ())), preferred_element_type=F32)


def loop(count, step):
    def body_of(index, carry):
        step(index)
        return carry

    lax.fori_loop(0, count, body_of, 0)


def at_block(index, size):
    if isinstance(index, int):
        return pl.ds(index * size, size)
    return pl.ds(pl.multiple_of(index * size, size), size)


def slope_of(values):
    gate = jax.nn.sigmoid(values)
    return gate * (1.0 + values * (1.0 - gate))


def fold(values):
    total = values[0:8]
    for start in range(8, values.shape[0], 8):
        total = total + values[start : start + 8]
    return total


def column_sums(count, width, terms):
    def step(index, carry):
        start = pl.multiple_of(index * CHUNK, CHUNK)
        return tuple(total + fold(one) for total, one in zip(carry, terms(start)))

    zero = jnp.zeros((8, LANES), F32)
    totals = lax.fori_loop(0, count, step, (zero,) * width)
    return [jnp.sum(one, axis=0, keepdims=True) for one in totals]


class Vectors:
    def __init__(self, ref):
        self.ref, self.used = ref, 0

    def put(self, row):
        at = self.used
        self.used += 1
        self.ref[at : at + 1, :] = row
        return at

    def get(self, at):
        return self.ref[at : at + 1, :]


class Totals:
    def __init__(self, place, short, long, tot, send, recv):
        self.place, self.short, self.long, self.tot, self.send, self.recv = place, short, long, tot, send, recv
        self.began = 0

    def start(self, rows_of_values):
        whole = not isinstance(rows_of_values, list)
        one = Total(self, 8 if whole else 4 * len(rows_of_values))
        own = one.slot(self.place.c)
        if whole:
            own[...] = rows_of_values
        for n, row in enumerate([] if whole else rows_of_values):
            for k in range(4):
                own[4 * n + k : 4 * n + k + 1, :] = row[:, 128 * k : 128 * (k + 1)]
        one.spread(self.place.c, ((0, 1),), 0)
        return one

    def row(self, index):
        at = 4 * index
        return jnp.concatenate([self.tot[at + k : at + k + 1, :] for k in range(4)], axis=1)

    def wide(self, at):
        return jnp.concatenate([self.tot[at : at + 1, :]] * 4, axis=1)


class Total:
    def __init__(self, all_of_them, rows):
        self.all, self.place, self.rows = all_of_them, all_of_them.place, rows
        self.is_long = rows > 8
        self.set = SHORT_SETS
        if not self.is_long:
            self.set = all_of_them.began % SHORT_SETS
            all_of_them.began += 1

    def slots(self, at, count):
        if self.is_long:
            return self.all.long.at[pl.ds(at, count), pl.ds(0, self.rows)]
        return self.all.short.at[self.set, pl.ds(at, count), pl.ds(0, self.rows)]

    def slot(self, at):
        if self.is_long:
            return self.all.long.at[at, pl.ds(0, self.rows)]
        return self.all.short.at[self.set, at, pl.ds(0, self.rows)]

    def spread(self, at, peers, phase):
        own = self.slot(at)
        for bits in peers:
            push(own, own, self.all.send.at[self.set, phase], self.all.recv.at[self.set, phase], self.place.peer(*bits))

    def gather(self, at, count, peers, phase):
        await_bytes(self.slots(at, peers), self.all.recv.at[self.set, phase])
        total = self.slot(at)[...]
        for index in range(at + 1, at + count):
            total = total + self.slot(index)[...]
        return total

    def middle(self):
        place = self.place
        total = self.gather(0, 2, 1, 0)
        if self.is_long:
            self.slot(2 + 2 * place.y + place.x)[...] = total
            self.spread(2 + 2 * place.y + place.x, ((1, 2), (1, 0), (0, 2)), 1)
        else:
            self.slot(2 + 2 * place.f + place.x)[...] = total
            self.spread(2 + 2 * place.f + place.x, CHIP_PEERS, 1)

    def late(self):
        if self.is_long:
            self.slot(6 + self.place.z)[...] = self.gather(2, 4, 3, 1)
            self.spread(6 + self.place.z, ((6, 0), (4, 0), (2, 0)), 2)

    def end(self):
        if self.is_long:
            self.all.tot[0 : self.rows, :] = self.gather(6, 4, 3, 2)
        else:
            self.all.tot[0 : self.rows, :] = self.gather(2, 16, 15, 1)
        for phase, count in enumerate((1, 3, 3) if self.is_long else (1, 15)):
            await_bytes(self.slots(0, count), self.all.send.at[self.set, phase])


def step_kernel(
    img_hbm,
    cot_hbm,
    sides,
    keep,
    widths,
    norm_in_a,
    norm_mid_a,
    norm_out_a,
    norm_proj_a,
    norm_in_b,
    norm_mid_b,
    norm_out_b,
    sh_in_a,
    sh_mid_a,
    sh_out_a,
    sh_proj_a,
    sh_in_b,
    sh_mid_b,
    sh_out_b,
    result_hbm,
    images_hbm,
    own_hbm_in_a,
    own_hbm_mid_a,
    own_hbm_out_a,
    own_hbm_proj_a,
    own_hbm_in_b,
    own_hbm_mid_b,
    own_hbm_out_b,
    out_hbm_in_a,
    out_hbm_mid_a,
    out_hbm_out_a,
    out_hbm_proj_a,
    out_hbm_in_b,
    out_hbm_mid_b,
    out_hbm_out_b,
    own_in_a,
    own_mid_a,
    own_out_a,
    own_proj_a,
    own_in_b,
    own_mid_b,
    own_out_b,
    out_in_a,
    out_mid_a,
    out_out_a,
    out_proj_a,
    out_in_b,
    out_mid_b,
    out_out_b,
    w_in_a,
    w_mid_a,
    w_out_a,
    w_proj_a,
    w_in_b,
    w_mid_b,
    w_out_b,
    raw,
    cot,
    x,
    c1,
    cols_a,
    c2,
    a2,
    c3,
    cp,
    bo,
    feed,
    d1,
    cols_b,
    d2,
    b2,
    d3,
    dz,
    dm,
    df,
    dout,
    dproj,
    g_mid,
    g_out,
    g_in,
    g_proj,
    mask_ref,
    gate_ref,
    move,
    norms,
    block_ref,
    vec_ref,
    short,
    long,
    tot,
    sums,
    io_sem,
    link_send,
    link_recv,
    ar_send,
    ar_recv,
    nb_sem,
    out_sem,
    free_sem,
):
    place = Place()
    shards = dict(zip(NAMES, (sh_in_a, sh_mid_a, sh_out_a, sh_proj_a, sh_in_b, sh_mid_b, sh_out_b)))
    wholes = dict(zip(NAMES, (w_in_a, w_mid_a, w_out_a, w_proj_a, w_in_b, w_mid_b, w_out_b)))
    outs = dict(zip(NAMES, (out_in_a, out_mid_a, out_out_a, out_proj_a, out_in_b, out_mid_b, out_out_b)))
    owned = dict(zip(NAMES, (own_in_a, own_mid_a, own_out_a, own_proj_a, own_in_b, own_mid_b, own_out_b)))
    own_hbm = (own_hbm_in_a, own_hbm_mid_a, own_hbm_out_a, own_hbm_proj_a, own_hbm_in_b, own_hbm_mid_b, own_hbm_out_b)
    out_hbm = (out_hbm_in_a, out_hbm_mid_a, out_hbm_out_a, out_hbm_proj_a, out_hbm_in_b, out_hbm_mid_b, out_hbm_out_b)
    own_copies = [pltpu.make_async_copy(owned[n], own_hbm[i], out_sem.at[0, i]) for i, n in enumerate(NAMES)]
    out_copies = [pltpu.make_async_copy(outs[n], out_hbm[i], out_sem.at[1, i]) for i, n in enumerate(NAMES)]
    small = dict(zip(NAMES, (norm_in_a, norm_mid_a, norm_out_a, norm_proj_a, norm_in_b, norm_mid_b, norm_out_b)))
    grads = dict(mid_a=g_mid, mid_b=g_mid, out_a=g_out, out_b=g_out, in_b=g_in, proj_a=g_proj)
    grads["in_a"] = g_in.at[pl.ds(0, wholes["in_a"].shape[0])]
    todo = {}

    def token(name):
        def keep_it(function):
            todo[name] = function
            return function

        return keep_it

    def tokens(name, count, each, step):
        def some(first):
            for k in range(each):
                step(first + k)

        for part in range(count):
            todo[f"{name}.{part}"] = functools.partial(some, part * each)

    gathers, scatters, at, going = {}, {}, 0, 0
    left = {name: len(WAYS_OUT[name]) for name in NAMES}

    def finish_piece(name, piece):
        piece.six()
        left[name] -= 1
        if not left[name]:
            out_copies[NAMES.index(name)].start()

    def tell(name):
        for bits in LINK_PEERS:
            sem = free_sem.at[NAMES.index(name)]
            pl.semaphore_signal(sem, inc=1, device_id=place.peer(*bits), device_id_type=BY_MESH)

    def send_core(name, n):
        if n == 0:
            pl.semaphore_wait(free_sem.at[NAMES.index(name)], len(LINK_PEERS))
        scatters[name, n].zero()

    for name in NAMES:
        for n, (start, rows, from_eighth, ways) in enumerate(WAYS_IN[name]):
            sems = link_send.at[at], link_recv.at[at]
            g = gathers[name, n] = Gather(
                place, shards[name], wholes[name], start, rows, from_eighth, ways, *sems
            )
            at += 1
            key = f"{name}.{n}"
            todo["z." + key], todo["o." + key], todo["L1." + key] = g.first, g.own, g.one
            todo["R." + key], todo["B." + key] = g.relay, g.beside
            todo["L2." + key], todo["L3." + key] = g.two, g.three
        eighth = shards[name].shape[1] // 16
        for n, (start, rows, wide) in enumerate(WAYS_OUT[name]):
            sems = link_send.at[going], link_recv.at[going]
            s = Scatter(place, grads[name], wholes[name], outs[name], start, rows, wide * eighth, *sems)
            scatters[name, n] = s
            going += 1
            key = f"{name}.{n}"
            todo["S0." + key], todo["S1." + key] = functools.partial(send_core, name, n), s.one
            todo["S2." + key], todo["S3." + key], todo["S4." + key] = s.two, s.three, s.four
            todo["S5." + key] = s.five
            todo["S6." + key] = functools.partial(finish_piece, name, s)
        def arrived(some):
            for one in some:
                one.four()

        mine = [gathers[name, n] for n in range(len(WAYS_IN[name]))]
        if name == "out_b":
            for n, one in enumerate(mine):
                todo[f"W.{name}.{n}"] = one.four
        else:
            todo["W." + name] = functools.partial(arrived, mine)

    vec = Vectors(vec_ref)
    totals = Totals(place, short, long, tot, ar_send, ar_recv)
    state, scales, params = {}, {}, {}
    sums_of = {}

    def begin(n, values):
        sums_of[n] = totals.start(values)

    for n in range(1, 20):
        todo[f"A{n}m"] = lambda n=n: sums_of[n].middle()
        todo[f"A{n}l"] = lambda n=n: sums_of[n].late()

    image_copy = pltpu.make_async_copy(img_hbm, raw, io_sem.at[0])
    cot_copy = pltpu.make_async_copy(cot_hbm, cot, io_sem.at[1])
    result_copy = pltpu.make_async_copy(cot, result_hbm, io_sem.at[2])
    grad_copy = pltpu.make_async_copy(raw, images_hbm, io_sem.at[3])

    @token("enter")
    def _():
        image_copy.start()
        cot_copy.start()
        odd = (place.f % 2).astype(F32)
        block_ref[...] = jnp.zeros_like(block_ref)
        at = 0
        for name in NAMES:
            values = small[name][...].astype(F32)
            if values.shape[1] < 128:
                move[0:8, 0:128] = jnp.zeros((8, 128), F32)
                move[0:2, 0 : values.shape[1]] = values
                plain = move[0:8, 0:128]
                values = (plain + (pltpu.roll(plain, 64, 1) - plain) * odd)[0:2]
            for lane in range(0, values.shape[1], 128):
                block_ref[at : at + 1, :] = values[0:1, lane : lane + 128]
                block_ref[at + 10 : at + 11, :] = values[1:2, lane : lane + 128]
                at += 1
        norms[place.f] = block_ref[...]
        enter(place, ((0, 1),) + CHIP_PEERS)
        for bits in (7, 6, 5, 4, 3, 2, 1):
            push(block_ref, norms.at[place.f], nb_sem.at[0], nb_sem.at[1], place.peer(bits, 0))

    @token("prep")
    def _():
        pixel = lax.broadcasted_iota(jnp.int32, (BLOCK, 128), 0)
        slot = pixel % 4

        def by_slot(values):
            return jnp.where(slot == 0, values[0], jnp.where(slot == 1, values[1], jnp.where(slot == 2, values[2], values[3])))

        half = by_slot([sides[i] // 2 for i in range(4)])
        inside = ((pixel // 4) % 8 < half) & (pixel // 32 < half)
        mask_ref[...] = jnp.where(inside, 1.0, 0.0).astype(F32)
        gate_ref[...] = by_slot([keep[i] for i in range(4)]).astype(F32)
        move[...] = jnp.zeros_like(move)
        image_copy.wait()

        def plane_rows(row):
            mask = jnp.concatenate([mask_ref[at_block(row, CHUNK), :]] * (x.shape[1] // 128), axis=1)
            for row_par in range(2):
                for col_par in range(2):
                    for col in range(SIDE):
                        move[4 * col : 4 * col + 4, :] = raw[2 * row + row_par, 2 * col + col_par].astype(F32)
                    start = (2 * row_par + col_par) * BLOCK + row * CHUNK
                    x[pl.ds(pl.multiple_of(start, CHUNK), CHUNK), :] = (move[...] * mask).astype(BF16)

        loop(SIDE, plane_rows)
        for p in range(4):
            x[(p + 1) * BLOCK - CHUNK : (p + 1) * BLOCK, :] = jnp.zeros((CHUNK, x.shape[1]), BF16)

    @token("norms")
    def _():
        await_bytes(norms.at[pl.ds(0, 7)], nb_sem.at[1])
        await_bytes(norms.at[pl.ds(0, 7)], nb_sem.at[0])

        def narrow_row(at):
            pieces = [norms[2 * k, at : at + 1, :] + norms[2 * k + 1, at : at + 1, :] for k in range(4)]
            return vec.put(jnp.concatenate(pieces, axis=1))

        def wide_rows(at):
            return [
                vec.put(
                    jnp.concatenate(
                        [norms[2 * j + k // 2, at + k % 2 : at + k % 2 + 1, :] for k in range(4)], axis=1
                    )
                )
                for j in range(4)
            ]

        params["in_a"] = ([narrow_row(0)], [narrow_row(10)])
        params["mid_a"] = ([narrow_row(1)], [narrow_row(11)])
        params["out_a"] = (wide_rows(2), wide_rows(12))
        params["proj_a"] = (wide_rows(4), wide_rows(14))
        params["in_b"] = ([narrow_row(6)], [narrow_row(16)])
        params["mid_b"] = ([narrow_row(7)], [narrow_row(17)])
        params["out_b"] = (wide_rows(8), wide_rows(18))
        lanes = lax.broadcasted_iota(jnp.int32, (1, LANES), 1)
        state["chan_a"] = vec.put(jnp.where(lanes < widths[0], 1.0, 0.0).astype(F32))
        state["chan_b"] = vec.put(jnp.where(lanes < widths[1], 1.0, 0.0).astype(F32))

    def wide_of(ref, start, size=CHUNK):
        return jnp.concatenate([ref[pl.ds(start, size), :]] * 4, axis=1)

    def mask_at(start):
        return wide_of(mask_ref, start)

    def gate_at(start):
        return wide_of(gate_ref, start)

    def set_norm(name, block, first_row, inverse, chan):
        inverse = vec.get(state[inverse])
        average = totals.row(first_row) * inverse
        rstd = lax.rsqrt(totals.row(first_row + 1) * inverse - average * average + EPSILON)
        gain, shift = (vec.get(rows[block]) for rows in params[name])
        keep_lanes = 1.0 if chan is None else vec.get(state[chan])
        by = gain * rstd
        scales[name, block] = dict(
            rstd=vec.put(rstd),
            off=vec.put(-average * rstd),
            by=vec.put(by),
            mul=vec.put(by * keep_lanes),
            add=vec.put((shift - average * by) * keep_lanes),
        )

    def normed(name, block, values):
        s = scales[name, block]
        return values * vec.get(s["mul"]) + vec.get(s["add"])

    def hat(name, block, values):
        s = scales[name, block]
        return values * vec.get(s["rstd"]) + vec.get(s["off"])

    def set_back(name, block, shift_row, gain_row):
        s = scales[name, block]
        inverse = vec.get(state["inv_in" if name == "in_a" else "inv_out"])
        by = vec.get(s["by"])
        pull = by * totals.row(gain_row) * inverse
        s["back_add"] = vec.put(by * totals.row(shift_row) * inverse + pull * vec.get(s["off"]))
        s["back_mul"] = vec.put(pull * vec.get(s["rstd"]))

    def back(name, block, grad, values):
        s = scales[name, block]
        return grad * vec.get(s["by"]) - vec.get(s["back_add"]) - values * vec.get(s["back_mul"])

    def square_terms(ref):
        def terms(start):
            values = ref[pl.ds(start, CHUNK), :]
            return values, values * values

        return terms

    def masked_terms(ref):
        def terms(start):
            values = ref[pl.ds(start, CHUNK), :]
            kept = values * mask_at(start)
            return kept, kept * values

        return terms

    def lane_row(at, lane):
        return vec_ref[at : at + 1, at_block(lane, 128)]

    def add_up(out, count, left, right, product=mm):
        total = product(left(0), right(0))
        for k in range(1, count):
            total = total + product(left(k), right(k))
        out[...] = total

    @token("A1s")
    def _():
        for p in range(4):
            c1[at_block(p, BLOCK), :] = mm(x[at_block(p, BLOCK), :], w_in_a[...])
        begin(1, column_sums(32, 2, square_terms(c1)))

    @token("A19s")
    def _():
        side = [sides[i] for i in range(4)]
        count_in = sum(s * s for s in side).astype(F32)
        count_out = sum((s // 2) * (s // 2) for s in side).astype(F32)
        at = lax.broadcasted_iota(jnp.int32, (8, 128), 0)
        begin(19, jnp.where(at == 0, count_in, jnp.where(at == 1, count_out, 0.0)))

    @token("A19e")
    def _():
        sums_of[19].end()
        state["inv_in"] = vec.put(1.0 / totals.wide(0))
        state["inv_out"] = vec.put(1.0 / totals.wide(1))

    @token("A1e")
    def _():
        sums_of[1].end()
        set_norm("in_a", 0, 0, "inv_in", "chan_a")
        s = scales["in_a", 0]

        def act_a(lane):
            for row_par in range(2):
                for col_par in range(2):
                    p = 2 * row_par + col_par
                    values = c1[p * BLOCK : (p + 1) * BLOCK, at_block(lane, 128)]
                    scaled = values * lane_row(s["mul"], lane) + lane_row(s["add"], lane)
                    act = scaled * jax.nn.sigmoid(scaled) * mask_ref[...]
                    for t, (u, v) in enumerate(TAPS):
                        if (u != 1) != bool(row_par) or (v != 1) != bool(col_par):
                            continue
                        shift = (32 if u == 0 else 0) + (4 if v == 0 else 0)
                        moved = pltpu.roll(act, shift, 0) if shift else act
                        cols_a[:, pl.ds(pl.multiple_of(t * LANES + lane * 128, 128), 128)] = moved.astype(BF16)

        loop(4, act_a)

    def conv_mid(out, cols, weight):
        add_up(out, 3, lambda k: cols[:, at_block(k, 1536)], lambda k: weight[at_block(k, 1536), :])

    def act_mid(act_ref, ref, name):
        def step(index):
            start = pl.multiple_of(index * CHUNK, CHUNK)
            scaled = normed(name, 0, ref[pl.ds(start, CHUNK), :])
            act_ref[pl.ds(start, CHUNK), :] = (scaled * jax.nn.sigmoid(scaled) * mask_at(start)).astype(BF16)

        loop(BLOCK // CHUNK, step)

    @token("A2s")
    def _():
        conv_mid(c2, cols_a, w_mid_a)
        begin(2, column_sums(8, 2, masked_terms(c2)))

    @token("A2e")
    def _():
        sums_of[2].end()
        set_norm("mid_a", 0, 0, "inv_out", "chan_a")
        act_mid(a2, c2, "mid_a")

    @token("proj")
    def _():
        def project(j):
            cp[at_block(j, BLOCK), :] = mm(x[0:BLOCK, :], w_proj_a[:, at_block(j, LANES)])

        loop(4, project)

    def blocked(ref, j):
        return square_terms(ref.at[pl.ds(j * BLOCK, BLOCK)])

    @token("A3s")
    def _():
        for j in range(4):
            c3[at_block(j, BLOCK), :] = mm(a2[...], w_out_a[:, at_block(j, LANES)])
        begin(3, [row for ref in (c3, cp) for j in range(4) for row in column_sums(8, 2, blocked(ref, j))])

    @token("A3e")
    def _():
        sums_of[3].end()
        for j in range(4):
            set_norm("out_a", j, 2 * j, "inv_out", None)
            set_norm("proj_a", j, 8 + 2 * j, "inv_out", None)
        for j in range(4):

            def join_a(index, j=j):
                start = pl.multiple_of(index * CHUNK, CHUNK)
                rows = pl.ds(j * BLOCK + start, CHUNK)
                pre = normed("out_a", j, c3[rows, :]) + normed("proj_a", j, cp[rows, :])
                out = pre * jax.nn.sigmoid(pre) * mask_at(start)
                bo[rows, :] = out
                feed[pl.ds(start, CHUNK), pl.ds(j * LANES, LANES)] = out.astype(BF16)

            loop(BLOCK // CHUNK, join_a)

    @token("A4s")
    def _():
        add_up(d1, 4, lambda k: feed[:, at_block(k, LANES)], lambda k: w_in_b[at_block(k, LANES), :])
        begin(4, column_sums(8, 2, square_terms(d1)))

    @token("A4e")
    def _():
        sums_of[4].end()
        set_norm("in_b", 0, 0, "inv_out", "chan_b")
        s = scales["in_b", 0]

        def act_b(lane):
            scaled = d1[:, at_block(lane, 128)] * lane_row(s["mul"], lane) + lane_row(s["add"], lane)
            act = scaled * jax.nn.sigmoid(scaled) * mask_ref[...]
            for t, (u, v) in enumerate(TAPS):
                shift = (-(32 * (u - 1) + 4 * (v - 1))) % BLOCK
                moved = pltpu.roll(act, shift, 0) if shift else act
                cols_b[:, pl.ds(pl.multiple_of(t * LANES + lane * 128, 128), 128)] = moved.astype(BF16)

        loop(4, act_b)

    @token("A5s")
    def _():
        conv_mid(d2, cols_b, w_mid_b)
        begin(5, column_sums(8, 2, masked_terms(d2)))

    @token("A5e")
    def _():
        sums_of[5].end()
        set_norm("mid_b", 0, 0, "inv_out", "chan_b")
        act_mid(b2, d2, "mid_b")

    PAIRS = ((0, 2), (1, 3))
    FORTH = {6: 0, 13: 2, 15: 1, 16: 3}
    BACK = {7: 0, 14: 2, 17: 1, 18: 3}

    def expand_b(n, j):
        d3[at_block(j, BLOCK), :] = mm(b2[...], w_out_b[:, at_block(j, LANES)])
        begin(n, column_sums(8, 2, blocked(d3, j)))

    def set_out_b(n, j):
        sums_of[n].end()
        set_norm("out_b", j, 0, "inv_out", None)

    def finish_b(n, j):
        if n == 7:
            cot_copy.wait()
        lanes = pl.ds(j * LANES, LANES)

        def finish(start):
            rows = pl.ds(j * BLOCK + start, CHUNK)
            row = start // CHUNK
            for col in range(SIDE):
                move[4 * col : 4 * col + 4, 0:LANES] = cot[row, col, :, lanes].astype(F32)
            mask, gate, hidden = mask_at(start), gate_at(start), d3[rows, :]
            pre = bo[rows, :] + gate * normed("out_b", j, hidden)
            part = jax.nn.sigmoid(pre)
            grad = move[:, 0:LANES] * mask * (part * (1.0 + pre * (1.0 - part)))
            move[:, LANES : 2 * LANES] = pre * part * mask
            for col in range(SIDE):
                cot[row, col, :, lanes] = move[4 * col : 4 * col + 4, LANES : 2 * LANES].astype(BF16)
            bo[rows, :] = grad
            grad = grad * gate
            return grad, grad * hat("out_b", j, hidden)

        values = column_sums(SIDE, 2, finish)
        bo[(j + 1) * BLOCK - CHUNK : (j + 1) * BLOCK, :] = jnp.zeros((CHUNK, LANES), F32)
        begin(n, values)
        if n == 18:
            result_copy.start()

    for n, j in FORTH.items():
        todo[f"A{n}s"], todo[f"A{n}e"] = functools.partial(expand_b, n, j), functools.partial(set_out_b, n, j)
    for n, j in BACK.items():
        todo[f"A{n}s"] = functools.partial(finish_b, n, j)

    @token("sent")
    def _():
        for one in gathers.values():
            one.sent()

    def keep_sums(n, at):
        rows = sums_of[n].rows
        sums[at : at + rows, :] = tot[0:rows, :]

    def low_out_b(n, j):
        sums_of[n].end()
        keep_sums(n, 16 * (j % 2) + 8 * (j // 2))
        set_back("out_b", j, 0, 1)

        def step(index):
            start = pl.multiple_of(index * CHUNK, CHUNK)
            rows = pl.ds(j * BLOCK + start, CHUNK)
            grad = back("out_b", j, bo[rows, :] * gate_at(start), d3[rows, :]) * mask_at(start)
            dout[pl.ds(start, CHUNK), pl.ds(j * LANES, LANES)] = grad.astype(BF16)

        loop(BLOCK // CHUNK, step)

    for n, j in BACK.items():
        todo[f"A{n}e"] = functools.partial(low_out_b, n, j)

    def through_out(weight):
        add_up(dz, 4, lambda k: dout[:, at_block(k, LANES)], lambda k: weight[:, at_block(k, LANES)], mm_nt)

    def slope_terms(grad_ref, ref, name, chan):
        def terms(start):
            rows = pl.ds(start, CHUNK)
            hidden = ref[rows, :]
            mask = mask_at(pl.multiple_of(start % BLOCK, CHUNK) if grad_ref.shape[0] > BLOCK else start)
            grad = grad_ref[rows, :] * mask * vec.get(state[chan]) * slope_of(normed(name, 0, hidden))
            grad_ref[rows, :] = grad
            return grad, grad * hat(name, 0, hidden)

        return terms

    def through_pair(pair):
        return [mm_nt(dout[:, at_block(j, LANES)], w_out_b[:, at_block(j, LANES)]) for j in pair]

    @token("D8")
    def _():
        first, second = through_pair(PAIRS[0])
        dz[...] = first + second

    @token("A8s")
    def _():
        first, second = through_pair(PAIRS[1])
        dz[...] += first + second
        tell("out_b")
        begin(8, column_sums(8, 2, slope_terms(dz, d2, "mid_b", "chan_b")))

    def grad_out(act_ref, j):
        g_out[:, at_block(j, LANES)] = mm_tn(act_ref[...], dout[:, at_block(j, LANES)]).astype(BF16)

    tokens("g.out_b", 2, 2, lambda k: grad_out(b2, 2 * (k % 2) + k // 2))

    @token("A8e")
    def _():
        sums_of[8].end()
        keep_sums(8, 32)
        set_back("mid_b", 0, 0, 1)

    def low_mid(name, ref, shifts):
        s = scales[name, 0]

        def step(lane):
            lanes = at_block(lane, 128)
            grad = (
                dz[:, lanes] * lane_row(s["by"], lane)
                - lane_row(s["back_add"], lane)
                - ref[:, lanes] * lane_row(s["back_mul"], lane)
            ) * mask_ref[...]
            dm[:, lanes] = grad.astype(BF16)
            for k, shift in enumerate(shifts):
                moved = pltpu.roll(grad, shift, 0) if shift else grad
                g_mid[k * BLOCK : (k + 1) * BLOCK, lanes] = moved.astype(BF16)

        loop(4, step)

    @token("A9s")
    def _():
        low_mid("mid_b", d2, [(32 * (u - 1) + 4 * (v - 1)) % BLOCK for u, v in TAPS])
        add_up(dz, 9, lambda t: g_mid[at_block(t, BLOCK), :], lambda t: w_mid_b[at_block(t, LANES), :], mm_nt)
        tell("mid_b")
        begin(9, column_sums(8, 2, slope_terms(dz, d1, "in_b", "chan_b")))

    def grad_mid(cols, t):
        g_mid[at_block(t, LANES), :] = mm_tn(cols[:, at_block(t, LANES)], dm[...]).astype(BF16)

    tokens("g.mid_b", 3, 3, lambda t: grad_mid(cols_b, t))

    @token("A9e")
    def _():
        sums_of[9].end()
        keep_sums(9, 40)
        set_back("in_b", 0, 0, 1)

    @token("A10s")
    def _():
        def low_first_b(index):
            start = pl.multiple_of(index * CHUNK, CHUNK)
            rows = pl.ds(start, CHUNK)
            df[rows, :] = (back("in_b", 0, dz[rows, :], d1[rows, :]) * mask_at(start)).astype(BF16)

        loop(BLOCK // CHUNK, low_first_b)

        for j in range(4):
            bo[at_block(j, BLOCK), :] += mm_nt(df[...], w_in_b[at_block(j, LANES), :])
        tell("in_b")
        values = []
        for j in range(4):

            def join_back(start, j=j):
                rows = pl.ds(j * BLOCK + start, CHUNK)
                left, right = c3[rows, :], cp[rows, :]
                pre = normed("out_a", j, left) + normed("proj_a", j, right)
                grad = bo[rows, :] * mask_at(start) * slope_of(pre)
                bo[rows, :] = grad
                return grad, grad * hat("out_a", j, left), grad * hat("proj_a", j, right)

            values += column_sums(8, 3, join_back)
        begin(10, values)

    def grad_in_b(j):
        g_in[at_block(j, LANES), :] = mm_tn(feed[:, at_block(j, LANES)], df[...]).astype(BF16)

    tokens("g.in_b", 2, 2, grad_in_b)

    @token("A10e")
    def _():
        sums_of[10].end()
        keep_sums(10, 48)
        for j in range(4):
            set_back("out_a", j, 3 * j, 3 * j + 1)
            set_back("proj_a", j, 3 * j, 3 * j + 2)

    @token("A11s")
    def _():
        for j in range(4):

            def low_both(index, j=j):
                start = pl.multiple_of(index * CHUNK, CHUNK)
                rows = pl.ds(j * BLOCK + start, CHUNK)
                near_rows, lanes = pl.ds(start, CHUNK), pl.ds(j * LANES, LANES)
                grad, mask = bo[rows, :], mask_at(start)
                dout[near_rows, lanes] = (back("out_a", j, grad, c3[rows, :]) * mask).astype(BF16)
                dproj[near_rows, lanes] = (back("proj_a", j, grad, cp[rows, :]) * mask).astype(BF16)

            loop(BLOCK // CHUNK, low_both)
        through_out(w_out_a)
        tell("out_a")
        begin(11, column_sums(8, 2, slope_terms(dz, c2, "mid_a", "chan_a")))

    tokens("g.out_a", 2, 2, lambda j: grad_out(a2, j))

    def grad_proj(n):
        i, j = n // 4, n % 4
        g_proj[at_block(i, LANES), at_block(j, LANES)] = mm_tn(
            x[0:BLOCK, at_block(i, LANES)], dproj[:, at_block(j, LANES)]
        ).astype(BF16)

    tokens("g.proj_a", 2, 4, grad_proj)

    def back_proj(n):
        out, rows = d3.at[pl.ds(n * BLOCK, BLOCK)], pl.ds(n * LANES, LANES)
        add_up(out, 4, lambda k: dproj[:, at_block(k, LANES)], lambda k: w_proj_a[rows, at_block(k, LANES)], mm_nt)

    @token("dproj.0")
    def _():
        back_proj(0)

    @token("dproj.1")
    def _():
        back_proj(1)
        tell("proj_a")

    @token("A11e")
    def _():
        sums_of[11].end()
        keep_sums(11, 96)
        set_back("mid_a", 0, 0, 1)

    @token("A12s")
    def _():
        low_mid("mid_a", c2, [(-(32 * r + 4 * s)) % BLOCK for r in range(2) for s in range(2)])
        for row_par in range(2):
            for col_par in range(2):
                grad = None
                for t, (u, v) in enumerate(TAPS):
                    if (u != 1) != bool(row_par) or (v != 1) != bool(col_par):
                        continue
                    moved = 2 * (1 if u == 0 else 0) + (1 if v == 0 else 0)
                    term = mm_nt(g_mid[moved * BLOCK : (moved + 1) * BLOCK, :], w_mid_a[t * LANES : (t + 1) * LANES, :])
                    grad = term if grad is None else grad + term
                bo[pl.ds((2 * row_par + col_par) * BLOCK, BLOCK), :] = grad
        tell("mid_a")
        begin(12, column_sums(32, 2, slope_terms(bo, c1, "in_a", "chan_a")))

    tokens("g.mid_a", 3, 3, lambda t: grad_mid(cols_a, t))

    @token("A12e")
    def _():
        sums_of[12].end()
        keep_sums(12, 104)
        set_back("in_a", 0, 0, 1)
        for p in range(4):

            def low_first_a(index, p=p):
                start = pl.multiple_of(index * CHUNK, CHUNK)
                rows = pl.ds(p * BLOCK + start, CHUNK)
                grad = back("in_a", 0, bo[rows, :], c1[rows, :]) * mask_at(start)
                cols_b[pl.ds(start, CHUNK), p * LANES : (p + 1) * LANES] = grad.astype(BF16)

            loop(BLOCK // CHUNK, low_first_a)

    def first_grad(p):
        return cols_b[:, p * LANES : (p + 1) * LANES]

    def grad_in_a(i):
        lanes = at_block(i, 256)
        total = mm_tn(x[0:BLOCK, lanes], first_grad(0))
        for p in range(1, 4):
            total = total + mm_tn(x[p * BLOCK : (p + 1) * BLOCK, lanes], first_grad(p))
        g_in[at_block(i, 256), :] = total.astype(BF16)

    tokens("g.in_a", 2, 2, grad_in_a)

    def image_grad(planes):
        for p in planes:
            for h in range(2):
                lanes = pl.ds(h * LANES, LANES)
                grad = mm_nt(first_grad(p), w_in_a[h * LANES : (h + 1) * LANES, :])
                dz[...] = grad + d3[h * BLOCK : (h + 1) * BLOCK, :] if p == 0 else grad

                def pixels(row, p=p, lanes=lanes):
                    move[:, 0:LANES] = dz[at_block(row, CHUNK), :]
                    for col in range(SIDE):
                        raw[2 * row + p // 2, 2 * col + p % 2, :, lanes] = move[4 * col : 4 * col + 4, 0:LANES].astype(BF16)

                loop(SIDE, pixels)

    @token("img.0")
    def _():
        image_grad((0, 1))

    @token("img.1")
    def _():
        image_grad((2, 3))
        grad_copy.start()
        tell("in_a")

    @token("own")
    def _():
        def own_row(at, out, k):
            if out.shape[1] >= 128:
                for lane in range(2):
                    line = sums[pl.ds(at + 2 * (place.f % 2) + lane, 1), :]
                    out[k : k + 1, lane * 128 : (lane + 1) * 128] = line
            else:
                odd = (place.f % 2).astype(F32)
                move[0:1, 0:128] = sums[pl.ds(at + place.f // 2, 1), :]
                line = move[0:8, 0:128]
                line = line + (pltpu.roll(line, 64, 1) - line) * odd
                out[k : k + 1, :] = line[0:1, 0 : out.shape[1]]

        for name, at in (("mid_b", 32), ("in_b", 40), ("mid_a", 96), ("in_a", 104)):
            own_row(at + 4, owned[name], 0)
            own_row(at, owned[name], 1)
        block = place.f // 2
        pair_at = 16 * (block % 2) + 8 * (block // 2)
        for name, at, gain in (("out_b", pair_at, 4), ("out_a", 48 + 12 * block, 4), ("proj_a", 48 + 12 * block, 8)):
            own_row(at + gain, owned[name], 0)
            own_row(at, owned[name], 1)
        for one in own_copies:
            one.start()

    steps = sorted(todo)
    if sorted(RUN) != list(range(len(steps))):
        raise ValueError(len(steps))
    for index in RUN:
        todo[steps[index]]()
    result_copy.wait()
    grad_copy.wait()
    for one in scatters.values():
        one.sent()
    for one in own_copies + out_copies:
        one.wait()


def finish_kernel(*refs):
    arrays_in, arrays_out, held, wide = refs[:16], refs[16:32], refs[32:48], refs[48:55]
    in_sem, out_sem = refs[55:]
    loads = [pltpu.make_async_copy(a, b, in_sem.at[i]) for i, (a, b) in enumerate(zip(arrays_in, held))]
    leaving = held[:9] + wide
    stores = [pltpu.make_async_copy(a, b, out_sem.at[i]) for i, (a, b) in enumerate(zip(leaving, arrays_out))]
    order = list(range(9, 16)) + list(range(9))
    for i in order:
        loads[i].start()
    for i in order:
        loads[i].wait()
        if i >= 9:
            narrow, target = held[i], wide[i - 9]
            rows, columns = narrow.shape
            chunk = chunk_of(rows, columns)

            def step(index, carry, narrow=narrow, target=target, chunk=chunk):
                at = pl.ds(pl.multiple_of(index * chunk, 16), chunk)
                target[at, :] = narrow[at, :].astype(F32)
                return carry

            lax.fori_loop(0, rows // chunk, step, 0)
        stores[i].start()
    for i in order:
        stores[i].wait()


def finish_call(plain, grads):
    anywhere = pl.BlockSpec(memory_space=pl.ANY)
    return pl.pallas_call(
        finish_kernel,
        out_shape=[jax.ShapeDtypeStruct(one.shape, one.dtype) for one in plain]
        + [jax.ShapeDtypeStruct(one.shape, F32) for one in grads],
        in_specs=[anywhere] * 16,
        out_specs=[anywhere] * 16,
        scratch_shapes=[pltpu.VMEM(one.shape, one.dtype) for one in (*plain, *grads)]
        + [pltpu.VMEM(one.shape, F32) for one in grads]
        + [pltpu.SemaphoreType.DMA((16,)), pltpu.SemaphoreType.DMA((16,))],
        compiler_params=pltpu.CompilerParams(vmem_limit_bytes=64 * 2**20),
        name="finish_step",
    )(*plain, *grads)


def body_fast(
    images,
    image_sides,
    widths,
    keep_gate,
    w_in_a,
    w_mid_a,
    w_out_a,
    w_proj_a,
    norm_in_a,
    norm_mid_a,
    norm_out_a,
    norm_proj_a,
    w_in_b,
    w_mid_b,
    w_out_b,
    norm_in_b,
    norm_mid_b,
    norm_out_b,
    cotangent,
):
    width_in, width_out = images.shape[3], cotangent.shape[3]
    turned = (1, 2, 0, 3)
    images, cotangent = images.transpose(turned), cotangent.transpose(turned)
    norms = (norm_in_a, norm_mid_a, norm_out_a, norm_proj_a, norm_in_b, norm_mid_b, norm_out_b)
    shards = (w_in_a, w_mid_a, w_out_a, w_proj_a, w_in_b, w_mid_b, w_out_b)
    vmem = pl.BlockSpec(memory_space=pltpu.VMEM)
    smem = pl.BlockSpec(memory_space=pltpu.SMEM)
    anywhere = pl.BlockSpec(memory_space=pl.ANY)
    wholes = [(8 * one.shape[0], one.shape[1]) for one in shards]
    pieces = max(sum(len(one) for one in ways.values()) for ways in (WAYS_IN, WAYS_OUT))
    outs = pl.pallas_call(
        step_kernel,
        out_shape=[jax.ShapeDtypeStruct(cotangent.shape, BF16), jax.ShapeDtypeStruct(images.shape, BF16)]
        + [jax.ShapeDtypeStruct(one.shape, F32) for one in norms]
        + [jax.ShapeDtypeStruct(one.shape, BF16) for one in shards],
        in_specs=[anywhere, anywhere, smem, smem, smem] + [vmem] * 7 + [anywhere] * 7,
        out_specs=[anywhere] * 16,
        scratch_shapes=[pltpu.VMEM(one.shape, F32) for one in norms]
        + [pltpu.VMEM(one.shape, BF16) for one in shards]
        + [pltpu.VMEM(shape, BF16) for shape in wholes]
        + [
            pltpu.VMEM(images.shape, BF16),
            pltpu.VMEM(cotangent.shape, BF16),
            pltpu.VMEM((4 * BLOCK, width_in), BF16),
            pltpu.VMEM((4 * BLOCK, LANES), F32),
            pltpu.VMEM((BLOCK, 9 * LANES), BF16),
            pltpu.VMEM((BLOCK, LANES), F32),
            pltpu.VMEM((BLOCK, LANES), BF16),
            pltpu.VMEM((4 * BLOCK, LANES), F32),
            pltpu.VMEM((4 * BLOCK, LANES), F32),
            pltpu.VMEM((4 * BLOCK, LANES), F32),
            pltpu.VMEM((BLOCK, width_out), BF16),
            pltpu.VMEM((BLOCK, LANES), F32),
            pltpu.VMEM((BLOCK, 9 * LANES), BF16),
            pltpu.VMEM((BLOCK, LANES), F32),
            pltpu.VMEM((BLOCK, LANES), BF16),
            pltpu.VMEM((4 * BLOCK, LANES), F32),
            pltpu.VMEM((BLOCK, LANES), F32),
            pltpu.VMEM((BLOCK, LANES), BF16),
            pltpu.VMEM((BLOCK, LANES), BF16),
            pltpu.VMEM((BLOCK, width_out), BF16),
            pltpu.VMEM((BLOCK, width_out), BF16),
            pltpu.VMEM(wholes[1], BF16),
            pltpu.VMEM(wholes[2], BF16),
            pltpu.VMEM(wholes[4], BF16),
            pltpu.VMEM(wholes[3], BF16),
            pltpu.VMEM((BLOCK, 128), F32),
            pltpu.VMEM((BLOCK, 128), F32),
            pltpu.VMEM((CHUNK, width_in), F32),
            pltpu.VMEM((8, 24, 128), F32),
            pltpu.VMEM((24, 128), F32),
            pltpu.VMEM((160, LANES), F32),
            pltpu.VMEM((SHORT_SETS, 18, 8, 128), F32),
            pltpu.VMEM((10, 64, 128), F32),
            pltpu.VMEM((64, 128), F32),
            pltpu.VMEM((112, 128), F32),
            pltpu.SemaphoreType.DMA((4,)),
            pltpu.SemaphoreType.DMA((pieces,)),
            pltpu.SemaphoreType.DMA((pieces, 6)),
            pltpu.SemaphoreType.DMA((SHORT_SETS + 1, 3)),
            pltpu.SemaphoreType.DMA((SHORT_SETS + 1, 3)),
            pltpu.SemaphoreType.DMA((2,)),
            pltpu.SemaphoreType.DMA((2, 7)),
            pltpu.SemaphoreType.REGULAR((7,)),
        ],
        compiler_params=pltpu.CompilerParams(
            collective_id=0, has_side_effects=True, vmem_limit_bytes=64 * 2**20
        ),
        name="whole_step",
    )(images, cotangent, image_sides, keep_gate, widths, *norms, *shards)
    back_turned = (2, 0, 1, 3)
    outs = finish_call(outs[:9], outs[9:])
    own, finals = outs[2:9], outs[9:]
    return (
        outs[0].transpose(back_turned),
        outs[1].transpose(back_turned),
        *finals[:4],
        *own[:4],
        *finals[4:],
        *own[4:],
    )


def fits(mesh):
    return mesh.shape[FSDP] == 8 and mesh.shape[DP] == 4


def gather_plain(shards):
    return [lax.all_gather(one, FSDP, axis=0, tiled=True) for one in shards]


def scatter_plain(grads):
    parts = [lax.psum_scatter(one, FSDP, scatter_dimension=0, tiled=True) for one in grads]
    return lax.psum(tuple(parts), DP)


def sum_pair(first, second):
    return lax.psum((first, second), (FSDP, DP))


def silu_slope(values):
    sigmoid_part = jax.nn.sigmoid(values)
    return sigmoid_part * (1.0 + values * (1.0 - sigmoid_part))


def pixel_masks(image_sides, side_in, side_out):
    half_sides = image_sides // 2
    rows_in = jnp.arange(side_in, dtype=jnp.int32)
    rows_out = jnp.arange(side_out, dtype=jnp.int32)
    inside_in = (rows_in[None, :, None] < image_sides[:, None, None]) & (
        rows_in[None, None, :] < image_sides[:, None, None]
    )
    inside_out = (rows_out[None, :, None] < half_sides[:, None, None]) & (
        rows_out[None, None, :] < half_sides[:, None, None]
    )
    local_counts = jnp.stack(
        [jnp.sum(image_sides * image_sides), jnp.sum(half_sides * half_sides)]
    ).astype(jnp.float32)
    return (
        inside_in.astype(jnp.float32)[..., None],
        inside_out.astype(jnp.float32)[..., None],
        local_counts,
    )


def norm_stats(hidden, pixel_mask, local_counts, count_slot):
    sum_values, sum_squares = sum_pair(
        jnp.sum(hidden * pixel_mask, axis=(0, 1, 2)),
        jnp.sum(hidden * hidden * pixel_mask, axis=(0, 1, 2)),
    )
    pixel_total = local_counts[count_slot]
    average = sum_values / pixel_total
    inv_std = lax.rsqrt(sum_squares / pixel_total - average * average + EPSILON)
    return (average, inv_std, pixel_total)


def normalize(hidden, stats_now, params, channel):
    average, inv_std, pixel_total = stats_now
    scaled = (hidden - average) * inv_std
    params_wide = params.astype(jnp.float32)
    return (scaled, (scaled * params_wide[0] + params_wide[1]) * channel)


def norm_backward(grad_norm, scaled, stats_now, params, pixel_mask):
    average, inv_std, pixel_total = stats_now
    shift_sum, gain_sum = sum_pair(
        jnp.sum(grad_norm, axis=(0, 1, 2)), jnp.sum(grad_norm * scaled, axis=(0, 1, 2))
    )
    gain_row = params[0].astype(jnp.float32)
    grad_hidden = (
        gain_row
        * inv_std
        * (grad_norm - shift_sum / pixel_total - scaled * gain_sum / pixel_total)
        * pixel_mask
    )
    return (grad_hidden.astype(jnp.bfloat16), gain_sum, shift_sum)


def taps_stride_two(activations):
    slot_count = activations.shape[0]
    half_side = activations.shape[1] // 2
    lane_count = activations.shape[3]
    padded = jnp.pad(activations, ((0, 0), (1, 1), (1, 1), (0, 0)))
    parity_grid = padded.reshape(slot_count, half_side + 1, 2, half_side + 1, 2, lane_count)
    pieces = [
        parity_grid[
            :,
            row_tap // 2 : row_tap // 2 + half_side,
            row_tap % 2,
            col_tap // 2 : col_tap // 2 + half_side,
            col_tap % 2,
            :,
        ]
        for row_tap in range(3)
        for col_tap in range(3)
    ]
    return jnp.concatenate(pieces, axis=-1)


def fold_stride_two(grad_cols, side_in):
    slot_count = grad_cols.shape[0]
    half_side = grad_cols.shape[1]
    lane_count = grad_cols.shape[3] // 9
    planes = [
        [
            jnp.zeros((slot_count, half_side + 1, half_side + 1, lane_count), jnp.float32)
            for col_par in range(2)
        ]
        for row_par in range(2)
    ]
    for row_tap in range(3):
        for col_tap in range(3):
            tap_index = row_tap * 3 + col_tap
            tap_piece = grad_cols[..., tap_index * lane_count : (tap_index + 1) * lane_count]
            placed = jnp.pad(
                tap_piece,
                (
                    (0, 0),
                    (row_tap // 2, 1 - row_tap // 2),
                    (col_tap // 2, 1 - col_tap // 2),
                    (0, 0),
                ),
            )
            planes[row_tap % 2][col_tap % 2] = planes[row_tap % 2][col_tap % 2] + placed
    parity_grid = jnp.stack([jnp.stack(planes[0], axis=3), jnp.stack(planes[1], axis=3)], axis=2)
    whole_grid = parity_grid.reshape(slot_count, side_in + 2, side_in + 2, lane_count)
    return whole_grid[:, 1:-1, 1:-1, :]


def taps_stride_one(activations):
    side_now = activations.shape[1]
    padded = jnp.pad(activations, ((0, 0), (1, 1), (1, 1), (0, 0)))
    pieces = [
        padded[:, row_tap : row_tap + side_now, col_tap : col_tap + side_now, :]
        for row_tap in range(3)
        for col_tap in range(3)
    ]
    return jnp.concatenate(pieces, axis=-1)


def fold_stride_one(grad_cols):
    lane_count = grad_cols.shape[3] // 9
    whole_grid = None
    for row_tap in range(3):
        for col_tap in range(3):
            tap_index = row_tap * 3 + col_tap
            tap_piece = grad_cols[..., tap_index * lane_count : (tap_index + 1) * lane_count]
            placed = jnp.pad(
                tap_piece, ((0, 0), (row_tap, 2 - row_tap), (col_tap, 2 - col_tap), (0, 0))
            )
            whole_grid = placed if whole_grid is None else whole_grid + placed
    return whole_grid[:, 1:-1, 1:-1, :]


def contract(left_side, right_side):
    return lax.dot_general(
        left_side,
        right_side,
        (((0, 1, 2), (0, 1, 2)), ((), ())),
        preferred_element_type=jnp.float32,
    )


def back_project(gradient, weight):
    return lax.dot_general(
        gradient, weight, (((3,), (1,)), ((), ())), preferred_element_type=jnp.float32
    )


def own_shard(pair_sums):
    gain_sum, shift_sum = pair_sums
    shard_width = gain_sum.shape[0] // lax.axis_size(FSDP)
    offset = lax.axis_index(FSDP) * shard_width
    return jnp.stack(
        [
            lax.dynamic_slice_in_dim(gain_sum, offset, shard_width, 0),
            lax.dynamic_slice_in_dim(shift_sum, offset, shard_width, 0),
        ]
    )


def block_a_forward(inputs, weights, mask_in, mask_out, local_counts, channel, saved_stats):
    w_in, w_mid, w_out, w_proj, norm_in, norm_mid, norm_out, norm_proj = weights
    conv_first = jnp.dot(inputs, w_in, preferred_element_type=jnp.float32)
    stats_first = (
        norm_stats(conv_first, mask_in, local_counts, 0) if saved_stats is None else saved_stats[0]
    )
    scaled_first, normed_first = normalize(conv_first, stats_first, norm_in, channel)
    act_first = (jax.nn.silu(normed_first) * mask_in).astype(jnp.bfloat16)
    cols_mid = taps_stride_two(act_first)
    conv_mid = jnp.dot(cols_mid, w_mid, preferred_element_type=jnp.float32)
    stats_mid = (
        norm_stats(conv_mid, mask_out, local_counts, 1) if saved_stats is None else saved_stats[1]
    )
    scaled_mid, normed_mid = normalize(conv_mid, stats_mid, norm_mid, channel)
    act_mid = (jax.nn.silu(normed_mid) * mask_out).astype(jnp.bfloat16)
    conv_out = jnp.dot(act_mid, w_out, preferred_element_type=jnp.float32)
    slot_count, side_in, lane_count = (inputs.shape[0], inputs.shape[1], inputs.shape[3])
    sampled = inputs.reshape(slot_count, side_in // 2, 2, side_in // 2, 2, lane_count)[
        :, :, 0, :, 0, :
    ]
    conv_proj = jnp.dot(sampled, w_proj, preferred_element_type=jnp.float32)
    conv_both = jnp.concatenate([conv_out, conv_proj], axis=-1)
    norm_both = jnp.concatenate([norm_out, norm_proj], axis=-1)
    stats_both = (
        norm_stats(conv_both, mask_out, local_counts, 1) if saved_stats is None else saved_stats[2]
    )
    scaled_both, normed_both = normalize(conv_both, stats_both, norm_both, 1.0)
    width_out = conv_out.shape[-1]
    pre_sum = normed_both[..., :width_out] + normed_both[..., width_out:]
    block_out = jax.nn.silu(pre_sum) * mask_out
    saved_values = (
        scaled_first,
        normed_first,
        act_first,
        cols_mid,
        scaled_mid,
        normed_mid,
        act_mid,
        sampled,
        scaled_both,
        pre_sum,
    )
    return (block_out, (stats_first, stats_mid, stats_both), saved_values)


def block_a_backward(
    grad_out, inputs, weights, stats_all, saved_values, mask_in, mask_out, channel
):
    w_in, w_mid, w_out, w_proj, norm_in, norm_mid, norm_out, norm_proj = weights
    stats_first, stats_mid, stats_both = stats_all
    (
        scaled_first,
        normed_first,
        act_first,
        cols_mid,
        scaled_mid,
        normed_mid,
        act_mid,
        sampled,
        scaled_both,
        pre_sum,
    ) = saved_values
    grad_pre = grad_out * mask_out * silu_slope(pre_sum)
    grad_both = jnp.concatenate([grad_pre, grad_pre], axis=-1)
    norm_both = jnp.concatenate([norm_out, norm_proj], axis=-1)
    low_both, gain_both, shift_both = norm_backward(
        grad_both, scaled_both, stats_both, norm_both, mask_out
    )
    width_out = grad_pre.shape[-1]
    low_out = low_both[..., :width_out]
    low_proj = low_both[..., width_out:]
    grad_w_out = contract(act_mid, low_out)
    grad_w_proj = contract(sampled, low_proj)
    grad_norm_mid = back_project(low_out, w_out) * mask_out * channel * silu_slope(normed_mid)
    low_mid, gain_mid, shift_mid = norm_backward(
        grad_norm_mid, scaled_mid, stats_mid, norm_mid, mask_out
    )
    grad_w_mid = contract(cols_mid, low_mid)
    grad_act_first = fold_stride_two(back_project(low_mid, w_mid), inputs.shape[1])
    grad_norm_first = grad_act_first * mask_in * channel * silu_slope(normed_first)
    low_first, gain_first, shift_first = norm_backward(
        grad_norm_first, scaled_first, stats_first, norm_in, mask_in
    )
    grad_w_in = contract(inputs, low_first)
    spread = lax.pad(
        back_project(low_proj, w_proj),
        jnp.float32(0.0),
        ((0, 0, 0), (0, 1, 1), (0, 1, 1), (0, 0, 0)),
    )
    grad_inputs = (back_project(low_first, w_in) + spread) * mask_in
    norm_grads = (
        (gain_first, shift_first),
        (gain_mid, shift_mid),
        (gain_both[:width_out], shift_both[:width_out]),
        (gain_both[width_out:], shift_both[width_out:]),
    )
    return (grad_inputs, (grad_w_in, grad_w_mid, grad_w_out, grad_w_proj), norm_grads)


def block_b_forward(block_in, weights, mask_out, local_counts, channel, depth_gate, saved_stats):
    w_in, w_mid, w_out, norm_in, norm_mid, norm_out = weights
    feed_in = block_in.astype(jnp.bfloat16)
    conv_first = jnp.dot(feed_in, w_in, preferred_element_type=jnp.float32)
    stats_first = (
        norm_stats(conv_first, mask_out, local_counts, 1) if saved_stats is None else saved_stats[0]
    )
    scaled_first, normed_first = normalize(conv_first, stats_first, norm_in, channel)
    act_first = (jax.nn.silu(normed_first) * mask_out).astype(jnp.bfloat16)
    cols_mid = taps_stride_one(act_first)
    conv_mid = jnp.dot(cols_mid, w_mid, preferred_element_type=jnp.float32)
    stats_mid = (
        norm_stats(conv_mid, mask_out, local_counts, 1) if saved_stats is None else saved_stats[1]
    )
    scaled_mid, normed_mid = normalize(conv_mid, stats_mid, norm_mid, channel)
    act_mid = (jax.nn.silu(normed_mid) * mask_out).astype(jnp.bfloat16)
    conv_out = jnp.dot(act_mid, w_out, preferred_element_type=jnp.float32)
    stats_out = (
        norm_stats(conv_out, mask_out, local_counts, 1) if saved_stats is None else saved_stats[2]
    )
    scaled_out, normed_out = normalize(conv_out, stats_out, norm_out, 1.0)
    pre_sum = block_in + depth_gate * normed_out
    result = jax.nn.silu(pre_sum) * mask_out
    saved_values = (
        feed_in,
        scaled_first,
        normed_first,
        act_first,
        cols_mid,
        scaled_mid,
        normed_mid,
        act_mid,
        scaled_out,
        pre_sum,
    )
    return (result, (stats_first, stats_mid, stats_out), saved_values)


def block_b_backward(grad_out, weights, stats_all, saved_values, mask_out, channel, depth_gate):
    w_in, w_mid, w_out, norm_in, norm_mid, norm_out = weights
    stats_first, stats_mid, stats_out = stats_all
    (
        feed_in,
        scaled_first,
        normed_first,
        act_first,
        cols_mid,
        scaled_mid,
        normed_mid,
        act_mid,
        scaled_out,
        pre_sum,
    ) = saved_values
    grad_pre = grad_out * mask_out * silu_slope(pre_sum)
    low_out, gain_out, shift_out = norm_backward(
        grad_pre * depth_gate, scaled_out, stats_out, norm_out, mask_out
    )
    grad_w_out = contract(act_mid, low_out)
    grad_norm_mid = back_project(low_out, w_out) * mask_out * channel * silu_slope(normed_mid)
    low_mid, gain_mid, shift_mid = norm_backward(
        grad_norm_mid, scaled_mid, stats_mid, norm_mid, mask_out
    )
    grad_w_mid = contract(cols_mid, low_mid)
    grad_norm_first = (
        fold_stride_one(back_project(low_mid, w_mid))
        * mask_out
        * channel
        * silu_slope(normed_first)
    )
    low_first, gain_first, shift_first = norm_backward(
        grad_norm_first, scaled_first, stats_first, norm_in, mask_out
    )
    grad_w_in = contract(feed_in, low_first)
    grad_in = grad_pre + back_project(low_first, w_in)
    norm_grads = ((gain_first, shift_first), (gain_mid, shift_mid), (gain_out, shift_out))
    return (grad_in, (grad_w_in, grad_w_mid, grad_w_out), norm_grads)


def body(
    images,
    image_sides,
    widths,
    keep_gate,
    w_in_a,
    w_mid_a,
    w_out_a,
    w_proj_a,
    norm_in_a,
    norm_mid_a,
    norm_out_a,
    norm_proj_a,
    w_in_b,
    w_mid_b,
    w_out_b,
    norm_in_b,
    norm_mid_b,
    norm_out_b,
    cotangent,
):
    mask_in, mask_out, local_counts = pixel_masks(image_sides, images.shape[1], cotangent.shape[1])
    lane_ids = jnp.arange(w_mid_a.shape[1], dtype=jnp.int32)
    channel_a = (lane_ids < widths[0]).astype(jnp.float32)
    channel_b = (lane_ids < widths[1]).astype(jnp.float32)
    depth_gate = keep_gate.astype(jnp.float32)[:, None, None, None]
    inputs = images * mask_in.astype(jnp.bfloat16)
    total_counts = lax.psum(local_counts, (FSDP, DP))
    gathered = gather_plain((w_in_a, w_mid_a, w_out_a, w_proj_a, w_in_b, w_mid_b, w_out_b))
    norms = lax.all_gather(
        jnp.concatenate(
            [norm_in_a, norm_mid_a, norm_out_a, norm_proj_a, norm_in_b, norm_mid_b, norm_out_b], axis=1
        ),
        FSDP,
        axis=0,
    )
    wide = []
    place = 0
    for one in (norm_in_a, norm_mid_a, norm_out_a, norm_proj_a, norm_in_b, norm_mid_b, norm_out_b):
        width = one.shape[1]
        wide.append(norms[:, :, place : place + width].transpose(1, 0, 2).reshape(2, -1))
        place += width
    weights_a = tuple(gathered[:4]) + tuple(wide[:4])
    weights_b = tuple(gathered[4:]) + tuple(wide[4:])
    block_out, stats_a, redone_a = block_a_forward(
        inputs, weights_a, mask_in, mask_out, total_counts, channel_a, None
    )
    result, stats_b, redone_b = block_b_forward(
        block_out, weights_b, mask_out, total_counts, channel_b, depth_gate, None
    )
    grad_block, grads_b, norms_b = block_b_backward(
        cotangent.astype(jnp.float32), weights_b, stats_b, redone_b, mask_out, channel_b, depth_gate
    )
    grad_inputs, grads_a, norms_a = block_a_backward(
        grad_block, inputs, weights_a, stats_a, redone_a, mask_in, mask_out, channel_a
    )
    finals = scatter_plain(tuple(one.astype(jnp.bfloat16) for one in grads_a + grads_b))
    final_in_a, final_mid_a, final_out_a, final_proj_a, final_in_b, final_mid_b, final_out_b = (
        one.astype(jnp.float32) for one in finals
    )
    return (
        result.astype(jnp.bfloat16),
        grad_inputs.astype(jnp.bfloat16),
        final_in_a,
        final_mid_a,
        final_out_a,
        final_proj_a,
        own_shard(norms_a[0]),
        own_shard(norms_a[1]),
        own_shard(norms_a[2]),
        own_shard(norms_a[3]),
        final_in_b,
        final_mid_b,
        final_out_b,
        own_shard(norms_b[0]),
        own_shard(norms_b[1]),
        own_shard(norms_b[2]),
    )


def solution(mesh):
    in_specs = (
        P((FSDP, DP), None, None, None),
        P((FSDP, DP)),
        P(),
        P((FSDP, DP)),
        P(FSDP, None),
        P(FSDP, None),
        P(FSDP, None),
        P(FSDP, None),
        P(None, FSDP),
        P(None, FSDP),
        P(None, FSDP),
        P(None, FSDP),
        P(FSDP, None),
        P(FSDP, None),
        P(FSDP, None),
        P(None, FSDP),
        P(None, FSDP),
        P(None, FSDP),
        P((FSDP, DP), None, None, None),
    )
    out_specs = (
        P((FSDP, DP), None, None, None),
        P((FSDP, DP), None, None, None),
        P(FSDP, None),
        P(FSDP, None),
        P(FSDP, None),
        P(FSDP, None),
        P(None, FSDP),
        P(None, FSDP),
        P(None, FSDP),
        P(None, FSDP),
        P(FSDP, None),
        P(FSDP, None),
        P(FSDP, None),
        P(None, FSDP),
        P(None, FSDP),
        P(None, FSDP),
    )
    step = body_fast if fits(mesh) else body
    return jax.shard_map(step, mesh=mesh, in_specs=in_specs, out_specs=out_specs, check_vma=False)
```

```python
import functools

import jax
import jax.numpy as jnp
from jax import lax
from jax.experimental import pallas as pl
from jax.experimental.pallas import tpu as pltpu
from jax.sharding import PartitionSpec as P

EPSILON = 1e-05
BY_MESH = pl.DeviceIdType.MESH
FSDP, DP = "fsdp", "dp"
F32 = jnp.float32
BF16 = jnp.bfloat16
NAMES = ("in_a", "mid_a", "out_a", "proj_a", "in_b", "mid_b", "out_b")
BLOCK = 256
LANES = 512
CHUNK = 32
SIDE = 7
ZYX, ZXY, YZX = range(3)
SHORT_SETS = 8
TAPS = [(u, v) for u in range(3) for v in range(3)]
LINK_PEERS = ((1, 0), (2, 0), (4, 0), (6, 0), (0, 2), (0, 1))
CHIP_PEERS = tuple((a, b) for a in (7, 6, 5, 4, 3, 2, 1, 0) for b in (2, 0) if a or b)
WAYS_IN = {
    "in_a": ((0, 64, 0, ((YZX, 4), (ZXY, 4))), (64, 64, 0, ((YZX, 4), (ZXY, 4)))),
    "mid_a": ((0, 96, 0, ((YZX, 4), (ZXY, 4))), (96, 96, 0, ((YZX, 4), (ZXY, 4))), (192, 96, 0, ((ZYX, 4), (ZXY, 4))), (288, 96, 0, ((YZX, 4), (ZXY, 4))), (384, 96, 0, ((YZX, 4), (ZXY, 4))), (480, 96, 0, ((ZYX, 4), (ZXY, 4)))),
    "out_a": ((0, 32, 0, ((ZXY, 5), (YZX, 3))), (32, 32, 0, ((ZXY, 5), (YZX, 3)))),
    "proj_a": ((0, 64, 0, ((ZXY, 5), (YZX, 3))), (64, 64, 0, ((ZXY, 5), (YZX, 3)))),
    "in_b": ((0, 128, 0, ((YZX, 4), (ZXY, 4))), (128, 128, 0, ((YZX, 4), (ZXY, 4)))),
    "mid_b": ((0, 96, 0, ((YZX, 4), (ZXY, 4))), (96, 96, 0, ((YZX, 4), (ZXY, 4))), (192, 96, 0, ((ZYX, 4), (ZXY, 4))), (288, 96, 0, ((YZX, 4), (ZXY, 4))), (384, 96, 0, ((YZX, 4), (ZXY, 4))), (480, 96, 0, ((ZYX, 4), (ZXY, 4)))),
    "out_b": ((0, 64, 0, ((ZXY, 2), (YZX, 2))), (0, 64, 4, ((ZXY, 2), (YZX, 2)))),
}
WAYS_OUT = {
    "in_a": ((0, 64, 4), (64, 64, 4)),
    "mid_a": ((0, 96, 4), (96, 96, 4), (192, 96, 4), (288, 96, 4), (384, 96, 4), (480, 96, 4)),
    "out_a": ((0, 32, 5), (32, 32, 5)),
    "proj_a": ((0, 32, 5), (32, 32, 5), (64, 32, 5), (96, 32, 5)),
    "in_b": ((0, 128, 4), (128, 128, 4)),
    "mid_b": ((0, 96, 4), (96, 96, 4), (192, 96, 4), (288, 96, 4), (384, 96, 4), (480, 96, 4)),
    "out_b": ((0, 32, 5), (32, 32, 5)),
}
RUN = [
    365, 411, 412, 385, 415, 386, 416, 390, 165, 417, 408, 391, 166, 384, 389, 39, 169, 76, 38, 418, 392, 170,
    99, 171, 419, 77, 420, 394, 100, 103, 82, 393, 121, 172, 104, 105, 173, 431, 80, 405, 85, 83, 174, 122,
    106, 107, 127, 84, 185, 432, 37, 406, 125, 143, 128, 81, 108, 129, 119, 144, 427, 355, 186, 428, 96, 413,
    402, 43, 126, 130, 401, 42, 150, 120, 182, 147, 414, 181, 141, 149, 97, 41, 116, 93, 387, 115, 151, 36,
    152, 92, 421, 40, 422, 148, 168, 142, 163, 357, 423, 138, 47, 175, 167, 137, 46, 395, 102, 45, 424, 164,
    397, 177, 425, 388, 176, 396, 160, 426, 429, 109, 101, 362, 159, 78, 409, 111, 44, 359, 51, 79, 178, 86,
    87, 50, 110, 398, 180, 124, 123, 179, 112, 183, 399, 49, 113, 400, 146, 89, 430, 145, 114, 132, 90, 88,
    403, 356, 133, 131, 48, 55, 184, 134, 91, 54, 53, 154, 136, 135, 153, 155, 404, 156, 117, 94, 158, 157,
    118, 52, 95, 358, 59, 139, 58, 140, 161, 162, 57, 360, 56, 63, 15, 361, 62, 14, 23, 27, 22, 26, 61, 60,
    67, 13, 12, 21, 19, 66, 65, 20, 25, 31, 24, 18, 35, 30, 34, 17, 410, 29, 64, 16, 98, 33, 28, 32, 71, 378,
    70, 69, 379, 205, 206, 229, 230, 68, 75, 373, 374, 74, 253, 375, 197, 221, 198, 254, 199, 222, 200, 277,
    73, 201, 224, 202, 72, 245, 3, 278, 368, 2, 246, 223, 369, 189, 226, 225, 248, 1, 247, 269, 302, 190, 213,
    250, 0, 270, 249, 7, 301, 272, 376, 377, 6, 214, 363, 203, 5, 271, 237, 204, 364, 227, 274, 273, 380, 381,
    228, 207, 238, 325, 4, 208, 11, 349, 251, 298, 209, 10, 232, 261, 233, 294, 370, 371, 262, 372, 191, 252,
    215, 256, 322, 231, 295, 9, 275, 192, 8, 193, 346, 276, 257, 366, 217, 194, 318, 280, 195, 239, 196, 367,
    342, 293, 326, 382, 296, 210, 255, 216, 383, 350, 218, 281, 241, 187, 219, 285, 188, 263, 240, 242, 279,
    220, 286, 212, 264, 320, 319, 304, 287, 234, 243, 266, 297, 265, 309, 211, 344, 343, 244, 333, 236, 258,
    305, 235, 328, 303, 288, 260, 289, 290, 300, 317, 268, 407, 299, 352, 282, 327, 267, 341, 313, 310, 312,
    259, 329, 284, 321, 351, 292, 314, 324, 337, 334, 336, 353, 306, 311, 345, 338, 291, 348, 323, 283, 316,
    308, 335, 347, 315, 330, 307, 340, 332, 339, 354, 331,
]


def flip(index, bits):
    out = index
    for bit in (1, 2, 4):
        if bits & bit:
            out = out + bit - 2 * bit * ((index // bit) % 2)
    return out


class Place:
    def __init__(self):
        self.f = lax.axis_index(FSDP)
        self.d = lax.axis_index(DP)
        self.y = self.f % 2
        self.z = self.f // 2
        self.c = self.d % 2
        self.x = self.d // 2
        self.inner = self.z * (3 - self.z) > 0

    def peer(self, f_bits, d_bits):
        return (flip(self.f, f_bits), flip(self.d, d_bits))


def enter(place, peers):
    barrier = pltpu.get_barrier_semaphore()
    for f_bits, d_bits in peers:
        pl.semaphore_signal(barrier, inc=1, device_id=place.peer(f_bits, d_bits), device_id_type=BY_MESH)
    pl.semaphore_wait(barrier, len(peers))


def push(source, target, send_sem, recv_sem, device):
    pltpu.make_async_remote_copy(
        src_ref=source,
        dst_ref=target,
        send_sem=send_sem,
        recv_sem=recv_sem,
        device_id=device,
        device_id_type=BY_MESH,
    ).start()


def await_bytes(view, sem):
    pltpu.make_async_copy(view, view, sem).wait()


def await_count(ref, count, sem):
    if not count:
        return
    rows_most, columns_most = ref.shape
    for columns in range(columns_most, 0, -128):
        rows = count // columns
        if count % columns == 0 and rows % 16 == 0 and rows <= rows_most:
            await_bytes(ref.at[pl.ds(0, rows), pl.ds(0, columns)], sem)
            return
    raise ValueError(count)


def rows_of(start, size):
    return pl.ds(pl.multiple_of(start, 16), size)


def cols_of(start, size):
    return pl.ds(pl.multiple_of(start, 128), size)


class Gather:
    def __init__(self, place, shard, whole, start, rows, from_eighth, groups, send, recv):
        self.place, self.shard, self.whole = place, shard, whole
        self.start, self.rows, self.send, self.recv = start, rows, send, recv
        self.total, columns = shard.shape
        half = columns // 2
        self.part = part = rows // 2
        self.col_0 = place.c * half + half * from_eighth // 8
        self.row_q = start + place.x * part
        self.row_o = start + part - place.x * part
        self.arriving, self.leaving = [0] * 6, 0
        self.groups, at = {}, 0
        for way, eighths in groups:
            self.groups[way] = (at, half * eighths // 8)
            at += half * eighths // 8
        self.wide = at

    def view(self, bits, row, rows, from_col, columns):
        block = flip(self.place.f, bits) * self.total
        return self.whole.at[rows_of(block + row, rows), cols_of(self.col_0 + from_col, columns)]

    def pass_on(self, bits, row, rows, group, leg, peer):
        from_col, columns = group
        view = self.view(bits, row, rows, from_col, columns)
        push(view, view, self.send, self.recv.at[leg or 0], self.place.peer(*peer))
        if leg is not None:
            self.arriving[leg] += rows * columns
            self.leaving += rows * columns

    def pass_own(self, row, rows, group, leg, peer):
        from_col, columns = group
        source = self.shard.at[rows_of(row, rows), cols_of(self.col_0 + from_col, columns)]
        push(source, self.view(0, row, rows, from_col, columns), self.send, self.recv.at[leg], self.place.peer(*peer))
        self.arriving[leg] += rows * columns
        self.leaving += rows * columns

    def arrive(self, leg):
        await_count(self.whole, self.arriving[leg], self.recv.at[leg])

    def first(self):
        pltpu.make_async_copy(
            self.shard.at[pl.ds(self.start, self.rows), cols_of(self.col_0, self.wide)],
            self.view(0, self.start, self.rows, 0, self.wide),
            self.recv.at[0],
        ).start()
        self.arriving[0] += self.rows * self.wide
        everything = (0, self.wide)

        @pl.when(self.place.inner)
        def _():
            self.pass_own(self.row_q, self.part, everything, 0, (6, 0))

        self.pass_own(self.row_q, self.part, everything, 4, (4, 0))
        self.pass_own(self.row_q, self.part, everything, 0, (2, 0))

    def relay(self):
        self.arrive(4)

        @pl.when(self.place.inner)
        def _():
            self.pass_on(4, self.row_q, self.part, (0, self.wide), None, (2, 0))

    def own(self):
        for way, group in self.groups.items():
            if way == ZXY:
                self.pass_own(self.start, self.rows, group, 5, (1, 0))
            else:
                self.pass_own(self.row_q, self.part, group, 5, (1, 0))

    def beside(self):
        self.arrive(5)
        if YZX in self.groups:
            for bits in (6, 4, 2):
                self.pass_on(1, self.row_q, self.part, self.groups[YZX], 1, (bits, 0))
            self.pass_on(1, self.row_q, self.part, self.groups[YZX], 1, (0, 2))

    def one(self):
        self.arrive(0)
        for way, group in self.groups.items():
            for bits in (2, 4, 6):
                if way != YZX:
                    self.pass_on(bits, self.row_q, self.part, group, 1, (1, 0))
                self.pass_on(bits, self.row_q, self.part, group, 1, (0, 2))

    def two(self):
        self.arrive(1)
        for way, group in self.groups.items():
            if way == ZXY:
                for bits in (2, 4, 6):
                    self.pass_on(bits, self.row_o, self.part, group, 2, (1, 0))
            else:
                for bits in (1, 3, 5, 7) if way == ZYX else (3, 5, 7):
                    self.pass_on(bits, self.row_q, self.part, group, 2, (0, 2))

    def three(self):
        self.arrive(2)
        for bits in range(8):
            self.pass_on(bits, self.start, self.rows, (0, self.wide), 3, (0, 1))

    def four(self):
        self.arrive(3)

    def sent(self):
        block = self.part * self.wide

        @pl.when(self.place.inner)
        def _():
            await_count(self.whole, self.leaving + block, self.send)

        @pl.when(jnp.logical_not(self.place.inner))
        def _():
            await_count(self.whole, self.leaving - block, self.send)


def chunk_of(rows, columns):
    best = 16
    for chunk in range(16, rows + 1, 16):
        if rows % chunk == 0 and chunk * columns <= 16384:
            best = chunk
    return best


def add_blocks(blocks, rows, columns, target, source):
    chunk = chunk_of(rows, columns)
    each = rows // chunk

    def step(index, carry):
        block, start = index // each, pl.multiple_of((index % each) * chunk, 16)
        into, more = target(block, start, chunk), source(block, start, chunk)
        into[...] = into[...] + more[...]
        return carry

    lax.fori_loop(0, blocks * each, step, 0)


class Scatter:
    def __init__(self, place, grad, room, out, start, rows, wide_a, send, recv):
        self.place, self.grad, self.out = place, grad, out
        self.start, self.rows, self.wide_a = start, rows, wide_a
        self.send, self.recv = send, recv
        total, columns = room.shape
        self.total = total = total // 8
        self.half = half = columns // 2
        self.wide_b = wide_b = half - wide_a
        self.part = part = rows // 2
        self.room = room
        self.from_core = room.at[:, pl.ds(0, half)]

        def landing(row, count, col, width):
            return room.at[pl.ds(row, count), pl.ds(half + col, width)] if width else None

        self.a_x = landing(4 * start, 4 * rows, 0, wide_a)
        self.a_y = landing(4 * total + 2 * start, 2 * rows, 0, wide_a)
        self.a_z = landing(6 * total + 3 * start // 2, 3 * part, 0, wide_a)
        self.b_y = landing(4 * start, 4 * rows, wide_a, wide_b)
        self.b_z = landing(4 * total + 3 * start, 3 * rows, wide_a, wide_b)
        self.b_x = landing(7 * total + start // 2, part, wide_a, wide_b)
        self.col_0 = place.c * half
        self.row_q = start + place.x * part
        self.row_o = start + part - place.x * part

    def push(self, source, target, leg, device):
        push(source, target, self.send, self.recv.at[leg], device)

    def zero(self):
        other = cols_of(self.half - self.col_0, self.half)
        for block in range(8):
            rows = pl.ds(block * self.total + self.start, self.rows)
            self.push(self.grad.at[rows, other], self.from_core.at[rows], 5, self.place.peer(0, 1))

    def core(self, row, rows, from_col, columns):
        return self.from_core.at[rows_of(row, rows), pl.ds(from_col, columns)]

    def mine(self, row, rows, from_col, columns):
        return self.core(self.place.f * self.total + row, rows, from_col, columns)

    def one(self):
        place, total, part, rows = self.place, self.total, self.part, self.rows
        await_count(self.room, 8 * rows * self.half, self.recv.at[5])
        add_blocks(
            8,
            rows,
            self.half,
            lambda b, s, n: self.core(b * total + self.start + s, n, 0, self.half),
            lambda b, s, n: self.grad.at[rows_of(b * total + self.start + s, n), cols_of(self.col_0, self.half)],
        )
        await_count(self.room, 8 * rows * self.half, self.send)
        if self.wide_a:
            for block in range(8):
                self.push(
                    self.core(block * total + self.row_o, part, 0, self.wide_a),
                    self.a_x.at[pl.ds(block * part, part)],
                    0,
                    place.peer(0, 2),
                )
        if self.wide_b:
            for level in range(4):
                self.push(
                    self.core((2 * level + 1 - place.y) * total + self.start, rows, self.wide_a, self.wide_b),
                    self.b_y.at[pl.ds(level * rows, rows)],
                    0,
                    place.peer(1, 0),
                )

    def two(self):
        place, total, part, rows = self.place, self.total, self.part, self.rows
        await_count(self.room, 4 * rows * self.half, self.recv.at[0])
        if self.wide_a:
            add_blocks(
                8,
                part,
                self.wide_a,
                lambda b, s, n: self.core(b * total + self.row_q + s, n, 0, self.wide_a),
                lambda b, s, n: self.a_x.at[rows_of(b * part + s, n)],
            )
            for level in range(4):
                self.push(
                    self.core((2 * level + 1 - place.y) * total + self.row_q, part, 0, self.wide_a),
                    self.a_y.at[pl.ds(level * part, part)],
                    1,
                    place.peer(1, 0),
                )
        if self.wide_b:
            add_blocks(
                4,
                rows,
                self.wide_b,
                lambda b, s, n: self.core((2 * b + place.y) * total + self.start + s, n, self.wide_a, self.wide_b),
                lambda b, s, n: self.b_y.at[rows_of(b * rows + s, n)],
            )
            for slot, bits in enumerate((6, 4, 2)):
                self.push(
                    self.core(flip(place.f, bits) * total + self.start, rows, self.wide_a, self.wide_b),
                    self.b_z.at[pl.ds(slot * rows, rows)],
                    1,
                    place.peer(bits, 0),
                )

    def sum_four(self, row, rows, col, wide, landed, store):
        chunk = chunk_of(rows, wide)

        def step(index, carry):
            start = pl.multiple_of(index * chunk, 16)
            total = self.mine(row + start, chunk, col, wide)[...].astype(F32)
            for slot in range(3):
                total = total + landed[rows_of(slot * rows + start, chunk)].astype(F32)
            store(start, chunk, total.astype(BF16))
            return carry

        lax.fori_loop(0, rows // chunk, step, 0)

    def three(self):
        place, total, part, rows = self.place, self.total, self.part, self.rows
        await_count(self.room, 2 * rows * self.wide_a + 3 * rows * self.wide_b, self.recv.at[1])
        if self.wide_a:
            add_blocks(
                4,
                part,
                self.wide_a,
                lambda b, s, n: self.core((2 * b + place.y) * total + self.row_q + s, n, 0, self.wide_a),
                lambda b, s, n: self.a_y.at[rows_of(b * part + s, n)],
            )
            for slot, bits in enumerate((6, 4, 2)):
                self.push(
                    self.core(flip(place.f, bits) * total + self.row_q, part, 0, self.wide_a),
                    self.a_z.at[pl.ds(slot * part, part)],
                    2,
                    place.peer(bits, 0),
                )
        if self.wide_b:

            def keep(start, chunk, value):
                self.mine(self.start + start, chunk, self.wide_a, self.wide_b)[...] = value

            self.sum_four(self.start, rows, self.wide_a, self.wide_b, self.b_z, keep)
            self.push(self.mine(self.row_o, part, self.wide_a, self.wide_b), self.b_x, 2, place.peer(0, 2))

    def four(self):
        place, part = self.place, self.part
        await_count(self.room, 3 * part * self.wide_a + part * self.wide_b, self.recv.at[2])
        if self.wide_a:

            def keep(start, chunk, value):
                self.out[rows_of(self.row_q + start, chunk), cols_of(self.col_0, self.wide_a)] = value

            self.sum_four(self.row_q, part, 0, self.wide_a, self.a_z, keep)
        if self.wide_b:
            chunk = chunk_of(part, self.wide_b)

            def step(index, carry):
                start = pl.multiple_of(index * chunk, 16)
                total = self.mine(self.row_q + start, chunk, self.wide_a, self.wide_b)[...].astype(F32)
                total = total + self.b_x[rows_of(start, chunk)].astype(F32)
                columns = cols_of(self.col_0 + self.wide_a, self.wide_b)
                self.out[rows_of(self.row_q + start, chunk), columns] = total.astype(BF16)
                return carry

            lax.fori_loop(0, part // chunk, step, 0)
        block = self.out.at[rows_of(self.row_q, part), cols_of(self.col_0, self.half)]
        self.push(block, block, 3, place.peer(0, 2))

    def five(self):
        await_bytes(self.out.at[pl.ds(0, self.part), pl.ds(0, self.half)], self.recv.at[3])
        block = self.out.at[pl.ds(self.start, self.rows), cols_of(self.col_0, self.half)]
        self.push(block, block, 4, self.place.peer(0, 1))

    def six(self):
        await_bytes(self.out.at[pl.ds(0, self.rows), pl.ds(0, self.half)], self.recv.at[4])

    def sent(self):
        await_count(self.room, 18 * self.part * self.half, self.send)


def mm(left, right):
    return jnp.dot(left, right, preferred_element_type=F32)


def mm_nt(left, right):
    return lax.dot_general(left, right, (((1,), (1,)), ((), ())), preferred_element_type=F32)


def mm_tn(left, right):
    return lax.dot_general(left, right, (((0,), (0,)), ((), ())), preferred_element_type=F32)


def loop(count, step):
    def body_of(index, carry):
        step(index)
        return carry

    lax.fori_loop(0, count, body_of, 0)


def at_block(index, size):
    if isinstance(index, int):
        return pl.ds(index * size, size)
    return pl.ds(pl.multiple_of(index * size, size), size)


def slope_of(values):
    gate = jax.nn.sigmoid(values)
    return gate * (1.0 + values * (1.0 - gate))


def fold(values):
    total = values[0:8]
    for start in range(8, values.shape[0], 8):
        total = total + values[start : start + 8]
    return total


def column_sums(count, width, terms):
    def step(index, carry):
        start = pl.multiple_of(index * CHUNK, CHUNK)
        return tuple(total + fold(one) for total, one in zip(carry, terms(start)))

    zero = jnp.zeros((8, LANES), F32)
    totals = lax.fori_loop(0, count, step, (zero,) * width)
    return [jnp.sum(one, axis=0, keepdims=True) for one in totals]


class Vectors:
    def __init__(self, ref):
        self.ref, self.used = ref, 0

    def put(self, row):
        at = self.used
        self.used += 1
        self.ref[at : at + 1, :] = row
        return at

    def get(self, at):
        return self.ref[at : at + 1, :]


class Totals:
    def __init__(self, place, short, long, tot, send, recv):
        self.place, self.short, self.long, self.tot, self.send, self.recv = place, short, long, tot, send, recv
        self.began = 0

    def start(self, rows_of_values):
        whole = not isinstance(rows_of_values, list)
        one = Total(self, 8 if whole else 4 * len(rows_of_values))
        own = one.slot(self.place.c)
        if whole:
            own[...] = rows_of_values
        for n, row in enumerate([] if whole else rows_of_values):
            for k in range(4):
                own[4 * n + k : 4 * n + k + 1, :] = row[:, 128 * k : 128 * (k + 1)]
        one.spread(self.place.c, ((0, 1),), 0)
        return one

    def row(self, index):
        at = 4 * index
        return jnp.concatenate([self.tot[at + k : at + k + 1, :] for k in range(4)], axis=1)

    def wide(self, at):
        return jnp.concatenate([self.tot[at : at + 1, :]] * 4, axis=1)


class Total:
    def __init__(self, all_of_them, rows):
        self.all, self.place, self.rows = all_of_them, all_of_them.place, rows
        self.is_long = rows > 8
        self.set = SHORT_SETS
        if not self.is_long:
            self.set = all_of_them.began % SHORT_SETS
            all_of_them.began += 1

    def slots(self, at, count):
        if self.is_long:
            return self.all.long.at[pl.ds(at, count), pl.ds(0, self.rows)]
        return self.all.short.at[self.set, pl.ds(at, count), pl.ds(0, self.rows)]

    def slot(self, at):
        if self.is_long:
            return self.all.long.at[at, pl.ds(0, self.rows)]
        return self.all.short.at[self.set, at, pl.ds(0, self.rows)]

    def spread(self, at, peers, phase):
        own = self.slot(at)
        for bits in peers:
            push(own, own, self.all.send.at[self.set], self.all.recv.at[2 * self.set + phase], self.place.peer(*bits))

    def gather(self, at, count, peers, phase):
        await_bytes(self.slots(at, peers), self.all.recv.at[2 * self.set + phase])
        total = self.slot(at)[...]
        for index in range(at + 1, at + count):
            total = total + self.slot(index)[...]
        return total

    def middle(self):
        place = self.place
        total = self.gather(0, 2, 1, 0)
        if self.is_long:
            self.slot(2 + 2 * place.y + place.x)[...] = total
            self.spread(2 + 2 * place.y + place.x, ((1, 2), (1, 0), (0, 2)), 1)
        else:
            self.slot(2 + 2 * place.f + place.x)[...] = total
            self.spread(2 + 2 * place.f + place.x, CHIP_PEERS, 1)

    def late(self):
        if self.is_long:
            self.slot(6 + self.place.z)[...] = self.gather(2, 4, 3, 1)
            self.spread(6 + self.place.z, ((6, 0), (4, 0), (2, 0)), 2)

    def end(self):
        if self.is_long:
            self.all.tot[0 : self.rows, :] = self.gather(6, 4, 3, 2)
        else:
            self.all.tot[0 : self.rows, :] = self.gather(2, 16, 15, 1)
        await_bytes(self.slots(0, 7 if self.is_long else 16), self.all.send.at[self.set])


def step_kernel(
    img_hbm,
    cot_hbm,
    sides,
    keep,
    widths,
    norm_in_a,
    norm_mid_a,
    norm_out_a,
    norm_proj_a,
    norm_in_b,
    norm_mid_b,
    norm_out_b,
    sh_in_a,
    sh_mid_a,
    sh_out_a,
    sh_proj_a,
    sh_in_b,
    sh_mid_b,
    sh_out_b,
    result_hbm,
    images_hbm,
    own_hbm_in_a,
    own_hbm_mid_a,
    own_hbm_out_a,
    own_hbm_proj_a,
    own_hbm_in_b,
    own_hbm_mid_b,
    own_hbm_out_b,
    out_hbm_in_a,
    out_hbm_mid_a,
    out_hbm_out_a,
    out_hbm_proj_a,
    out_hbm_in_b,
    out_hbm_mid_b,
    out_hbm_out_b,
    own_in_a,
    own_mid_a,
    own_out_a,
    own_proj_a,
    own_in_b,
    own_mid_b,
    own_out_b,
    out_in_a,
    out_mid_a,
    out_out_a,
    out_proj_a,
    out_in_b,
    out_mid_b,
    out_out_b,
    w_in_a,
    w_mid_a,
    w_out_a,
    w_proj_a,
    w_in_b,
    w_mid_b,
    w_out_b,
    raw,
    cot,
    x,
    c1,
    cols_a,
    c2,
    a2,
    c3,
    cp,
    bo,
    feed,
    d1,
    cols_b,
    d2,
    b2,
    d3,
    dz,
    dm,
    df,
    dout,
    dproj,
    g_mid,
    g_out,
    g_in,
    g_proj,
    mask_ref,
    gate_ref,
    move,
    norms,
    block_ref,
    vec_ref,
    short,
    long,
    tot,
    sums,
    io_sem,
    link_send,
    link_recv,
    ar_send,
    ar_recv,
    nb_sem,
    out_sem,
    free_sem,
):
    place = Place()
    shards = dict(zip(NAMES, (sh_in_a, sh_mid_a, sh_out_a, sh_proj_a, sh_in_b, sh_mid_b, sh_out_b)))
    wholes = dict(zip(NAMES, (w_in_a, w_mid_a, w_out_a, w_proj_a, w_in_b, w_mid_b, w_out_b)))
    outs = dict(zip(NAMES, (out_in_a, out_mid_a, out_out_a, out_proj_a, out_in_b, out_mid_b, out_out_b)))
    owned = dict(zip(NAMES, (own_in_a, own_mid_a, own_out_a, own_proj_a, own_in_b, own_mid_b, own_out_b)))
    own_hbm = (own_hbm_in_a, own_hbm_mid_a, own_hbm_out_a, own_hbm_proj_a, own_hbm_in_b, own_hbm_mid_b, own_hbm_out_b)
    out_hbm = (out_hbm_in_a, out_hbm_mid_a, out_hbm_out_a, out_hbm_proj_a, out_hbm_in_b, out_hbm_mid_b, out_hbm_out_b)
    own_copies = [pltpu.make_async_copy(owned[n], own_hbm[i], out_sem.at[0, i]) for i, n in enumerate(NAMES)]
    out_copies = [pltpu.make_async_copy(outs[n], out_hbm[i], out_sem.at[1, i]) for i, n in enumerate(NAMES)]
    small = dict(zip(NAMES, (norm_in_a, norm_mid_a, norm_out_a, norm_proj_a, norm_in_b, norm_mid_b, norm_out_b)))
    grads = dict(mid_a=g_mid, mid_b=g_mid, out_a=g_out, out_b=g_out, in_b=g_in, proj_a=g_proj)
    grads["in_a"] = g_in.at[pl.ds(0, wholes["in_a"].shape[0])]
    todo = {}

    def token(name):
        def keep_it(function):
            todo[name] = function
            return function

        return keep_it

    def tokens(name, count, each, step):
        def some(first):
            for k in range(each):
                step(first + k)

        for part in range(count):
            todo[f"{name}.{part}"] = functools.partial(some, part * each)

    gathers, scatters, at, going = {}, {}, 0, 0
    left = {name: len(WAYS_OUT[name]) for name in NAMES}

    def finish_piece(name, piece):
        piece.six()
        left[name] -= 1
        if not left[name]:
            out_copies[NAMES.index(name)].start()

    def tell(name):
        for bits in LINK_PEERS:
            sem = free_sem.at[NAMES.index(name)]
            pl.semaphore_signal(sem, inc=1, device_id=place.peer(*bits), device_id_type=BY_MESH)

    def send_core(name, n):
        if n == 0:
            pl.semaphore_wait(free_sem.at[NAMES.index(name)], len(LINK_PEERS))
        scatters[name, n].zero()

    for name in NAMES:
        for n, (start, rows, from_eighth, ways) in enumerate(WAYS_IN[name]):
            sems = link_send.at[at], link_recv.at[at]
            g = gathers[name, n] = Gather(
                place, shards[name], wholes[name], start, rows, from_eighth, ways, *sems
            )
            at += 1
            key = f"{name}.{n}"
            todo["z." + key], todo["o." + key], todo["L1." + key] = g.first, g.own, g.one
            todo["R." + key], todo["B." + key] = g.relay, g.beside
            todo["L2." + key], todo["L3." + key] = g.two, g.three
        eighth = shards[name].shape[1] // 16
        for n, (start, rows, wide) in enumerate(WAYS_OUT[name]):
            sems = link_send.at[going], link_recv.at[going]
            s = Scatter(place, grads[name], wholes[name], outs[name], start, rows, wide * eighth, *sems)
            scatters[name, n] = s
            going += 1
            key = f"{name}.{n}"
            todo["S0." + key], todo["S1." + key] = functools.partial(send_core, name, n), s.one
            todo["S2." + key], todo["S3." + key], todo["S4." + key] = s.two, s.three, s.four
            todo["S5." + key] = s.five
            todo["S6." + key] = functools.partial(finish_piece, name, s)
        def arrived(some):
            for one in some:
                one.four()

        mine = [gathers[name, n] for n in range(len(WAYS_IN[name]))]
        if name == "out_b":
            for n, one in enumerate(mine):
                todo[f"W.{name}.{n}"] = one.four
        else:
            todo["W." + name] = functools.partial(arrived, mine)

    vec = Vectors(vec_ref)
    totals = Totals(place, short, long, tot, ar_send, ar_recv)
    state, scales, params = {}, {}, {}
    sums_of = {}

    def begin(n, values):
        sums_of[n] = totals.start(values)

    for n in range(1, 20):
        todo[f"A{n}m"] = lambda n=n: sums_of[n].middle()
        todo[f"A{n}l"] = lambda n=n: sums_of[n].late()

    image_copy = pltpu.make_async_copy(img_hbm, raw, io_sem.at[0])
    cot_copy = pltpu.make_async_copy(cot_hbm, cot, io_sem.at[1])
    result_copy = pltpu.make_async_copy(cot, result_hbm, io_sem.at[2])
    grad_copy = pltpu.make_async_copy(raw, images_hbm, io_sem.at[3])

    @token("enter")
    def _():
        image_copy.start()
        cot_copy.start()
        odd = (place.f % 2).astype(F32)
        block_ref[...] = jnp.zeros_like(block_ref)
        at = 0
        for name in NAMES:
            values = small[name][...].astype(F32)
            if values.shape[1] < 128:
                move[0:8, 0:128] = jnp.zeros((8, 128), F32)
                move[0:2, 0 : values.shape[1]] = values
                plain = move[0:8, 0:128]
                values = (plain + (pltpu.roll(plain, 64, 1) - plain) * odd)[0:2]
            for lane in range(0, values.shape[1], 128):
                block_ref[at : at + 1, :] = values[0:1, lane : lane + 128]
                block_ref[at + 10 : at + 11, :] = values[1:2, lane : lane + 128]
                at += 1
        norms[place.f] = block_ref[...]
        enter(place, ((0, 1),) + CHIP_PEERS)
        for bits in (7, 6, 5, 4, 3, 2, 1):
            push(block_ref, norms.at[place.f], nb_sem.at[0], nb_sem.at[1], place.peer(bits, 0))

    @token("prep")
    def _():
        pixel = lax.broadcasted_iota(jnp.int32, (BLOCK, 128), 0)
        slot = pixel % 4

        def by_slot(values):
            return jnp.where(slot == 0, values[0], jnp.where(slot == 1, values[1], jnp.where(slot == 2, values[2], values[3])))

        half = by_slot([sides[i] // 2 for i in range(4)])
        inside = ((pixel // 4) % 8 < half) & (pixel // 32 < half)
        mask_ref[...] = jnp.where(inside, 1.0, 0.0).astype(F32)
        gate_ref[...] = by_slot([keep[i] for i in range(4)]).astype(F32)
        move[...] = jnp.zeros_like(move)
        image_copy.wait()

        def plane_rows(row):
            mask = jnp.concatenate([mask_ref[at_block(row, CHUNK), :]] * (x.shape[1] // 128), axis=1)
            for row_par in range(2):
                for col_par in range(2):
                    for col in range(SIDE):
                        move[4 * col : 4 * col + 4, :] = raw[2 * row + row_par, 2 * col + col_par].astype(F32)
                    start = (2 * row_par + col_par) * BLOCK + row * CHUNK
                    x[pl.ds(pl.multiple_of(start, CHUNK), CHUNK), :] = (move[...] * mask).astype(BF16)

        loop(SIDE, plane_rows)
        for p in range(4):
            x[(p + 1) * BLOCK - CHUNK : (p + 1) * BLOCK, :] = jnp.zeros((CHUNK, x.shape[1]), BF16)

    @token("norms")
    def _():
        await_bytes(norms.at[pl.ds(0, 7)], nb_sem.at[1])
        await_bytes(norms.at[pl.ds(0, 7)], nb_sem.at[0])

        def narrow_row(at):
            pieces = [norms[2 * k, at : at + 1, :] + norms[2 * k + 1, at : at + 1, :] for k in range(4)]
            return vec.put(jnp.concatenate(pieces, axis=1))

        def wide_rows(at):
            return [
                vec.put(
                    jnp.concatenate(
                        [norms[2 * j + k // 2, at + k % 2 : at + k % 2 + 1, :] for k in range(4)], axis=1
                    )
                )
                for j in range(4)
            ]

        params["in_a"] = ([narrow_row(0)], [narrow_row(10)])
        params["mid_a"] = ([narrow_row(1)], [narrow_row(11)])
        params["out_a"] = (wide_rows(2), wide_rows(12))
        params["proj_a"] = (wide_rows(4), wide_rows(14))
        params["in_b"] = ([narrow_row(6)], [narrow_row(16)])
        params["mid_b"] = ([narrow_row(7)], [narrow_row(17)])
        params["out_b"] = (wide_rows(8), wide_rows(18))
        lanes = lax.broadcasted_iota(jnp.int32, (1, LANES), 1)
        state["chan_a"] = vec.put(jnp.where(lanes < widths[0], 1.0, 0.0).astype(F32))
        state["chan_b"] = vec.put(jnp.where(lanes < widths[1], 1.0, 0.0).astype(F32))

    def wide_of(ref, start, size=CHUNK):
        return jnp.concatenate([ref[pl.ds(start, size), :]] * 4, axis=1)

    def mask_at(start):
        return wide_of(mask_ref, start)

    def gate_at(start):
        return wide_of(gate_ref, start)

    def set_norm(name, block, first_row, inverse, chan):
        inverse = vec.get(state[inverse])
        average = totals.row(first_row) * inverse
        rstd = lax.rsqrt(totals.row(first_row + 1) * inverse - average * average + EPSILON)
        gain, shift = (vec.get(rows[block]) for rows in params[name])
        keep_lanes = 1.0 if chan is None else vec.get(state[chan])
        by = gain * rstd
        scales[name, block] = dict(
            rstd=vec.put(rstd),
            off=vec.put(-average * rstd),
            by=vec.put(by),
            mul=vec.put(by * keep_lanes),
            add=vec.put((shift - average * by) * keep_lanes),
        )

    def normed(name, block, values):
        s = scales[name, block]
        return values * vec.get(s["mul"]) + vec.get(s["add"])

    def hat(name, block, values):
        s = scales[name, block]
        return values * vec.get(s["rstd"]) + vec.get(s["off"])

    def set_back(name, block, shift_row, gain_row):
        s = scales[name, block]
        inverse = vec.get(state["inv_in" if name == "in_a" else "inv_out"])
        by = vec.get(s["by"])
        pull = by * totals.row(gain_row) * inverse
        s["back_add"] = vec.put(by * totals.row(shift_row) * inverse + pull * vec.get(s["off"]))
        s["back_mul"] = vec.put(pull * vec.get(s["rstd"]))

    def back(name, block, grad, values):
        s = scales[name, block]
        return grad * vec.get(s["by"]) - vec.get(s["back_add"]) - values * vec.get(s["back_mul"])

    def square_terms(ref):
        def terms(start):
            values = ref[pl.ds(start, CHUNK), :]
            return values, values * values

        return terms

    def masked_terms(ref):
        def terms(start):
            values = ref[pl.ds(start, CHUNK), :]
            kept = values * mask_at(start)
            return kept, kept * values

        return terms

    def lane_row(at, lane):
        return vec_ref[at : at + 1, at_block(lane, 128)]

    def add_up(out, count, left, right, product=mm):
        total = product(left(0), right(0))
        for k in range(1, count):
            total = total + product(left(k), right(k))
        out[...] = total

    @token("A1s")
    def _():
        for p in range(4):
            c1[at_block(p, BLOCK), :] = mm(x[at_block(p, BLOCK), :], w_in_a[...])
        begin(1, column_sums(32, 2, square_terms(c1)))

    @token("A19s")
    def _():
        side = [sides[i] for i in range(4)]
        count_in = sum(s * s for s in side).astype(F32)
        count_out = sum((s // 2) * (s // 2) for s in side).astype(F32)
        at = lax.broadcasted_iota(jnp.int32, (8, 128), 0)
        begin(19, jnp.where(at == 0, count_in, jnp.where(at == 1, count_out, 0.0)))

    @token("A19e")
    def _():
        sums_of[19].end()
        state["inv_in"] = vec.put(1.0 / totals.wide(0))
        state["inv_out"] = vec.put(1.0 / totals.wide(1))

    @token("A1e")
    def _():
        sums_of[1].end()
        set_norm("in_a", 0, 0, "inv_in", "chan_a")
        s = scales["in_a", 0]

        def act_a(lane):
            for row_par in range(2):
                for col_par in range(2):
                    p = 2 * row_par + col_par
                    values = c1[p * BLOCK : (p + 1) * BLOCK, at_block(lane, 128)]
                    scaled = values * lane_row(s["mul"], lane) + lane_row(s["add"], lane)
                    act = scaled * jax.nn.sigmoid(scaled) * mask_ref[...]
                    for t, (u, v) in enumerate(TAPS):
                        if (u != 1) != bool(row_par) or (v != 1) != bool(col_par):
                            continue
                        shift = (32 if u == 0 else 0) + (4 if v == 0 else 0)
                        moved = pltpu.roll(act, shift, 0) if shift else act
                        cols_a[:, pl.ds(pl.multiple_of(t * LANES + lane * 128, 128), 128)] = moved.astype(BF16)

        loop(4, act_a)

    def conv_mid(out, cols, weight):
        add_up(out, 3, lambda k: cols[:, at_block(k, 1536)], lambda k: weight[at_block(k, 1536), :])

    def act_mid(act_ref, ref, name):
        def step(index):
            start = pl.multiple_of(index * CHUNK, CHUNK)
            scaled = normed(name, 0, ref[pl.ds(start, CHUNK), :])
            act_ref[pl.ds(start, CHUNK), :] = (scaled * jax.nn.sigmoid(scaled) * mask_at(start)).astype(BF16)

        loop(BLOCK // CHUNK, step)

    @token("A2s")
    def _():
        conv_mid(c2, cols_a, w_mid_a)
        begin(2, column_sums(8, 2, masked_terms(c2)))

    @token("A2e")
    def _():
        sums_of[2].end()
        set_norm("mid_a", 0, 0, "inv_out", "chan_a")
        act_mid(a2, c2, "mid_a")

    @token("proj")
    def _():
        def project(j):
            cp[at_block(j, BLOCK), :] = mm(x[0:BLOCK, :], w_proj_a[:, at_block(j, LANES)])

        loop(4, project)

    def blocked(ref, j):
        return square_terms(ref.at[pl.ds(j * BLOCK, BLOCK)])

    @token("A3s")
    def _():
        for j in range(4):
            c3[at_block(j, BLOCK), :] = mm(a2[...], w_out_a[:, at_block(j, LANES)])
        begin(3, [row for ref in (c3, cp) for j in range(4) for row in column_sums(8, 2, blocked(ref, j))])

    @token("A3e")
    def _():
        sums_of[3].end()
        for j in range(4):
            set_norm("out_a", j, 2 * j, "inv_out", None)
            set_norm("proj_a", j, 8 + 2 * j, "inv_out", None)
        for j in range(4):

            def join_a(index, j=j):
                start = pl.multiple_of(index * CHUNK, CHUNK)
                rows = pl.ds(j * BLOCK + start, CHUNK)
                pre = normed("out_a", j, c3[rows, :]) + normed("proj_a", j, cp[rows, :])
                out = pre * jax.nn.sigmoid(pre) * mask_at(start)
                bo[rows, :] = out
                feed[pl.ds(start, CHUNK), pl.ds(j * LANES, LANES)] = out.astype(BF16)

            loop(BLOCK // CHUNK, join_a)

    @token("A4s")
    def _():
        add_up(d1, 4, lambda k: feed[:, at_block(k, LANES)], lambda k: w_in_b[at_block(k, LANES), :])
        begin(4, column_sums(8, 2, square_terms(d1)))

    @token("A4e")
    def _():
        sums_of[4].end()
        set_norm("in_b", 0, 0, "inv_out", "chan_b")
        s = scales["in_b", 0]

        def act_b(lane):
            scaled = d1[:, at_block(lane, 128)] * lane_row(s["mul"], lane) + lane_row(s["add"], lane)
            act = scaled * jax.nn.sigmoid(scaled) * mask_ref[...]
            for t, (u, v) in enumerate(TAPS):
                shift = (-(32 * (u - 1) + 4 * (v - 1))) % BLOCK
                moved = pltpu.roll(act, shift, 0) if shift else act
                cols_b[:, pl.ds(pl.multiple_of(t * LANES + lane * 128, 128), 128)] = moved.astype(BF16)

        loop(4, act_b)

    @token("A5s")
    def _():
        conv_mid(d2, cols_b, w_mid_b)
        begin(5, column_sums(8, 2, masked_terms(d2)))

    @token("A5e")
    def _():
        sums_of[5].end()
        set_norm("mid_b", 0, 0, "inv_out", "chan_b")
        act_mid(b2, d2, "mid_b")

    PAIRS = ((0, 2), (1, 3))
    FORTH = {6: 0, 13: 2, 15: 1, 16: 3}
    BACK = {7: 0, 14: 2, 17: 1, 18: 3}

    def expand_b(n, j):
        d3[at_block(j, BLOCK), :] = mm(b2[...], w_out_b[:, at_block(j, LANES)])
        begin(n, column_sums(8, 2, blocked(d3, j)))

    def set_out_b(n, j):
        sums_of[n].end()
        set_norm("out_b", j, 0, "inv_out", None)

    def finish_b(n, j):
        if n == 7:
            cot_copy.wait()
        lanes = pl.ds(j * LANES, LANES)

        def finish(start):
            rows = pl.ds(j * BLOCK + start, CHUNK)
            row = start // CHUNK
            for col in range(SIDE):
                move[4 * col : 4 * col + 4, 0:LANES] = cot[row, col, :, lanes].astype(F32)
            mask, gate, hidden = mask_at(start), gate_at(start), d3[rows, :]
            pre = bo[rows, :] + gate * normed("out_b", j, hidden)
            part = jax.nn.sigmoid(pre)
            grad = move[:, 0:LANES] * mask * (part * (1.0 + pre * (1.0 - part)))
            move[:, LANES : 2 * LANES] = pre * part * mask
            for col in range(SIDE):
                cot[row, col, :, lanes] = move[4 * col : 4 * col + 4, LANES : 2 * LANES].astype(BF16)
            bo[rows, :] = grad
            grad = grad * gate
            return grad, grad * hat("out_b", j, hidden)

        values = column_sums(SIDE, 2, finish)
        bo[(j + 1) * BLOCK - CHUNK : (j + 1) * BLOCK, :] = jnp.zeros((CHUNK, LANES), F32)
        begin(n, values)
        if n == 18:
            result_copy.start()

    for n, j in FORTH.items():
        todo[f"A{n}s"], todo[f"A{n}e"] = functools.partial(expand_b, n, j), functools.partial(set_out_b, n, j)
    for n, j in BACK.items():
        todo[f"A{n}s"] = functools.partial(finish_b, n, j)

    @token("sent")
    def _():
        for one in gathers.values():
            one.sent()

    def keep_sums(n, at):
        rows = sums_of[n].rows
        sums[at : at + rows, :] = tot[0:rows, :]

    def low_out_b(n, j):
        sums_of[n].end()
        keep_sums(n, 16 * (j % 2) + 8 * (j // 2))
        set_back("out_b", j, 0, 1)

        def step(index):
            start = pl.multiple_of(index * CHUNK, CHUNK)
            rows = pl.ds(j * BLOCK + start, CHUNK)
            grad = back("out_b", j, bo[rows, :] * gate_at(start), d3[rows, :]) * mask_at(start)
            dout[pl.ds(start, CHUNK), pl.ds(j * LANES, LANES)] = grad.astype(BF16)

        loop(BLOCK // CHUNK, step)

    for n, j in BACK.items():
        todo[f"A{n}e"] = functools.partial(low_out_b, n, j)

    def through_out(weight):
        add_up(dz, 4, lambda k: dout[:, at_block(k, LANES)], lambda k: weight[:, at_block(k, LANES)], mm_nt)

    def slope_terms(grad_ref, ref, name, chan):
        def terms(start):
            rows = pl.ds(start, CHUNK)
            hidden = ref[rows, :]
            mask = mask_at(pl.multiple_of(start % BLOCK, CHUNK) if grad_ref.shape[0] > BLOCK else start)
            grad = grad_ref[rows, :] * mask * vec.get(state[chan]) * slope_of(normed(name, 0, hidden))
            grad_ref[rows, :] = grad
            return grad, grad * hat(name, 0, hidden)

        return terms

    def through_pair(pair):
        return [mm_nt(dout[:, at_block(j, LANES)], w_out_b[:, at_block(j, LANES)]) for j in pair]

    @token("D8")
    def _():
        first, second = through_pair(PAIRS[0])
        dz[...] = first + second

    @token("A8s")
    def _():
        first, second = through_pair(PAIRS[1])
        dz[...] += first + second
        tell("out_b")
        begin(8, column_sums(8, 2, slope_terms(dz, d2, "mid_b", "chan_b")))

    def grad_out(act_ref, j):
        g_out[:, at_block(j, LANES)] = mm_tn(act_ref[...], dout[:, at_block(j, LANES)]).astype(BF16)

    tokens("g.out_b", 2, 2, lambda k: grad_out(b2, 2 * (k % 2) + k // 2))

    @token("A8e")
    def _():
        sums_of[8].end()
        keep_sums(8, 32)
        set_back("mid_b", 0, 0, 1)

    def low_mid(name, ref, shifts):
        s = scales[name, 0]

        def step(lane):
            lanes = at_block(lane, 128)
            grad = (
                dz[:, lanes] * lane_row(s["by"], lane)
                - lane_row(s["back_add"], lane)
                - ref[:, lanes] * lane_row(s["back_mul"], lane)
            ) * mask_ref[...]
            dm[:, lanes] = grad.astype(BF16)
            for k, shift in enumerate(shifts):
                moved = pltpu.roll(grad, shift, 0) if shift else grad
                g_mid[k * BLOCK : (k + 1) * BLOCK, lanes] = moved.astype(BF16)

        loop(4, step)

    @token("A9s")
    def _():
        low_mid("mid_b", d2, [(32 * (u - 1) + 4 * (v - 1)) % BLOCK for u, v in TAPS])
        add_up(dz, 9, lambda t: g_mid[at_block(t, BLOCK), :], lambda t: w_mid_b[at_block(t, LANES), :], mm_nt)
        tell("mid_b")
        begin(9, column_sums(8, 2, slope_terms(dz, d1, "in_b", "chan_b")))

    def grad_mid(cols, t):
        g_mid[at_block(t, LANES), :] = mm_tn(cols[:, at_block(t, LANES)], dm[...]).astype(BF16)

    tokens("g.mid_b", 3, 3, lambda t: grad_mid(cols_b, t))

    @token("A9e")
    def _():
        sums_of[9].end()
        keep_sums(9, 40)
        set_back("in_b", 0, 0, 1)

    @token("A10s")
    def _():
        def low_first_b(index):
            start = pl.multiple_of(index * CHUNK, CHUNK)
            rows = pl.ds(start, CHUNK)
            df[rows, :] = (back("in_b", 0, dz[rows, :], d1[rows, :]) * mask_at(start)).astype(BF16)

        loop(BLOCK // CHUNK, low_first_b)

        for j in range(4):
            bo[at_block(j, BLOCK), :] += mm_nt(df[...], w_in_b[at_block(j, LANES), :])
        tell("in_b")
        values = []
        for j in range(4):

            def join_back(start, j=j):
                rows = pl.ds(j * BLOCK + start, CHUNK)
                left, right = c3[rows, :], cp[rows, :]
                pre = normed("out_a", j, left) + normed("proj_a", j, right)
                grad = bo[rows, :] * mask_at(start) * slope_of(pre)
                bo[rows, :] = grad
                return grad, grad * hat("out_a", j, left), grad * hat("proj_a", j, right)

            values += column_sums(8, 3, join_back)
        begin(10, values)

    def grad_in_b(j):
        g_in[at_block(j, LANES), :] = mm_tn(feed[:, at_block(j, LANES)], df[...]).astype(BF16)

    tokens("g.in_b", 2, 2, grad_in_b)

    @token("A10e")
    def _():
        sums_of[10].end()
        keep_sums(10, 48)
        for j in range(4):
            set_back("out_a", j, 3 * j, 3 * j + 1)
            set_back("proj_a", j, 3 * j, 3 * j + 2)

    @token("A11s")
    def _():
        for j in range(4):

            def low_both(index, j=j):
                start = pl.multiple_of(index * CHUNK, CHUNK)
                rows = pl.ds(j * BLOCK + start, CHUNK)
                near_rows, lanes = pl.ds(start, CHUNK), pl.ds(j * LANES, LANES)
                grad, mask = bo[rows, :], mask_at(start)
                dout[near_rows, lanes] = (back("out_a", j, grad, c3[rows, :]) * mask).astype(BF16)
                dproj[near_rows, lanes] = (back("proj_a", j, grad, cp[rows, :]) * mask).astype(BF16)

            loop(BLOCK // CHUNK, low_both)
        through_out(w_out_a)
        tell("out_a")
        begin(11, column_sums(8, 2, slope_terms(dz, c2, "mid_a", "chan_a")))

    tokens("g.out_a", 2, 2, lambda j: grad_out(a2, j))

    def grad_proj(n):
        i, j = n // 4, n % 4
        g_proj[at_block(i, LANES), at_block(j, LANES)] = mm_tn(
            x[0:BLOCK, at_block(i, LANES)], dproj[:, at_block(j, LANES)]
        ).astype(BF16)

    tokens("g.proj_a", 2, 4, grad_proj)

    def back_proj(n):
        out, rows = d3.at[pl.ds(n * BLOCK, BLOCK)], pl.ds(n * LANES, LANES)
        add_up(out, 4, lambda k: dproj[:, at_block(k, LANES)], lambda k: w_proj_a[rows, at_block(k, LANES)], mm_nt)

    @token("dproj.0")
    def _():
        back_proj(0)

    @token("dproj.1")
    def _():
        back_proj(1)
        tell("proj_a")

    @token("A11e")
    def _():
        sums_of[11].end()
        keep_sums(11, 96)
        set_back("mid_a", 0, 0, 1)

    @token("A12s")
    def _():
        low_mid("mid_a", c2, [(-(32 * r + 4 * s)) % BLOCK for r in range(2) for s in range(2)])
        for row_par in range(2):
            for col_par in range(2):
                grad = None
                for t, (u, v) in enumerate(TAPS):
                    if (u != 1) != bool(row_par) or (v != 1) != bool(col_par):
                        continue
                    moved = 2 * (1 if u == 0 else 0) + (1 if v == 0 else 0)
                    term = mm_nt(g_mid[moved * BLOCK : (moved + 1) * BLOCK, :], w_mid_a[t * LANES : (t + 1) * LANES, :])
                    grad = term if grad is None else grad + term
                bo[pl.ds((2 * row_par + col_par) * BLOCK, BLOCK), :] = grad
        tell("mid_a")
        begin(12, column_sums(32, 2, slope_terms(bo, c1, "in_a", "chan_a")))

    tokens("g.mid_a", 3, 3, lambda t: grad_mid(cols_a, t))

    @token("A12e")
    def _():
        sums_of[12].end()
        keep_sums(12, 104)
        set_back("in_a", 0, 0, 1)
        for p in range(4):

            def low_first_a(index, p=p):
                start = pl.multiple_of(index * CHUNK, CHUNK)
                rows = pl.ds(p * BLOCK + start, CHUNK)
                grad = back("in_a", 0, bo[rows, :], c1[rows, :]) * mask_at(start)
                cols_b[pl.ds(start, CHUNK), p * LANES : (p + 1) * LANES] = grad.astype(BF16)

            loop(BLOCK // CHUNK, low_first_a)

    def first_grad(p):
        return cols_b[:, p * LANES : (p + 1) * LANES]

    def grad_in_a(i):
        lanes = at_block(i, 256)
        total = mm_tn(x[0:BLOCK, lanes], first_grad(0))
        for p in range(1, 4):
            total = total + mm_tn(x[p * BLOCK : (p + 1) * BLOCK, lanes], first_grad(p))
        g_in[at_block(i, 256), :] = total.astype(BF16)

    tokens("g.in_a", 2, 2, grad_in_a)

    def image_grad(planes):
        for p in planes:
            for h in range(2):
                lanes = pl.ds(h * LANES, LANES)
                grad = mm_nt(first_grad(p), w_in_a[h * LANES : (h + 1) * LANES, :])
                dz[...] = grad + d3[h * BLOCK : (h + 1) * BLOCK, :] if p == 0 else grad

                def pixels(row, p=p, lanes=lanes):
                    move[:, 0:LANES] = dz[at_block(row, CHUNK), :]
                    for col in range(SIDE):
                        raw[2 * row + p // 2, 2 * col + p % 2, :, lanes] = move[4 * col : 4 * col + 4, 0:LANES].astype(BF16)

                loop(SIDE, pixels)

    @token("img.0")
    def _():
        image_grad((0, 1))

    @token("img.1")
    def _():
        image_grad((2, 3))
        grad_copy.start()
        tell("in_a")

    @token("own")
    def _():
        def own_row(at, out, k):
            if out.shape[1] >= 128:
                for lane in range(2):
                    line = sums[pl.ds(at + 2 * (place.f % 2) + lane, 1), :]
                    out[k : k + 1, lane * 128 : (lane + 1) * 128] = line
            else:
                odd = (place.f % 2).astype(F32)
                move[0:1, 0:128] = sums[pl.ds(at + place.f // 2, 1), :]
                line = move[0:8, 0:128]
                line = line + (pltpu.roll(line, 64, 1) - line) * odd
                out[k : k + 1, :] = line[0:1, 0 : out.shape[1]]

        for name, at in (("mid_b", 32), ("in_b", 40), ("mid_a", 96), ("in_a", 104)):
            own_row(at + 4, owned[name], 0)
            own_row(at, owned[name], 1)
        block = place.f // 2
        pair_at = 16 * (block % 2) + 8 * (block // 2)
        for name, at, gain in (("out_b", pair_at, 4), ("out_a", 48 + 12 * block, 4), ("proj_a", 48 + 12 * block, 8)):
            own_row(at + gain, owned[name], 0)
            own_row(at, owned[name], 1)
        for one in own_copies:
            one.start()

    steps = sorted(todo)
    if sorted(RUN) != list(range(len(steps))):
        raise ValueError(len(steps))
    for index in RUN:
        todo[steps[index]]()
    result_copy.wait()
    grad_copy.wait()
    for one in scatters.values():
        one.sent()
    for one in own_copies + out_copies:
        one.wait()


def finish_kernel(*refs):
    arrays_in, arrays_out, held, wide = refs[:16], refs[16:32], refs[32:48], refs[48:55]
    in_sem, out_sem = refs[55:]
    loads = [pltpu.make_async_copy(a, b, in_sem.at[i]) for i, (a, b) in enumerate(zip(arrays_in, held))]
    leaving = held[:9] + wide
    stores = [pltpu.make_async_copy(a, b, out_sem.at[i]) for i, (a, b) in enumerate(zip(leaving, arrays_out))]
    order = list(range(9, 16)) + list(range(9))
    for i in order:
        loads[i].start()
    for i in order:
        loads[i].wait()
        if i >= 9:
            narrow, target = held[i], wide[i - 9]
            rows, columns = narrow.shape
            chunk = chunk_of(rows, columns)

            def step(index, carry, narrow=narrow, target=target, chunk=chunk):
                at = pl.ds(pl.multiple_of(index * chunk, 16), chunk)
                target[at, :] = narrow[at, :].astype(F32)
                return carry

            lax.fori_loop(0, rows // chunk, step, 0)
        stores[i].start()
    for i in order:
        stores[i].wait()


def finish_call(plain, grads):
    anywhere = pl.BlockSpec(memory_space=pl.ANY)
    return pl.pallas_call(
        finish_kernel,
        out_shape=[jax.ShapeDtypeStruct(one.shape, one.dtype) for one in plain]
        + [jax.ShapeDtypeStruct(one.shape, F32) for one in grads],
        in_specs=[anywhere] * 16,
        out_specs=[anywhere] * 16,
        scratch_shapes=[pltpu.VMEM(one.shape, one.dtype) for one in (*plain, *grads)]
        + [pltpu.VMEM(one.shape, F32) for one in grads]
        + [pltpu.SemaphoreType.DMA((16,)), pltpu.SemaphoreType.DMA((16,))],
        compiler_params=pltpu.CompilerParams(vmem_limit_bytes=64 * 2**20),
        name="finish_step",
    )(*plain, *grads)


def body_fast(
    images,
    image_sides,
    widths,
    keep_gate,
    w_in_a,
    w_mid_a,
    w_out_a,
    w_proj_a,
    norm_in_a,
    norm_mid_a,
    norm_out_a,
    norm_proj_a,
    w_in_b,
    w_mid_b,
    w_out_b,
    norm_in_b,
    norm_mid_b,
    norm_out_b,
    cotangent,
):
    width_in, width_out = images.shape[3], cotangent.shape[3]
    turned = (1, 2, 0, 3)
    images, cotangent = images.transpose(turned), cotangent.transpose(turned)
    norms = (norm_in_a, norm_mid_a, norm_out_a, norm_proj_a, norm_in_b, norm_mid_b, norm_out_b)
    shards = (w_in_a, w_mid_a, w_out_a, w_proj_a, w_in_b, w_mid_b, w_out_b)
    vmem = pl.BlockSpec(memory_space=pltpu.VMEM)
    smem = pl.BlockSpec(memory_space=pltpu.SMEM)
    anywhere = pl.BlockSpec(memory_space=pl.ANY)
    wholes = [(8 * one.shape[0], one.shape[1]) for one in shards]
    pieces = max(sum(len(one) for one in ways.values()) for ways in (WAYS_IN, WAYS_OUT))
    outs = pl.pallas_call(
        step_kernel,
        out_shape=[jax.ShapeDtypeStruct(cotangent.shape, BF16), jax.ShapeDtypeStruct(images.shape, BF16)]
        + [jax.ShapeDtypeStruct(one.shape, F32) for one in norms]
        + [jax.ShapeDtypeStruct(one.shape, BF16) for one in shards],
        in_specs=[anywhere, anywhere, smem, smem, smem] + [vmem] * 7 + [anywhere] * 7,
        out_specs=[anywhere] * 16,
        scratch_shapes=[pltpu.VMEM(one.shape, F32) for one in norms]
        + [pltpu.VMEM(one.shape, BF16) for one in shards]
        + [pltpu.VMEM(shape, BF16) for shape in wholes]
        + [
            pltpu.VMEM(images.shape, BF16),
            pltpu.VMEM(cotangent.shape, BF16),
            pltpu.VMEM((4 * BLOCK, width_in), BF16),
            pltpu.VMEM((4 * BLOCK, LANES), F32),
            pltpu.VMEM((BLOCK, 9 * LANES), BF16),
            pltpu.VMEM((BLOCK, LANES), F32),
            pltpu.VMEM((BLOCK, LANES), BF16),
            pltpu.VMEM((4 * BLOCK, LANES), F32),
            pltpu.VMEM((4 * BLOCK, LANES), F32),
            pltpu.VMEM((4 * BLOCK, LANES), F32),
            pltpu.VMEM((BLOCK, width_out), BF16),
            pltpu.VMEM((BLOCK, LANES), F32),
            pltpu.VMEM((BLOCK, 9 * LANES), BF16),
            pltpu.VMEM((BLOCK, LANES), F32),
            pltpu.VMEM((BLOCK, LANES), BF16),
            pltpu.VMEM((4 * BLOCK, LANES), F32),
            pltpu.VMEM((BLOCK, LANES), F32),
            pltpu.VMEM((BLOCK, LANES), BF16),
            pltpu.VMEM((BLOCK, LANES), BF16),
            pltpu.VMEM((BLOCK, width_out), BF16),
            pltpu.VMEM((BLOCK, width_out), BF16),
            pltpu.VMEM(wholes[1], BF16),
            pltpu.VMEM(wholes[2], BF16),
            pltpu.VMEM(wholes[4], BF16),
            pltpu.VMEM(wholes[3], BF16),
            pltpu.VMEM((BLOCK, 128), F32),
            pltpu.VMEM((BLOCK, 128), F32),
            pltpu.VMEM((CHUNK, width_in), F32),
            pltpu.VMEM((8, 24, 128), F32),
            pltpu.VMEM((24, 128), F32),
            pltpu.VMEM((160, LANES), F32),
            pltpu.VMEM((SHORT_SETS, 18, 8, 128), F32),
            pltpu.VMEM((10, 64, 128), F32),
            pltpu.VMEM((64, 128), F32),
            pltpu.VMEM((112, 128), F32),
            pltpu.SemaphoreType.DMA((4,)),
            pltpu.SemaphoreType.DMA((pieces,)),
            pltpu.SemaphoreType.DMA((pieces, 6)),
            pltpu.SemaphoreType.DMA((SHORT_SETS + 1,)),
            pltpu.SemaphoreType.DMA((2 * SHORT_SETS + 3,)),
            pltpu.SemaphoreType.DMA((2,)),
            pltpu.SemaphoreType.DMA((2, 7)),
            pltpu.SemaphoreType.REGULAR((7,)),
        ],
        compiler_params=pltpu.CompilerParams(
            collective_id=0, has_side_effects=True, vmem_limit_bytes=64 * 2**20
        ),
        name="whole_step",
    )(images, cotangent, image_sides, keep_gate, widths, *norms, *shards)
    back_turned = (2, 0, 1, 3)
    outs = finish_call(outs[:9], outs[9:])
    own, finals = outs[2:9], outs[9:]
    return (
        outs[0].transpose(back_turned),
        outs[1].transpose(back_turned),
        *finals[:4],
        *own[:4],
        *finals[4:],
        *own[4:],
    )


def fits(mesh):
    return mesh.shape[FSDP] == 8 and mesh.shape[DP] == 4


def gather_plain(shards):
    return [lax.all_gather(one, FSDP, axis=0, tiled=True) for one in shards]


def scatter_plain(grads):
    parts = [lax.psum_scatter(one, FSDP, scatter_dimension=0, tiled=True) for one in grads]
    return lax.psum(tuple(parts), DP)


def sum_pair(first, second):
    return lax.psum((first, second), (FSDP, DP))


def silu_slope(values):
    sigmoid_part = jax.nn.sigmoid(values)
    return sigmoid_part * (1.0 + values * (1.0 - sigmoid_part))


def pixel_masks(image_sides, side_in, side_out):
    half_sides = image_sides // 2
    rows_in = jnp.arange(side_in, dtype=jnp.int32)
    rows_out = jnp.arange(side_out, dtype=jnp.int32)
    inside_in = (rows_in[None, :, None] < image_sides[:, None, None]) & (
        rows_in[None, None, :] < image_sides[:, None, None]
    )
    inside_out = (rows_out[None, :, None] < half_sides[:, None, None]) & (
        rows_out[None, None, :] < half_sides[:, None, None]
    )
    local_counts = jnp.stack(
        [jnp.sum(image_sides * image_sides), jnp.sum(half_sides * half_sides)]
    ).astype(jnp.float32)
    return (
        inside_in.astype(jnp.float32)[..., None],
        inside_out.astype(jnp.float32)[..., None],
        local_counts,
    )


def norm_stats(hidden, pixel_mask, local_counts, count_slot):
    sum_values, sum_squares = sum_pair(
        jnp.sum(hidden * pixel_mask, axis=(0, 1, 2)),
        jnp.sum(hidden * hidden * pixel_mask, axis=(0, 1, 2)),
    )
    pixel_total = local_counts[count_slot]
    average = sum_values / pixel_total
    inv_std = lax.rsqrt(sum_squares / pixel_total - average * average + EPSILON)
    return (average, inv_std, pixel_total)


def normalize(hidden, stats_now, params, channel):
    average, inv_std, pixel_total = stats_now
    scaled = (hidden - average) * inv_std
    params_wide = params.astype(jnp.float32)
    return (scaled, (scaled * params_wide[0] + params_wide[1]) * channel)


def norm_backward(grad_norm, scaled, stats_now, params, pixel_mask):
    average, inv_std, pixel_total = stats_now
    shift_sum, gain_sum = sum_pair(
        jnp.sum(grad_norm, axis=(0, 1, 2)), jnp.sum(grad_norm * scaled, axis=(0, 1, 2))
    )
    gain_row = params[0].astype(jnp.float32)
    grad_hidden = (
        gain_row
        * inv_std
        * (grad_norm - shift_sum / pixel_total - scaled * gain_sum / pixel_total)
        * pixel_mask
    )
    return (grad_hidden.astype(jnp.bfloat16), gain_sum, shift_sum)


def taps_stride_two(activations):
    slot_count = activations.shape[0]
    half_side = activations.shape[1] // 2
    lane_count = activations.shape[3]
    padded = jnp.pad(activations, ((0, 0), (1, 1), (1, 1), (0, 0)))
    parity_grid = padded.reshape(slot_count, half_side + 1, 2, half_side + 1, 2, lane_count)
    pieces = [
        parity_grid[
            :,
            row_tap // 2 : row_tap // 2 + half_side,
            row_tap % 2,
            col_tap // 2 : col_tap // 2 + half_side,
            col_tap % 2,
            :,
        ]
        for row_tap in range(3)
        for col_tap in range(3)
    ]
    return jnp.concatenate(pieces, axis=-1)


def fold_stride_two(grad_cols, side_in):
    slot_count = grad_cols.shape[0]
    half_side = grad_cols.shape[1]
    lane_count = grad_cols.shape[3] // 9
    planes = [
        [
            jnp.zeros((slot_count, half_side + 1, half_side + 1, lane_count), jnp.float32)
            for col_par in range(2)
        ]
        for row_par in range(2)
    ]
    for row_tap in range(3):
        for col_tap in range(3):
            tap_index = row_tap * 3 + col_tap
            tap_piece = grad_cols[..., tap_index * lane_count : (tap_index + 1) * lane_count]
            placed = jnp.pad(
                tap_piece,
                (
                    (0, 0),
                    (row_tap // 2, 1 - row_tap // 2),
                    (col_tap // 2, 1 - col_tap // 2),
                    (0, 0),
                ),
            )
            planes[row_tap % 2][col_tap % 2] = planes[row_tap % 2][col_tap % 2] + placed
    parity_grid = jnp.stack([jnp.stack(planes[0], axis=3), jnp.stack(planes[1], axis=3)], axis=2)
    whole_grid = parity_grid.reshape(slot_count, side_in + 2, side_in + 2, lane_count)
    return whole_grid[:, 1:-1, 1:-1, :]


def taps_stride_one(activations):
    side_now = activations.shape[1]
    padded = jnp.pad(activations, ((0, 0), (1, 1), (1, 1), (0, 0)))
    pieces = [
        padded[:, row_tap : row_tap + side_now, col_tap : col_tap + side_now, :]
        for row_tap in range(3)
        for col_tap in range(3)
    ]
    return jnp.concatenate(pieces, axis=-1)


def fold_stride_one(grad_cols):
    lane_count = grad_cols.shape[3] // 9
    whole_grid = None
    for row_tap in range(3):
        for col_tap in range(3):
            tap_index = row_tap * 3 + col_tap
            tap_piece = grad_cols[..., tap_index * lane_count : (tap_index + 1) * lane_count]
            placed = jnp.pad(
                tap_piece, ((0, 0), (row_tap, 2 - row_tap), (col_tap, 2 - col_tap), (0, 0))
            )
            whole_grid = placed if whole_grid is None else whole_grid + placed
    return whole_grid[:, 1:-1, 1:-1, :]


def contract(left_side, right_side):
    return lax.dot_general(
        left_side,
        right_side,
        (((0, 1, 2), (0, 1, 2)), ((), ())),
        preferred_element_type=jnp.float32,
    )


def back_project(gradient, weight):
    return lax.dot_general(
        gradient, weight, (((3,), (1,)), ((), ())), preferred_element_type=jnp.float32
    )


def own_shard(pair_sums):
    gain_sum, shift_sum = pair_sums
    shard_width = gain_sum.shape[0] // lax.axis_size(FSDP)
    offset = lax.axis_index(FSDP) * shard_width
    return jnp.stack(
        [
            lax.dynamic_slice_in_dim(gain_sum, offset, shard_width, 0),
            lax.dynamic_slice_in_dim(shift_sum, offset, shard_width, 0),
        ]
    )


def block_a_forward(inputs, weights, mask_in, mask_out, local_counts, channel, saved_stats):
    w_in, w_mid, w_out, w_proj, norm_in, norm_mid, norm_out, norm_proj = weights
    conv_first = jnp.dot(inputs, w_in, preferred_element_type=jnp.float32)
    stats_first = (
        norm_stats(conv_first, mask_in, local_counts, 0) if saved_stats is None else saved_stats[0]
    )
    scaled_first, normed_first = normalize(conv_first, stats_first, norm_in, channel)
    act_first = (jax.nn.silu(normed_first) * mask_in).astype(jnp.bfloat16)
    cols_mid = taps_stride_two(act_first)
    conv_mid = jnp.dot(cols_mid, w_mid, preferred_element_type=jnp.float32)
    stats_mid = (
        norm_stats(conv_mid, mask_out, local_counts, 1) if saved_stats is None else saved_stats[1]
    )
    scaled_mid, normed_mid = normalize(conv_mid, stats_mid, norm_mid, channel)
    act_mid = (jax.nn.silu(normed_mid) * mask_out).astype(jnp.bfloat16)
    conv_out = jnp.dot(act_mid, w_out, preferred_element_type=jnp.float32)
    slot_count, side_in, lane_count = (inputs.shape[0], inputs.shape[1], inputs.shape[3])
    sampled = inputs.reshape(slot_count, side_in // 2, 2, side_in // 2, 2, lane_count)[
        :, :, 0, :, 0, :
    ]
    conv_proj = jnp.dot(sampled, w_proj, preferred_element_type=jnp.float32)
    conv_both = jnp.concatenate([conv_out, conv_proj], axis=-1)
    norm_both = jnp.concatenate([norm_out, norm_proj], axis=-1)
    stats_both = (
        norm_stats(conv_both, mask_out, local_counts, 1) if saved_stats is None else saved_stats[2]
    )
    scaled_both, normed_both = normalize(conv_both, stats_both, norm_both, 1.0)
    width_out = conv_out.shape[-1]
    pre_sum = normed_both[..., :width_out] + normed_both[..., width_out:]
    block_out = jax.nn.silu(pre_sum) * mask_out
    saved_values = (
        scaled_first,
        normed_first,
        act_first,
        cols_mid,
        scaled_mid,
        normed_mid,
        act_mid,
        sampled,
        scaled_both,
        pre_sum,
    )
    return (block_out, (stats_first, stats_mid, stats_both), saved_values)


def block_a_backward(
    grad_out, inputs, weights, stats_all, saved_values, mask_in, mask_out, channel
):
    w_in, w_mid, w_out, w_proj, norm_in, norm_mid, norm_out, norm_proj = weights
    stats_first, stats_mid, stats_both = stats_all
    (
        scaled_first,
        normed_first,
        act_first,
        cols_mid,
        scaled_mid,
        normed_mid,
        act_mid,
        sampled,
        scaled_both,
        pre_sum,
    ) = saved_values
    grad_pre = grad_out * mask_out * silu_slope(pre_sum)
    grad_both = jnp.concatenate([grad_pre, grad_pre], axis=-1)
    norm_both = jnp.concatenate([norm_out, norm_proj], axis=-1)
    low_both, gain_both, shift_both = norm_backward(
        grad_both, scaled_both, stats_both, norm_both, mask_out
    )
    width_out = grad_pre.shape[-1]
    low_out = low_both[..., :width_out]
    low_proj = low_both[..., width_out:]
    grad_w_out = contract(act_mid, low_out)
    grad_w_proj = contract(sampled, low_proj)
    grad_norm_mid = back_project(low_out, w_out) * mask_out * channel * silu_slope(normed_mid)
    low_mid, gain_mid, shift_mid = norm_backward(
        grad_norm_mid, scaled_mid, stats_mid, norm_mid, mask_out
    )
    grad_w_mid = contract(cols_mid, low_mid)
    grad_act_first = fold_stride_two(back_project(low_mid, w_mid), inputs.shape[1])
    grad_norm_first = grad_act_first * mask_in * channel * silu_slope(normed_first)
    low_first, gain_first, shift_first = norm_backward(
        grad_norm_first, scaled_first, stats_first, norm_in, mask_in
    )
    grad_w_in = contract(inputs, low_first)
    spread = lax.pad(
        back_project(low_proj, w_proj),
        jnp.float32(0.0),
        ((0, 0, 0), (0, 1, 1), (0, 1, 1), (0, 0, 0)),
    )
    grad_inputs = (back_project(low_first, w_in) + spread) * mask_in
    norm_grads = (
        (gain_first, shift_first),
        (gain_mid, shift_mid),
        (gain_both[:width_out], shift_both[:width_out]),
        (gain_both[width_out:], shift_both[width_out:]),
    )
    return (grad_inputs, (grad_w_in, grad_w_mid, grad_w_out, grad_w_proj), norm_grads)


def block_b_forward(block_in, weights, mask_out, local_counts, channel, depth_gate, saved_stats):
    w_in, w_mid, w_out, norm_in, norm_mid, norm_out = weights
    feed_in = block_in.astype(jnp.bfloat16)
    conv_first = jnp.dot(feed_in, w_in, preferred_element_type=jnp.float32)
    stats_first = (
        norm_stats(conv_first, mask_out, local_counts, 1) if saved_stats is None else saved_stats[0]
    )
    scaled_first, normed_first = normalize(conv_first, stats_first, norm_in, channel)
    act_first = (jax.nn.silu(normed_first) * mask_out).astype(jnp.bfloat16)
    cols_mid = taps_stride_one(act_first)
    conv_mid = jnp.dot(cols_mid, w_mid, preferred_element_type=jnp.float32)
    stats_mid = (
        norm_stats(conv_mid, mask_out, local_counts, 1) if saved_stats is None else saved_stats[1]
    )
    scaled_mid, normed_mid = normalize(conv_mid, stats_mid, norm_mid, channel)
    act_mid = (jax.nn.silu(normed_mid) * mask_out).astype(jnp.bfloat16)
    conv_out = jnp.dot(act_mid, w_out, preferred_element_type=jnp.float32)
    stats_out = (
        norm_stats(conv_out, mask_out, local_counts, 1) if saved_stats is None else saved_stats[2]
    )
    scaled_out, normed_out = normalize(conv_out, stats_out, norm_out, 1.0)
    pre_sum = block_in + depth_gate * normed_out
    result = jax.nn.silu(pre_sum) * mask_out
    saved_values = (
        feed_in,
        scaled_first,
        normed_first,
        act_first,
        cols_mid,
        scaled_mid,
        normed_mid,
        act_mid,
        scaled_out,
        pre_sum,
    )
    return (result, (stats_first, stats_mid, stats_out), saved_values)


def block_b_backward(grad_out, weights, stats_all, saved_values, mask_out, channel, depth_gate):
    w_in, w_mid, w_out, norm_in, norm_mid, norm_out = weights
    stats_first, stats_mid, stats_out = stats_all
    (
        feed_in,
        scaled_first,
        normed_first,
        act_first,
        cols_mid,
        scaled_mid,
        normed_mid,
        act_mid,
        scaled_out,
        pre_sum,
    ) = saved_values
    grad_pre = grad_out * mask_out * silu_slope(pre_sum)
    low_out, gain_out, shift_out = norm_backward(
        grad_pre * depth_gate, scaled_out, stats_out, norm_out, mask_out
    )
    grad_w_out = contract(act_mid, low_out)
    grad_norm_mid = back_project(low_out, w_out) * mask_out * channel * silu_slope(normed_mid)
    low_mid, gain_mid, shift_mid = norm_backward(
        grad_norm_mid, scaled_mid, stats_mid, norm_mid, mask_out
    )
    grad_w_mid = contract(cols_mid, low_mid)
    grad_norm_first = (
        fold_stride_one(back_project(low_mid, w_mid))
        * mask_out
        * channel
        * silu_slope(normed_first)
    )
    low_first, gain_first, shift_first = norm_backward(
        grad_norm_first, scaled_first, stats_first, norm_in, mask_out
    )
    grad_w_in = contract(feed_in, low_first)
    grad_in = grad_pre + back_project(low_first, w_in)
    norm_grads = ((gain_first, shift_first), (gain_mid, shift_mid), (gain_out, shift_out))
    return (grad_in, (grad_w_in, grad_w_mid, grad_w_out), norm_grads)


def body(
    images,
    image_sides,
    widths,
    keep_gate,
    w_in_a,
    w_mid_a,
    w_out_a,
    w_proj_a,
    norm_in_a,
    norm_mid_a,
    norm_out_a,
    norm_proj_a,
    w_in_b,
    w_mid_b,
    w_out_b,
    norm_in_b,
    norm_mid_b,
    norm_out_b,
    cotangent,
):
    mask_in, mask_out, local_counts = pixel_masks(image_sides, images.shape[1], cotangent.shape[1])
    lane_ids = jnp.arange(w_mid_a.shape[1], dtype=jnp.int32)
    channel_a = (lane_ids < widths[0]).astype(jnp.float32)
    channel_b = (lane_ids < widths[1]).astype(jnp.float32)
    depth_gate = keep_gate.astype(jnp.float32)[:, None, None, None]
    inputs = images * mask_in.astype(jnp.bfloat16)
    total_counts = lax.psum(local_counts, (FSDP, DP))
    gathered = gather_plain((w_in_a, w_mid_a, w_out_a, w_proj_a, w_in_b, w_mid_b, w_out_b))
    norms = lax.all_gather(
        jnp.concatenate(
            [norm_in_a, norm_mid_a, norm_out_a, norm_proj_a, norm_in_b, norm_mid_b, norm_out_b], axis=1
        ),
        FSDP,
        axis=0,
    )
    wide = []
    place = 0
    for one in (norm_in_a, norm_mid_a, norm_out_a, norm_proj_a, norm_in_b, norm_mid_b, norm_out_b):
        width = one.shape[1]
        wide.append(norms[:, :, place : place + width].transpose(1, 0, 2).reshape(2, -1))
        place += width
    weights_a = tuple(gathered[:4]) + tuple(wide[:4])
    weights_b = tuple(gathered[4:]) + tuple(wide[4:])
    block_out, stats_a, redone_a = block_a_forward(
        inputs, weights_a, mask_in, mask_out, total_counts, channel_a, None
    )
    result, stats_b, redone_b = block_b_forward(
        block_out, weights_b, mask_out, total_counts, channel_b, depth_gate, None
    )
    grad_block, grads_b, norms_b = block_b_backward(
        cotangent.astype(jnp.float32), weights_b, stats_b, redone_b, mask_out, channel_b, depth_gate
    )
    grad_inputs, grads_a, norms_a = block_a_backward(
        grad_block, inputs, weights_a, stats_a, redone_a, mask_in, mask_out, channel_a
    )
    finals = scatter_plain(tuple(one.astype(jnp.bfloat16) for one in grads_a + grads_b))
    final_in_a, final_mid_a, final_out_a, final_proj_a, final_in_b, final_mid_b, final_out_b = (
        one.astype(jnp.float32) for one in finals
    )
    return (
        result.astype(jnp.bfloat16),
        grad_inputs.astype(jnp.bfloat16),
        final_in_a,
        final_mid_a,
        final_out_a,
        final_proj_a,
        own_shard(norms_a[0]),
        own_shard(norms_a[1]),
        own_shard(norms_a[2]),
        own_shard(norms_a[3]),
        final_in_b,
        final_mid_b,
        final_out_b,
        own_shard(norms_b[0]),
        own_shard(norms_b[1]),
        own_shard(norms_b[2]),
    )


def solution(mesh):
    in_specs = (
        P((FSDP, DP), None, None, None),
        P((FSDP, DP)),
        P(),
        P((FSDP, DP)),
        P(FSDP, None),
        P(FSDP, None),
        P(FSDP, None),
        P(FSDP, None),
        P(None, FSDP),
        P(None, FSDP),
        P(None, FSDP),
        P(None, FSDP),
        P(FSDP, None),
        P(FSDP, None),
        P(FSDP, None),
        P(None, FSDP),
        P(None, FSDP),
        P(None, FSDP),
        P((FSDP, DP), None, None, None),
    )
    out_specs = (
        P((FSDP, DP), None, None, None),
        P((FSDP, DP), None, None, None),
        P(FSDP, None),
        P(FSDP, None),
        P(FSDP, None),
        P(FSDP, None),
        P(None, FSDP),
        P(None, FSDP),
        P(None, FSDP),
        P(None, FSDP),
        P(FSDP, None),
        P(FSDP, None),
        P(FSDP, None),
        P(None, FSDP),
        P(None, FSDP),
        P(None, FSDP),
    )
    step = body_fast if fits(mesh) else body
    return jax.shard_map(step, mesh=mesh, in_specs=in_specs, out_specs=out_specs, check_vma=False)
```

```python
import functools

import jax
import jax.numpy as jnp
from jax import lax
from jax.experimental import pallas as pl
from jax.experimental.pallas import tpu as pltpu
from jax.sharding import PartitionSpec as P

EPSILON = 1e-05
BY_MESH = pl.DeviceIdType.MESH
FSDP, DP = "fsdp", "dp"
F32 = jnp.float32
BF16 = jnp.bfloat16
NAMES = ("in_a", "mid_a", "out_a", "proj_a", "in_b", "mid_b", "out_b")
BLOCK = 256
LANES = 512
CHUNK = 32
SIDE = 7
ZYX, ZXY, YZX = range(3)
SHORT_SETS = 8
TAPS = [(u, v) for u in range(3) for v in range(3)]
LINK_PEERS = ((1, 0), (2, 0), (4, 0), (6, 0), (0, 2), (0, 1))
CHIP_PEERS = tuple((a, b) for a in (7, 6, 5, 4, 3, 2, 1, 0) for b in (2, 0) if a or b)
WAYS_IN = {
    "in_a": ((0, 64, 0, ((YZX, 4), (ZXY, 4))), (64, 64, 0, ((YZX, 4), (ZXY, 4)))),
    "mid_a": ((0, 96, 0, ((YZX, 4), (ZXY, 4))), (96, 96, 0, ((YZX, 4), (ZXY, 4))), (192, 96, 0, ((ZYX, 4), (ZXY, 4))), (288, 96, 0, ((YZX, 4), (ZXY, 4))), (384, 96, 0, ((YZX, 4), (ZXY, 4))), (480, 96, 0, ((ZYX, 4), (ZXY, 4)))),
    "out_a": ((0, 32, 0, ((ZXY, 5), (YZX, 3))), (32, 32, 0, ((ZXY, 5), (YZX, 3)))),
    "proj_a": ((0, 64, 0, ((ZXY, 5), (YZX, 3))), (64, 64, 0, ((ZXY, 5), (YZX, 3)))),
    "in_b": ((0, 128, 0, ((YZX, 4), (ZXY, 4))), (128, 128, 0, ((YZX, 4), (ZXY, 4)))),
    "mid_b": ((0, 96, 0, ((YZX, 4), (ZXY, 4))), (96, 96, 0, ((YZX, 4), (ZXY, 4))), (192, 96, 0, ((ZYX, 4), (ZXY, 4))), (288, 96, 0, ((YZX, 4), (ZXY, 4))), (384, 96, 0, ((YZX, 4), (ZXY, 4))), (480, 96, 0, ((ZYX, 4), (ZXY, 4)))),
    "out_b": ((0, 64, 0, ((ZXY, 2), (YZX, 2))), (0, 64, 4, ((ZXY, 2), (YZX, 2)))),
}
WAYS_OUT = {
    "in_a": ((0, 64, 4), (64, 64, 4)),
    "mid_a": ((0, 96, 4), (96, 96, 4), (192, 96, 4), (288, 96, 4), (384, 96, 4), (480, 96, 4)),
    "out_a": ((0, 32, 5), (32, 32, 5)),
    "proj_a": ((0, 32, 5), (32, 32, 5), (64, 32, 5), (96, 32, 5)),
    "in_b": ((0, 128, 4), (128, 128, 4)),
    "mid_b": ((0, 96, 4), (96, 96, 4), (192, 96, 4), (288, 96, 4), (384, 96, 4), (480, 96, 4)),
    "out_b": ((0, 32, 5), (32, 32, 5)),
}
RUN = [
    365, 411, 412, 385, 415, 386, 416, 390, 165, 417, 408, 391, 166, 389, 39, 169, 76, 38, 418, 392, 170, 99,
    171, 419, 77, 420, 394, 100, 103, 82, 393, 121, 172, 104, 105, 173, 431, 80, 405, 85, 83, 174, 122, 106,
    107, 127, 84, 185, 432, 37, 406, 125, 143, 128, 81, 108, 129, 119, 144, 427, 355, 186, 428, 96, 413, 402,
    43, 126, 130, 401, 42, 150, 120, 182, 147, 414, 181, 141, 149, 97, 41, 116, 93, 387, 115, 151, 36, 384,
    152, 92, 421, 40, 422, 148, 168, 142, 163, 357, 423, 138, 47, 175, 167, 137, 46, 395, 102, 45, 424, 164,
    397, 177, 425, 388, 176, 396, 160, 426, 429, 109, 101, 362, 159, 78, 409, 111, 44, 359, 51, 79, 178, 86,
    87, 50, 110, 398, 180, 124, 123, 179, 112, 183, 399, 49, 113, 400, 146, 89, 430, 145, 114, 132, 90, 88,
    403, 356, 133, 131, 48, 55, 184, 134, 91, 54, 53, 154, 136, 135, 153, 155, 404, 156, 117, 94, 158, 157,
    118, 52, 95, 358, 59, 139, 58, 140, 161, 162, 57, 360, 56, 63, 15, 361, 62, 14, 23, 27, 22, 26, 61, 60,
    67, 13, 12, 21, 19, 66, 65, 20, 25, 31, 24, 18, 35, 30, 34, 17, 410, 29, 64, 16, 98, 33, 28, 32, 71, 378,
    70, 69, 379, 205, 206, 229, 230, 68, 75, 373, 374, 74, 253, 375, 197, 221, 198, 254, 199, 222, 200, 277,
    73, 201, 224, 202, 72, 245, 3, 278, 368, 2, 246, 223, 369, 189, 226, 225, 248, 1, 247, 269, 302, 190, 213,
    250, 0, 270, 249, 7, 301, 272, 376, 377, 6, 214, 363, 203, 5, 271, 237, 204, 364, 227, 274, 273, 380, 381,
    228, 207, 238, 325, 4, 208, 11, 349, 251, 298, 209, 10, 232, 261, 233, 294, 370, 371, 262, 372, 191, 252,
    215, 256, 322, 231, 295, 9, 275, 192, 8, 193, 346, 276, 257, 366, 217, 194, 318, 280, 195, 239, 196, 367,
    342, 293, 326, 382, 296, 210, 255, 216, 383, 350, 218, 281, 241, 187, 219, 285, 188, 263, 240, 242, 279,
    220, 286, 212, 264, 320, 319, 304, 287, 234, 243, 266, 297, 265, 309, 211, 344, 343, 244, 333, 236, 258,
    305, 235, 328, 303, 288, 260, 289, 290, 300, 317, 268, 407, 299, 352, 282, 327, 267, 341, 313, 310, 312,
    259, 329, 284, 321, 351, 292, 314, 324, 337, 334, 336, 353, 306, 311, 345, 338, 291, 348, 323, 283, 316,
    308, 335, 347, 315, 330, 307, 340, 332, 339, 354, 331,
]


def flip(index, bits):
    out = index
    for bit in (1, 2, 4):
        if bits & bit:
            out = out + bit - 2 * bit * ((index // bit) % 2)
    return out


class Place:
    def __init__(self):
        self.f = lax.axis_index(FSDP)
        self.d = lax.axis_index(DP)
        self.y = self.f % 2
        self.z = self.f // 2
        self.c = self.d % 2
        self.x = self.d // 2
        self.inner = self.z * (3 - self.z) > 0

    def peer(self, f_bits, d_bits):
        return (flip(self.f, f_bits), flip(self.d, d_bits))


def enter(place, peers):
    barrier = pltpu.get_barrier_semaphore()
    for f_bits, d_bits in peers:
        pl.semaphore_signal(barrier, inc=1, device_id=place.peer(f_bits, d_bits), device_id_type=BY_MESH)
    pl.semaphore_wait(barrier, len(peers))


def push(source, target, send_sem, recv_sem, device):
    pltpu.make_async_remote_copy(
        src_ref=source,
        dst_ref=target,
        send_sem=send_sem,
        recv_sem=recv_sem,
        device_id=device,
        device_id_type=BY_MESH,
    ).start()


def await_bytes(view, sem):
    pltpu.make_async_copy(view, view, sem).wait()


def await_count(ref, count, sem):
    if not count:
        return
    rows_most, columns_most = ref.shape
    for columns in range(columns_most, 0, -128):
        rows = count // columns
        if count % columns == 0 and rows % 16 == 0 and rows <= rows_most:
            await_bytes(ref.at[pl.ds(0, rows), pl.ds(0, columns)], sem)
            return
    raise ValueError(count)


def rows_of(start, size):
    return pl.ds(pl.multiple_of(start, 16), size)


def cols_of(start, size):
    return pl.ds(pl.multiple_of(start, 128), size)


class Gather:
    def __init__(self, place, shard, whole, start, rows, from_eighth, groups, send, recv):
        self.place, self.shard, self.whole = place, shard, whole
        self.start, self.rows, self.send, self.recv = start, rows, send, recv
        self.total, columns = shard.shape
        half = columns // 2
        self.part = part = rows // 2
        self.col_0 = place.c * half + half * from_eighth // 8
        self.row_q = start + place.x * part
        self.row_o = start + part - place.x * part
        self.arriving, self.leaving = [0] * 6, 0
        self.groups, at = {}, 0
        for way, eighths in groups:
            self.groups[way] = (at, half * eighths // 8)
            at += half * eighths // 8
        self.wide = at

    def view(self, bits, row, rows, from_col, columns):
        block = flip(self.place.f, bits) * self.total
        return self.whole.at[rows_of(block + row, rows), cols_of(self.col_0 + from_col, columns)]

    def pass_on(self, bits, row, rows, group, leg, peer):
        from_col, columns = group
        view = self.view(bits, row, rows, from_col, columns)
        push(view, view, self.send, self.recv.at[leg or 0], self.place.peer(*peer))
        if leg is not None:
            self.arriving[leg] += rows * columns
            self.leaving += rows * columns

    def pass_own(self, row, rows, group, leg, peer):
        from_col, columns = group
        source = self.shard.at[rows_of(row, rows), cols_of(self.col_0 + from_col, columns)]
        push(source, self.view(0, row, rows, from_col, columns), self.send, self.recv.at[leg], self.place.peer(*peer))
        self.arriving[leg] += rows * columns
        self.leaving += rows * columns

    def arrive(self, leg):
        await_count(self.whole, self.arriving[leg], self.recv.at[leg])

    def first(self):
        pltpu.make_async_copy(
            self.shard.at[pl.ds(self.start, self.rows), cols_of(self.col_0, self.wide)],
            self.view(0, self.start, self.rows, 0, self.wide),
            self.recv.at[0],
        ).start()
        self.arriving[0] += self.rows * self.wide
        everything = (0, self.wide)

        @pl.when(self.place.inner)
        def _():
            self.pass_own(self.row_q, self.part, everything, 0, (6, 0))

        self.pass_own(self.row_q, self.part, everything, 4, (4, 0))
        self.pass_own(self.row_q, self.part, everything, 0, (2, 0))

    def relay(self):
        self.arrive(4)

        @pl.when(self.place.inner)
        def _():
            self.pass_on(4, self.row_q, self.part, (0, self.wide), None, (2, 0))

    def own(self):
        for way, group in self.groups.items():
            if way == ZXY:
                self.pass_own(self.start, self.rows, group, 5, (1, 0))
            else:
                self.pass_own(self.row_q, self.part, group, 5, (1, 0))

    def beside(self):
        self.arrive(5)
        if YZX in self.groups:
            for bits in (6, 4, 2):
                self.pass_on(1, self.row_q, self.part, self.groups[YZX], 1, (bits, 0))
            self.pass_on(1, self.row_q, self.part, self.groups[YZX], 1, (0, 2))

    def one(self):
        self.arrive(0)
        for way, group in self.groups.items():
            for bits in (2, 4, 6):
                if way != YZX:
                    self.pass_on(bits, self.row_q, self.part, group, 1, (1, 0))
                self.pass_on(bits, self.row_q, self.part, group, 1, (0, 2))

    def two(self):
        self.arrive(1)
        for way, group in self.groups.items():
            if way == ZXY:
                for bits in (2, 4, 6):
                    self.pass_on(bits, self.row_o, self.part, group, 2, (1, 0))
            else:
                for bits in (1, 3, 5, 7) if way == ZYX else (3, 5, 7):
                    self.pass_on(bits, self.row_q, self.part, group, 2, (0, 2))

    def three(self):
        self.arrive(2)
        for bits in range(8):
            self.pass_on(bits, self.start, self.rows, (0, self.wide), 3, (0, 1))

    def four(self):
        self.arrive(3)

    def sent(self):
        block = self.part * self.wide

        @pl.when(self.place.inner)
        def _():
            await_count(self.whole, self.leaving + block, self.send)

        @pl.when(jnp.logical_not(self.place.inner))
        def _():
            await_count(self.whole, self.leaving - block, self.send)


def chunk_of(rows, columns):
    best = 16
    for chunk in range(16, rows + 1, 16):
        if rows % chunk == 0 and chunk * columns <= 16384:
            best = chunk
    return best


def add_blocks(blocks, rows, columns, target, source):
    chunk = chunk_of(rows, columns)
    each = rows // chunk

    def step(index, carry):
        block, start = index // each, pl.multiple_of((index % each) * chunk, 16)
        into, more = target(block, start, chunk), source(block, start, chunk)
        into[...] = into[...] + more[...]
        return carry

    lax.fori_loop(0, blocks * each, step, 0)


class Scatter:
    def __init__(self, place, grad, room, out, start, rows, wide_a, send, recv):
        self.place, self.grad, self.out = place, grad, out
        self.start, self.rows, self.wide_a = start, rows, wide_a
        self.send, self.recv = send, recv
        total, columns = room.shape
        self.total = total = total // 8
        self.half = half = columns // 2
        self.wide_b = wide_b = half - wide_a
        self.part = part = rows // 2
        self.room = room
        self.from_core = room.at[:, pl.ds(0, half)]

        def landing(row, count, col, width):
            return room.at[pl.ds(row, count), pl.ds(half + col, width)] if width else None

        self.a_x = landing(4 * start, 4 * rows, 0, wide_a)
        self.a_y = landing(4 * total + 2 * start, 2 * rows, 0, wide_a)
        self.a_z = landing(6 * total + 3 * start // 2, 3 * part, 0, wide_a)
        self.b_y = landing(4 * start, 4 * rows, wide_a, wide_b)
        self.b_z = landing(4 * total + 3 * start, 3 * rows, wide_a, wide_b)
        self.b_x = landing(7 * total + start // 2, part, wide_a, wide_b)
        self.col_0 = place.c * half
        self.row_q = start + place.x * part
        self.row_o = start + part - place.x * part

    def push(self, source, target, leg, device):
        push(source, target, self.send, self.recv.at[leg], device)

    def zero(self):
        other = cols_of(self.half - self.col_0, self.half)
        for block in range(8):
            rows = pl.ds(block * self.total + self.start, self.rows)
            self.push(self.grad.at[rows, other], self.from_core.at[rows], 5, self.place.peer(0, 1))

    def core(self, row, rows, from_col, columns):
        return self.from_core.at[rows_of(row, rows), pl.ds(from_col, columns)]

    def mine(self, row, rows, from_col, columns):
        return self.core(self.place.f * self.total + row, rows, from_col, columns)

    def one(self):
        place, total, part, rows = self.place, self.total, self.part, self.rows
        await_count(self.room, 8 * rows * self.half, self.recv.at[5])
        add_blocks(
            8,
            rows,
            self.half,
            lambda b, s, n: self.core(b * total + self.start + s, n, 0, self.half),
            lambda b, s, n: self.grad.at[rows_of(b * total + self.start + s, n), cols_of(self.col_0, self.half)],
        )
        await_count(self.room, 8 * rows * self.half, self.send)
        if self.wide_a:
            for block in range(8):
                self.push(
                    self.core(block * total + self.row_o, part, 0, self.wide_a),
                    self.a_x.at[pl.ds(block * part, part)],
                    0,
                    place.peer(0, 2),
                )
        if self.wide_b:
            for level in range(4):
                self.push(
                    self.core((2 * level + 1 - place.y) * total + self.start, rows, self.wide_a, self.wide_b),
                    self.b_y.at[pl.ds(level * rows, rows)],
                    0,
                    place.peer(1, 0),
                )

    def two(self):
        place, total, part, rows = self.place, self.total, self.part, self.rows
        await_count(self.room, 4 * rows * self.half, self.recv.at[0])
        if self.wide_a:
            add_blocks(
                8,
                part,
                self.wide_a,
                lambda b, s, n: self.core(b * total + self.row_q + s, n, 0, self.wide_a),
                lambda b, s, n: self.a_x.at[rows_of(b * part + s, n)],
            )
            for level in range(4):
                self.push(
                    self.core((2 * level + 1 - place.y) * total + self.row_q, part, 0, self.wide_a),
                    self.a_y.at[pl.ds(level * part, part)],
                    1,
                    place.peer(1, 0),
                )
        if self.wide_b:
            add_blocks(
                4,
                rows,
                self.wide_b,
                lambda b, s, n: self.core((2 * b + place.y) * total + self.start + s, n, self.wide_a, self.wide_b),
                lambda b, s, n: self.b_y.at[rows_of(b * rows + s, n)],
            )
            for slot, bits in enumerate((6, 4, 2)):
                self.push(
                    self.core(flip(place.f, bits) * total + self.start, rows, self.wide_a, self.wide_b),
                    self.b_z.at[pl.ds(slot * rows, rows)],
                    1,
                    place.peer(bits, 0),
                )

    def sum_four(self, row, rows, col, wide, landed, store):
        chunk = chunk_of(rows, wide)

        def step(index, carry):
            start = pl.multiple_of(index * chunk, 16)
            total = self.mine(row + start, chunk, col, wide)[...].astype(F32)
            for slot in range(3):
                total = total + landed[rows_of(slot * rows + start, chunk)].astype(F32)
            store(start, chunk, total.astype(BF16))
            return carry

        lax.fori_loop(0, rows // chunk, step, 0)

    def three(self):
        place, total, part, rows = self.place, self.total, self.part, self.rows
        await_count(self.room, 2 * rows * self.wide_a + 3 * rows * self.wide_b, self.recv.at[1])
        if self.wide_a:
            add_blocks(
                4,
                part,
                self.wide_a,
                lambda b, s, n: self.core((2 * b + place.y) * total + self.row_q + s, n, 0, self.wide_a),
                lambda b, s, n: self.a_y.at[rows_of(b * part + s, n)],
            )
            for slot, bits in enumerate((6, 4, 2)):
                self.push(
                    self.core(flip(place.f, bits) * total + self.row_q, part, 0, self.wide_a),
                    self.a_z.at[pl.ds(slot * part, part)],
                    2,
                    place.peer(bits, 0),
                )
        if self.wide_b:

            def keep(start, chunk, value):
                self.mine(self.start + start, chunk, self.wide_a, self.wide_b)[...] = value

            self.sum_four(self.start, rows, self.wide_a, self.wide_b, self.b_z, keep)
            self.push(self.mine(self.row_o, part, self.wide_a, self.wide_b), self.b_x, 2, place.peer(0, 2))

    def four(self):
        place, part = self.place, self.part
        await_count(self.room, 3 * part * self.wide_a + part * self.wide_b, self.recv.at[2])
        if self.wide_a:

            def keep(start, chunk, value):
                self.out[rows_of(self.row_q + start, chunk), cols_of(self.col_0, self.wide_a)] = value

            self.sum_four(self.row_q, part, 0, self.wide_a, self.a_z, keep)
        if self.wide_b:
            chunk = chunk_of(part, self.wide_b)

            def step(index, carry):
                start = pl.multiple_of(index * chunk, 16)
                total = self.mine(self.row_q + start, chunk, self.wide_a, self.wide_b)[...].astype(F32)
                total = total + self.b_x[rows_of(start, chunk)].astype(F32)
                columns = cols_of(self.col_0 + self.wide_a, self.wide_b)
                self.out[rows_of(self.row_q + start, chunk), columns] = total.astype(BF16)
                return carry

            lax.fori_loop(0, part // chunk, step, 0)
        block = self.out.at[rows_of(self.row_q, part), cols_of(self.col_0, self.half)]
        self.push(block, block, 3, place.peer(0, 2))

    def five(self):
        await_bytes(self.out.at[pl.ds(0, self.part), pl.ds(0, self.half)], self.recv.at[3])
        block = self.out.at[pl.ds(self.start, self.rows), cols_of(self.col_0, self.half)]
        self.push(block, block, 4, self.place.peer(0, 1))

    def six(self):
        await_bytes(self.out.at[pl.ds(0, self.rows), pl.ds(0, self.half)], self.recv.at[4])

    def sent(self):
        await_count(self.room, 18 * self.part * self.half, self.send)


def mm(left, right):
    return jnp.dot(left, right, preferred_element_type=F32)


def mm_nt(left, right):
    return lax.dot_general(left, right, (((1,), (1,)), ((), ())), preferred_element_type=F32)


def mm_tn(left, right):
    return lax.dot_general(left, right, (((0,), (0,)), ((), ())), preferred_element_type=F32)


def loop(count, step):
    def body_of(index, carry):
        step(index)
        return carry

    lax.fori_loop(0, count, body_of, 0)


def at_block(index, size):
    if isinstance(index, int):
        return pl.ds(index * size, size)
    return pl.ds(pl.multiple_of(index * size, size), size)


def slope_of(values):
    gate = jax.nn.sigmoid(values)
    return gate * (1.0 + values * (1.0 - gate))


def fold(values):
    total = values[0:8]
    for start in range(8, values.shape[0], 8):
        total = total + values[start : start + 8]
    return total


def column_sums(count, width, terms):
    def step(index, carry):
        start = pl.multiple_of(index * CHUNK, CHUNK)
        return tuple(total + fold(one) for total, one in zip(carry, terms(start)))

    zero = jnp.zeros((8, LANES), F32)
    totals = lax.fori_loop(0, count, step, (zero,) * width)
    return [jnp.sum(one, axis=0, keepdims=True) for one in totals]


class Vectors:
    def __init__(self, ref):
        self.ref, self.used = ref, 0

    def put(self, row):
        at = self.used
        self.used += 1
        self.ref[at : at + 1, :] = row
        return at

    def get(self, at):
        return self.ref[at : at + 1, :]


class Totals:
    def __init__(self, place, short, long, tot, send, recv):
        self.place, self.short, self.long, self.tot, self.send, self.recv = place, short, long, tot, send, recv
        self.began = 0

    def start(self, rows_of_values):
        whole = not isinstance(rows_of_values, list)
        one = Total(self, 8 if whole else 4 * len(rows_of_values))
        own = one.slot(self.place.c)
        if whole:
            own[...] = rows_of_values
        for n, row in enumerate([] if whole else rows_of_values):
            for k in range(4):
                own[4 * n + k : 4 * n + k + 1, :] = row[:, 128 * k : 128 * (k + 1)]
        one.spread(self.place.c, ((0, 1),), 0)
        return one

    def row(self, index):
        at = 4 * index
        return jnp.concatenate([self.tot[at + k : at + k + 1, :] for k in range(4)], axis=1)

    def wide(self, at):
        return jnp.concatenate([self.tot[at : at + 1, :]] * 4, axis=1)


class Total:
    def __init__(self, all_of_them, rows):
        self.all, self.place, self.rows = all_of_them, all_of_them.place, rows
        self.is_long = rows > 8
        self.set = SHORT_SETS
        if not self.is_long:
            self.set = all_of_them.began % SHORT_SETS
            all_of_them.began += 1

    def slots(self, at, count):
        if self.is_long:
            return self.all.long.at[pl.ds(at, count), pl.ds(0, self.rows)]
        return self.all.short.at[self.set, pl.ds(at, count), pl.ds(0, self.rows)]

    def slot(self, at):
        if self.is_long:
            return self.all.long.at[at, pl.ds(0, self.rows)]
        return self.all.short.at[self.set, at, pl.ds(0, self.rows)]

    def spread(self, at, peers, phase):
        own = self.slot(at)
        for bits in peers:
            push(own, own, self.all.send.at[self.set], self.all.recv.at[2 * self.set + phase], self.place.peer(*bits))

    def gather(self, at, count, peers, phase):
        await_bytes(self.slots(at, peers), self.all.recv.at[2 * self.set + phase])
        total = self.slot(at)[...]
        for index in range(at + 1, at + count):
            total = total + self.slot(index)[...]
        return total

    def middle(self):
        place = self.place
        total = self.gather(0, 2, 1, 0)
        if self.is_long:
            self.slot(2 + 2 * place.y + place.x)[...] = total
            self.spread(2 + 2 * place.y + place.x, ((1, 2), (1, 0), (0, 2)), 1)
        else:
            self.slot(2 + 2 * place.f + place.x)[...] = total
            self.spread(2 + 2 * place.f + place.x, CHIP_PEERS, 1)

    def late(self):
        if self.is_long:
            self.slot(6 + self.place.z)[...] = self.gather(2, 4, 3, 1)
            self.spread(6 + self.place.z, ((6, 0), (4, 0), (2, 0)), 2)

    def end(self):
        if self.is_long:
            self.all.tot[0 : self.rows, :] = self.gather(6, 4, 3, 2)
        else:
            self.all.tot[0 : self.rows, :] = self.gather(2, 16, 15, 1)
        await_bytes(self.slots(0, 7 if self.is_long else 16), self.all.send.at[self.set])


def step_kernel(
    img_hbm,
    cot_hbm,
    sides,
    keep,
    widths,
    norm_in_a,
    norm_mid_a,
    norm_out_a,
    norm_proj_a,
    norm_in_b,
    norm_mid_b,
    norm_out_b,
    sh_in_a,
    sh_mid_a,
    sh_out_a,
    sh_proj_a,
    sh_in_b,
    sh_mid_b,
    sh_out_b,
    result_hbm,
    images_hbm,
    own_hbm_in_a,
    own_hbm_mid_a,
    own_hbm_out_a,
    own_hbm_proj_a,
    own_hbm_in_b,
    own_hbm_mid_b,
    own_hbm_out_b,
    out_hbm_in_a,
    out_hbm_mid_a,
    out_hbm_out_a,
    out_hbm_proj_a,
    out_hbm_in_b,
    out_hbm_mid_b,
    out_hbm_out_b,
    own_in_a,
    own_mid_a,
    own_out_a,
    own_proj_a,
    own_in_b,
    own_mid_b,
    own_out_b,
    out_in_a,
    out_mid_a,
    out_out_a,
    out_proj_a,
    out_in_b,
    out_mid_b,
    out_out_b,
    w_in_a,
    w_mid_a,
    w_out_a,
    w_proj_a,
    w_in_b,
    w_mid_b,
    w_out_b,
    raw,
    cot,
    x,
    c1,
    cols_a,
    c2,
    a2,
    c3,
    cp,
    bo,
    feed,
    d1,
    cols_b,
    d2,
    b2,
    d3,
    dz,
    dm,
    df,
    dout,
    dproj,
    g_mid,
    g_out,
    g_in,
    g_proj,
    mask_ref,
    gate_ref,
    move,
    norms,
    block_ref,
    vec_ref,
    short,
    long,
    tot,
    sums,
    io_sem,
    link_send,
    link_recv,
    ar_send,
    ar_recv,
    nb_sem,
    out_sem,
    free_sem,
):
    place = Place()
    shards = dict(zip(NAMES, (sh_in_a, sh_mid_a, sh_out_a, sh_proj_a, sh_in_b, sh_mid_b, sh_out_b)))
    wholes = dict(zip(NAMES, (w_in_a, w_mid_a, w_out_a, w_proj_a, w_in_b, w_mid_b, w_out_b)))
    outs = dict(zip(NAMES, (out_in_a, out_mid_a, out_out_a, out_proj_a, out_in_b, out_mid_b, out_out_b)))
    owned = dict(zip(NAMES, (own_in_a, own_mid_a, own_out_a, own_proj_a, own_in_b, own_mid_b, own_out_b)))
    own_hbm = (own_hbm_in_a, own_hbm_mid_a, own_hbm_out_a, own_hbm_proj_a, own_hbm_in_b, own_hbm_mid_b, own_hbm_out_b)
    out_hbm = (out_hbm_in_a, out_hbm_mid_a, out_hbm_out_a, out_hbm_proj_a, out_hbm_in_b, out_hbm_mid_b, out_hbm_out_b)
    own_copies = [pltpu.make_async_copy(owned[n], own_hbm[i], out_sem.at[0, i]) for i, n in enumerate(NAMES)]
    out_copies = [pltpu.make_async_copy(outs[n], out_hbm[i], out_sem.at[1, i]) for i, n in enumerate(NAMES)]
    small = dict(zip(NAMES, (norm_in_a, norm_mid_a, norm_out_a, norm_proj_a, norm_in_b, norm_mid_b, norm_out_b)))
    grads = dict(mid_a=g_mid, mid_b=g_mid, out_a=g_out, out_b=g_out, in_b=g_in, proj_a=g_proj)
    grads["in_a"] = g_in.at[pl.ds(0, wholes["in_a"].shape[0])]
    todo = {}

    def token(name):
        def keep_it(function):
            todo[name] = function
            return function

        return keep_it

    def tokens(name, count, each, step):
        def some(first):
            for k in range(each):
                step(first + k)

        for part in range(count):
            todo[f"{name}.{part}"] = functools.partial(some, part * each)

    gathers, scatters, at, going = {}, {}, 0, 0
    left = {name: len(WAYS_OUT[name]) for name in NAMES}

    def finish_piece(name, piece):
        piece.six()
        left[name] -= 1
        if not left[name]:
            out_copies[NAMES.index(name)].start()

    def tell(name):
        for bits in LINK_PEERS:
            sem = free_sem.at[NAMES.index(name)]
            pl.semaphore_signal(sem, inc=1, device_id=place.peer(*bits), device_id_type=BY_MESH)

    def send_core(name, n):
        if n == 0:
            pl.semaphore_wait(free_sem.at[NAMES.index(name)], len(LINK_PEERS))
        scatters[name, n].zero()

    for name in NAMES:
        for n, (start, rows, from_eighth, ways) in enumerate(WAYS_IN[name]):
            sems = link_send.at[at], link_recv.at[at]
            g = gathers[name, n] = Gather(
                place, shards[name], wholes[name], start, rows, from_eighth, ways, *sems
            )
            at += 1
            key = f"{name}.{n}"
            todo["z." + key], todo["o." + key], todo["L1." + key] = g.first, g.own, g.one
            todo["R." + key], todo["B." + key] = g.relay, g.beside
            todo["L2." + key], todo["L3." + key] = g.two, g.three
        eighth = shards[name].shape[1] // 16
        for n, (start, rows, wide) in enumerate(WAYS_OUT[name]):
            sems = link_send.at[going], link_recv.at[going]
            s = Scatter(place, grads[name], wholes[name], outs[name], start, rows, wide * eighth, *sems)
            scatters[name, n] = s
            going += 1
            key = f"{name}.{n}"
            todo["S0." + key], todo["S1." + key] = functools.partial(send_core, name, n), s.one
            todo["S2." + key], todo["S3." + key], todo["S4." + key] = s.two, s.three, s.four
            todo["S5." + key] = s.five
            todo["S6." + key] = functools.partial(finish_piece, name, s)
        def arrived(some):
            for one in some:
                one.four()

        mine = [gathers[name, n] for n in range(len(WAYS_IN[name]))]
        if name == "out_b":
            for n, one in enumerate(mine):
                todo[f"W.{name}.{n}"] = one.four
        else:
            todo["W." + name] = functools.partial(arrived, mine)

    vec = Vectors(vec_ref)
    totals = Totals(place, short, long, tot, ar_send, ar_recv)
    state, scales, params = {}, {}, {}
    sums_of = {}

    def begin(n, values):
        sums_of[n] = totals.start(values)

    for n in range(1, 20):
        todo[f"A{n}m"] = lambda n=n: sums_of[n].middle()
        todo[f"A{n}l"] = lambda n=n: sums_of[n].late()

    image_copy = pltpu.make_async_copy(img_hbm, raw, io_sem.at[0])
    cot_copy = pltpu.make_async_copy(cot_hbm, cot, io_sem.at[1])
    result_copy = pltpu.make_async_copy(cot, result_hbm, io_sem.at[2])
    grad_copy = pltpu.make_async_copy(raw, images_hbm, io_sem.at[3])

    @token("enter")
    def _():
        image_copy.start()
        cot_copy.start()
        odd = (place.f % 2).astype(F32)
        block_ref[...] = jnp.zeros_like(block_ref)
        at = 0
        for name in NAMES:
            values = small[name][...].astype(F32)
            if values.shape[1] < 128:
                move[0:8, 0:128] = jnp.zeros((8, 128), F32)
                move[0:2, 0 : values.shape[1]] = values
                plain = move[0:8, 0:128]
                values = (plain + (pltpu.roll(plain, 64, 1) - plain) * odd)[0:2]
            for lane in range(0, values.shape[1], 128):
                block_ref[at : at + 1, :] = values[0:1, lane : lane + 128]
                block_ref[at + 10 : at + 11, :] = values[1:2, lane : lane + 128]
                at += 1
        norms[place.f] = block_ref[...]
        enter(place, ((0, 1),) + CHIP_PEERS)

    @token("prep")
    def _():
        pixel = lax.broadcasted_iota(jnp.int32, (BLOCK, 128), 0)
        slot = pixel % 4

        def by_slot(values):
            return jnp.where(slot == 0, values[0], jnp.where(slot == 1, values[1], jnp.where(slot == 2, values[2], values[3])))

        half = by_slot([sides[i] // 2 for i in range(4)])
        inside = ((pixel // 4) % 8 < half) & (pixel // 32 < half)
        mask_ref[...] = jnp.where(inside, 1.0, 0.0).astype(F32)
        gate_ref[...] = by_slot([keep[i] for i in range(4)]).astype(F32)
        move[...] = jnp.zeros_like(move)
        image_copy.wait()

        def plane_rows(row):
            mask = jnp.concatenate([mask_ref[at_block(row, CHUNK), :]] * (x.shape[1] // 128), axis=1)
            for row_par in range(2):
                for col_par in range(2):
                    for col in range(SIDE):
                        move[4 * col : 4 * col + 4, :] = raw[2 * row + row_par, 2 * col + col_par].astype(F32)
                    start = (2 * row_par + col_par) * BLOCK + row * CHUNK
                    x[pl.ds(pl.multiple_of(start, CHUNK), CHUNK), :] = (move[...] * mask).astype(BF16)

        loop(SIDE, plane_rows)
        for p in range(4):
            x[(p + 1) * BLOCK - CHUNK : (p + 1) * BLOCK, :] = jnp.zeros((CHUNK, x.shape[1]), BF16)

    @token("norms")
    def _():
        await_bytes(norms.at[pl.ds(0, 7)], nb_sem.at[1])
        await_bytes(norms.at[pl.ds(0, 7)], nb_sem.at[0])

        def narrow_row(at):
            pieces = [norms[2 * k, at : at + 1, :] + norms[2 * k + 1, at : at + 1, :] for k in range(4)]
            return vec.put(jnp.concatenate(pieces, axis=1))

        def wide_rows(at):
            return [
                vec.put(
                    jnp.concatenate(
                        [norms[2 * j + k // 2, at + k % 2 : at + k % 2 + 1, :] for k in range(4)], axis=1
                    )
                )
                for j in range(4)
            ]

        params["in_a"] = ([narrow_row(0)], [narrow_row(10)])
        params["mid_a"] = ([narrow_row(1)], [narrow_row(11)])
        params["out_a"] = (wide_rows(2), wide_rows(12))
        params["proj_a"] = (wide_rows(4), wide_rows(14))
        params["in_b"] = ([narrow_row(6)], [narrow_row(16)])
        params["mid_b"] = ([narrow_row(7)], [narrow_row(17)])
        params["out_b"] = (wide_rows(8), wide_rows(18))
        lanes = lax.broadcasted_iota(jnp.int32, (1, LANES), 1)
        state["chan_a"] = vec.put(jnp.where(lanes < widths[0], 1.0, 0.0).astype(F32))
        state["chan_b"] = vec.put(jnp.where(lanes < widths[1], 1.0, 0.0).astype(F32))

    def wide_of(ref, start, size=CHUNK):
        return jnp.concatenate([ref[pl.ds(start, size), :]] * 4, axis=1)

    def mask_at(start):
        return wide_of(mask_ref, start)

    def gate_at(start):
        return wide_of(gate_ref, start)

    def set_norm(name, block, first_row, inverse, chan):
        inverse = vec.get(state[inverse])
        average = totals.row(first_row) * inverse
        rstd = lax.rsqrt(totals.row(first_row + 1) * inverse - average * average + EPSILON)
        gain, shift = (vec.get(rows[block]) for rows in params[name])
        keep_lanes = 1.0 if chan is None else vec.get(state[chan])
        by = gain * rstd
        scales[name, block] = dict(
            rstd=vec.put(rstd),
            off=vec.put(-average * rstd),
            by=vec.put(by),
            mul=vec.put(by * keep_lanes),
            add=vec.put((shift - average * by) * keep_lanes),
        )

    def normed(name, block, values):
        s = scales[name, block]
        return values * vec.get(s["mul"]) + vec.get(s["add"])

    def hat(name, block, values):
        s = scales[name, block]
        return values * vec.get(s["rstd"]) + vec.get(s["off"])

    def set_back(name, block, shift_row, gain_row):
        s = scales[name, block]
        inverse = vec.get(state["inv_in" if name == "in_a" else "inv_out"])
        by = vec.get(s["by"])
        pull = by * totals.row(gain_row) * inverse
        s["back_add"] = vec.put(by * totals.row(shift_row) * inverse + pull * vec.get(s["off"]))
        s["back_mul"] = vec.put(pull * vec.get(s["rstd"]))

    def back(name, block, grad, values):
        s = scales[name, block]
        return grad * vec.get(s["by"]) - vec.get(s["back_add"]) - values * vec.get(s["back_mul"])

    def square_terms(ref):
        def terms(start):
            values = ref[pl.ds(start, CHUNK), :]
            return values, values * values

        return terms

    def masked_terms(ref):
        def terms(start):
            values = ref[pl.ds(start, CHUNK), :]
            kept = values * mask_at(start)
            return kept, kept * values

        return terms

    def lane_row(at, lane):
        return vec_ref[at : at + 1, at_block(lane, 128)]

    def add_up(out, count, left, right, product=mm):
        total = product(left(0), right(0))
        for k in range(1, count):
            total = total + product(left(k), right(k))
        out[...] = total

    @token("A1s")
    def _():
        for p in range(4):
            c1[at_block(p, BLOCK), :] = mm(x[at_block(p, BLOCK), :], w_in_a[...])
        begin(1, column_sums(32, 2, square_terms(c1)))

    @token("A19s")
    def _():
        side = [sides[i] for i in range(4)]
        count_in = sum(s * s for s in side).astype(F32)
        count_out = sum((s // 2) * (s // 2) for s in side).astype(F32)
        at = lax.broadcasted_iota(jnp.int32, (8, 128), 0)
        begin(19, jnp.where(at == 0, count_in, jnp.where(at == 1, count_out, 0.0)))
        for bits in (7, 6, 5, 4, 3, 2, 1):
            push(block_ref, norms.at[place.f], nb_sem.at[0], nb_sem.at[1], place.peer(bits, 0))

    @token("A19e")
    def _():
        sums_of[19].end()
        state["inv_in"] = vec.put(1.0 / totals.wide(0))
        state["inv_out"] = vec.put(1.0 / totals.wide(1))

    @token("A1e")
    def _():
        sums_of[1].end()
        set_norm("in_a", 0, 0, "inv_in", "chan_a")
        s = scales["in_a", 0]

        def act_a(lane):
            for row_par in range(2):
                for col_par in range(2):
                    p = 2 * row_par + col_par
                    values = c1[p * BLOCK : (p + 1) * BLOCK, at_block(lane, 128)]
                    scaled = values * lane_row(s["mul"], lane) + lane_row(s["add"], lane)
                    act = scaled * jax.nn.sigmoid(scaled) * mask_ref[...]
                    for t, (u, v) in enumerate(TAPS):
                        if (u != 1) != bool(row_par) or (v != 1) != bool(col_par):
                            continue
                        shift = (32 if u == 0 else 0) + (4 if v == 0 else 0)
                        moved = pltpu.roll(act, shift, 0) if shift else act
                        cols_a[:, pl.ds(pl.multiple_of(t * LANES + lane * 128, 128), 128)] = moved.astype(BF16)

        loop(4, act_a)

    def conv_mid(out, cols, weight):
        add_up(out, 3, lambda k: cols[:, at_block(k, 1536)], lambda k: weight[at_block(k, 1536), :])

    def act_mid(act_ref, ref, name):
        def step(index):
            start = pl.multiple_of(index * CHUNK, CHUNK)
            scaled = normed(name, 0, ref[pl.ds(start, CHUNK), :])
            act_ref[pl.ds(start, CHUNK), :] = (scaled * jax.nn.sigmoid(scaled) * mask_at(start)).astype(BF16)

        loop(BLOCK // CHUNK, step)

    @token("A2s")
    def _():
        conv_mid(c2, cols_a, w_mid_a)
        begin(2, column_sums(8, 2, masked_terms(c2)))

    @token("A2e")
    def _():
        sums_of[2].end()
        set_norm("mid_a", 0, 0, "inv_out", "chan_a")
        act_mid(a2, c2, "mid_a")

    @token("proj")
    def _():
        def project(j):
            cp[at_block(j, BLOCK), :] = mm(x[0:BLOCK, :], w_proj_a[:, at_block(j, LANES)])

        loop(4, project)

    def blocked(ref, j):
        return square_terms(ref.at[pl.ds(j * BLOCK, BLOCK)])

    @token("A3s")
    def _():
        for j in range(4):
            c3[at_block(j, BLOCK), :] = mm(a2[...], w_out_a[:, at_block(j, LANES)])
        begin(3, [row for ref in (c3, cp) for j in range(4) for row in column_sums(8, 2, blocked(ref, j))])

    @token("A3e")
    def _():
        sums_of[3].end()
        for j in range(4):
            set_norm("out_a", j, 2 * j, "inv_out", None)
            set_norm("proj_a", j, 8 + 2 * j, "inv_out", None)
        for j in range(4):

            def join_a(index, j=j):
                start = pl.multiple_of(index * CHUNK, CHUNK)
                rows = pl.ds(j * BLOCK + start, CHUNK)
                pre = normed("out_a", j, c3[rows, :]) + normed("proj_a", j, cp[rows, :])
                out = pre * jax.nn.sigmoid(pre) * mask_at(start)
                bo[rows, :] = out
                feed[pl.ds(start, CHUNK), pl.ds(j * LANES, LANES)] = out.astype(BF16)

            loop(BLOCK // CHUNK, join_a)

    @token("A4s")
    def _():
        add_up(d1, 4, lambda k: feed[:, at_block(k, LANES)], lambda k: w_in_b[at_block(k, LANES), :])
        begin(4, column_sums(8, 2, square_terms(d1)))

    @token("A4e")
    def _():
        sums_of[4].end()
        set_norm("in_b", 0, 0, "inv_out", "chan_b")
        s = scales["in_b", 0]

        def act_b(lane):
            scaled = d1[:, at_block(lane, 128)] * lane_row(s["mul"], lane) + lane_row(s["add"], lane)
            act = scaled * jax.nn.sigmoid(scaled) * mask_ref[...]
            for t, (u, v) in enumerate(TAPS):
                shift = (-(32 * (u - 1) + 4 * (v - 1))) % BLOCK
                moved = pltpu.roll(act, shift, 0) if shift else act
                cols_b[:, pl.ds(pl.multiple_of(t * LANES + lane * 128, 128), 128)] = moved.astype(BF16)

        loop(4, act_b)

    @token("A5s")
    def _():
        conv_mid(d2, cols_b, w_mid_b)
        begin(5, column_sums(8, 2, masked_terms(d2)))

    @token("A5e")
    def _():
        sums_of[5].end()
        set_norm("mid_b", 0, 0, "inv_out", "chan_b")
        act_mid(b2, d2, "mid_b")

    PAIRS = ((0, 2), (1, 3))
    FORTH = {6: 0, 13: 2, 15: 1, 16: 3}
    BACK = {7: 0, 14: 2, 17: 1, 18: 3}

    def expand_b(n, j):
        d3[at_block(j, BLOCK), :] = mm(b2[...], w_out_b[:, at_block(j, LANES)])
        begin(n, column_sums(8, 2, blocked(d3, j)))

    def set_out_b(n, j):
        sums_of[n].end()
        set_norm("out_b", j, 0, "inv_out", None)

    def finish_b(n, j):
        if n == 7:
            cot_copy.wait()
        lanes = pl.ds(j * LANES, LANES)

        def finish(start):
            rows = pl.ds(j * BLOCK + start, CHUNK)
            row = start // CHUNK
            for col in range(SIDE):
                move[4 * col : 4 * col + 4, 0:LANES] = cot[row, col, :, lanes].astype(F32)
            mask, gate, hidden = mask_at(start), gate_at(start), d3[rows, :]
            pre = bo[rows, :] + gate * normed("out_b", j, hidden)
            part = jax.nn.sigmoid(pre)
            grad = move[:, 0:LANES] * mask * (part * (1.0 + pre * (1.0 - part)))
            move[:, LANES : 2 * LANES] = pre * part * mask
            for col in range(SIDE):
                cot[row, col, :, lanes] = move[4 * col : 4 * col + 4, LANES : 2 * LANES].astype(BF16)
            bo[rows, :] = grad
            grad = grad * gate
            return grad, grad * hat("out_b", j, hidden)

        values = column_sums(SIDE, 2, finish)
        bo[(j + 1) * BLOCK - CHUNK : (j + 1) * BLOCK, :] = jnp.zeros((CHUNK, LANES), F32)
        begin(n, values)
        if n == 18:
            result_copy.start()

    for n, j in FORTH.items():
        todo[f"A{n}s"], todo[f"A{n}e"] = functools.partial(expand_b, n, j), functools.partial(set_out_b, n, j)
    for n, j in BACK.items():
        todo[f"A{n}s"] = functools.partial(finish_b, n, j)

    @token("sent")
    def _():
        for one in gathers.values():
            one.sent()

    def keep_sums(n, at):
        rows = sums_of[n].rows
        sums[at : at + rows, :] = tot[0:rows, :]

    def low_out_b(n, j):
        sums_of[n].end()
        keep_sums(n, 16 * (j % 2) + 8 * (j // 2))
        set_back("out_b", j, 0, 1)

        def step(index):
            start = pl.multiple_of(index * CHUNK, CHUNK)
            rows = pl.ds(j * BLOCK + start, CHUNK)
            grad = back("out_b", j, bo[rows, :] * gate_at(start), d3[rows, :]) * mask_at(start)
            dout[pl.ds(start, CHUNK), pl.ds(j * LANES, LANES)] = grad.astype(BF16)

        loop(BLOCK // CHUNK, step)

    for n, j in BACK.items():
        todo[f"A{n}e"] = functools.partial(low_out_b, n, j)

    def through_out(weight):
        add_up(dz, 4, lambda k: dout[:, at_block(k, LANES)], lambda k: weight[:, at_block(k, LANES)], mm_nt)

    def slope_terms(grad_ref, ref, name, chan):
        def terms(start):
            rows = pl.ds(start, CHUNK)
            hidden = ref[rows, :]
            mask = mask_at(pl.multiple_of(start % BLOCK, CHUNK) if grad_ref.shape[0] > BLOCK else start)
            grad = grad_ref[rows, :] * mask * vec.get(state[chan]) * slope_of(normed(name, 0, hidden))
            grad_ref[rows, :] = grad
            return grad, grad * hat(name, 0, hidden)

        return terms

    def through_pair(pair):
        return [mm_nt(dout[:, at_block(j, LANES)], w_out_b[:, at_block(j, LANES)]) for j in pair]

    @token("D8")
    def _():
        first, second = through_pair(PAIRS[0])
        dz[...] = first + second

    @token("A8s")
    def _():
        first, second = through_pair(PAIRS[1])
        dz[...] += first + second
        tell("out_b")
        begin(8, column_sums(8, 2, slope_terms(dz, d2, "mid_b", "chan_b")))

    def grad_out(act_ref, j):
        g_out[:, at_block(j, LANES)] = mm_tn(act_ref[...], dout[:, at_block(j, LANES)]).astype(BF16)

    tokens("g.out_b", 2, 2, lambda k: grad_out(b2, 2 * (k % 2) + k // 2))

    @token("A8e")
    def _():
        sums_of[8].end()
        keep_sums(8, 32)
        set_back("mid_b", 0, 0, 1)

    def low_mid(name, ref, shifts):
        s = scales[name, 0]

        def step(lane):
            lanes = at_block(lane, 128)
            grad = (
                dz[:, lanes] * lane_row(s["by"], lane)
                - lane_row(s["back_add"], lane)
                - ref[:, lanes] * lane_row(s["back_mul"], lane)
            ) * mask_ref[...]
            dm[:, lanes] = grad.astype(BF16)
            for k, shift in enumerate(shifts):
                moved = pltpu.roll(grad, shift, 0) if shift else grad
                g_mid[k * BLOCK : (k + 1) * BLOCK, lanes] = moved.astype(BF16)

        loop(4, step)

    @token("A9s")
    def _():
        low_mid("mid_b", d2, [(32 * (u - 1) + 4 * (v - 1)) % BLOCK for u, v in TAPS])
        add_up(dz, 9, lambda t: g_mid[at_block(t, BLOCK), :], lambda t: w_mid_b[at_block(t, LANES), :], mm_nt)
        tell("mid_b")
        begin(9, column_sums(8, 2, slope_terms(dz, d1, "in_b", "chan_b")))

    def grad_mid(cols, t):
        g_mid[at_block(t, LANES), :] = mm_tn(cols[:, at_block(t, LANES)], dm[...]).astype(BF16)

    tokens("g.mid_b", 3, 3, lambda t: grad_mid(cols_b, t))

    @token("A9e")
    def _():
        sums_of[9].end()
        keep_sums(9, 40)
        set_back("in_b", 0, 0, 1)

    @token("A10s")
    def _():
        def low_first_b(index):
            start = pl.multiple_of(index * CHUNK, CHUNK)
            rows = pl.ds(start, CHUNK)
            df[rows, :] = (back("in_b", 0, dz[rows, :], d1[rows, :]) * mask_at(start)).astype(BF16)

        loop(BLOCK // CHUNK, low_first_b)

        for j in range(4):
            bo[at_block(j, BLOCK), :] += mm_nt(df[...], w_in_b[at_block(j, LANES), :])
        tell("in_b")
        values = []
        for j in range(4):

            def join_back(start, j=j):
                rows = pl.ds(j * BLOCK + start, CHUNK)
                left, right = c3[rows, :], cp[rows, :]
                pre = normed("out_a", j, left) + normed("proj_a", j, right)
                grad = bo[rows, :] * mask_at(start) * slope_of(pre)
                bo[rows, :] = grad
                return grad, grad * hat("out_a", j, left), grad * hat("proj_a", j, right)

            values += column_sums(8, 3, join_back)
        begin(10, values)

    def grad_in_b(j):
        g_in[at_block(j, LANES), :] = mm_tn(feed[:, at_block(j, LANES)], df[...]).astype(BF16)

    tokens("g.in_b", 2, 2, grad_in_b)

    @token("A10e")
    def _():
        sums_of[10].end()
        keep_sums(10, 48)
        for j in range(4):
            set_back("out_a", j, 3 * j, 3 * j + 1)
            set_back("proj_a", j, 3 * j, 3 * j + 2)

    @token("A11s")
    def _():
        for j in range(4):

            def low_both(index, j=j):
                start = pl.multiple_of(index * CHUNK, CHUNK)
                rows = pl.ds(j * BLOCK + start, CHUNK)
                near_rows, lanes = pl.ds(start, CHUNK), pl.ds(j * LANES, LANES)
                grad, mask = bo[rows, :], mask_at(start)
                dout[near_rows, lanes] = (back("out_a", j, grad, c3[rows, :]) * mask).astype(BF16)
                dproj[near_rows, lanes] = (back("proj_a", j, grad, cp[rows, :]) * mask).astype(BF16)

            loop(BLOCK // CHUNK, low_both)
        through_out(w_out_a)
        tell("out_a")
        begin(11, column_sums(8, 2, slope_terms(dz, c2, "mid_a", "chan_a")))

    tokens("g.out_a", 2, 2, lambda j: grad_out(a2, j))

    def grad_proj(n):
        i, j = n // 4, n % 4
        g_proj[at_block(i, LANES), at_block(j, LANES)] = mm_tn(
            x[0:BLOCK, at_block(i, LANES)], dproj[:, at_block(j, LANES)]
        ).astype(BF16)

    tokens("g.proj_a", 2, 4, grad_proj)

    def back_proj(n):
        out, rows = d3.at[pl.ds(n * BLOCK, BLOCK)], pl.ds(n * LANES, LANES)
        add_up(out, 4, lambda k: dproj[:, at_block(k, LANES)], lambda k: w_proj_a[rows, at_block(k, LANES)], mm_nt)

    @token("dproj.0")
    def _():
        back_proj(0)

    @token("dproj.1")
    def _():
        back_proj(1)
        tell("proj_a")

    @token("A11e")
    def _():
        sums_of[11].end()
        keep_sums(11, 96)
        set_back("mid_a", 0, 0, 1)

    @token("A12s")
    def _():
        low_mid("mid_a", c2, [(-(32 * r + 4 * s)) % BLOCK for r in range(2) for s in range(2)])
        for row_par in range(2):
            for col_par in range(2):
                grad = None
                for t, (u, v) in enumerate(TAPS):
                    if (u != 1) != bool(row_par) or (v != 1) != bool(col_par):
                        continue
                    moved = 2 * (1 if u == 0 else 0) + (1 if v == 0 else 0)
                    term = mm_nt(g_mid[moved * BLOCK : (moved + 1) * BLOCK, :], w_mid_a[t * LANES : (t + 1) * LANES, :])
                    grad = term if grad is None else grad + term
                bo[pl.ds((2 * row_par + col_par) * BLOCK, BLOCK), :] = grad
        tell("mid_a")
        begin(12, column_sums(32, 2, slope_terms(bo, c1, "in_a", "chan_a")))

    tokens("g.mid_a", 3, 3, lambda t: grad_mid(cols_a, t))

    @token("A12e")
    def _():
        sums_of[12].end()
        keep_sums(12, 104)
        set_back("in_a", 0, 0, 1)
        for p in range(4):

            def low_first_a(index, p=p):
                start = pl.multiple_of(index * CHUNK, CHUNK)
                rows = pl.ds(p * BLOCK + start, CHUNK)
                grad = back("in_a", 0, bo[rows, :], c1[rows, :]) * mask_at(start)
                cols_b[pl.ds(start, CHUNK), p * LANES : (p + 1) * LANES] = grad.astype(BF16)

            loop(BLOCK // CHUNK, low_first_a)

    def first_grad(p):
        return cols_b[:, p * LANES : (p + 1) * LANES]

    def grad_in_a(i):
        lanes = at_block(i, 256)
        total = mm_tn(x[0:BLOCK, lanes], first_grad(0))
        for p in range(1, 4):
            total = total + mm_tn(x[p * BLOCK : (p + 1) * BLOCK, lanes], first_grad(p))
        g_in[at_block(i, 256), :] = total.astype(BF16)

    tokens("g.in_a", 2, 2, grad_in_a)

    def image_grad(planes):
        for p in planes:
            for h in range(2):
                lanes = pl.ds(h * LANES, LANES)
                grad = mm_nt(first_grad(p), w_in_a[h * LANES : (h + 1) * LANES, :])
                dz[...] = grad + d3[h * BLOCK : (h + 1) * BLOCK, :] if p == 0 else grad

                def pixels(row, p=p, lanes=lanes):
                    move[:, 0:LANES] = dz[at_block(row, CHUNK), :]
                    for col in range(SIDE):
                        raw[2 * row + p // 2, 2 * col + p % 2, :, lanes] = move[4 * col : 4 * col + 4, 0:LANES].astype(BF16)

                loop(SIDE, pixels)

    @token("img.0")
    def _():
        image_grad((0, 1))

    @token("img.1")
    def _():
        image_grad((2, 3))
        grad_copy.start()
        tell("in_a")

    @token("own")
    def _():
        def own_row(at, out, k):
            if out.shape[1] >= 128:
                for lane in range(2):
                    line = sums[pl.ds(at + 2 * (place.f % 2) + lane, 1), :]
                    out[k : k + 1, lane * 128 : (lane + 1) * 128] = line
            else:
                odd = (place.f % 2).astype(F32)
                move[0:1, 0:128] = sums[pl.ds(at + place.f // 2, 1), :]
                line = move[0:8, 0:128]
                line = line + (pltpu.roll(line, 64, 1) - line) * odd
                out[k : k + 1, :] = line[0:1, 0 : out.shape[1]]

        for name, at in (("mid_b", 32), ("in_b", 40), ("mid_a", 96), ("in_a", 104)):
            own_row(at + 4, owned[name], 0)
            own_row(at, owned[name], 1)
        block = place.f // 2
        pair_at = 16 * (block % 2) + 8 * (block // 2)
        for name, at, gain in (("out_b", pair_at, 4), ("out_a", 48 + 12 * block, 4), ("proj_a", 48 + 12 * block, 8)):
            own_row(at + gain, owned[name], 0)
            own_row(at, owned[name], 1)
        for one in own_copies:
            one.start()

    steps = sorted(todo)
    if sorted(RUN) != list(range(len(steps))):
        raise ValueError(len(steps))
    for index in RUN:
        todo[steps[index]]()
    result_copy.wait()
    grad_copy.wait()
    for one in scatters.values():
        one.sent()
    for one in own_copies + out_copies:
        one.wait()


def finish_kernel(*refs):
    arrays_in, arrays_out, held, wide = refs[:16], refs[16:32], refs[32:48], refs[48:55]
    in_sem, out_sem = refs[55:]
    loads = [pltpu.make_async_copy(a, b, in_sem.at[i]) for i, (a, b) in enumerate(zip(arrays_in, held))]
    leaving = held[:9] + wide
    stores = [pltpu.make_async_copy(a, b, out_sem.at[i]) for i, (a, b) in enumerate(zip(leaving, arrays_out))]
    order = list(range(9, 16)) + list(range(9))
    for i in order:
        loads[i].start()
    for i in order:
        loads[i].wait()
        if i >= 9:
            narrow, target = held[i], wide[i - 9]
            rows, columns = narrow.shape
            chunk = chunk_of(rows, columns)

            def step(index, carry, narrow=narrow, target=target, chunk=chunk):
                at = pl.ds(pl.multiple_of(index * chunk, 16), chunk)
                target[at, :] = narrow[at, :].astype(F32)
                return carry

            lax.fori_loop(0, rows // chunk, step, 0)
        stores[i].start()
    for i in order:
        stores[i].wait()


def finish_call(plain, grads):
    anywhere = pl.BlockSpec(memory_space=pl.ANY)
    return pl.pallas_call(
        finish_kernel,
        out_shape=[jax.ShapeDtypeStruct(one.shape, one.dtype) for one in plain]
        + [jax.ShapeDtypeStruct(one.shape, F32) for one in grads],
        in_specs=[anywhere] * 16,
        out_specs=[anywhere] * 16,
        scratch_shapes=[pltpu.VMEM(one.shape, one.dtype) for one in (*plain, *grads)]
        + [pltpu.VMEM(one.shape, F32) for one in grads]
        + [pltpu.SemaphoreType.DMA((16,)), pltpu.SemaphoreType.DMA((16,))],
        compiler_params=pltpu.CompilerParams(vmem_limit_bytes=64 * 2**20),
        name="finish_step",
    )(*plain, *grads)


def body_fast(
    images,
    image_sides,
    widths,
    keep_gate,
    w_in_a,
    w_mid_a,
    w_out_a,
    w_proj_a,
    norm_in_a,
    norm_mid_a,
    norm_out_a,
    norm_proj_a,
    w_in_b,
    w_mid_b,
    w_out_b,
    norm_in_b,
    norm_mid_b,
    norm_out_b,
    cotangent,
):
    width_in, width_out = images.shape[3], cotangent.shape[3]
    turned = (1, 2, 0, 3)
    images, cotangent = images.transpose(turned), cotangent.transpose(turned)
    norms = (norm_in_a, norm_mid_a, norm_out_a, norm_proj_a, norm_in_b, norm_mid_b, norm_out_b)
    shards = (w_in_a, w_mid_a, w_out_a, w_proj_a, w_in_b, w_mid_b, w_out_b)
    vmem = pl.BlockSpec(memory_space=pltpu.VMEM)
    smem = pl.BlockSpec(memory_space=pltpu.SMEM)
    anywhere = pl.BlockSpec(memory_space=pl.ANY)
    wholes = [(8 * one.shape[0], one.shape[1]) for one in shards]
    pieces = max(sum(len(one) for one in ways.values()) for ways in (WAYS_IN, WAYS_OUT))
    outs = pl.pallas_call(
        step_kernel,
        out_shape=[jax.ShapeDtypeStruct(cotangent.shape, BF16), jax.ShapeDtypeStruct(images.shape, BF16)]
        + [jax.ShapeDtypeStruct(one.shape, F32) for one in norms]
        + [jax.ShapeDtypeStruct(one.shape, BF16) for one in shards],
        in_specs=[anywhere, anywhere, smem, smem, smem] + [vmem] * 7 + [anywhere] * 7,
        out_specs=[anywhere] * 16,
        scratch_shapes=[pltpu.VMEM(one.shape, F32) for one in norms]
        + [pltpu.VMEM(one.shape, BF16) for one in shards]
        + [pltpu.VMEM(shape, BF16) for shape in wholes]
        + [
            pltpu.VMEM(images.shape, BF16),
            pltpu.VMEM(cotangent.shape, BF16),
            pltpu.VMEM((4 * BLOCK, width_in), BF16),
            pltpu.VMEM((4 * BLOCK, LANES), F32),
            pltpu.VMEM((BLOCK, 9 * LANES), BF16),
            pltpu.VMEM((BLOCK, LANES), F32),
            pltpu.VMEM((BLOCK, LANES), BF16),
            pltpu.VMEM((4 * BLOCK, LANES), F32),
            pltpu.VMEM((4 * BLOCK, LANES), F32),
            pltpu.VMEM((4 * BLOCK, LANES), F32),
            pltpu.VMEM((BLOCK, width_out), BF16),
            pltpu.VMEM((BLOCK, LANES), F32),
            pltpu.VMEM((BLOCK, 9 * LANES), BF16),
            pltpu.VMEM((BLOCK, LANES), F32),
            pltpu.VMEM((BLOCK, LANES), BF16),
            pltpu.VMEM((4 * BLOCK, LANES), F32),
            pltpu.VMEM((BLOCK, LANES), F32),
            pltpu.VMEM((BLOCK, LANES), BF16),
            pltpu.VMEM((BLOCK, LANES), BF16),
            pltpu.VMEM((BLOCK, width_out), BF16),
            pltpu.VMEM((BLOCK, width_out), BF16),
            pltpu.VMEM(wholes[1], BF16),
            pltpu.VMEM(wholes[2], BF16),
            pltpu.VMEM(wholes[4], BF16),
            pltpu.VMEM(wholes[3], BF16),
            pltpu.VMEM((BLOCK, 128), F32),
            pltpu.VMEM((BLOCK, 128), F32),
            pltpu.VMEM((CHUNK, width_in), F32),
            pltpu.VMEM((8, 24, 128), F32),
            pltpu.VMEM((24, 128), F32),
            pltpu.VMEM((160, LANES), F32),
            pltpu.VMEM((SHORT_SETS, 18, 8, 128), F32),
            pltpu.VMEM((10, 64, 128), F32),
            pltpu.VMEM((64, 128), F32),
            pltpu.VMEM((112, 128), F32),
            pltpu.SemaphoreType.DMA((4,)),
            pltpu.SemaphoreType.DMA((pieces,)),
            pltpu.SemaphoreType.DMA((pieces, 6)),
            pltpu.SemaphoreType.DMA((SHORT_SETS + 1,)),
            pltpu.SemaphoreType.DMA((2 * SHORT_SETS + 3,)),
            pltpu.SemaphoreType.DMA((2,)),
            pltpu.SemaphoreType.DMA((2, 7)),
            pltpu.SemaphoreType.REGULAR((7,)),
        ],
        compiler_params=pltpu.CompilerParams(
            collective_id=0, has_side_effects=True, vmem_limit_bytes=64 * 2**20
        ),
        name="whole_step",
    )(images, cotangent, image_sides, keep_gate, widths, *norms, *shards)
    back_turned = (2, 0, 1, 3)
    outs = finish_call(outs[:9], outs[9:])
    own, finals = outs[2:9], outs[9:]
    return (
        outs[0].transpose(back_turned),
        outs[1].transpose(back_turned),
        *finals[:4],
        *own[:4],
        *finals[4:],
        *own[4:],
    )


def fits(mesh):
    return mesh.shape[FSDP] == 8 and mesh.shape[DP] == 4


def gather_plain(shards):
    return [lax.all_gather(one, FSDP, axis=0, tiled=True) for one in shards]


def scatter_plain(grads):
    parts = [lax.psum_scatter(one, FSDP, scatter_dimension=0, tiled=True) for one in grads]
    return lax.psum(tuple(parts), DP)


def sum_pair(first, second):
    return lax.psum((first, second), (FSDP, DP))


def silu_slope(values):
    sigmoid_part = jax.nn.sigmoid(values)
    return sigmoid_part * (1.0 + values * (1.0 - sigmoid_part))


def pixel_masks(image_sides, side_in, side_out):
    half_sides = image_sides // 2
    rows_in = jnp.arange(side_in, dtype=jnp.int32)
    rows_out = jnp.arange(side_out, dtype=jnp.int32)
    inside_in = (rows_in[None, :, None] < image_sides[:, None, None]) & (
        rows_in[None, None, :] < image_sides[:, None, None]
    )
    inside_out = (rows_out[None, :, None] < half_sides[:, None, None]) & (
        rows_out[None, None, :] < half_sides[:, None, None]
    )
    local_counts = jnp.stack(
        [jnp.sum(image_sides * image_sides), jnp.sum(half_sides * half_sides)]
    ).astype(jnp.float32)
    return (
        inside_in.astype(jnp.float32)[..., None],
        inside_out.astype(jnp.float32)[..., None],
        local_counts,
    )


def norm_stats(hidden, pixel_mask, local_counts, count_slot):
    sum_values, sum_squares = sum_pair(
        jnp.sum(hidden * pixel_mask, axis=(0, 1, 2)),
        jnp.sum(hidden * hidden * pixel_mask, axis=(0, 1, 2)),
    )
    pixel_total = local_counts[count_slot]
    average = sum_values / pixel_total
    inv_std = lax.rsqrt(sum_squares / pixel_total - average * average + EPSILON)
    return (average, inv_std, pixel_total)


def normalize(hidden, stats_now, params, channel):
    average, inv_std, pixel_total = stats_now
    scaled = (hidden - average) * inv_std
    params_wide = params.astype(jnp.float32)
    return (scaled, (scaled * params_wide[0] + params_wide[1]) * channel)


def norm_backward(grad_norm, scaled, stats_now, params, pixel_mask):
    average, inv_std, pixel_total = stats_now
    shift_sum, gain_sum = sum_pair(
        jnp.sum(grad_norm, axis=(0, 1, 2)), jnp.sum(grad_norm * scaled, axis=(0, 1, 2))
    )
    gain_row = params[0].astype(jnp.float32)
    grad_hidden = (
        gain_row
        * inv_std
        * (grad_norm - shift_sum / pixel_total - scaled * gain_sum / pixel_total)
        * pixel_mask
    )
    return (grad_hidden.astype(jnp.bfloat16), gain_sum, shift_sum)


def taps_stride_two(activations):
    slot_count = activations.shape[0]
    half_side = activations.shape[1] // 2
    lane_count = activations.shape[3]
    padded = jnp.pad(activations, ((0, 0), (1, 1), (1, 1), (0, 0)))
    parity_grid = padded.reshape(slot_count, half_side + 1, 2, half_side + 1, 2, lane_count)
    pieces = [
        parity_grid[
            :,
            row_tap // 2 : row_tap // 2 + half_side,
            row_tap % 2,
            col_tap // 2 : col_tap // 2 + half_side,
            col_tap % 2,
            :,
        ]
        for row_tap in range(3)
        for col_tap in range(3)
    ]
    return jnp.concatenate(pieces, axis=-1)


def fold_stride_two(grad_cols, side_in):
    slot_count = grad_cols.shape[0]
    half_side = grad_cols.shape[1]
    lane_count = grad_cols.shape[3] // 9
    planes = [
        [
            jnp.zeros((slot_count, half_side + 1, half_side + 1, lane_count), jnp.float32)
            for col_par in range(2)
        ]
        for row_par in range(2)
    ]
    for row_tap in range(3):
        for col_tap in range(3):
            tap_index = row_tap * 3 + col_tap
            tap_piece = grad_cols[..., tap_index * lane_count : (tap_index + 1) * lane_count]
            placed = jnp.pad(
                tap_piece,
                (
                    (0, 0),
                    (row_tap // 2, 1 - row_tap // 2),
                    (col_tap // 2, 1 - col_tap // 2),
                    (0, 0),
                ),
            )
            planes[row_tap % 2][col_tap % 2] = planes[row_tap % 2][col_tap % 2] + placed
    parity_grid = jnp.stack([jnp.stack(planes[0], axis=3), jnp.stack(planes[1], axis=3)], axis=2)
    whole_grid = parity_grid.reshape(slot_count, side_in + 2, side_in + 2, lane_count)
    return whole_grid[:, 1:-1, 1:-1, :]


def taps_stride_one(activations):
    side_now = activations.shape[1]
    padded = jnp.pad(activations, ((0, 0), (1, 1), (1, 1), (0, 0)))
    pieces = [
        padded[:, row_tap : row_tap + side_now, col_tap : col_tap + side_now, :]
        for row_tap in range(3)
        for col_tap in range(3)
    ]
    return jnp.concatenate(pieces, axis=-1)


def fold_stride_one(grad_cols):
    lane_count = grad_cols.shape[3] // 9
    whole_grid = None
    for row_tap in range(3):
        for col_tap in range(3):
            tap_index = row_tap * 3 + col_tap
            tap_piece = grad_cols[..., tap_index * lane_count : (tap_index + 1) * lane_count]
            placed = jnp.pad(
                tap_piece, ((0, 0), (row_tap, 2 - row_tap), (col_tap, 2 - col_tap), (0, 0))
            )
            whole_grid = placed if whole_grid is None else whole_grid + placed
    return whole_grid[:, 1:-1, 1:-1, :]


def contract(left_side, right_side):
    return lax.dot_general(
        left_side,
        right_side,
        (((0, 1, 2), (0, 1, 2)), ((), ())),
        preferred_element_type=jnp.float32,
    )


def back_project(gradient, weight):
    return lax.dot_general(
        gradient, weight, (((3,), (1,)), ((), ())), preferred_element_type=jnp.float32
    )


def own_shard(pair_sums):
    gain_sum, shift_sum = pair_sums
    shard_width = gain_sum.shape[0] // lax.axis_size(FSDP)
    offset = lax.axis_index(FSDP) * shard_width
    return jnp.stack(
        [
            lax.dynamic_slice_in_dim(gain_sum, offset, shard_width, 0),
            lax.dynamic_slice_in_dim(shift_sum, offset, shard_width, 0),
        ]
    )


def block_a_forward(inputs, weights, mask_in, mask_out, local_counts, channel, saved_stats):
    w_in, w_mid, w_out, w_proj, norm_in, norm_mid, norm_out, norm_proj = weights
    conv_first = jnp.dot(inputs, w_in, preferred_element_type=jnp.float32)
    stats_first = (
        norm_stats(conv_first, mask_in, local_counts, 0) if saved_stats is None else saved_stats[0]
    )
    scaled_first, normed_first = normalize(conv_first, stats_first, norm_in, channel)
    act_first = (jax.nn.silu(normed_first) * mask_in).astype(jnp.bfloat16)
    cols_mid = taps_stride_two(act_first)
    conv_mid = jnp.dot(cols_mid, w_mid, preferred_element_type=jnp.float32)
    stats_mid = (
        norm_stats(conv_mid, mask_out, local_counts, 1) if saved_stats is None else saved_stats[1]
    )
    scaled_mid, normed_mid = normalize(conv_mid, stats_mid, norm_mid, channel)
    act_mid = (jax.nn.silu(normed_mid) * mask_out).astype(jnp.bfloat16)
    conv_out = jnp.dot(act_mid, w_out, preferred_element_type=jnp.float32)
    slot_count, side_in, lane_count = (inputs.shape[0], inputs.shape[1], inputs.shape[3])
    sampled = inputs.reshape(slot_count, side_in // 2, 2, side_in // 2, 2, lane_count)[
        :, :, 0, :, 0, :
    ]
    conv_proj = jnp.dot(sampled, w_proj, preferred_element_type=jnp.float32)
    conv_both = jnp.concatenate([conv_out, conv_proj], axis=-1)
    norm_both = jnp.concatenate([norm_out, norm_proj], axis=-1)
    stats_both = (
        norm_stats(conv_both, mask_out, local_counts, 1) if saved_stats is None else saved_stats[2]
    )
    scaled_both, normed_both = normalize(conv_both, stats_both, norm_both, 1.0)
    width_out = conv_out.shape[-1]
    pre_sum = normed_both[..., :width_out] + normed_both[..., width_out:]
    block_out = jax.nn.silu(pre_sum) * mask_out
    saved_values = (
        scaled_first,
        normed_first,
        act_first,
        cols_mid,
        scaled_mid,
        normed_mid,
        act_mid,
        sampled,
        scaled_both,
        pre_sum,
    )
    return (block_out, (stats_first, stats_mid, stats_both), saved_values)


def block_a_backward(
    grad_out, inputs, weights, stats_all, saved_values, mask_in, mask_out, channel
):
    w_in, w_mid, w_out, w_proj, norm_in, norm_mid, norm_out, norm_proj = weights
    stats_first, stats_mid, stats_both = stats_all
    (
        scaled_first,
        normed_first,
        act_first,
        cols_mid,
        scaled_mid,
        normed_mid,
        act_mid,
        sampled,
        scaled_both,
        pre_sum,
    ) = saved_values
    grad_pre = grad_out * mask_out * silu_slope(pre_sum)
    grad_both = jnp.concatenate([grad_pre, grad_pre], axis=-1)
    norm_both = jnp.concatenate([norm_out, norm_proj], axis=-1)
    low_both, gain_both, shift_both = norm_backward(
        grad_both, scaled_both, stats_both, norm_both, mask_out
    )
    width_out = grad_pre.shape[-1]
    low_out = low_both[..., :width_out]
    low_proj = low_both[..., width_out:]
    grad_w_out = contract(act_mid, low_out)
    grad_w_proj = contract(sampled, low_proj)
    grad_norm_mid = back_project(low_out, w_out) * mask_out * channel * silu_slope(normed_mid)
    low_mid, gain_mid, shift_mid = norm_backward(
        grad_norm_mid, scaled_mid, stats_mid, norm_mid, mask_out
    )
    grad_w_mid = contract(cols_mid, low_mid)
    grad_act_first = fold_stride_two(back_project(low_mid, w_mid), inputs.shape[1])
    grad_norm_first = grad_act_first * mask_in * channel * silu_slope(normed_first)
    low_first, gain_first, shift_first = norm_backward(
        grad_norm_first, scaled_first, stats_first, norm_in, mask_in
    )
    grad_w_in = contract(inputs, low_first)
    spread = lax.pad(
        back_project(low_proj, w_proj),
        jnp.float32(0.0),
        ((0, 0, 0), (0, 1, 1), (0, 1, 1), (0, 0, 0)),
    )
    grad_inputs = (back_project(low_first, w_in) + spread) * mask_in
    norm_grads = (
        (gain_first, shift_first),
        (gain_mid, shift_mid),
        (gain_both[:width_out], shift_both[:width_out]),
        (gain_both[width_out:], shift_both[width_out:]),
    )
    return (grad_inputs, (grad_w_in, grad_w_mid, grad_w_out, grad_w_proj), norm_grads)


def block_b_forward(block_in, weights, mask_out, local_counts, channel, depth_gate, saved_stats):
    w_in, w_mid, w_out, norm_in, norm_mid, norm_out = weights
    feed_in = block_in.astype(jnp.bfloat16)
    conv_first = jnp.dot(feed_in, w_in, preferred_element_type=jnp.float32)
    stats_first = (
        norm_stats(conv_first, mask_out, local_counts, 1) if saved_stats is None else saved_stats[0]
    )
    scaled_first, normed_first = normalize(conv_first, stats_first, norm_in, channel)
    act_first = (jax.nn.silu(normed_first) * mask_out).astype(jnp.bfloat16)
    cols_mid = taps_stride_one(act_first)
    conv_mid = jnp.dot(cols_mid, w_mid, preferred_element_type=jnp.float32)
    stats_mid = (
        norm_stats(conv_mid, mask_out, local_counts, 1) if saved_stats is None else saved_stats[1]
    )
    scaled_mid, normed_mid = normalize(conv_mid, stats_mid, norm_mid, channel)
    act_mid = (jax.nn.silu(normed_mid) * mask_out).astype(jnp.bfloat16)
    conv_out = jnp.dot(act_mid, w_out, preferred_element_type=jnp.float32)
    stats_out = (
        norm_stats(conv_out, mask_out, local_counts, 1) if saved_stats is None else saved_stats[2]
    )
    scaled_out, normed_out = normalize(conv_out, stats_out, norm_out, 1.0)
    pre_sum = block_in + depth_gate * normed_out
    result = jax.nn.silu(pre_sum) * mask_out
    saved_values = (
        feed_in,
        scaled_first,
        normed_first,
        act_first,
        cols_mid,
        scaled_mid,
        normed_mid,
        act_mid,
        scaled_out,
        pre_sum,
    )
    return (result, (stats_first, stats_mid, stats_out), saved_values)


def block_b_backward(grad_out, weights, stats_all, saved_values, mask_out, channel, depth_gate):
    w_in, w_mid, w_out, norm_in, norm_mid, norm_out = weights
    stats_first, stats_mid, stats_out = stats_all
    (
        feed_in,
        scaled_first,
        normed_first,
        act_first,
        cols_mid,
        scaled_mid,
        normed_mid,
        act_mid,
        scaled_out,
        pre_sum,
    ) = saved_values
    grad_pre = grad_out * mask_out * silu_slope(pre_sum)
    low_out, gain_out, shift_out = norm_backward(
        grad_pre * depth_gate, scaled_out, stats_out, norm_out, mask_out
    )
    grad_w_out = contract(act_mid, low_out)
    grad_norm_mid = back_project(low_out, w_out) * mask_out * channel * silu_slope(normed_mid)
    low_mid, gain_mid, shift_mid = norm_backward(
        grad_norm_mid, scaled_mid, stats_mid, norm_mid, mask_out
    )
    grad_w_mid = contract(cols_mid, low_mid)
    grad_norm_first = (
        fold_stride_one(back_project(low_mid, w_mid))
        * mask_out
        * channel
        * silu_slope(normed_first)
    )
    low_first, gain_first, shift_first = norm_backward(
        grad_norm_first, scaled_first, stats_first, norm_in, mask_out
    )
    grad_w_in = contract(feed_in, low_first)
    grad_in = grad_pre + back_project(low_first, w_in)
    norm_grads = ((gain_first, shift_first), (gain_mid, shift_mid), (gain_out, shift_out))
    return (grad_in, (grad_w_in, grad_w_mid, grad_w_out), norm_grads)


def body(
    images,
    image_sides,
    widths,
    keep_gate,
    w_in_a,
    w_mid_a,
    w_out_a,
    w_proj_a,
    norm_in_a,
    norm_mid_a,
    norm_out_a,
    norm_proj_a,
    w_in_b,
    w_mid_b,
    w_out_b,
    norm_in_b,
    norm_mid_b,
    norm_out_b,
    cotangent,
):
    mask_in, mask_out, local_counts = pixel_masks(image_sides, images.shape[1], cotangent.shape[1])
    lane_ids = jnp.arange(w_mid_a.shape[1], dtype=jnp.int32)
    channel_a = (lane_ids < widths[0]).astype(jnp.float32)
    channel_b = (lane_ids < widths[1]).astype(jnp.float32)
    depth_gate = keep_gate.astype(jnp.float32)[:, None, None, None]
    inputs = images * mask_in.astype(jnp.bfloat16)
    total_counts = lax.psum(local_counts, (FSDP, DP))
    gathered = gather_plain((w_in_a, w_mid_a, w_out_a, w_proj_a, w_in_b, w_mid_b, w_out_b))
    norms = lax.all_gather(
        jnp.concatenate(
            [norm_in_a, norm_mid_a, norm_out_a, norm_proj_a, norm_in_b, norm_mid_b, norm_out_b], axis=1
        ),
        FSDP,
        axis=0,
    )
    wide = []
    place = 0
    for one in (norm_in_a, norm_mid_a, norm_out_a, norm_proj_a, norm_in_b, norm_mid_b, norm_out_b):
        width = one.shape[1]
        wide.append(norms[:, :, place : place + width].transpose(1, 0, 2).reshape(2, -1))
        place += width
    weights_a = tuple(gathered[:4]) + tuple(wide[:4])
    weights_b = tuple(gathered[4:]) + tuple(wide[4:])
    block_out, stats_a, redone_a = block_a_forward(
        inputs, weights_a, mask_in, mask_out, total_counts, channel_a, None
    )
    result, stats_b, redone_b = block_b_forward(
        block_out, weights_b, mask_out, total_counts, channel_b, depth_gate, None
    )
    grad_block, grads_b, norms_b = block_b_backward(
        cotangent.astype(jnp.float32), weights_b, stats_b, redone_b, mask_out, channel_b, depth_gate
    )
    grad_inputs, grads_a, norms_a = block_a_backward(
        grad_block, inputs, weights_a, stats_a, redone_a, mask_in, mask_out, channel_a
    )
    finals = scatter_plain(tuple(one.astype(jnp.bfloat16) for one in grads_a + grads_b))
    final_in_a, final_mid_a, final_out_a, final_proj_a, final_in_b, final_mid_b, final_out_b = (
        one.astype(jnp.float32) for one in finals
    )
    return (
        result.astype(jnp.bfloat16),
        grad_inputs.astype(jnp.bfloat16),
        final_in_a,
        final_mid_a,
        final_out_a,
        final_proj_a,
        own_shard(norms_a[0]),
        own_shard(norms_a[1]),
        own_shard(norms_a[2]),
        own_shard(norms_a[3]),
        final_in_b,
        final_mid_b,
        final_out_b,
        own_shard(norms_b[0]),
        own_shard(norms_b[1]),
        own_shard(norms_b[2]),
    )


def solution(mesh):
    in_specs = (
        P((FSDP, DP), None, None, None),
        P((FSDP, DP)),
        P(),
        P((FSDP, DP)),
        P(FSDP, None),
        P(FSDP, None),
        P(FSDP, None),
        P(FSDP, None),
        P(None, FSDP),
        P(None, FSDP),
        P(None, FSDP),
        P(None, FSDP),
        P(FSDP, None),
        P(FSDP, None),
        P(FSDP, None),
        P(None, FSDP),
        P(None, FSDP),
        P(None, FSDP),
        P((FSDP, DP), None, None, None),
    )
    out_specs = (
        P((FSDP, DP), None, None, None),
        P((FSDP, DP), None, None, None),
        P(FSDP, None),
        P(FSDP, None),
        P(FSDP, None),
        P(FSDP, None),
        P(None, FSDP),
        P(None, FSDP),
        P(None, FSDP),
        P(None, FSDP),
        P(FSDP, None),
        P(FSDP, None),
        P(FSDP, None),
        P(None, FSDP),
        P(None, FSDP),
        P(None, FSDP),
    )
    step = body_fast if fits(mesh) else body
    return jax.shard_map(step, mesh=mesh, in_specs=in_specs, out_specs=out_specs, check_vma=False)
```
